32 devices in a mesh: ctx: 8 (over y, x, core), fsdp: 4 (over z).
Axes of the slice: x: 2, y: 2, z: 4, core: 2. Of those that a mesh axis runs over, the one named last changes fastest.
Arguments:
- tokens: bfloat16 [4, 2048, 1536], P('fsdp', 'ctx'), may hold values from -6 to 6
- doc_ids: int32 [4, 2048], P('fsdp', 'ctx'), may hold values from 0 to 8, as said below
- routes: int32 [4, 2048, 8], P('fsdp', 'ctx'), may hold values from 0 to 39, all different within a row
- slot_order: int32 [4, 2048, 8], P('fsdp', 'ctx'), may hold values from 0 to 2047, as said below
- norm1_gain: float32 [1536], replicated, may hold values from 0.5 to 1.5
- norm2_gain: float32 [1536], replicated, may hold values from 0.5 to 1.5
- w_query: bfloat16 [1536, 1536], P('fsdp'), may hold values from -0.15625 to 0.15625
- key_matrix: bfloat16 [1536, 512], P('fsdp'), may hold values from -0.15625 to 0.15625
- value_matrix: bfloat16 [1536, 512], P('fsdp'), may hold values from -0.15625 to 0.15625
- w_out: bfloat16 [1536, 1536], P('fsdp'), may hold values from -2.5 to 2.5
- w_router: bfloat16 [1536, 40], P('fsdp'), may hold values from -0.078125 to 0.078125
- w_gate: bfloat16 [8, 1536, 512], P(None, 'fsdp'), may hold values from -0.15625 to 0.15625
- w_up: bfloat16 [8, 1536, 512], P(None, 'fsdp'), may hold values from -0.15625 to 0.15625
- w_down: bfloat16 [8, 512, 1536], P(None, 'fsdp'), may hold values from -2 to 2
- cotangent: bfloat16 [4, 2048, 1536], P('fsdp', 'ctx'), may hold values from -6 to 6
Outputs:
- output: bfloat16 [4, 2048, 1536], P('fsdp', 'ctx')
- input_grad: float32 [4, 2048, 1536], P('fsdp', 'ctx')
- grad_norm1: float32 [1536], P('fsdp')
- grad_norm2: float32 [1536], P('fsdp')
- grad_w_query: float32 [1536, 1536], P('fsdp')
- grad_w_key: float32 [1536, 512], P('fsdp')
- grad_w_value: float32 [1536, 512], P('fsdp')
- grad_w_out: float32 [1536, 1536], P('fsdp')
- grad_w_router: float32 [1536, 40], P('fsdp')
- grad_w_gate: float32 [8, 1536, 512], P(None, 'fsdp')
- grad_w_up: float32 [8, 1536, 512], P(None, 'fsdp')
- grad_w_down: float32 [8, 512, 1536], P(None, 'fsdp')
The draws below stay inside these ranges and needn't reach their ends.
Inputs may be any that keep to these rules, and one draw needn't show every extreme that they name: `doc_ids`: along each stream the document numbers never fall and begin at 0; one document begins within the first 256 tokens and ends within the last 256 tokens. `slot_order`: within each aligned block of 256 tokens of a stream the 2048 entries are a permutation.
All inputs are finite; a program needn't handle non-finite values.
Results may differ from the reference program's by a relative error of at most 0.025.
Values may be sent and summed in bfloat16 or wider, within the bound.
A program may use at most 320 MiB of HBM per device.

```python
import jax
import jax.numpy as jnp
from jax import lax

MODEL_DIM = 1536
QUERY_HEADS = 24
KEY_VALUE_HEADS = 8
HEAD_DIM = 64
FE = 512
EXPERTS = 40
TOPK = 8
EXP_WIN = 8
TOK_DEV = 256
STREAMS = 4
STREAM_LENGTH = 2048
CAP = 64


def draw_doc_ids(key, part):
    key = jax.random.fold_in(key, 11)
    sub_keys = jax.random.split(key, 4)
    length = STREAM_LENGTH
    long_start = jax.random.randint(sub_keys[0], (STREAMS, 1), 2, TOK_DEV)
    long_end = length - jax.random.randint(sub_keys[1], (STREAMS, 1), 2, TOK_DEV)
    early_cuts = jax.random.randint(sub_keys[2], (STREAMS, 3), 1, long_start)
    late_cuts = jax.random.randint(sub_keys[3], (STREAMS, 3), long_end + 1, length)
    positions = jnp.arange(length, dtype=jnp.int32)[None, :]
    numbers = (positions >= long_start).astype(jnp.int32) + (positions >= long_end).astype(jnp.int32)
    numbers = numbers + jnp.sum((positions[:, :, None] >= early_cuts[:, None, :]).astype(jnp.int32), axis=2)
    numbers = numbers + jnp.sum((positions[:, :, None] >= late_cuts[:, None, :]).astype(jnp.int32), axis=2)
    return numbers.astype(jnp.int32)


def draw_slot_order(key, part):
    key = jax.random.fold_in(key, 23)
    block_count = STREAMS * (STREAM_LENGTH // TOK_DEV)
    block_keys = jax.random.split(key, block_count)
    orders = jax.vmap(lambda block_key: jax.random.permutation(block_key, TOK_DEV * TOPK))(block_keys)
    return orders.reshape(STREAMS, STREAM_LENGTH, TOPK).astype(jnp.int32)


def steps_of(stream_key, extent, shards, least, top_value):
    level, own = 1.0, jax.random.fold_in(stream_key, 6)
    for axis_at, parts in shards:
        draws = jnp.exp(jax.random.uniform(jax.random.fold_in(own, axis_at), (parts,), jnp.float32, least / len(shards), top_value / len(shards)))
        level = level * jnp.repeat(draws, extent[axis_at] // parts).reshape([-1 if axis == axis_at else 1 for axis in range(len(extent))])
    return level


def different_ones(stream_key, rows, count, top, lift):
    order = jax.random.permutation(jax.random.fold_in(stream_key, 1), count)
    pull = order
    for power in range(3):
        pull = pull * pull // count
    pull = pull * lift // count
    tickets = jax.random.randint(jax.random.fold_in(stream_key, 2), (rows, count), 0, 4096) + pull
    fixed_rows = jax.random.permutation(jax.random.fold_in(stream_key, 3), rows)[jnp.arange(count) % rows]
    tickets = jnp.where(jnp.arange(rows)[:, None] == fixed_rows[None, :], 1 << 14, tickets)
    score = tickets * count + jnp.arange(count)
    return lax.top_k(score.astype(jnp.int32), top)[1].astype(jnp.int32)


def centred(own_key, extent, scale, most, cuts=(), kind=jnp.bfloat16):
    values = jax.random.normal(own_key, extent, jnp.float32) * scale
    if len(cuts) > 0:
        values = steps_of(own_key, extent, cuts, -0.22, 0.18) * values
    return jnp.clip(values, min=-most, max=most).astype(kind)


def setup_inputs(seed: int = 0) -> dict:
    key_of = jax.random.split(jax.random.key(seed), 16)
    tokens = centred(key_of[0], (STREAMS, STREAM_LENGTH, MODEL_DIM), 1.0, 6.0, ((0, 4), (1, 8)))
    doc_ids = draw_doc_ids(jax.random.fold_in(key_of[15], 71), 0)
    routes = different_ones(key_of[2], STREAMS * STREAM_LENGTH, EXPERTS, TOPK, 1638).reshape((STREAMS, STREAM_LENGTH, TOPK))
    slot_order = draw_slot_order(jax.random.fold_in(key_of[15], 71), 0)
    norm1_gain = jnp.clip(1.0 + 0.1 * jax.random.normal(key_of[4], (MODEL_DIM,), jnp.float32), 0.5, 1.5)
    norm2_gain = jnp.clip(1.0 + 0.1 * jax.random.normal(key_of[5], (MODEL_DIM,), jnp.float32), 0.5, 1.5)
    w_query = centred(key_of[6], (MODEL_DIM, QUERY_HEADS * HEAD_DIM), MODEL_DIM ** -0.5, 0.15625, ((0, 4),))
    key_matrix = centred(key_of[7], (MODEL_DIM, KEY_VALUE_HEADS * HEAD_DIM), MODEL_DIM ** -0.5, 0.15625, ((0, 4),))
    value_matrix = centred(key_of[8], (MODEL_DIM, KEY_VALUE_HEADS * HEAD_DIM), MODEL_DIM ** -0.5, 0.15625, ((0, 4),))
    w_out = centred(key_of[9], (QUERY_HEADS * HEAD_DIM, MODEL_DIM), (max(QUERY_HEADS * HEAD_DIM // 256, 1)) ** -0.5, 2.5, ((0, 4),))
    w_router = centred(key_of[10], (MODEL_DIM, EXPERTS), (4 * MODEL_DIM) ** -0.5, 0.078125, ((0, 4),))
    w_gate = centred(key_of[11], (EXP_WIN, MODEL_DIM, FE), MODEL_DIM ** -0.5, 0.15625, ((1, 4),))
    w_up = centred(key_of[12], (EXP_WIN, MODEL_DIM, FE), MODEL_DIM ** -0.5, 0.15625, ((1, 4),))
    w_down = centred(key_of[13], (EXP_WIN, FE, MODEL_DIM), (max(FE // 64, 1)) ** -0.5, 2.0, ((1, 4),))
    cotangent = centred(key_of[14], (STREAMS, STREAM_LENGTH, MODEL_DIM), 1.0, 6.0, ((0, 4), (1, 8)))
    return {"tokens": tokens, "doc_ids": doc_ids, "routes": routes, "slot_order": slot_order, "norm1_gain": norm1_gain, "norm2_gain": norm2_gain, "w_query": w_query, "key_matrix": key_matrix, "value_matrix": value_matrix, "w_out": w_out, "w_router": w_router, "w_gate": w_gate, "w_up": w_up, "w_down": w_down, "cotangent": cotangent}


epsilon = 1e-06
score_masked = -1e+30
highest = lax.Precision.HIGHEST

@jax.custom_vjp
def reduced_precision(v):
    return lax.optimization_barrier(v.astype(jnp.bfloat16)).astype(jnp.float32)

@jax.custom_vjp
def reduced_backward(v):
    return v

def low_keep(v):
    return (reduced_precision(v), None)

def low_pass(kept, grad):
    return (grad,)

def back_keep(v):
    return (v, None)

def back_low(kept, grad):
    return (reduced_precision(grad),)
reduced_precision.defvjp(low_keep, low_pass)
reduced_backward.defvjp(back_keep, back_low)

def precise_product(left, right):
    return jnp.dot(left, right, precision=highest, preferred_element_type=jnp.float32)

def rotary_embed(value_rows_all, cosine_lookup, sine_lookup):
    half_width = value_rows_all.shape[-1] // 2
    leading = value_rows_all[..., :half_width]
    trailing = value_rows_all[..., half_width:]
    return jnp.concatenate([leading * cosine_lookup - trailing * sine_lookup, trailing * cosine_lookup + leading * sine_lookup], axis=-1)

def rotary_tables(positions):
    frequencies = 10000.0 ** (-(jnp.arange(HEAD_DIM // 2, dtype=jnp.float32) * 2.0) / HEAD_DIM)
    angles = positions[:, None] * frequencies[None, :]
    return (jnp.cos(angles)[:, None, :], jnp.sin(angles)[:, None, :])

def rms_norm(value_rows_all, gain):
    scaling = lax.rsqrt(lax.optimization_barrier(jnp.mean(value_rows_all * value_rows_all, axis=-1, keepdims=True)) + epsilon)
    return value_rows_all * scaling * gain

def slot_tables(route_block, order_block):
    pair_count = TOK_DEV * TOPK
    experts_flat = route_block.reshape(pair_count)
    priority = order_block.reshape(pair_count)
    by_rank = jnp.zeros((pair_count,), jnp.int32).at[priority].set(jnp.arange(pair_count, dtype=jnp.int32))
    ranked = experts_flat[by_rank]
    onehot = (ranked[:, None] == jnp.arange(EXP_WIN, dtype=jnp.int32)[None, :]).astype(jnp.int32)
    before = jnp.cumsum(onehot, axis=0) - onehot
    slot_ranked = lax.optimization_barrier(jnp.sum(before * onehot, axis=1))
    slot_of_pair = jnp.zeros((pair_count,), jnp.int32).at[by_rank].set(slot_ranked)
    kept_pairs = (experts_flat < EXP_WIN) & (slot_of_pair < CAP)
    target = jnp.where(kept_pairs, experts_flat * CAP + slot_of_pair, EXP_WIN * CAP)
    slot_table = jnp.full((EXP_WIN * CAP,), -1, jnp.int32).at[target].set(jnp.arange(pair_count, dtype=jnp.int32), mode='drop')
    return slot_table.reshape(EXP_WIN, CAP)

def attend(query_rows, keys, value_rows_all, documents):
    block_rows = min(512, STREAM_LENGTH)
    key_positions = jnp.arange(STREAM_LENGTH, dtype=jnp.int32)

    def one_block(block_index):
        block_start = block_index * block_rows
        query_block = lax.dynamic_slice_in_dim(query_rows, block_start, block_rows, 0)
        query_docs = lax.dynamic_slice_in_dim(documents, block_start, block_rows, 0)
        query_positions = block_start + jnp.arange(block_rows, dtype=jnp.int32)
        scores = reduced_backward(jnp.einsum('qhgd,khd->hgqk', query_block, keys, precision=highest) * HEAD_DIM ** (-0.5))
        visible = (query_docs[:, None] == documents[None, :]) & (key_positions[None, :] <= query_positions[:, None])
        probabilities = jax.nn.softmax(jnp.where(visible, scores, score_masked), axis=-1)
        return jnp.einsum('hgqk,khd->qhgd', reduced_precision(probabilities), value_rows_all, precision=highest)
    blocks_out = lax.map(jax.checkpoint(one_block), jnp.arange(STREAM_LENGTH // block_rows, dtype=jnp.int32))
    return blocks_out.reshape(STREAM_LENGTH, QUERY_HEADS * HEAD_DIM)

def experts_block(normed, gate_block, slot_table, w_gate, w_up, w_down):
    usable = slot_table >= 0
    pair_index = jnp.maximum(slot_table, 0)
    token_index = pair_index // TOPK
    buffer_rows = jnp.where(usable[..., None], normed[token_index], 0.0)
    gate_in = reduced_backward(jnp.einsum('ecd,edf->ecf', buffer_rows, w_gate, precision=highest))
    up_in = reduced_backward(jnp.einsum('ecd,edf->ecf', buffer_rows, w_up, precision=highest))
    activation = reduced_precision(jax.nn.silu(gate_in) * up_in)
    expert_out = reduced_backward(jnp.einsum('ecf,efd->ecd', activation, w_down, precision=highest))
    slot_gates = jnp.where(usable, gate_block[pair_index], 0.0)
    return jnp.zeros((TOK_DEV, MODEL_DIM), jnp.float32).at[token_index.reshape(-1)].add((expert_out * slot_gates[..., None]).reshape(-1, MODEL_DIM))

def layer_forward(stream, documents, route_rows, tables, gain1, gain2, w_query, key_matrix, value_matrix, w_out, w_router, w_gate, w_up, w_down):
    query_group_width = QUERY_HEADS // KEY_VALUE_HEADS
    cosine_lookup, sine_lookup = rotary_tables(jnp.arange(STREAM_LENGTH, dtype=jnp.int32).astype(jnp.float32))
    first_normalized = reduced_precision(rms_norm(stream, gain1))
    query_linear = reduced_backward(precise_product(first_normalized, w_query)).reshape(STREAM_LENGTH, QUERY_HEADS, HEAD_DIM)
    key_linear = reduced_backward(precise_product(first_normalized, key_matrix)).reshape(STREAM_LENGTH, KEY_VALUE_HEADS, HEAD_DIM)
    value_rows_all = reduced_backward(reduced_precision(precise_product(first_normalized, value_matrix))).reshape(STREAM_LENGTH, KEY_VALUE_HEADS, HEAD_DIM)
    query_rows = reduced_precision(rotary_embed(query_linear, cosine_lookup, sine_lookup)).reshape(STREAM_LENGTH, KEY_VALUE_HEADS, query_group_width, HEAD_DIM)
    keys = reduced_precision(rotary_embed(key_linear, cosine_lookup, sine_lookup))
    attended = reduced_backward(reduced_precision(attend(query_rows, keys, value_rows_all, documents)))
    residual = stream + reduced_backward(precise_product(attended, w_out))
    normed2 = reduced_precision(rms_norm(residual, gain2))
    logits = reduced_backward(precise_product(normed2, w_router))
    gate_weights = jax.nn.softmax(jnp.take_along_axis(logits, route_rows, axis=1), axis=-1)
    blocks = STREAM_LENGTH // TOK_DEV
    expert_mix = jax.vmap(experts_block, in_axes=(0, 0, 0, None, None, None))(normed2.reshape(blocks, TOK_DEV, MODEL_DIM), gate_weights.reshape(blocks, TOK_DEV * TOPK), tables, w_gate, w_up, w_down)
    return residual + expert_mix.reshape(STREAM_LENGTH, MODEL_DIM)

def reference(tokens, doc_ids, routes, slot_order, norm1_gain, norm2_gain, w_query, key_matrix, value_matrix, w_out, w_router, w_gate, w_up, w_down, cotangent):
    blocks = STREAM_LENGTH // TOK_DEV
    tables = jax.vmap(slot_tables)(routes.reshape(STREAMS * blocks, TOK_DEV, TOPK), slot_order.reshape(STREAMS * blocks, TOK_DEV, TOPK)).reshape(STREAMS, blocks, EXP_WIN, CAP)
    params = tuple((weight.astype(jnp.float32) for weight in (norm1_gain, norm2_gain, w_query, key_matrix, value_matrix, w_out, w_router, w_gate, w_up, w_down)))

    def forward(inputs, gain1, gain2, query_w, key_w, value_w, out_w, router_w, gate_w, up_w, down_w):
        return lax.map(lambda stream_data: layer_forward(stream_data[0], stream_data[1], stream_data[2], stream_data[3], gain1, gain2, query_w, key_w, value_w, out_w, router_w, gate_w, up_w, down_w), (inputs, doc_ids, routes, tables))
    result, pullback = jax.vjp(forward, tokens.astype(jnp.float32), *params)
    gradients = pullback(cotangent.astype(jnp.float32))
    return (result.astype(jnp.bfloat16), gradients[0], gradients[1], gradients[2], gradients[3], gradients[4], gradients[5], gradients[6], gradients[7], gradients[8], gradients[9], gradients[10])
```

```python
import functools

import jax
import jax.numpy as jnp
from jax import lax
from jax.experimental import pallas as pl
from jax.experimental.pallas import tpu as pltpu
from jax.sharding import PartitionSpec as P

QUERY_HEADS = 24
KEY_VALUE_HEADS = 8
HEAD_DIM = 64
TOPK = 8
EXP_WIN = 8
TOK_DEV = 256
CAP = 64
GROUP = 8
HEADS = QUERY_HEADS // KEY_VALUE_HEADS
QW = HEADS * HEAD_DIM
HW = QW + 2 * HEAD_DIM

epsilon = 1e-06
score_masked = -1e30
bf16 = jnp.bfloat16
f32 = jnp.float32
VMEM = pltpu.VMEM


def dot(left, right, dims=((1,), (0,))):
    return lax.dot_general(left, right, (dims, ((), ())), preferred_element_type=f32)


def block(index, size=TOK_DEV):
    return pl.ds(pl.multiple_of(index * size, size), size)

def attend_forward(n_blocks, first_ref, q_ref, k_ref, v_ref, docs_row_ref, docs_col_ref,
                   o_ref, lse_ref, vt_ref, top_ref, sum_ref, acc_ref):
    T = TOK_DEV
    first = first_ref[0]

    def turn(i, _):
        vt_ref[:, block(i)] = v_ref[block(i), :].T
        return 0
    lax.fori_loop(0, n_blocks, turn, 0)

    def tile(kb, qb, mask):
        kt = k_ref[block(kb), :]
        vt = vt_ref[:, block(kb)]
        heads = range(HEADS)
        parts = [slice(h * 64, (h + 1) * 64) for h in heads]
        s = [dot(kt, q_ref[block(qb), parts[h]], ((1,), (1,))) for h in heads]
        if mask is not None:
            s = [jnp.where(mask, x, score_masked) for x in s]
        old = [top_ref[h:h + 1, :] for h in heads]
        new = [jnp.maximum(old[h], jnp.max(s[h], axis=0, keepdims=True)) for h in heads]
        p = [jnp.exp(s[h] - new[h]) for h in heads]
        factor = [jnp.exp(old[h] - new[h]) for h in heads]
        total = [sum_ref[h:h + 1, :] * factor[h] + jnp.sum(p[h], axis=0, keepdims=True) for h in heads]
        mixed = [acc_ref[parts[h], :] * factor[h] + dot(vt, p[h].astype(bf16)) for h in heads]
        for h in heads:
            top_ref[h:h + 1, :] = new[h]
            sum_ref[h:h + 1, :] = total[h]
            acc_ref[parts[h], :] = mixed[h]

    def same(kb, gq):
        return docs_col_ref[block(kb), :] == docs_row_ref[:, block(gq)]

    def q_block(qb, _):
        gq = first + qb
        top_ref[...] = jnp.full_like(top_ref, score_masked)
        sum_ref[...] = jnp.zeros_like(sum_ref)
        acc_ref[...] = jnp.zeros_like(acc_ref)
        last = gq == n_blocks - 1

        def k_block(kb, _):
            edge = jnp.logical_or(kb == 0, last)

            @pl.when(edge)
            def _():
                tile(kb, qb, same(kb, gq))

            @pl.when(jnp.logical_not(edge))
            def _():
                tile(kb, qb, None)
            return 0

        lax.fori_loop(0, gq, k_block, 0)
        keys = lax.broadcasted_iota(jnp.int32, (T, T), 0)
        queries = lax.broadcasted_iota(jnp.int32, (T, T), 1)
        tile(gq, qb, same(gq, gq) & (keys <= queries))
        lse_ref[qb] = top_ref[...] + jnp.log(sum_ref[...])
        for h in range(HEADS):
            part = slice(h * 64, (h + 1) * 64)
            acc_ref[part, :] = acc_ref[part, :] / sum_ref[h:h + 1, :]
        o_ref[block(qb), :] = acc_ref[...].T
        return 0

    lax.fori_loop(0, GROUP, q_block, 0)


def attend_backward(n_blocks, first_ref, q_ref, k_ref, v_ref, do_ref, o_ref, lse_ref,
                    docs_row_ref, docs_col_ref, dq_ref, dk_ref, dv_ref,
                    kt_ref, dqt_ref, delta_ref):
    T = TOK_DEV
    first = first_ref[0]
    rows = lax.broadcasted_iota(jnp.int32, (8, QW), 0)
    lanes = lax.broadcasted_iota(jnp.int32, (8, QW), 1)
    pick = jnp.where((lanes >= rows * 64) & (lanes < rows * 64 + 64), 1.0, 0.0).astype(bf16)

    def turn(i, _):
        kt_ref[:, block(i)] = k_ref[block(i), :].T
        return 0
    lax.fori_loop(0, n_blocks, turn, 0)

    def prepare(i, _):
        product = o_ref[block(i), :] * do_ref[block(i), :].astype(f32)
        high = product.astype(bf16)
        low = (product - high.astype(f32)).astype(bf16)
        delta_ref[i] = dot(pick, high, ((1,), (1,))) + dot(pick, low, ((1,), (1,)))
        return 0
    lax.fori_loop(0, GROUP, prepare, 0)
    dqt_ref[...] = jnp.zeros_like(dqt_ref)

    def tile(kb, qb, mask):
        kt = k_ref[block(kb), :]
        vt = v_ref[block(kb), :]
        k_turned = kt_ref[:, block(kb)]
        heads = range(HEADS)
        parts = [slice(h * 64, (h + 1) * 64) for h in heads]
        q = [q_ref[block(qb), part] for part in parts]
        do = [do_ref[block(qb), part] for part in parts]
        s = [dot(kt, x, ((1,), (1,))) for x in q]
        dp = [dot(vt, x, ((1,), (1,))) for x in do]
        p = [jnp.exp(s[h] - lse_ref[qb, h:h + 1, :]) for h in heads]
        if mask is not None:
            p = [jnp.where(mask, x, 0.0) for x in p]
        ds = [(p[h] * (dp[h] - delta_ref[qb, h:h + 1, :])).astype(bf16) for h in heads]
        pb = [x.astype(bf16) for x in p]
        dv_ref[block(kb), :] += dot(pb[0], do[0]) + dot(pb[1], do[1]) + dot(pb[2], do[2])
        dk_ref[block(kb), :] += dot(ds[0], q[0]) + dot(ds[1], q[1]) + dot(ds[2], q[2])
        for h in heads:
            dqt_ref[parts[h], block(qb)] += dot(k_turned, ds[h])

    def same(kb, gq):
        return docs_col_ref[block(kb), :] == docs_row_ref[:, block(gq)]

    def k_block(kb, _):
        dk_ref[block(kb), :] = jnp.zeros((T, HEAD_DIM), f32)
        dv_ref[block(kb), :] = jnp.zeros((T, HEAD_DIM), f32)

        @pl.when(kb >= first)
        def _():
            keys = lax.broadcasted_iota(jnp.int32, (T, T), 0)
            queries = lax.broadcasted_iota(jnp.int32, (T, T), 1)
            tile(kb, kb - first, same(kb, kb) & (keys <= queries))

        def q_block(qb, _):
            gq = first + qb
            edge = jnp.logical_or(kb == 0, gq == n_blocks - 1)

            @pl.when(edge)
            def _():
                tile(kb, qb, same(kb, gq))

            @pl.when(jnp.logical_not(edge))
            def _():
                tile(kb, qb, None)
            return 0

        lax.fori_loop(jnp.maximum(kb - first + 1, 0), GROUP, q_block, 0)
        return 0

    lax.fori_loop(0, first + GROUP, k_block, 0)

    def finish(i, _):
        dq_ref[block(i), :] = dqt_ref[:, block(i)].T
        return 0
    lax.fori_loop(0, GROUP, finish, 0)

    def clear(kb, _):
        dk_ref[block(kb), :] = jnp.zeros((T, HEAD_DIM), f32)
        dv_ref[block(kb), :] = jnp.zeros((T, HEAD_DIM), f32)
        return 0
    lax.fori_loop(first + GROUP, n_blocks, clear, 0)


def forward_call(first, q, k, v, docs):
    n = k.shape[0] // TOK_DEV
    span = q.shape[0]
    v_spec = pl.BlockSpec(memory_space=VMEM)
    return pl.pallas_call(
        functools.partial(attend_forward, n),
        out_shape=(jax.ShapeDtypeStruct((span, QW), f32), jax.ShapeDtypeStruct((GROUP, 8, TOK_DEV), f32)),
        in_specs=[pl.BlockSpec(memory_space=pltpu.SMEM)] + [v_spec] * 5,
        out_specs=(v_spec, v_spec),
        scratch_shapes=[VMEM((64, n * TOK_DEV), bf16), VMEM((8, TOK_DEV), f32), VMEM((8, TOK_DEV), f32), VMEM((QW, TOK_DEV), f32)],
        compiler_params=pltpu.CompilerParams(vmem_limit_bytes=56 << 20),
        name="attend_forward",
    )(first, q, k, v, docs[None, :], docs[:, None])

def backward_call(first, q, k, v, do, o, lse, docs):
    n = k.shape[0] // TOK_DEV
    span = q.shape[0]
    v_spec = pl.BlockSpec(memory_space=VMEM)
    return pl.pallas_call(
        functools.partial(attend_backward, n),
        out_shape=(jax.ShapeDtypeStruct((span, QW), f32), jax.ShapeDtypeStruct((n*TOK_DEV, 64), f32), jax.ShapeDtypeStruct((n*TOK_DEV, 64), f32)),
        in_specs=[pl.BlockSpec(memory_space=pltpu.SMEM)] + [v_spec] * 8,
        out_specs=(v_spec, v_spec, v_spec),
        scratch_shapes=[VMEM((64, n * TOK_DEV), bf16), VMEM((QW, span), f32), VMEM((GROUP, 8, TOK_DEV), f32)],
        compiler_params=pltpu.CompilerParams(vmem_limit_bytes=56 << 20),
        name="attend_backward",
    )(first, q, k, v, do, o, lse, docs[None, :], docs[:, None])


def rotary_tables(positions):
    frequencies = 10000.0 ** (-(jnp.arange(HEAD_DIM // 2, dtype=f32) * 2.0) / HEAD_DIM)
    angles = positions[:, None] * frequencies[None, :]
    return jnp.cos(angles)[:, None, :], jnp.sin(angles)[:, None, :]


def rotate(values, cosine, sine):
    half = values.shape[-1] // 2
    lead, trail = values[..., :half], values[..., half:]
    return jnp.concatenate(
        [lead * cosine - trail * sine, trail * cosine + lead * sine], axis=-1
    )


def norm_backward(rows, scaling, gain, grad_out):
    scaled = grad_out * gain
    inner_mean = jnp.mean(scaled * rows, axis=-1, keepdims=True)
    grad_in = scaling * scaled - rows * scaling * scaling * scaling * inner_mean
    grad_gain = jnp.sum(grad_out * rows * scaling, axis=0)
    return grad_in, grad_gain


def shards(
    tokens,
    doc_ids,
    routes,
    slot_order,
    norm1_gain,
    norm2_gain,
    w_query,
    key_matrix,
    value_matrix,
    w_out,
    w_router,
    w_gate,
    w_up,
    w_down,
    cotangent,
):
    rows = tokens.shape[1]
    width = tokens.shape[2]
    ctx = lax.axis_size("ctx")
    place = lax.axis_index("ctx")
    parts = ctx // GROUP
    head, part = place % GROUP, place // GROUP
    near = [[p * GROUP + i for i in range(GROUP)] for p in range(parts)] if parts > 1 else None
    far = [[p * GROUP + i for p in range(parts)] for i in range(GROUP)]
    span = GROUP * rows

    def swap(value):
        return lax.all_to_all(value, "ctx", 0, 0, axis_index_groups=near, tiled=True)

    def gather_near(value, axis=0):
        return lax.all_gather(value, "ctx", axis=axis, axis_index_groups=near, tiled=True)

    def gather_z(value):
        return lax.all_gather(value, "fsdp", axis=0, tiled=True)

    def reduce_z(value):
        value = lax.psum_scatter(value.astype(bf16), "fsdp", scatter_dimension=0, tiled=True)
        if parts > 1:
            value = lax.psum(value, "ctx", axis_index_groups=far)
        return value

    def own(weight, size):
        return lax.dynamic_slice_in_dim(weight, head * size, size, 1)

    weight_h = gather_z(
        jnp.concatenate(
            [own(w_query, QW), own(key_matrix, HEAD_DIM), own(value_matrix, HEAD_DIM)], axis=1
        )
    )
    out_h = gather_z(own(w_out, w_out.shape[1] // GROUP))
    router = gather_z(w_router)
    gate_up = gather_z(
        jnp.concatenate(
            [
                lax.dynamic_index_in_dim(w_gate, head, 0, False),
                lax.dynamic_index_in_dim(w_up, head, 0, False),
            ],
            axis=1,
        )
    )
    down = gather_z(lax.dynamic_index_in_dim(w_down, head, 0, False))

    x = tokens[0].astype(f32)
    scale1 = lax.rsqrt(jnp.mean(x * x, axis=-1, keepdims=True) + epsilon)
    normed1 = (x * scale1 * norm1_gain).astype(bf16)
    normed1_all = gather_near(normed1)
    linear = dot(normed1_all, weight_h)
    positions = (part * span + jnp.arange(span, dtype=jnp.int32)).astype(f32)
    cosine, sine = rotary_tables(positions)
    scaling = HEAD_DIM ** (-0.5)
    queries = rotate(linear[:, :QW].reshape(span, HEADS, HEAD_DIM), cosine, sine) * scaling
    queries = queries.astype(bf16).reshape(span, QW)
    keys = rotate(linear[:, QW : QW + HEAD_DIM].reshape(span, 1, HEAD_DIM), cosine, sine)
    keys = keys.astype(bf16)[:, 0]
    values = linear[:, QW + HEAD_DIM :].astype(bf16)

    documents = lax.all_gather(doc_ids, "ctx", axis=1, tiled=True)[0]
    if parts > 1:
        keys_all = lax.all_gather(keys, "ctx", axis_index_groups=far, tiled=True)
        values_all = lax.all_gather(values, "ctx", axis_index_groups=far, tiled=True)
    else:
        keys_all, values_all = keys, values
    first = jnp.reshape(part * GROUP, (1,)).astype(jnp.int32)
    attended_f32, log_total = forward_call(first, queries, keys_all, values_all, documents)
    attended_h = attended_f32.astype(bf16)

    attended = swap(attended_h.reshape(GROUP, rows, QW))
    attended = jnp.transpose(attended, (1, 0, 2)).reshape(rows, QUERY_HEADS * HEAD_DIM)
    out_weight = gather_near(out_h, axis=1)
    residual = x + dot(attended, out_weight)
    scale2 = lax.rsqrt(jnp.mean(residual * residual, axis=-1, keepdims=True) + epsilon)
    normed2 = (residual * scale2 * norm2_gain).astype(bf16)
    logits = dot(normed2, router)
    experts = router.shape[1]
    route_rows, order_rows = routes[0], slot_order[0]
    picks = route_rows[:, :, None] == jnp.arange(experts, dtype=jnp.int32)[None, None, :]
    chosen = jnp.any(picks, axis=1)
    logits = jnp.where(chosen, logits, score_masked)
    gates = jnp.where(chosen, jnp.exp(logits - jnp.max(logits, axis=-1, keepdims=True)), 0.0)
    gates = gates / jnp.sum(gates, axis=-1, keepdims=True)

    never = jnp.int32(2**30)
    priority = jnp.min(
        jnp.where(picks[:, :, :EXP_WIN], order_rows[:, :, None], never), axis=1
    )
    earlier = jnp.sum(
        (priority[None, :, :] < priority[:, None, :]).astype(jnp.int32), axis=1
    )
    kept = (priority < never) & (earlier < CAP)
    slots = jnp.where(kept, earlier, -1)
    placed = (
        slots.T[:, None, :] == jnp.arange(CAP, dtype=jnp.int32)[None, :, None]
    ).astype(bf16)
    placed = placed.reshape(EXP_WIN * CAP, rows)
    slot_gates = jnp.sum(
        jnp.where(
            placed.reshape(EXP_WIN, CAP, rows) > 0, gates[:, :EXP_WIN].T[:, None, :], 0.0
        ),
        axis=-1,
    ).reshape(EXP_WIN * CAP, 1)

    grad_final = cotangent[0].astype(f32)
    sent_rows = dot(placed, normed2).astype(bf16)
    routed_grad = dot(placed, cotangent[0])
    sent_grads = (routed_grad * slot_gates).astype(bf16)
    both = jnp.concatenate(
        [sent_rows.reshape(GROUP, CAP, width), sent_grads.reshape(GROUP, CAP, width)], axis=1
    )
    both = swap(both)
    buffer_rows = both[:, :CAP].reshape(GROUP * CAP, width)
    grad_rows = both[:, CAP:].reshape(GROUP * CAP, width)

    hidden = down.shape[0]
    gate_up_in = dot(buffer_rows, gate_up)
    gate_in, up_in = gate_up_in[:, :hidden], gate_up_in[:, hidden:]
    sigmoid_gate = jax.nn.sigmoid(gate_in)
    activation = (gate_in * sigmoid_gate * up_in).astype(bf16)
    expert_out = dot(activation, down)
    grad_activation = dot(grad_rows, down, ((1,), (1,)))
    grad_gate_in = grad_activation * up_in * sigmoid_gate * (1.0 + gate_in * (1.0 - sigmoid_gate))
    grad_up_in = grad_activation * gate_in * sigmoid_gate
    grad_gate_up = jnp.concatenate([grad_gate_in, grad_up_in], axis=1).astype(bf16)
    grad_buffer = dot(grad_gate_up, gate_up, ((1,), (1,)))
    back = jnp.concatenate(
        [
            expert_out.astype(bf16).reshape(GROUP, CAP, width),
            grad_buffer.astype(bf16).reshape(GROUP, CAP, width),
        ],
        axis=1,
    )
    back = swap(back)
    grad_w_gate_up = reduce_z(dot(buffer_rows, grad_gate_up, ((0,), (0,))))
    grad_w_down = reduce_z(dot(activation, grad_rows, ((0,), (0,))))

    out_rows = back[:, :CAP].reshape(EXP_WIN * CAP, width).astype(f32)
    grad_back = back[:, CAP:].reshape(EXP_WIN * CAP, width)
    mix = dot(placed, (out_rows * slot_gates).astype(bf16), ((0,), (0,)))
    output = (residual + mix).astype(bf16)
    slot_grad = jnp.sum(routed_grad * out_rows, axis=-1, keepdims=True)
    grad_gates = jnp.sum(
        jnp.where(placed > 0, slot_grad, 0.0).reshape(EXP_WIN, CAP, rows), axis=1
    ).T
    grad_gates = jnp.pad(grad_gates, ((0, 0), (0, experts - EXP_WIN)))
    weighted_sum = jnp.sum(gates * grad_gates, axis=-1, keepdims=True)
    grad_logits = (gates * (grad_gates - weighted_sum)).astype(bf16)
    grad_normed2 = dot(placed, grad_back, ((0,), (0,))) + dot(grad_logits, router, ((1,), (1,)))
    grad_router = dot(normed2, grad_logits, ((0,), (0,)))
    grad_residual_in, grad_gain2 = norm_backward(residual, scale2, norm2_gain, grad_normed2)
    grad_residual = grad_final + grad_residual_in
    grad_attn = grad_residual.astype(bf16)
    grad_attended = dot(grad_attn, out_weight, ((1,), (1,))).astype(bf16)

    def by_head(value):
        return jnp.transpose(value.reshape(rows, GROUP, -1), (1, 0, 2))

    head_gradients = swap(by_head(grad_attended)).reshape(span, QW)
    grad_attn_columns = swap(by_head(grad_attn)).reshape(span, width // GROUP)
    attended_all = gather_near(attended_h, axis=1)
    grad_w_out = reduce_z(dot(attended_all, grad_attn_columns, ((0,), (0,))))

    grad_queries, grad_keys, grad_values = backward_call(
        first, queries, keys_all, values_all, head_gradients, attended_f32, log_total, documents
    )
    grad_queries = grad_queries.reshape(span, HEADS, HEAD_DIM)
    if parts > 1:
        grad_keys = lax.psum_scatter(grad_keys, "ctx", axis_index_groups=far, tiled=True)
        grad_values = lax.psum_scatter(grad_values, "ctx", axis_index_groups=far, tiled=True)
    grad_linear = jnp.concatenate(
        [
            rotate(grad_queries * scaling, cosine, -sine).reshape(span, QW),
            rotate(grad_keys[:, None], cosine, -sine)[:, 0],
            grad_values,
        ],
        axis=1,
    ).astype(bf16)
    grad_w_h = reduce_z(dot(normed1_all, grad_linear, ((0,), (0,))))
    grad_own = swap(grad_linear.reshape(GROUP, rows, HW))
    grad_own = jnp.transpose(grad_own, (1, 0, 2)).reshape(rows, GROUP * HW)
    weight_all = gather_near(weight_h, axis=1)
    grad_normed1 = dot(grad_own, weight_all, ((1,), (1,)))
    grad_input_in, grad_gain1 = norm_backward(x, scale1, norm1_gain, grad_normed1)
    input_grad = grad_residual + grad_input_in

    small = jnp.concatenate([grad_router, grad_gain1[:, None], grad_gain2[:, None]], axis=1)
    small = lax.psum_scatter(small, "fsdp", scatter_dimension=0, tiled=True)
    small = lax.psum(small, "ctx")

    def spread(value):
        return gather_near(value[None])

    heads_w = spread(grad_w_h).astype(f32)

    def columns(value):
        return jnp.transpose(value, (1, 0, 2)).reshape(value.shape[1], -1)

    gate_up_w = spread(grad_w_gate_up).astype(f32)
    return (
        output[None],
        input_grad[None],
        small[:, experts],
        small[:, experts + 1],
        columns(heads_w[:, :, :QW]),
        columns(heads_w[:, :, QW : QW + HEAD_DIM]),
        columns(heads_w[:, :, QW + HEAD_DIM :]),
        columns(spread(grad_w_out).astype(f32)),
        small[:, :experts],
        gate_up_w[:, :, :hidden],
        gate_up_w[:, :, hidden:],
        spread(grad_w_down).astype(f32),
    )


def solution(mesh):
    token_spec = P("fsdp", "ctx", None)
    row_spec, expert_spec = P("fsdp", None), P(None, "fsdp", None)
    return jax.shard_map(
        shards,
        mesh=mesh,
        in_specs=(
            token_spec,
            P("fsdp", "ctx"),
            token_spec,
            token_spec,
            P(),
            P(),
            row_spec,
            row_spec,
            row_spec,
            row_spec,
            row_spec,
            expert_spec,
            expert_spec,
            expert_spec,
            token_spec,
        ),
        out_specs=(
            token_spec,
            token_spec,
            P("fsdp"),
            P("fsdp"),
            row_spec,
            row_spec,
            row_spec,
            row_spec,
            row_spec,
            expert_spec,
            expert_spec,
            expert_spec,
        ),
        check_vma=False,
    )
```

```python
import functools

import jax
import jax.numpy as jnp
import numpy as np
from jax import lax
from jax.experimental import pallas as pl
from jax.experimental.pallas import tpu as pltpu
from jax.sharding import PartitionSpec as P

QUERY_HEADS = 24
KEY_VALUE_HEADS = 8
HEAD_DIM = 64
TOPK = 8
EXP_WIN = 8
TOK_DEV = 256
CAP = 64
GROUP = 8
HEADS = QUERY_HEADS // KEY_VALUE_HEADS
QW = HEADS * HEAD_DIM
HW = QW + 2 * HEAD_DIM
WIDE = HW + HEAD_DIM
ROUTER = HEAD_DIM
EXPERTS_MOST = 40
LANES = 128

epsilon = 1e-06
score_masked = -1e30
bf16 = jnp.bfloat16
f32 = jnp.float32
VMEM = pltpu.VMEM
MESH = pl.DeviceIdType.MESH
DMA = pltpu.SemaphoreType.DMA
IN_VMEM = pl.BlockSpec(memory_space=VMEM)
IN_ANY = pl.BlockSpec(memory_space=pl.ANY)


def dot(left, right, dims=((1,), (0,))):
    return lax.dot_general(left, right, (dims, ((), ())), preferred_element_type=f32)


def block(index, size=TOK_DEV):
    return pl.ds(pl.multiple_of(index * size, size), size)


def shape(dims, dtype):
    return jax.ShapeDtypeStruct(dims, dtype)


def params(collective_id=None, limit=56):
    return pltpu.CompilerParams(
        collective_id=collective_id,
        has_side_effects=collective_id is not None,
        vmem_limit_bytes=limit << 20,
    )


def flip(index, bit):
    return index + (1 - 2 * ((index // bit) % 2)) * bit


class Place:
    def __init__(self):
        ctx = lax.axis_index("ctx")
        self.base = (ctx // GROUP) * GROUP
        self.me = ctx - self.base
        self.z = lax.axis_index("fsdp")
        self.depth = lax.axis_size("fsdp")
        self.near = [flip(self.me, bit) for bit in (1, 2, 4)]

    def ctx(self, index):
        return {"ctx": self.base + index}

    def fsdp(self, index):
        return {"fsdp": index}

    def others(self):
        return [self.ctx(lax.rem(self.me + j, GROUP)) for j in range(1, GROUP)]

    def layers(self):
        return [self.fsdp(lax.rem(self.z + j, self.depth)) for j in range(1, self.depth)]


def greet(devices):
    ready = pltpu.get_barrier_semaphore()
    for device in devices:
        pl.semaphore_signal(ready, inc=1, device_id=device, device_id_type=MESH)
    pl.semaphore_wait(ready, len(devices))


def remote(source, target, send, receive, device):
    return pltpu.make_async_remote_copy(
        src_ref=source,
        dst_ref=target,
        send_sem=send,
        recv_sem=receive,
        device_id=device,
        device_id_type=MESH,
    )


class Spread:
    SEMS = 14

    def __init__(self, place, source, land, part, send, receive):
        me = place.me
        core, side, row = place.near
        across = flip(side, 4)

        def plan(slot, owner, half, device):
            target = part(land(owner), half)
            first = part(source, half) if slot < 6 else target
            return remote(first, target, send.at[slot], receive.at[slot], place.ctx(device))

        self.copies = [
            plan(0, me, 0, side), plan(1, me, 1, side), plan(2, me, 0, row), plan(3, me, 1, row),
            plan(4, me, 0, core), plan(5, me, 1, core), plan(6, side, 0, core),
            plan(7, side, 1, core), plan(8, row, 0, core), plan(9, row, 1, core),
            plan(10, side, 1, row), plan(11, row, 0, side), plan(12, across, 0, core),
            plan(13, across, 1, core),
        ]

    def go(self, *slots):
        for slot in slots:
            self.copies[slot].start()

    def wait(self, *slots):
        for slot in slots:
            self.copies[slot].wait_recv()

    def start(self):
        self.go(1, 2, 0, 3, 4, 5)

    def step1(self):
        self.wait(1)
        self.go(10, 7)
        self.wait(2)
        self.go(11, 8)

    def step2(self):
        self.wait(0)
        self.go(6)
        self.wait(3)
        self.go(9)

    def step3(self):
        self.wait(10)
        self.go(13)
        self.wait(11)
        self.go(12)

    def sent(self):
        for copy in self.copies:
            copy.wait_send()

    def last(self):
        self.wait(4, 5, 6, 7, 8, 9, 12, 13)


def turned(values, cosine, sine):
    lane = lax.broadcasted_iota(jnp.int32, values.shape, 1) % HEAD_DIM
    low = lane < HEAD_DIM // 2
    other = jnp.where(
        low, -pltpu.roll(values, LANES - HEAD_DIM // 2, 1), pltpu.roll(values, HEAD_DIM // 2, 1)
    )
    return values * cosine + other * sine


def project_kernel(
    tokens_ref, gain_ref, w_ref, w_out_ref, cos_ref, sin_ref, docs_ref,
    normed_ref, w_all_ref, w_out_all_ref, q_ref, k_ref, v_ref, docs_all_ref,
    z_send, z_recv, o_send, o_recv, d_send, d_recv, c_send, c_recv, local,
):
    place = Place()
    me, z = place.me, place.z
    strip = w_out_all_ref.shape[1]
    greet(place.others() + place.layers())
    own_out = w_out_ref.at[pl.ds(pl.multiple_of(me * strip, strip), strip), :]
    moves = [
        pltpu.make_async_copy(w_ref, w_all_ref.at[z], local.at[0]),
        pltpu.make_async_copy(own_out, w_out_all_ref.at[z], local.at[1]),
    ]
    for move in moves:
        move.start()
    weights = []
    for j, device in enumerate(place.layers()):
        weights.append(remote(w_ref, w_all_ref.at[z], z_send.at[j], z_recv.at[j], device))
        weights[-1].start()

    x = tokens_ref[...].astype(f32)
    scale = lax.rsqrt(jnp.mean(x * x, axis=-1, keepdims=True) + epsilon)
    normed_ref[me] = (x * scale * gain_ref[...]).astype(bf16)
    half = TOK_DEV // 2
    spread = Spread(
        place, normed_ref.at[me], lambda owner: normed_ref.at[owner],
        lambda ref, h: ref.at[pl.ds(h * half, half)], c_send, c_recv,
    )
    spread.start()
    docs_all_ref[me] = docs_ref[...]
    outs = []
    for j, device in enumerate(place.others()):
        outs.append(
            remote(docs_ref, docs_all_ref.at[me], d_send.at[j], d_recv.at[j], device)
        )
        outs[-1].start()
    for j, device in enumerate(place.layers()):
        outs.append(remote(own_out, w_out_all_ref.at[z], o_send.at[j], o_recv.at[j], device))
        outs[-1].start()
    for copy in weights:
        copy.wait_recv()
    moves[0].wait()

    def project(owner):
        weight = w_all_ref[...].reshape(-1, WIDE)
        linear = dot(normed_ref[owner], weight)
        cosine, sine = cos_ref[block(owner), :], sin_ref[block(owner), :]
        first = turned(linear[:, :LANES], cosine, sine) * HEAD_DIM ** (-0.5)
        second = turned(linear[:, LANES : 2 * LANES], cosine, sine)
        q_ref[block(owner), :LANES] = first.astype(bf16)
        q_ref[block(owner), LANES:] = (second[:, :HEAD_DIM] * HEAD_DIM ** (-0.5)).astype(bf16)
        k_ref[block(owner), :] = second[:, HEAD_DIM:].astype(bf16)
        v_ref[block(owner), :] = linear[:, 2 * LANES : HW].astype(bf16)

    core, side, row = place.near
    across = flip(side, 4)
    order = [me, core, side, row, flip(side, 1), flip(row, 1), across, flip(across, 1)]

    def step(i, _):
        @pl.when(i == 1)
        def _():
            spread.step1()
            spread.wait(4, 5)

        @pl.when(i == 2)
        def _():
            spread.step2()

        @pl.when(i == 4)
        def _():
            spread.wait(6, 7)

        @pl.when(i == 5)
        def _():
            spread.wait(8, 9)

        @pl.when(i == 6)
        def _():
            spread.step3()

        @pl.when(i == 7)
        def _():
            spread.wait(12, 13)

        owner = order[7]
        for at in range(7):
            owner = jnp.where(i == at, order[at], owner)
        project(owner)
        return 0

    lax.fori_loop(0, GROUP, step, 0)
    for copy in outs:
        copy.wait()
    for copy in weights:
        copy.wait_send()
    moves[1].wait()
    spread.sent()


def project_call(tokens, gain, w_h, w_out, cosine, sine, docs, depth):
    rows, width = tokens.shape
    span = GROUP * rows
    strip = w_out.shape[0] // GROUP
    sems = [DMA((depth - 1,))] * 4 + [DMA((GROUP - 1,))] * 2
    sems += [DMA((Spread.SEMS,))] * 2 + [DMA((2,))]
    return pl.pallas_call(
        project_kernel,
        out_shape=(
            shape((GROUP, rows, width), bf16),
            shape((depth,) + w_h.shape, bf16),
            shape((depth, strip, w_out.shape[1]), bf16),
            shape((span, QW), bf16),
            shape((span, HEAD_DIM), bf16),
            shape((span, HEAD_DIM), bf16),
            shape((GROUP,) + docs.shape, jnp.int32),
        ),
        in_specs=[IN_VMEM, IN_VMEM, IN_VMEM, IN_ANY, IN_VMEM, IN_VMEM, IN_VMEM],
        out_specs=(IN_VMEM, IN_VMEM, IN_ANY, IN_VMEM, IN_VMEM, IN_VMEM, IN_VMEM),
        scratch_shapes=sems,
        compiler_params=params(1),
        name="project",
    )(tokens, gain, w_h, w_out, cosine, sine, docs)


def docs_column(row):
    return jnp.broadcast_to(row.astype(f32), (8, row.shape[1])).T[:, :1]


def attend_kernel(
    n_blocks, q_ref, k_ref, v_ref, docs_ref, strips_ref,
    o_ref, lse_ref, attended_ref, out_weight_ref, staged_ref,
    vt_ref, docs_col_ref, top_ref, sum_ref, acc_ref, a_send, a_recv, w_send, w_recv, local,
):
    T = TOK_DEV
    place = Place()
    me = place.me
    first = place.base
    greet(place.others())
    depth = strips_ref.shape[0]
    move = pltpu.make_async_copy(strips_ref, out_weight_ref.at[:, me], local.at[0])
    move.start()
    spread = Spread(
        place, strips_ref, lambda owner: out_weight_ref.at[:, owner],
        lambda ref, h: ref.at[pl.ds(h * (depth // 2), depth // 2)], w_send, w_recv,
    )
    spread.start()

    def turn(i, _):
        vt_ref[:, block(i)] = v_ref[block(i), :].T
        docs_col_ref[i] = docs_column(docs_ref[i])
        return 0

    lax.fori_loop(0, n_blocks, turn, 0)

    def tile(kb, qb, mask):
        kt = k_ref[block(kb), :]
        vt = vt_ref[:, block(kb)]
        heads = range(HEADS)
        parts = [slice(h * 64, (h + 1) * 64) for h in heads]
        s = [dot(kt, q_ref[block(qb), parts[h]], ((1,), (1,))) for h in heads]
        if mask is not None:
            s = [jnp.where(mask, x, score_masked) for x in s]
        old = [top_ref[h : h + 1, :] for h in heads]
        new = [jnp.maximum(old[h], jnp.max(s[h], axis=0, keepdims=True)) for h in heads]
        p = [jnp.exp(s[h] - new[h]) for h in heads]
        factor = [jnp.exp(old[h] - new[h]) for h in heads]
        total = [
            sum_ref[h : h + 1, :] * factor[h] + jnp.sum(p[h], axis=0, keepdims=True) for h in heads
        ]
        mixed = [acc_ref[parts[h], :] * factor[h] + dot(vt, p[h].astype(bf16)) for h in heads]
        for h in heads:
            top_ref[h : h + 1, :] = new[h]
            sum_ref[h : h + 1, :] = total[h]
            acc_ref[parts[h], :] = mixed[h]

    def same(kb, gq):
        return docs_col_ref[kb] == docs_ref[gq].astype(f32)

    def attended_copy(j, qb):
        return remote(
            staged_ref.at[qb], attended_ref.at[me], a_send.at[j], a_recv.at[j], place.ctx(qb)
        )

    def q_block(j, _):
        @pl.when(j == 1)
        def _():
            spread.step1()

        @pl.when(j == 2)
        def _():
            spread.step2()

        @pl.when(j == 4)
        def _():
            spread.step3()

        qb = lax.rem(me + j, GROUP)
        gq = first + qb
        top_ref[...] = jnp.full_like(top_ref, score_masked)
        sum_ref[...] = jnp.ones_like(sum_ref)
        acc_ref[...] = jnp.zeros_like(acc_ref)
        last = gq == n_blocks - 1

        def k_block(kb, _):
            edge = jnp.logical_or(kb == 0, last)

            @pl.when(edge)
            def _():
                tile(kb, qb, same(kb, gq))

            @pl.when(jnp.logical_not(edge))
            def _():
                tile(kb, qb, None)

            return 0

        lax.fori_loop(0, gq, k_block, 0)
        keys = lax.broadcasted_iota(jnp.int32, (T, T), 0)
        queries = lax.broadcasted_iota(jnp.int32, (T, T), 1)
        tile(gq, qb, same(gq, gq) & (keys <= queries))
        lse_ref[qb] = top_ref[...] + jnp.log(sum_ref[...])
        for h in range(HEADS):
            part = slice(h * 64, (h + 1) * 64)
            acc_ref[part, :] = acc_ref[part, :] / sum_ref[h : h + 1, :]
        mixed = acc_ref[...].T
        o_ref[block(qb), :] = mixed
        staged_ref[qb] = mixed.astype(bf16)

        @pl.when(j > 0)
        def _():
            attended_copy(j, qb).start()

        return 0

    lax.fori_loop(0, GROUP, q_block, 0)
    own = pltpu.make_async_copy(staged_ref.at[me], attended_ref.at[me], local.at[1])
    own.start()
    own.wait()
    move.wait()
    for j in range(1, GROUP):
        attended_copy(j, lax.rem(me + j, GROUP)).wait()
    spread.last()
    spread.sent()


def attend_call(q, k, v, docs, strips):
    n = k.shape[0] // TOK_DEV
    span = q.shape[0]
    return pl.pallas_call(
        functools.partial(attend_kernel, n),
        out_shape=(
            shape((span, QW), f32),
            shape((GROUP, 8, TOK_DEV), f32),
            shape((GROUP, TOK_DEV, QW), bf16),
            shape((strips.shape[0], GROUP) + strips.shape[1:], bf16),
            shape((GROUP, TOK_DEV, QW), bf16),
        ),
        in_specs=[IN_VMEM] * 4 + [IN_ANY],
        out_specs=(IN_VMEM, IN_VMEM, IN_VMEM, IN_ANY, IN_VMEM),
        scratch_shapes=[
            VMEM((64, n * TOK_DEV), bf16),
            VMEM((n, TOK_DEV, 1), f32),
            VMEM((8, TOK_DEV), f32),
            VMEM((8, TOK_DEV), f32),
            VMEM((QW, TOK_DEV), f32),
            DMA((GROUP,)),
            DMA((GROUP,)),
            DMA((Spread.SEMS,)),
            DMA((Spread.SEMS,)),
            DMA((2,)),
        ],
        compiler_params=params(2),
        name="attend",
    )(q, k, v, docs, strips)


NEVER = 4096.0


def dispatch_kernel(
    attended_ref, weight_ref, tokens_ref, gain_ref, w_all_ref, routes_ref, order_ref,
    cotangent_ref,
    residual_ref, normed_ref, gates_ref, placed_ref, slot_gates_ref, rows_ref, grads_ref,
    mixed_ref, own_rows, own_grads, r_send, r_recv, g_send, g_recv, local,
):
    place = Place()
    me = place.me
    greet(place.others())
    rows, width = tokens_ref.shape
    for j in range(GROUP):
        mixed_ref[:, j * QW : (j + 1) * QW] = attended_ref[j]

    def out_columns(i, _):
        columns = block(i)
        residual_ref[:, columns] = tokens_ref[:, columns].astype(f32) + dot(
            mixed_ref[...], weight_ref[:, columns]
        )
        return 0

    lax.fori_loop(0, width // TOK_DEV, out_columns, 0)
    residual = residual_ref[...]
    scale = lax.rsqrt(jnp.mean(residual * residual, axis=-1, keepdims=True) + epsilon)
    normed_ref[...] = (residual * scale * gain_ref[...]).astype(bf16)
    router = w_all_ref[:, :, WIDE - LANES :].reshape(width, LANES)
    logits = dot(normed_ref[...], router)
    lane = lax.broadcasted_iota(jnp.int32, (rows, LANES), 1)
    chosen = lane < 0
    priority = jnp.full((rows, LANES), NEVER, f32)
    for k in range(TOPK):
        pick = lane == routes_ref[:, k : k + 1] + ROUTER
        chosen = chosen | pick
        priority = jnp.where(pick, order_ref[:, k : k + 1].astype(f32), priority)
    logits = jnp.where(chosen, logits, score_masked)
    top = jnp.max(logits, axis=-1, keepdims=True)
    gates = jnp.where(chosen, jnp.exp(logits - top), 0.0)
    gates = gates / jnp.sum(gates, axis=-1, keepdims=True)
    gates_ref[...] = gates
    gates_turned, priority_turned = gates.T, priority.T
    slot = lax.broadcasted_iota(jnp.int32, (CAP, rows), 0).astype(f32)
    for e in range(EXP_WIN):
        at = ROUTER + e
        mine = priority_turned[at : at + 1, :]
        before = jnp.where(priority[:, at : at + 1] < mine, 1.0, 0.0)
        before = jnp.sum(before, axis=0, keepdims=True)
        placed = (slot == before) & (mine < NEVER)
        placed_ref[e] = jnp.where(placed, 1.0, 0.0).astype(bf16)
        slot_gates_ref[e] = jnp.sum(
            jnp.where(placed, gates_turned[at : at + 1, :], 0.0), axis=1, keepdims=True
        )

    def copy(source, target, send, receive, j):
        to = lax.rem(me + j, GROUP)
        return remote(
            source.at[to], target.at[me], send.at[j], receive.at[j], place.ctx(to)
        )

    def send_rows(j, _):
        to = lax.rem(me + j, GROUP)
        own_rows[to] = dot(placed_ref[to], normed_ref[...]).astype(bf16)

        @pl.when(j < GROUP)
        def _():
            copy(own_rows, rows_ref, r_send, r_recv, j).start()

        return 0

    def send_grads(j, _):
        to = lax.rem(me + j, GROUP)
        routed = dot(placed_ref[to], cotangent_ref[...])
        own_grads[to] = (routed * slot_gates_ref[to]).astype(bf16)

        @pl.when(j < GROUP)
        def _():
            copy(own_grads, grads_ref, g_send, g_recv, j).start()

        return 0

    lax.fori_loop(1, GROUP + 1, send_rows, 0)
    lax.fori_loop(1, GROUP + 1, send_grads, 0)
    moves = [
        pltpu.make_async_copy(own_rows.at[me], rows_ref.at[me], local.at[0]),
        pltpu.make_async_copy(own_grads.at[me], grads_ref.at[me], local.at[1]),
    ]
    for move in moves:
        move.start()
    for j in range(1, GROUP):
        copy(own_rows, rows_ref, r_send, r_recv, j).wait()
    for j in range(1, GROUP):
        copy(own_grads, grads_ref, g_send, g_recv, j).wait()
    for move in moves:
        move.wait()


def dispatch_call(attended, weight, tokens, gain, w_all, routes, order, cotangent):
    rows, width = tokens.shape
    slots = (GROUP, CAP, width)
    return pl.pallas_call(
        dispatch_kernel,
        out_shape=(
            shape((rows, width), f32),
            shape((rows, width), bf16),
            shape((rows, LANES), f32),
            shape((EXP_WIN, CAP, rows), bf16),
            shape((EXP_WIN, CAP, 1), f32),
            shape(slots, bf16),
            shape(slots, bf16),
        ),
        in_specs=[IN_VMEM] * 8,
        out_specs=(IN_VMEM,) * 5 + (IN_ANY,) * 2,
        scratch_shapes=[
            VMEM((rows, GROUP * QW), bf16),
            VMEM(slots, bf16),
            VMEM(slots, bf16),
        ]
        + [DMA((GROUP,))] * 4
        + [DMA((2,))],
        compiler_params=params(3),
        name="dispatch",
    )(attended, weight, tokens, gain, w_all, routes, order, cotangent)


def combine_kernel(
    sent_out_ref, sent_grad_ref, residual_ref, normed_ref, gates_ref, placed_ref, slot_gates_ref,
    cotangent_ref, gain_ref, w_all_ref, weight_ref,
    output_ref, grad_residual_ref, heads_ref, grad_router_ref, grad_gain_ref,
    out_ref, back_ref, sum_ref, turned_ref, staged_ref, attn_ref, attended_ref,
    o_send, o_recv, b_send, b_recv, h_send, h_recv, local,
):
    place = Place()
    me = place.me
    greet(place.others())
    rows, width = residual_ref.shape

    def copy(source, target, send, receive, j):
        to = lax.rem(me + j, GROUP)
        return remote(
            source.at[to], target.at[me], send.at[j], receive.at[j], place.ctx(to)
        )

    outs = [copy(sent_out_ref, out_ref, o_send, o_recv, j) for j in range(1, GROUP)]
    backs = [copy(sent_grad_ref, back_ref, b_send, b_recv, j) for j in range(1, GROUP)]
    for one in outs + backs:
        one.start()
    moves = [
        pltpu.make_async_copy(sent_out_ref.at[me], out_ref.at[me], local.at[0]),
        pltpu.make_async_copy(sent_grad_ref.at[me], back_ref.at[me], local.at[1]),
    ]
    for move in moves:
        move.start()
    sum_ref[...] = residual_ref[...]
    turned_ref[...] = jnp.zeros_like(turned_ref)
    moves[0].wait()
    for one in outs:
        one.wait_recv()

    def add_expert(e, _):
        placed = placed_ref[e]
        came = out_ref[e].astype(f32)
        sum_ref[...] += dot(placed, (came * slot_gates_ref[e]).astype(bf16), ((0,), (0,)))
        routed = dot(placed, cotangent_ref[...])
        slot_grad = jnp.sum(routed * came, axis=1, keepdims=True)
        turned_ref[pl.ds(ROUTER + e, 1), :] = jnp.sum(
            placed.astype(f32) * slot_grad, axis=0, keepdims=True
        )
        return 0

    lax.fori_loop(0, EXP_WIN, add_expert, 0)
    output_ref[...] = sum_ref[...].astype(bf16)

    gates = gates_ref[...]
    grad_gates = turned_ref[...].T
    weighted = jnp.sum(gates * grad_gates, axis=-1, keepdims=True)
    grad_logits = (gates * (grad_gates - weighted)).astype(bf16)
    router = w_all_ref[:, :, WIDE - LANES :].reshape(width, LANES)
    sum_ref[...] = dot(grad_logits, router, ((1,), (1,)))
    grad_router_ref[...] = dot(normed_ref[...], grad_logits, ((0,), (0,)))
    moves[1].wait()
    for one in backs:
        one.wait_recv()

    def add_back(e, _):
        sum_ref[...] += dot(placed_ref[e], back_ref[e], ((0,), (0,)))
        return 0

    lax.fori_loop(0, EXP_WIN, add_back, 0)
    residual = residual_ref[...]
    grad_normed = sum_ref[...]
    scale = lax.rsqrt(jnp.mean(residual * residual, axis=-1, keepdims=True) + epsilon)
    scaled = grad_normed * gain_ref[...]
    inner = jnp.mean(scaled * residual, axis=-1, keepdims=True)
    grad = scale * scaled - residual * (scale * scale * scale * inner)
    grad_gain_ref[...] = jnp.sum(grad_normed * residual * scale, axis=0, keepdims=True)
    grad_residual = cotangent_ref[...].astype(f32) + grad
    grad_residual_ref[...] = grad_residual
    attn_ref[...] = grad_residual.astype(bf16)

    def out_rows(i, _):
        attended_ref[:, block(i)] = dot(attn_ref[...], weight_ref[block(i), :], ((1,), (1,))).astype(
            bf16
        )
        return 0

    lax.fori_loop(0, width // TOK_DEV, out_rows, 0)
    for h in range(GROUP):
        staged_ref[h, :, :QW] = attended_ref[:, h * QW : (h + 1) * QW]
        staged_ref[h, :, QW:] = attn_ref[:, h * QW : (h + 1) * QW]
    heads = [copy(staged_ref, heads_ref, h_send, h_recv, j) for j in range(1, GROUP)]
    for one in heads:
        one.start()
    move = pltpu.make_async_copy(staged_ref.at[me], heads_ref.at[me], local.at[2])
    move.start()
    for one in outs + backs:
        one.wait_send()
    for one in heads:
        one.wait()
    move.wait()


def combine_call(
    sent_out, sent_grad, residual, normed, gates, placed, slot_gates, cotangent, gain, w_all, weight
):
    rows, width = residual.shape
    slots = (GROUP, CAP, width)
    return pl.pallas_call(
        combine_kernel,
        out_shape=(
            shape((rows, width), bf16),
            shape((rows, width), f32),
            shape((GROUP, rows, 2 * QW), bf16),
            shape((width, LANES), f32),
            shape((1, width), f32),
        ),
        in_specs=[IN_ANY] * 2 + [IN_VMEM] * 9,
        out_specs=(IN_VMEM, IN_VMEM, IN_ANY, IN_VMEM, IN_VMEM),
        scratch_shapes=[
            VMEM(slots, bf16),
            VMEM(slots, bf16),
            VMEM((rows, width), f32),
            VMEM((LANES, rows), f32),
            VMEM((GROUP, rows, 2 * QW), bf16),
            VMEM((rows, width), bf16),
            VMEM((rows, GROUP * QW), bf16),
        ]
        + [DMA((GROUP,))] * 6
        + [DMA((3,))],
        compiler_params=params(4),
        name="combine",
    )(sent_out, sent_grad, residual, normed, gates, placed, slot_gates, cotangent, gain, w_all, weight)


def backward_kernel(
    n_blocks, q_ref, k_ref, v_ref, heads_ref, o_ref, lse_ref, docs_ref, staged_ref, w_all_ref,
    dq_ref, dk_ref, dv_ref, attended_ref, weights_ref,
    kt_ref, docs_col_ref, dqt_ref, delta_ref, a_send, a_recv, w_send, w_recv, local,
):
    T = TOK_DEV
    place = Place()
    me = place.me
    first = place.base
    greet([place.ctx(i) for i in place.near])
    moves = [
        pltpu.make_async_copy(staged_ref, attended_ref.at[me], local.at[0]),
        pltpu.make_async_copy(w_all_ref, weights_ref.at[me], local.at[1]),
    ]
    for move in moves:
        move.start()

    def halves(size):
        return lambda ref, h: ref.at[pl.ds(h * (size // 2), size // 2)]

    spreads = [
        Spread(
            place, staged_ref, lambda owner: attended_ref.at[owner], halves(GROUP), a_send, a_recv
        ),
        Spread(
            place, w_all_ref, lambda owner: weights_ref.at[owner],
            halves(w_all_ref.shape[0]), w_send, w_recv,
        ),
    ]
    for spread in spreads:
        spread.start()
    rows = lax.broadcasted_iota(jnp.int32, (8, QW), 0)
    lanes = lax.broadcasted_iota(jnp.int32, (8, QW), 1)
    pick = (lanes >= rows * HEAD_DIM) & (lanes < rows * HEAD_DIM + HEAD_DIM)
    pick = jnp.where(pick, 1.0, 0.0).astype(bf16)

    def turn(i, _):
        kt_ref[:, block(i)] = k_ref[block(i), :].T
        docs_col_ref[i] = docs_column(docs_ref[i])
        return 0

    lax.fori_loop(0, n_blocks, turn, 0)

    def prepare(i, _):
        product = o_ref[block(i), :] * heads_ref[i, :, :QW].astype(f32)
        high = product.astype(bf16)
        low = (product - high.astype(f32)).astype(bf16)
        delta_ref[i] = dot(pick, high, ((1,), (1,))) + dot(pick, low, ((1,), (1,)))
        return 0

    lax.fori_loop(0, GROUP, prepare, 0)
    dqt_ref[...] = jnp.zeros_like(dqt_ref)

    def tile(kb, qb, mask):
        kt = k_ref[block(kb), :]
        vt = v_ref[block(kb), :]
        k_turned = kt_ref[:, block(kb)]
        heads = range(HEADS)
        parts = [slice(h * 64, (h + 1) * 64) for h in heads]
        q = [q_ref[block(qb), part] for part in parts]
        do = [heads_ref[qb, :, part] for part in parts]
        s = [dot(kt, x, ((1,), (1,))) for x in q]
        dp = [dot(vt, x, ((1,), (1,))) for x in do]
        p = [jnp.exp(s[h] - lse_ref[qb, h : h + 1, :]) for h in heads]
        if mask is not None:
            p = [jnp.where(mask, x, 0.0) for x in p]
        ds = [(p[h] * (dp[h] - delta_ref[qb, h : h + 1, :])).astype(bf16) for h in heads]
        pb = [x.astype(bf16) for x in p]
        dv_ref[block(kb), :] += dot(pb[0], do[0]) + dot(pb[1], do[1]) + dot(pb[2], do[2])
        dk_ref[block(kb), :] += dot(ds[0], q[0]) + dot(ds[1], q[1]) + dot(ds[2], q[2])
        for h in heads:
            dqt_ref[parts[h], block(qb)] += dot(k_turned, ds[h])

    def same(kb, gq):
        return docs_col_ref[kb] == docs_ref[gq].astype(f32)

    def k_block(kb, _):
        for at, act in (
            (1, spreads[0].step1), (2, spreads[0].step2), (3, spreads[0].step3),
            (4, spreads[1].step1), (5, spreads[1].step2), (6, spreads[1].step3),
        ):
            pl.when(kb == first + at)(act)
        dk_ref[block(kb), :] = jnp.zeros((T, HEAD_DIM), f32)
        dv_ref[block(kb), :] = jnp.zeros((T, HEAD_DIM), f32)

        @pl.when(kb >= first)
        def _():
            keys = lax.broadcasted_iota(jnp.int32, (T, T), 0)
            queries = lax.broadcasted_iota(jnp.int32, (T, T), 1)
            tile(kb, kb - first, same(kb, kb) & (keys <= queries))

        def q_block(qb, _):
            gq = first + qb
            edge = jnp.logical_or(kb == 0, gq == n_blocks - 1)

            @pl.when(edge)
            def _():
                tile(kb, qb, same(kb, gq))

            @pl.when(jnp.logical_not(edge))
            def _():
                tile(kb, qb, None)

            return 0

        lax.fori_loop(jnp.maximum(kb - first + 1, 0), GROUP, q_block, 0)
        return 0

    lax.fori_loop(0, first + GROUP, k_block, 0)

    def finish(i, _):
        dq_ref[block(i), :] = dqt_ref[:, block(i)].T
        return 0

    lax.fori_loop(0, GROUP, finish, 0)

    def clear(kb, _):
        dk_ref[block(kb), :] = jnp.zeros((T, HEAD_DIM), f32)
        dv_ref[block(kb), :] = jnp.zeros((T, HEAD_DIM), f32)
        return 0

    lax.fori_loop(first + GROUP, n_blocks, clear, 0)
    for spread in spreads:
        spread.last()
        spread.sent()
    for move in moves:
        move.wait()


def backward_call(q, k, v, heads, o, lse, docs, staged, w_all):
    n = k.shape[0] // TOK_DEV
    span = q.shape[0]
    return pl.pallas_call(
        functools.partial(backward_kernel, n),
        out_shape=(
            shape((span, QW), f32),
            shape(k.shape, f32),
            shape(k.shape, f32),
            shape((GROUP,) + staged.shape, bf16),
            shape((GROUP,) + w_all.shape, bf16),
        ),
        in_specs=[IN_VMEM] * 7 + [IN_ANY] * 2,
        out_specs=(IN_VMEM,) * 3 + (IN_ANY,) * 2,
        scratch_shapes=[
            VMEM((64, n * TOK_DEV), bf16),
            VMEM((n, TOK_DEV, 1), f32),
            VMEM((QW, span), f32),
            VMEM((GROUP, 8, TOK_DEV), f32),
        ]
        + [DMA((Spread.SEMS,))] * 4
        + [DMA((2,))],
        compiler_params=params(5),
        name="backward",
    )(q, k, v, heads, o, lse, docs, staged, w_all)


def finish_kernel(
    dq_ref, dk_ref, dv_ref, cos_ref, sin_ref, normed_ref, attended_ref, heads_ref, weights_ref,
    tokens_ref, gain_ref, grad_residual_ref, grad_router_ref, grad_gain2_ref,
    input_grad_ref, grads_ref,
    linear_ref, came_ref, columns_ref, sum_ref, gains_ref, g_send, g_recv,
):
    place = Place()
    me = place.me
    greet(place.others())
    rows, width = tokens_ref.shape
    span = GROUP * rows

    def copy(j):
        to = lax.rem(me + j, GROUP)
        return remote(
            linear_ref.at[to], came_ref.at[me], g_send.at[j], g_recv.at[j], place.ctx(to)
        )

    def turn_back(j, _):
        to = lax.rem(me + j, GROUP)
        cosine, sine = cos_ref[block(to), :], -sin_ref[block(to), :]
        dq = dq_ref[block(to), :] * HEAD_DIM ** (-0.5)
        second = jnp.concatenate([dq[:, LANES:], dk_ref[block(to), :]], axis=1)
        third = jnp.concatenate([dv_ref[block(to), :], jnp.zeros((rows, HEAD_DIM), f32)], axis=1)
        linear_ref[to, :, :LANES] = turned(dq[:, :LANES], cosine, sine).astype(bf16)
        linear_ref[to, :, LANES : 2 * LANES] = turned(second, cosine, sine).astype(bf16)
        linear_ref[to, :, 2 * LANES :] = third.astype(bf16)

        @pl.when(j < GROUP)
        def _():
            copy(j).start()

        return 0

    lax.fori_loop(1, GROUP + 1, turn_back, 0)
    came_ref[me] = linear_ref[me]
    columns_ref[...] = heads_ref[:, :, QW:].reshape(span, QW)

    def own_weights(i, _):
        left = normed_ref[:, :, block(i)].reshape(span, TOK_DEV)
        grads_ref[block(i), : 3 * LANES] = dot(
            left, linear_ref[...].reshape(span, WIDE), ((0,), (0,))
        ).astype(bf16)
        return 0

    lax.fori_loop(0, width // TOK_DEV, own_weights, 0)

    def out_weights(j, _):
        left = attended_ref[j].reshape(span, QW)
        grads_ref[block(j, QW), 3 * LANES :] = dot(left, columns_ref[...], ((0,), (0,))).astype(bf16)
        return 0

    lax.fori_loop(0, GROUP, out_weights, 0)
    sum_ref[...] = jnp.zeros_like(sum_ref)
    for j in range(1, GROUP):
        copy(j).wait_recv()

    def add_head(j, _):
        sum_ref[...] += dot(came_ref[j], weights_ref[j].reshape(width, WIDE), ((1,), (1,)))
        return 0

    lax.fori_loop(0, GROUP, add_head, 0)
    x = tokens_ref[...].astype(f32)
    grad_normed = sum_ref[...]
    scale = lax.rsqrt(jnp.mean(x * x, axis=-1, keepdims=True) + epsilon)
    scaled = grad_normed * gain_ref[...]
    inner = jnp.mean(scaled * x, axis=-1, keepdims=True)
    grad = scale * scaled - x * (scale * scale * scale * inner)
    input_grad_ref[...] = grad_residual_ref[...] + grad
    gains_ref[...] = jnp.zeros_like(gains_ref)
    at = ROUTER + EXPERTS_MOST
    gains_ref[at : at + 1, :] = jnp.sum(grad_normed * x * scale, axis=0, keepdims=True)
    gains_ref[at + 1 : at + 2, :] = grad_gain2_ref[...]
    extra = grad_router_ref[...] + gains_ref[...].T
    lane = lax.broadcasted_iota(jnp.int32, extra.shape, 1)
    last = slice(2 * LANES, 3 * LANES)
    grads_ref[:, last] = jnp.where(lane < ROUTER, grads_ref[:, last].astype(f32), extra).astype(bf16)
    for j in range(1, GROUP):
        copy(j).wait_send()


def finish_call(
    dq, dk, dv, cosine, sine, normed, attended, heads, weights, tokens, gain, grad_residual,
    grad_router, grad_gain2,
):
    rows, width = tokens.shape
    return pl.pallas_call(
        finish_kernel,
        out_shape=(shape((rows, width), f32), shape((width, WIDE + QW), bf16)),
        in_specs=[IN_VMEM] * 14,
        out_specs=(IN_VMEM,) * 2,
        scratch_shapes=[
            VMEM((GROUP, rows, WIDE), bf16),
            VMEM((GROUP, rows, WIDE), bf16),
            VMEM((GROUP * rows, QW), bf16),
            VMEM((rows, width), f32),
            VMEM((LANES, width), f32),
            DMA((GROUP,)),
            DMA((GROUP,)),
        ],
        compiler_params=params(6),
        name="finish",
    )(
        dq, dk, dv, cosine, sine, normed, attended, heads, weights, tokens, gain, grad_residual,
        grad_router, grad_gain2,
    )


def share_kernel(count, *refs):
    sources, outs, sems = refs[:count], refs[count : 2 * count], refs[2 * count :]
    place = Place()
    greet([place.ctx(i) for i in place.near])
    spreads, moves = [], []
    for i in range(count):
        size = sources[i].shape[0] // 2
        spreads.append(
            Spread(
                place, sources[i], lambda owner, out=outs[i]: out.at[owner],
                lambda ref, h, size=size: ref.at[pl.ds(h * size, size)],
                sems[2 * i], sems[2 * i + 1],
            )
        )
        moves.append(
            pltpu.make_async_copy(sources[i], outs[i].at[place.me], sems[2 * count].at[i])
        )
        spreads[i].start()
        moves[i].start()
    for spread in spreads:
        spread.step1()
    for spread in spreads:
        spread.step2()
    for spread in spreads:
        spread.step3()
    for spread in spreads:
        spread.last()
        spread.sent()
    for move in moves:
        move.wait()


def share_call(collective_id, *values):
    count = len(values)
    return pl.pallas_call(
        functools.partial(share_kernel, count),
        out_shape=tuple(shape((GROUP,) + v.shape, v.dtype) for v in values),
        in_specs=[IN_ANY] * count,
        out_specs=(IN_ANY,) * count,
        scratch_shapes=[DMA((Spread.SEMS,))] * (2 * count) + [DMA((count,))],
        compiler_params=params(collective_id),
        name="share",
    )(*values)


def rotary_tables(length):
    frequencies = 10000.0 ** (-(np.arange(HEAD_DIM // 2) * 2.0) / HEAD_DIM)
    angles = np.arange(length)[:, None] * frequencies[None, :]
    repeat = LANES // (HEAD_DIM // 2)
    return (
        np.tile(np.cos(angles), (1, repeat)).astype(np.float32),
        np.tile(np.sin(angles), (1, repeat)).astype(np.float32),
    )


def shards(
    tables,
    tokens,
    doc_ids,
    routes,
    slot_order,
    norm1_gain,
    norm2_gain,
    w_query,
    key_matrix,
    value_matrix,
    w_out,
    w_router,
    w_gate,
    w_up,
    w_down,
    cotangent,
):
    rows, width = tokens.shape[1:]
    ctx, depth = lax.axis_size("ctx"), lax.axis_size("fsdp")
    place = lax.axis_index("ctx")
    parts = ctx // GROUP
    head, part = place % GROUP, place // GROUP
    far = [[p * GROUP + i for p in range(parts)] for i in range(GROUP)]
    span = GROUP * rows
    experts = w_router.shape[1]
    hidden = w_gate.shape[2]

    def gather_z(value):
        return lax.all_gather(value, "fsdp", axis=0, tiled=True)

    def reduce_z(value):
        value = lax.psum_scatter(value.astype(bf16), "fsdp", scatter_dimension=0, tiled=True)
        if parts > 1:
            value = lax.psum(value, "ctx", axis_index_groups=far)
        return value

    def own(weight, size):
        return lax.dynamic_slice_in_dim(weight, head * size, size, 1)

    w_h = jnp.concatenate(
        [
            own(w_query, QW), own(key_matrix, HEAD_DIM), own(value_matrix, HEAD_DIM),
            jnp.pad(w_router, ((0, 0), (0, HEAD_DIM - experts))),
        ],
        axis=1,
    )
    gate_up = gather_z(
        jnp.concatenate(
            [
                lax.dynamic_index_in_dim(w_gate, head, 0, False),
                lax.dynamic_index_in_dim(w_up, head, 0, False),
            ],
            axis=1,
        )
    )
    down = gather_z(lax.dynamic_index_in_dim(w_down, head, 0, False))
    cosine, sine = tables
    if parts > 1:
        cosine = lax.dynamic_slice_in_dim(cosine, part * span, span, 0)
        sine = lax.dynamic_slice_in_dim(sine, part * span, span, 0)
    own_tokens, own_cotangent = tokens[0], cotangent[0]
    gain1, gain2 = norm1_gain[None, :], norm2_gain[None, :]

    normed1, w_all, strips, queries, keys, values, docs = project_call(
        own_tokens, gain1, w_h, w_out, cosine, sine, doc_ids, depth
    )
    if parts > 1:
        keys = lax.all_gather(keys, "ctx", axis_index_groups=far, tiled=True)
        values = lax.all_gather(values, "ctx", axis_index_groups=far, tiled=True)
        docs = lax.all_gather(docs, "ctx", axis_index_groups=far, tiled=True)
    attended_f32, log_total, attended, out_weight, staged = attend_call(
        queries, keys, values, docs, strips
    )
    out_weight = out_weight.reshape(width, width)
    residual, normed2, gates, placed, slot_gates, sent_rows, sent_grads = dispatch_call(
        attended, out_weight, own_tokens, gain2, w_all, routes[0], slot_order[0], own_cotangent
    )
    buffer_rows = sent_rows.reshape(GROUP * CAP, width)
    grad_rows = sent_grads.reshape(GROUP * CAP, width)

    gate_up_in = dot(buffer_rows, gate_up)
    gate_in, up_in = gate_up_in[:, :hidden], gate_up_in[:, hidden:]
    sigmoid_gate = jax.nn.sigmoid(gate_in)
    activation = (gate_in * sigmoid_gate * up_in).astype(bf16)
    expert_out = dot(activation, down).astype(bf16)
    grad_activation = dot(grad_rows, down, ((1,), (1,)))
    grad_gate_in = grad_activation * up_in * sigmoid_gate * (1.0 + gate_in * (1.0 - sigmoid_gate))
    grad_up_in = grad_activation * gate_in * sigmoid_gate
    grad_gate_up = jnp.concatenate([grad_gate_in, grad_up_in], axis=1).astype(bf16)
    grad_buffer = dot(grad_gate_up, gate_up, ((1,), (1,))).astype(bf16)
    grad_w_down = reduce_z(dot(activation, grad_rows, ((0,), (0,))))
    grad_w_gate_up = reduce_z(dot(buffer_rows, grad_gate_up, ((0,), (0,))))

    output, grad_residual, heads, grad_router, grad_gain2 = combine_call(
        expert_out.reshape(sent_rows.shape), grad_buffer.reshape(sent_rows.shape), residual,
        normed2, gates, placed, slot_gates, own_cotangent, gain2, w_all, out_weight,
    )
    dq, dk, dv, attended_all, weights_all = backward_call(
        queries, keys, values, heads, attended_f32, log_total, docs, staged, w_all
    )
    if parts > 1:
        dk = lax.psum_scatter(dk, "ctx", axis_index_groups=far, tiled=True)
        dv = lax.psum_scatter(dv, "ctx", axis_index_groups=far, tiled=True)
    input_grad, grads = finish_call(
        dq, dk, dv, cosine, sine, normed1, attended_all, heads, weights_all, own_tokens, gain1,
        grad_residual, grad_router, grad_gain2,
    )
    gate_up_w, down_w = share_call(7, grad_w_gate_up, grad_w_down)
    (shared,) = share_call(8, reduce_z(grads))
    shared = shared.astype(f32)

    def columns(value):
        return jnp.transpose(value, (1, 0, 2)).reshape(value.shape[1], -1)

    small = jnp.sum(shared[:, :, HW : HW + experts + 2], axis=0)
    gate_up_w = gate_up_w.astype(f32)
    return (
        output[None],
        input_grad[None],
        small[:, experts],
        small[:, experts + 1],
        columns(shared[:, :, :QW]),
        columns(shared[:, :, QW : QW + HEAD_DIM]),
        columns(shared[:, :, QW + HEAD_DIM : HW]),
        columns(shared[:, :, WIDE:]),
        small[:, :experts],
        gate_up_w[:, :, :hidden],
        gate_up_w[:, :, hidden:],
        down_w.astype(f32),
    )


def solution(mesh):
    token_spec = P("fsdp", "ctx", None)
    row_spec, expert_spec = P("fsdp", None), P(None, "fsdp", None)
    tables = rotary_tables(mesh.shape["ctx"] * TOK_DEV)

    def program(*arguments):
        return jax.shard_map(
            functools.partial(shards, tuple(jnp.asarray(t) for t in tables)),
            mesh=mesh,
            in_specs=(
                token_spec,
                P("fsdp", "ctx"),
                token_spec,
                token_spec,
                P(),
                P(),
                row_spec,
                row_spec,
                row_spec,
                row_spec,
                row_spec,
                expert_spec,
                expert_spec,
                expert_spec,
                token_spec,
            ),
            out_specs=(
                token_spec,
                token_spec,
                P("fsdp"),
                P("fsdp"),
                row_spec,
                row_spec,
                row_spec,
                row_spec,
                row_spec,
                expert_spec,
                expert_spec,
                expert_spec,
            ),
            check_vma=False,
        )(*arguments)

    return program
```

```python
import functools

import jax
import jax.numpy as jnp
import numpy as np
from jax import lax
from jax.experimental import pallas as pl
from jax.experimental.pallas import tpu as pltpu
from jax.sharding import PartitionSpec as P

QUERY_HEADS = 24
KEY_VALUE_HEADS = 8
HEAD_DIM = 64
TOPK = 8
EXP_WIN = 8
TOK_DEV = 256
CAP = 64
GROUP = 8
HEADS = QUERY_HEADS // KEY_VALUE_HEADS
QW = HEADS * HEAD_DIM
HW = QW + 2 * HEAD_DIM
ROUTER = 48
ALL = HW + ROUTER
FIRST = 96

epsilon = 1e-06
score_masked = -1e30
bf16 = jnp.bfloat16
f32 = jnp.float32
VMEM = pltpu.VMEM
MESH = pl.DeviceIdType.MESH
DMA = pltpu.SemaphoreType.DMA
IN_VMEM = pl.BlockSpec(memory_space=VMEM)
IN_ANY = pl.BlockSpec(memory_space=pl.ANY)


def dot(left, right, dims=((1,), (0,))):
    return lax.dot_general(left, right, (dims, ((), ())), preferred_element_type=f32)


def block(index, size=TOK_DEV):
    return pl.ds(pl.multiple_of(index * size, size), size)


def shape(dims, dtype):
    return jax.ShapeDtypeStruct(dims, dtype)


def params(collective_id=None, limit=56):
    return pltpu.CompilerParams(
        collective_id=collective_id,
        has_side_effects=collective_id is not None,
        vmem_limit_bytes=limit << 20,
    )


def flip(index, bit):
    return index + (1 - 2 * ((index // bit) % 2)) * bit


class Place:
    def __init__(self):
        ctx = lax.axis_index("ctx")
        self.base = (ctx // GROUP) * GROUP
        self.me = ctx - self.base
        self.z = lax.axis_index("fsdp")
        self.depth = lax.axis_size("fsdp")
        self.near = [flip(self.me, bit) for bit in (1, 2, 4)]

    def ctx(self, index):
        return {"ctx": self.base + index}

    def fsdp(self, index):
        return {"fsdp": index}

    def others(self):
        return [self.ctx(lax.rem(self.me + j, GROUP)) for j in range(1, GROUP)]

    def layers(self):
        return [self.fsdp(lax.rem(self.z + j, self.depth)) for j in range(1, self.depth)]


def greet(devices):
    ready = pltpu.get_barrier_semaphore()
    for device in devices:
        pl.semaphore_signal(ready, inc=1, device_id=device, device_id_type=MESH)
    return lambda: pl.semaphore_wait(ready, len(devices))


def remote(source, target, send, receive, device):
    return pltpu.make_async_remote_copy(
        src_ref=source,
        dst_ref=target,
        send_sem=send,
        recv_sem=receive,
        device_id=device,
        device_id_type=MESH,
    )


def halves(count):
    cut = -(-count // 32) * 16

    def part(ref, half):
        return ref.at[pl.ds(0, cut)] if half == 0 else ref.at[pl.ds(cut, count - cut)]

    return part


class Spread:
    SEMS = 14

    def __init__(self, place, source, land, part, send, receive):
        me = place.me
        core, side, row = place.near
        across = flip(side, 4)

        def plan(slot, owner, half, device):
            target = part(land(owner), half)
            first = part(source, half) if slot < 6 else target
            return remote(first, target, send.at[slot], receive.at[slot], place.ctx(device))

        self.copies = [
            plan(0, me, 0, side), plan(1, me, 1, side), plan(2, me, 0, row), plan(3, me, 1, row),
            plan(4, me, 0, core), plan(5, me, 1, core), plan(6, side, 0, core),
            plan(7, side, 1, core), plan(8, row, 0, core), plan(9, row, 1, core),
            plan(10, side, 1, row), plan(11, row, 0, side), plan(12, across, 0, core),
            plan(13, across, 1, core),
        ]

    def go(self, *slots):
        for slot in slots:
            self.copies[slot].start()

    def wait(self, *slots):
        for slot in slots:
            self.copies[slot].wait_recv()

    def start(self):
        self.go(1, 2, 0, 3, 4, 5)

    def step1(self):
        self.wait(1)
        self.go(10, 7)
        self.wait(2)
        self.go(11, 8)

    def step2(self):
        self.wait(0)
        self.go(6)
        self.wait(3)
        self.go(9)

    def step3(self):
        self.wait(10)
        self.go(13)
        self.wait(11)
        self.go(12)

    def sent(self):
        for copy in self.copies:
            copy.wait_send()

    def last(self):
        self.wait(4, 5, 6, 7, 8, 9, 12, 13)


NEVER = 4096.0


def turned(values, cosine, sine):
    half = HEAD_DIM // 2
    out = []
    for at in range(0, values.shape[0], HEAD_DIM):
        low, high = values[at : at + half], values[at + half : at + HEAD_DIM]
        out += [low * cosine - high * sine, high * cosine + low * sine]
    return jnp.concatenate(out, axis=0)


def place_slots(routes_ref, order_ref, placed_ref):
    rows = routes_ref.shape[1]
    expert = lax.broadcasted_iota(jnp.int32, (EXP_WIN, rows), 0)
    priority = jnp.full((EXP_WIN, rows), NEVER, f32)
    for k in range(TOPK):
        pick = expert == routes_ref[k : k + 1, :]
        priority = jnp.where(pick, order_ref[k : k + 1, :].astype(f32), priority)
    priority_turned = priority.T
    slot = lax.broadcasted_iota(jnp.int32, (CAP, rows), 0).astype(f32)
    for e in range(EXP_WIN):
        mine = priority[e : e + 1, :]
        before = jnp.where(priority_turned[:, e : e + 1] < mine, 1.0, 0.0)
        before = jnp.sum(before, axis=0, keepdims=True)
        placed = (slot == before) & (mine < NEVER)
        placed_ref[e] = jnp.where(placed, 1.0, 0.0).astype(bf16)


def project_kernel(
    tokens_ref, gain_ref, router_ref, cos_ref, sin_ref, docs_ref, routes_ref, order_ref, w_out_ref,
    w_query_ref, key_matrix_ref, value_matrix_ref,
    w_all_ref, qt_ref, kt_ref, vt_ref, k_ref, v_ref, docs_all_ref, placed_ref, turned_ref, normed_ref,
    strips_ref, weights_ref,
    held_ref, own_out, query_held, key_held, value_held,
    w_send, w_recv, o_send, o_recv, d_send, d_recv, c_send, c_recv, q_send, q_recv, local,
):
    place = Place()
    me, z = place.me, place.z
    met = greet(place.others() + place.layers())
    strip = strips_ref.shape[1]
    odd = lax.rem(me, 2)

    def window(first, size):
        return pl.ds(pl.multiple_of(first * 128, 128), size)

    pair = lax.div(me, 2)
    fetches = [
        pltpu.make_async_copy(
            w_query_ref.at[:, window(pair * 3 + odd, 2 * 128)], query_held, local.at[GROUP]
        ),
        pltpu.make_async_copy(
            key_matrix_ref.at[:, window(pair, 128)], key_held, local.at[GROUP + 1]
        ),
        pltpu.make_async_copy(
            value_matrix_ref.at[:, window(pair, 128)], value_held, local.at[GROUP + 2]
        ),
        pltpu.make_async_copy(
            w_out_ref.at[pl.ds(pl.multiple_of(me * strip, strip), strip), :], own_out,
            local.at[GROUP + 3],
        ),
    ]
    for fetch in fetches:
        fetch.start()
    x = tokens_ref[...].astype(f32)
    scale = lax.rsqrt(jnp.mean(x * x, axis=-1, keepdims=True) + epsilon)
    held_ref[me] = (x * scale * gain_ref[...]).astype(bf16)
    for fetch in fetches:
        fetch.wait()

    def half(held, columns):
        turned_rows = held[...].T
        return jnp.where(odd == 1, turned_rows[HEAD_DIM:], turned_rows[:columns])

    own = w_all_ref.at[z]
    own[:QW, :] = half(query_held, QW)
    own[QW : QW + HEAD_DIM, :] = half(key_held, HEAD_DIM)
    own[QW + HEAD_DIM : HW, :] = half(value_held, HEAD_DIM)
    own[HW:, :] = router_ref[...]
    met()
    spread = Spread(
        place, held_ref.at[me], lambda owner: held_ref.at[owner],
        halves(TOK_DEV), c_send, c_recv,
    )
    sent = []
    for j, device in enumerate(place.layers()):
        sent.append(remote(own, own, w_send.at[j], w_recv.at[j], device))
        sent[-1].start()
    spread.start()
    docs_all_ref[me] = docs_ref[...]
    others = []
    for j, device in enumerate(place.others()):
        others.append(remote(docs_ref, docs_all_ref.at[me], d_send.at[j], d_recv.at[j], device))
        others[-1].start()
    place_slots(routes_ref, order_ref, placed_ref)
    turned_ref[...] = placed_ref[...].reshape(EXP_WIN * CAP, -1).T
    spread.step1()
    spread.step2()
    spread.step3()
    for copy in sent:
        copy.wait_recv()
    for j, device in enumerate(place.layers()):
        others.append(remote(own_out, strips_ref.at[z], o_send.at[j], o_recv.at[j], device))
        others[-1].start()
    depth = w_all_ref.shape[0]
    weights = Spread(
        place, w_all_ref.at[:, :FIRST], lambda owner: weights_ref.at[owner],
        lambda ref, h: ref.at[pl.ds(h * (depth // 2), depth // 2)], q_send, q_recv,
    )
    weights.start()
    own_moves = [
        pltpu.make_async_copy(own_out, strips_ref.at[z], local.at[GROUP]),
        pltpu.make_async_copy(w_all_ref.at[:, :FIRST], weights_ref.at[me], local.at[GROUP + 1]),
    ]
    for move in own_moves:
        move.start()
    core, side, row = place.near
    across = flip(side, 4)
    order = [me, side, row, across, core, flip(side, 1), flip(row, 1), flip(across, 1)]

    def to_normed(owner):
        return pltpu.make_async_copy(held_ref.at[owner], normed_ref.at[owner], local.at[owner])

    def project(i, _):
        for at, slots in ((4, (4, 5)), (5, (6, 7)), (6, (8, 9)), (7, (12, 13))):

            @pl.when(i == at)
            def _(slots=slots):
                spread.wait(*slots)

        pl.when(i == 5)(weights.step1)
        pl.when(i == 7)(weights.step2)
        owner = order[-1]
        for at in range(GROUP - 1):
            owner = jnp.where(i == at, order[at], owner)
        to_normed(owner).start()
        linear = None
        for s in range(w_all_ref.shape[0]):
            size = w_all_ref.shape[2]
            term = dot(
                w_all_ref[s, :HW, :], held_ref[owner, :, s * size : (s + 1) * size], ((1,), (1,))
            )
            linear = term if linear is None else linear + term
        tokens = block(owner)
        cosine, sine = cos_ref[:, tokens], sin_ref[:, tokens]
        queries = turned(linear[:QW], cosine, sine) * HEAD_DIM ** (-0.5)
        qt_ref[:, tokens] = queries.astype(bf16)
        keys = turned(linear[QW : QW + HEAD_DIM], cosine, sine)
        kt_ref[:, tokens] = keys.astype(bf16)
        k_ref[tokens, :] = keys.T.astype(bf16)
        values = linear[QW + HEAD_DIM :]
        vt_ref[:, tokens] = values.astype(bf16)
        v_ref[tokens, :] = values.T.astype(bf16)
        return 0

    lax.fori_loop(0, GROUP, project, 0)
    weights.step3()
    for copy in sent:
        copy.wait_send()
    for copy in others:
        copy.wait()
    for move in own_moves:
        move.wait()
    for owner in range(GROUP):
        to_normed(owner).wait()
    spread.sent()
    weights.last()
    weights.sent()


def project_call(
    tokens, gain, router, cosine, sine, docs, routes, order, w_out, w_query, key_matrix,
    value_matrix, depth,
):
    rows, width = tokens.shape
    span = GROUP * rows
    strip = w_out.shape[0] // GROUP
    size = w_out.shape[0]
    return pl.pallas_call(
        project_kernel,
        out_shape=(
            shape((depth, ALL, size), bf16),
            shape((QW, span), bf16),
            shape((HEAD_DIM, span), bf16),
            shape((HEAD_DIM, span), bf16),
            shape((span, HEAD_DIM), bf16),
            shape((span, HEAD_DIM), bf16),
            shape((GROUP,) + docs.shape, jnp.int32),
            shape((EXP_WIN, CAP, rows), bf16),
            shape((rows, EXP_WIN * CAP), bf16),
            shape((GROUP, rows, width), bf16),
            shape((depth, strip, w_out.shape[1]), bf16),
            shape((GROUP, depth, FIRST, size), bf16),
        ),
        in_specs=[IN_VMEM] * 8 + [IN_ANY] * 4,
        out_specs=(IN_VMEM,) * 9 + (IN_ANY,) * 3,
        scratch_shapes=[
            VMEM((GROUP, rows, width), bf16),
            VMEM((strip, width), bf16),
            VMEM((size, 2 * 128), bf16),
            VMEM((size, 128), bf16),
            VMEM((size, 128), bf16),
        ]
        + [DMA((depth - 1,))] * 4
        + [DMA((GROUP - 1,))] * 2
        + [DMA((Spread.SEMS,))] * 4
        + [DMA((GROUP + 4,))],
        compiler_params=params(1),
        name="project",
    )(
        tokens, gain, router, cosine, sine, docs, routes, order, w_out, w_query, key_matrix,
        value_matrix,
    )


def docs_column(row):
    return jnp.broadcast_to(row.astype(f32), (8, row.shape[1])).T[:, :1]


def attend_kernel(
    n_blocks, qt_ref, k_ref, vt_ref, docs_ref, strips_ref, w_all_ref,
    o_ref, lse_ref, attended_ref, out_weight_ref, weights_ref,
    staged_ref, docs_col_ref, top_ref, sum_ref, acc_ref,
    a_send, a_recv, s_send, s_recv, w_send, w_recv, local,
):
    T = TOK_DEV
    place = Place()
    me = place.me
    first = place.base
    met = greet(place.others())
    depth = strips_ref.shape[0]
    moves = [
        pltpu.make_async_copy(strips_ref, out_weight_ref.at[:, me], local.at[0]),
        pltpu.make_async_copy(w_all_ref.at[:, FIRST:HW], weights_ref.at[me], local.at[1]),
    ]

    def layers(ref, h):
        return ref.at[pl.ds(h * (depth // 2), depth // 2)]

    spreads = [
        Spread(place, strips_ref, lambda owner: out_weight_ref.at[:, owner], layers, s_send, s_recv),
        Spread(
            place, w_all_ref.at[:, FIRST:HW], lambda owner: weights_ref.at[owner], layers, w_send, w_recv
        ),
    ]

    def turn(i, _):
        docs_col_ref[i] = docs_column(docs_ref[i])
        return 0

    lax.fori_loop(0, n_blocks, turn, 0)
    met()
    spreads[0].start()
    for move in moves:
        move.start()

    def tile(kb, qb, mask):
        kt = k_ref[block(kb), :]
        vt = vt_ref[:, block(kb)]
        heads = range(HEADS)
        parts = [slice(h * HEAD_DIM, (h + 1) * HEAD_DIM) for h in heads]
        s = [dot(kt, qt_ref[parts[h], block(qb)]) for h in heads]
        if mask is not None:
            s = [jnp.where(mask, x, score_masked) for x in s]
        old = [top_ref[h : h + 1, :] for h in heads]
        new = [jnp.maximum(old[h], jnp.max(s[h], axis=0, keepdims=True)) for h in heads]
        p = [jnp.exp(s[h] - new[h]) for h in heads]
        factor = [jnp.exp(old[h] - new[h]) for h in heads]
        total = [
            sum_ref[h : h + 1, :] * factor[h] + jnp.sum(p[h], axis=0, keepdims=True) for h in heads
        ]
        mixed = [acc_ref[parts[h], :] * factor[h] + dot(vt, p[h].astype(bf16)) for h in heads]
        for h in heads:
            top_ref[h : h + 1, :] = new[h]
            sum_ref[h : h + 1, :] = total[h]
            acc_ref[parts[h], :] = mixed[h]

    def same(kb, gq):
        return docs_col_ref[kb] == docs_ref[gq].astype(f32)

    def attended_copy(to, slot):
        return remote(
            staged_ref.at[to], attended_ref.at[slot], a_send.at[to], a_recv.at[slot], place.ctx(to)
        )

    def q_block(j, _):
        for at, act in (
            (2, spreads[0].step1), (4, spreads[0].step2), (4, spreads[1].start),
            (6, spreads[0].step3),
        ):
            pl.when(j == at)(act)
        qb = GROUP - 1 - j
        gq = first + qb
        top_ref[...] = jnp.full_like(top_ref, score_masked)
        sum_ref[...] = jnp.ones_like(sum_ref)
        acc_ref[...] = jnp.zeros_like(acc_ref)
        last = gq == n_blocks - 1

        def k_block(kb, _):
            edge = jnp.logical_or(kb == 0, last)

            @pl.when(edge)
            def _():
                tile(kb, qb, same(kb, gq))

            @pl.when(jnp.logical_not(edge))
            def _():
                tile(kb, qb, None)

            return 0

        lax.fori_loop(0, gq, k_block, 0)
        keys = lax.broadcasted_iota(jnp.int32, (T, T), 0)
        queries = lax.broadcasted_iota(jnp.int32, (T, T), 1)
        tile(gq, qb, same(gq, gq) & (keys <= queries))
        lse_ref[qb] = top_ref[...] + jnp.log(sum_ref[...])
        for h in range(HEADS):
            part = slice(h * HEAD_DIM, (h + 1) * HEAD_DIM)
            mixed = acc_ref[part, :] / sum_ref[h : h + 1, :]
            o_ref[part, block(qb)] = mixed
            staged_ref[qb, part, :] = mixed.astype(bf16)

        @pl.when(qb != me)
        def _():
            attended_copy(qb, me).start()

        return 0

    lax.fori_loop(0, GROUP, q_block, 0)
    own = pltpu.make_async_copy(staged_ref.at[me], attended_ref.at[me], local.at[2])
    own.start()
    spreads[1].step1()
    spreads[1].step2()
    spreads[1].step3()
    for j in range(1, GROUP):
        other = lax.rem(me + j, GROUP)
        attended_copy(other, other).wait()
    for spread in spreads:
        spread.last()
        spread.sent()
    for move in moves:
        move.wait()
    own.wait()


def attend_call(qt, k, vt, docs, strips, w_all):
    n = k.shape[0] // TOK_DEV
    span = qt.shape[1]
    depth, _, size = w_all.shape
    return pl.pallas_call(
        functools.partial(attend_kernel, n),
        out_shape=(
            shape((QW, span), f32),
            shape((GROUP, 8, TOK_DEV), f32),
            shape((GROUP, QW, TOK_DEV), bf16),
            shape((depth, GROUP) + strips.shape[1:], bf16),
            shape((GROUP, depth, HW - FIRST, size), bf16),
        ),
        in_specs=[IN_VMEM] * 6,
        out_specs=(IN_VMEM, IN_VMEM, IN_ANY, IN_ANY, IN_ANY),
        scratch_shapes=[
            VMEM((GROUP, QW, TOK_DEV), bf16),
            VMEM((n, TOK_DEV, 1), f32),
            VMEM((8, TOK_DEV), f32),
            VMEM((8, TOK_DEV), f32),
            VMEM((QW, TOK_DEV), f32),
            DMA((GROUP,)),
            DMA((GROUP,)),
        ]
        + [DMA((Spread.SEMS,))] * 4
        + [DMA((3,))],
        compiler_params=params(2),
        name="attend",
    )(qt, k, vt, docs, strips, w_all)


def router_of(w_all_ref):
    return [w_all_ref[s, HW:, :] for s in range(w_all_ref.shape[0])]


def dispatch_kernel(
    attended_ref, weight_ref, gate_up_ref, tokens_ref, gain_ref, w_all_ref, routes_ref, placed_ref,
    cotangent_ref,
    residual_ref, normed_ref, gates_ref, slot_gates_ref, rows_ref, grads_ref, gate_ref, up_ref,
    active_ref, grad_down_ref, columns_ref,
    held_ref, weight_held, gate_up_held, mixed_ref, own_rows, own_grads,
    r_send, r_recv, g_send, g_recv, c_send, c_recv, local,
):
    place = Place()
    me = place.me
    fetches = [
        pltpu.make_async_copy(attended_ref, held_ref, local.at[0]),
        pltpu.make_async_copy(weight_ref, weight_held, local.at[1]),
        pltpu.make_async_copy(gate_up_ref, gate_up_held, local.at[3]),
    ]
    met = greet(place.others())
    for fetch in fetches:
        fetch.start()
    rows, width = tokens_ref.shape
    experts_wide = gates_ref.shape[0]

    def copy(source, target, send, receive, j):
        to = lax.rem(me + j, GROUP)
        return remote(source.at[to], target.at[me], send.at[j], receive.at[j], place.ctx(to))

    def strip_copy(j):
        to = lax.rem(me + j, GROUP)
        return remote(
            attended_ref.at[:, to], columns_ref.at[me], c_send.at[j], c_recv.at[j], place.ctx(to)
        )

    fetches[0].wait()
    met()
    for j in range(1, GROUP):
        strip_copy(j).start()
    own_strip = pltpu.make_async_copy(held_ref.at[:, me], columns_ref.at[me], local.at[2])
    own_strip.start()
    mixed_ref[...] = held_ref[...].reshape(width, rows).T
    fetches[1].wait()

    def out_columns(i, _):
        columns = block(i)
        residual_ref[:, columns] = tokens_ref[:, columns].astype(f32) + dot(
            mixed_ref[...], weight_held[:, columns]
        )
        return 0

    lax.fori_loop(0, width // TOK_DEV, out_columns, 0)
    residual = residual_ref[...]
    scale = lax.rsqrt(jnp.mean(residual * residual, axis=-1, keepdims=True) + epsilon)
    normed_ref[...] = (residual * scale * gain_ref[...]).astype(bf16)
    logits = None
    for s, router in enumerate(router_of(w_all_ref)):
        size = router.shape[1]
        term = dot(router, normed_ref[:, s * size : (s + 1) * size], ((1,), (1,)))
        logits = term if logits is None else logits + term
    expert = lax.broadcasted_iota(jnp.int32, (experts_wide, rows), 0)
    chosen = expert < 0
    for k in range(TOPK):
        chosen = chosen | (expert == routes_ref[k : k + 1, :])
    logits = jnp.where(chosen, logits, score_masked)
    top = jnp.max(logits, axis=0, keepdims=True)
    gates = jnp.where(chosen, jnp.exp(logits - top), 0.0)
    gates = gates / jnp.sum(gates, axis=0, keepdims=True)
    gates_ref[...] = gates
    for e in range(EXP_WIN):
        slot_gates_ref[e] = jnp.sum(
            placed_ref[e].astype(f32) * gates[e : e + 1, :], axis=1, keepdims=True
        )

    def send_rows(j, _):
        to = lax.rem(me + j, GROUP)
        own_rows[to] = dot(placed_ref[to], normed_ref[...]).astype(bf16)

        @pl.when(j < GROUP)
        def _():
            copy(own_rows, rows_ref, r_send, r_recv, j).start()

        return 0

    def send_grads(j, _):
        to = lax.rem(me + j, GROUP)
        routed = dot(placed_ref[to], cotangent_ref[...])
        own_grads[to] = (routed * slot_gates_ref[to]).astype(bf16)

        @pl.when(j < GROUP)
        def _():
            copy(own_grads, grads_ref, g_send, g_recv, j).start()

        return 0

    lax.fori_loop(1, GROUP + 1, send_rows, 0)
    lax.fori_loop(1, GROUP + 1, send_grads, 0)
    rows_ref[me] = own_rows[me]
    grads_ref[me] = own_grads[me]
    fetches[2].wait()
    for j in range(1, GROUP):
        copy(own_rows, rows_ref, r_send, r_recv, j).wait_recv()
    slots = GROUP * CAP
    hidden = gate_ref.shape[1]
    tiles = hidden // TOK_DEV

    def expert_up(i, _):
        came = rows_ref[...].reshape(slots, width)
        gate = dot(came, gate_up_held[:, block(i)])
        up = dot(came, gate_up_held[:, block(tiles + i)])
        gate_ref[:, block(i)] = gate
        up_ref[:, block(i)] = up
        active_ref[:, block(i)] = (gate * jax.nn.sigmoid(gate) * up).astype(bf16)
        return 0

    lax.fori_loop(0, tiles, expert_up, 0)
    for j in range(1, GROUP):
        copy(own_grads, grads_ref, g_send, g_recv, j).wait_recv()

    def expert_over(i, _):
        grad_down_ref[:, block(i)] = dot(
            active_ref[...], grads_ref[:, :, block(i)].reshape(slots, TOK_DEV), ((0,), (0,))
        ).astype(bf16)
        return 0

    lax.fori_loop(0, width // TOK_DEV, expert_over, 0)
    for j in range(1, GROUP):
        strip_copy(j).wait()
        copy(own_rows, rows_ref, r_send, r_recv, j).wait_send()
        copy(own_grads, grads_ref, g_send, g_recv, j).wait_send()
    own_strip.wait()


def dispatch_call(attended, weight, gate_up, tokens, gain, w_all, routes, placed, cotangent):
    rows, width = tokens.shape
    hidden = gate_up.shape[1] // 2
    count = GROUP * CAP
    slots = (GROUP, CAP, width)
    depth = w_all.shape[0]
    attended = attended.reshape(depth, GROUP, -1, rows)
    return pl.pallas_call(
        dispatch_kernel,
        out_shape=(
            shape((rows, width), f32),
            shape((rows, width), bf16),
            shape((ROUTER, rows), f32),
            shape((EXP_WIN, CAP, 1), f32),
            shape(slots, bf16),
            shape(slots, bf16),
            shape((count, hidden), f32),
            shape((count, hidden), f32),
            shape((count, hidden), bf16),
            shape((hidden, width), bf16),
            shape((GROUP, depth) + attended.shape[2:], bf16),
        ),
        in_specs=[IN_ANY] * 3 + [IN_VMEM] * 6,
        out_specs=(IN_VMEM,) * 10 + (IN_ANY,),
        scratch_shapes=[
            VMEM(attended.shape, bf16),
            VMEM(weight.shape, bf16),
            VMEM(gate_up.shape, bf16),
            VMEM((rows, width), bf16),
            VMEM(slots, bf16),
            VMEM(slots, bf16),
        ]
        + [DMA((GROUP,))] * 6
        + [DMA((4,))],
        compiler_params=params(3),
        name="dispatch",
    )(attended, weight, gate_up, tokens, gain, w_all, routes, placed, cotangent)


def expert_kernel(
    active_ref, down_ref, grads_ref, rows_ref, gate_ref, up_ref, gate_up_ref,
    out_ref, back_ref, grad_gate_up_ref,
    grads_held, rows_held, gate_up_held, own_ref, grad_ref, send, receive, local,
):
    place = Place()
    me = place.me
    met = greet(place.others())
    fetches = [
        pltpu.make_async_copy(grads_ref, grads_held, local.at[0]),
        pltpu.make_async_copy(rows_ref, rows_held, local.at[1]),
        pltpu.make_async_copy(gate_up_ref, gate_up_held, local.at[2]),
    ]
    for fetch in fetches:
        fetch.start()
    count, hidden = active_ref.shape
    width = down_ref.shape[1]
    T = TOK_DEV
    tiles = hidden // T

    def copy(j):
        to = lax.rem(me + j, GROUP)
        return remote(own_ref.at[to], out_ref.at[me], send.at[j], receive.at[j], place.ctx(to))

    def out(i, _):
        value = dot(active_ref[...], down_ref[:, block(i)]).astype(bf16)
        own_ref[:, :, block(i)] = value.reshape(GROUP, CAP, T)
        return 0

    lax.fori_loop(0, width // T, out, 0)
    met()
    for j in range(1, GROUP):
        copy(j).start()
    move = pltpu.make_async_copy(own_ref.at[me], out_ref.at[me], local.at[3])
    move.start()
    fetches[0].wait()

    def back(i, _):
        grad = dot(grads_held[...], down_ref[block(i), :], ((1,), (1,)))
        gate, up = gate_ref[:, block(i)], up_ref[:, block(i)]
        sigmoid = jax.nn.sigmoid(gate)
        grad_gate = grad * up * sigmoid * (1.0 + gate * (1.0 - sigmoid))
        grad_ref[:, block(i)] = grad_gate.astype(bf16)
        grad_ref[:, block(tiles + i)] = (grad * gate * sigmoid).astype(bf16)
        return 0

    lax.fori_loop(0, tiles, back, 0)
    fetches[1].wait()
    fetches[2].wait()

    def over(i, _):
        grad_gate_up_ref[block(i), :] = dot(
            rows_held[:, block(i)], grad_ref[...], ((0,), (0,))
        ).astype(bf16)
        back_ref[:, block(i)] = dot(
            grad_ref[...], gate_up_held[block(i), :], ((1,), (1,))
        ).astype(bf16)
        return 0

    lax.fori_loop(0, width // T, over, 0)
    for j in range(1, GROUP):
        copy(j).wait()
    move.wait()


def expert_call(active, down, grads, rows, gate, up, gate_up):
    count, width = rows.shape
    hidden = down.shape[0]
    slots = (GROUP, CAP, width)
    return pl.pallas_call(
        expert_kernel,
        out_shape=(
            shape(slots, bf16),
            shape((count, width), bf16),
            shape((width, 2 * hidden), bf16),
        ),
        in_specs=[IN_VMEM] * 2 + [IN_ANY] * 2 + [IN_VMEM] * 2 + [IN_ANY],
        out_specs=(IN_ANY,) + (IN_VMEM,) * 2,
        scratch_shapes=[
            VMEM(grads.shape, bf16),
            VMEM(rows.shape, bf16),
            VMEM(gate_up.shape, bf16),
            VMEM(slots, bf16),
            VMEM((count, 2 * hidden), bf16),
            DMA((GROUP,)),
            DMA((GROUP,)),
            DMA((4,)),
        ],
        compiler_params=params(7),
        name="expert",
    )(active, down, grads, rows, gate, up, gate_up)


def combine_kernel(
    out_ref, sent_grad_ref, weight_ref, residual_ref, normed_ref, gates_ref, placed_ref,
    placed_t_ref, slot_gates_ref, cotangent_ref, gain_ref, w_all_ref,
    output_ref, grad_residual_ref, heads_ref, attn_ref, grad_router_ref, grad_gain_ref,
    back_ref, weight_held, sum_ref, turned_ref, staged_ref, scaled_ref,
    b_send, b_recv, h_send, h_recv, local,
):
    place = Place()
    me = place.me
    met = greet(place.others())
    fetch = pltpu.make_async_copy(weight_ref, weight_held, local.at[0])
    fetch.start()
    rows, width = residual_ref.shape

    def copy(source, target, send, receive, j):
        to = lax.rem(me + j, GROUP)
        return remote(source.at[to], target.at[me], send.at[j], receive.at[j], place.ctx(to))

    backs = [copy(sent_grad_ref, back_ref, b_send, b_recv, j) for j in range(1, GROUP)]
    met()
    for one in backs:
        one.start()
    move = pltpu.make_async_copy(sent_grad_ref.at[me], back_ref.at[me], local.at[1])
    move.start()
    turned_ref[...] = jnp.zeros_like(turned_ref)

    def add_expert(e, _):
        came = out_ref[e].astype(f32)
        scaled_ref[e] = (came * slot_gates_ref[e]).astype(bf16)
        routed = dot(placed_ref[e], cotangent_ref[...])
        slot_grad = jnp.sum(routed * came, axis=1, keepdims=True)
        turned_ref[pl.ds(e, 1), :] = jnp.sum(
            placed_ref[e].astype(f32) * slot_grad, axis=0, keepdims=True
        )
        return 0

    lax.fori_loop(0, EXP_WIN, add_expert, 0)
    slots = EXP_WIN * CAP

    def mix(i, _):
        columns = block(i)
        mixed = dot(placed_t_ref[...], scaled_ref[:, :, columns].reshape(slots, TOK_DEV))
        output_ref[:, columns] = (residual_ref[:, columns] + mixed).astype(bf16)
        return 0

    lax.fori_loop(0, width // TOK_DEV, mix, 0)
    gates = gates_ref[...]
    grad_gates = turned_ref[...]
    weighted = jnp.sum(gates * grad_gates, axis=0, keepdims=True)
    grad_logits = (gates * (grad_gates - weighted)).astype(bf16)
    for s, router in enumerate(router_of(w_all_ref)):
        size = router.shape[1]
        sum_ref[:, s * size : (s + 1) * size] = dot(grad_logits, router, ((0,), (0,)))
    grad_router_ref[...] = dot(grad_logits, normed_ref[...])
    fetch.wait()
    move.wait()
    for one in backs:
        one.wait_recv()

    def add_back(i, _):
        columns = block(i)
        sum_ref[:, columns] += dot(
            placed_t_ref[...], back_ref[:, :, columns].reshape(slots, TOK_DEV)
        )
        return 0

    lax.fori_loop(0, width // TOK_DEV, add_back, 0)
    residual = residual_ref[...]
    grad_normed = sum_ref[...]
    scale = lax.rsqrt(jnp.mean(residual * residual, axis=-1, keepdims=True) + epsilon)
    scaled = grad_normed * gain_ref[...]
    inner = jnp.mean(scaled * residual, axis=-1, keepdims=True)
    grad = scale * scaled - residual * (scale * scale * scale * inner)
    grad_gain_ref[...] = jnp.sum(grad_normed * residual * scale, axis=0, keepdims=True)
    grad_residual = cotangent_ref[...].astype(f32) + grad
    grad_residual_ref[...] = grad_residual
    attn_ref[...] = grad_residual.astype(bf16)

    def head_rows(j, _):
        to = lax.rem(me + j, GROUP)
        staged_ref[to] = dot(weight_held[block(to, QW), :], attn_ref[...], ((1,), (1,))).astype(bf16)

        @pl.when(j < GROUP)
        def _():
            copy(staged_ref, heads_ref, h_send, h_recv, j).start()

        return 0

    lax.fori_loop(1, GROUP + 1, head_rows, 0)
    move = pltpu.make_async_copy(staged_ref.at[me], heads_ref.at[me], local.at[2])
    move.start()
    for one in backs:
        one.wait_send()
    for j in range(1, GROUP):
        copy(staged_ref, heads_ref, h_send, h_recv, j).wait()
    move.wait()


def combine_call(
    out, sent_grad, weight, residual, normed, gates, placed, placed_t, slot_gates, cotangent,
    gain, w_all,
):
    rows, width = residual.shape
    slots = (GROUP, CAP, width)
    return pl.pallas_call(
        combine_kernel,
        out_shape=(
            shape((rows, width), bf16),
            shape((rows, width), f32),
            shape((GROUP, QW, rows), bf16),
            shape((rows, width), bf16),
            shape((ROUTER, width), f32),
            shape((1, width), f32),
        ),
        in_specs=[IN_VMEM] + [IN_ANY] * 2 + [IN_VMEM] * 9,
        out_specs=(IN_VMEM, IN_VMEM, IN_ANY, IN_VMEM, IN_VMEM, IN_VMEM),
        scratch_shapes=[
            VMEM(slots, bf16),
            VMEM(weight.shape, bf16),
            VMEM((rows, width), f32),
            VMEM((ROUTER, rows), f32),
            VMEM((GROUP, QW, rows), bf16),
            VMEM(slots, bf16),
        ]
        + [DMA((GROUP,))] * 4
        + [DMA((3,))],
        compiler_params=params(4),
        name="combine",
    )(
        out, sent_grad, weight, residual, normed, gates, placed, placed_t, slot_gates, cotangent,
        gain, w_all,
    )


def backward_kernel(
    n_blocks, qt_ref, k_ref, kt_ref, v_ref, heads_ref, o_ref, lse_ref, docs_ref, attn_ref,
    columns_ref, down_ref,
    dq_ref, dk_ref, dv_ref, out_shard_ref, down_all_ref,
    grad_out_ref, out_in, attn_all_ref, docs_col_ref, delta_ref, dk_acc, dv_acc, a_send, a_recv, e_send, e_recv, o_send, o_recv,
    local,
):
    T = TOK_DEV
    place = Place()
    me = place.me
    first = place.base
    met = greet([place.ctx(i) for i in place.near] + place.layers())
    z, layers = place.z, place.depth
    move = pltpu.make_async_copy(attn_ref, attn_all_ref.at[me], local.at[0])
    move.start()
    spread = Spread(
        place, attn_ref, lambda owner: attn_all_ref.at[owner],
        halves(T), a_send, a_recv,
    )
    met()
    spread.start()
    down_move = pltpu.make_async_copy(down_ref, down_all_ref.at[me], local.at[1])
    down_move.start()
    down_spread = Spread(
        place, down_ref, lambda owner: down_all_ref.at[owner],
        halves(down_ref.shape[0]), e_send, e_recv,
    )

    def turn(i, _):
        docs_col_ref[i] = docs_column(docs_ref[i])
        return 0

    lax.fori_loop(0, n_blocks, turn, 0)
    heads = range(HEADS)
    parts = [slice(h * HEAD_DIM, (h + 1) * HEAD_DIM) for h in heads]

    def prepare(i, _):
        for h in heads:
            product = o_ref[parts[h], block(i)] * heads_ref[i, parts[h], :].astype(f32)
            delta_ref[i, h : h + 1, :] = jnp.sum(product, axis=0, keepdims=True)
        return 0

    lax.fori_loop(0, GROUP, prepare, 0)
    dq_ref[...] = jnp.zeros_like(dq_ref)

    def tile(kb, qb, mask):
        k = k_ref[block(kb), :]
        v = v_ref[block(kb), :]
        kt = kt_ref[:, block(kb)]
        q = [qt_ref[part, block(qb)] for part in parts]
        do = [heads_ref[qb, part, :] for part in parts]
        s = [dot(k, x) for x in q]
        dp = [dot(v, x) for x in do]
        p = [jnp.exp(s[h] - lse_ref[qb, h : h + 1, :]) for h in heads]
        if mask is not None:
            p = [jnp.where(mask, x, 0.0) for x in p]
        ds = [(p[h] * (dp[h] - delta_ref[qb, h : h + 1, :])).astype(bf16) for h in heads]
        pb = [x.astype(bf16) for x in p]
        turn = ((1,), (1,))
        dv_acc[...] += dot(pb[0], do[0], turn) + dot(pb[1], do[1], turn) + dot(pb[2], do[2], turn)
        dk_acc[...] += dot(ds[0], q[0], turn) + dot(ds[1], q[1], turn) + dot(ds[2], q[2], turn)
        for h in heads:
            dq_ref[parts[h], block(qb)] += dot(kt, ds[h])

    def same(kb, gq):
        return docs_col_ref[kb] == docs_ref[gq].astype(f32)

    depth, strip, width = grad_out_ref.shape

    def down_copy(j):
        to = lax.rem(z + j, layers)
        return remote(
            grad_out_ref.at[to], out_in.at[z], o_send.at[j], o_recv.at[j], place.fsdp(to)
        )

    def out_weights():
        move.wait()
        spread.last()

        def columns(i, _):
            total = None
            for b in range(GROUP):
                term = dot(columns_ref[b].reshape(depth * strip, T), attn_all_ref[b, :, block(i)])
                total = term if total is None else total + term
            grad_out_ref[:, :, block(i)] = total.astype(bf16).reshape(depth, strip, T)
            return 0

        lax.fori_loop(0, width // T, columns, 0)
        for j in range(1, layers):
            down_copy(j).start()

    def k_block(kb, _):
        for at, act in (
            (2, spread.step1), (3, spread.step2), (3, down_spread.start), (5, spread.step3),
            (6, down_spread.step1), (7, out_weights),
        ):
            pl.when(kb == first + at)(act)
        dk_acc[...] = jnp.zeros_like(dk_acc)
        dv_acc[...] = jnp.zeros_like(dv_acc)

        @pl.when(kb >= first)
        def _():
            keys = lax.broadcasted_iota(jnp.int32, (T, T), 0)
            queries = lax.broadcasted_iota(jnp.int32, (T, T), 1)
            tile(kb, kb - first, same(kb, kb) & (keys <= queries))

        def q_block(qb, _):
            gq = first + qb
            edge = jnp.logical_or(kb == 0, gq == n_blocks - 1)

            @pl.when(edge)
            def _():
                tile(kb, qb, same(kb, gq))

            @pl.when(jnp.logical_not(edge))
            def _():
                tile(kb, qb, None)

            return 0

        lax.fori_loop(jnp.maximum(kb - first + 1, 0), GROUP, q_block, 0)
        dk_ref[:, block(kb)] = dk_acc[...].T
        dv_ref[:, block(kb)] = dv_acc[...].T
        return 0

    lax.fori_loop(0, first + GROUP, k_block, 0)

    def clear(kb, _):
        dk_ref[:, block(kb)] = jnp.zeros((HEAD_DIM, T), f32)
        dv_ref[:, block(kb)] = jnp.zeros((HEAD_DIM, T), f32)
        return 0

    lax.fori_loop(first + GROUP, n_blocks, clear, 0)
    down_spread.step2()
    down_spread.step3()
    for j in range(1, layers):
        down_copy(j).wait()
    out_in[z] = grad_out_ref[z]
    total = out_in[0].astype(f32)
    for s in range(1, layers):
        total = total + out_in[s].astype(f32)
    out_shard_ref[...] = total.astype(bf16)
    down_spread.last()
    down_spread.sent()
    down_move.wait()
    spread.sent()


def backward_call(qt, k, kt, v, heads, o, lse, docs, attn, columns, down):
    n = k.shape[0] // TOK_DEV
    span = qt.shape[1]
    rows, width = attn.shape
    _, depth, strip, _ = columns.shape
    return pl.pallas_call(
        functools.partial(backward_kernel, n),
        out_shape=(
            shape((QW, span), f32),
            shape(kt.shape, f32),
            shape(kt.shape, f32),
            shape((strip, width), bf16),
            shape((GROUP,) + down.shape, bf16),
        ),
        in_specs=[IN_VMEM] * 11,
        out_specs=(IN_VMEM,) * 4 + (IN_ANY,),
        scratch_shapes=[
            VMEM((depth, strip, width), bf16),
            VMEM((depth, strip, width), bf16),
            VMEM((GROUP, rows, width), bf16),
            VMEM((n, TOK_DEV, 1), f32),
            VMEM((GROUP, 8, TOK_DEV), f32),
            VMEM((TOK_DEV, HEAD_DIM), f32),
            VMEM((TOK_DEV, HEAD_DIM), f32),
        ]
        + [DMA((Spread.SEMS,))] * 4
        + [DMA((depth,))] * 2
        + [DMA((2,))],
        compiler_params=params(5),
        name="backward",
    )(qt, k, kt, v, heads, o, lse, docs, attn, columns, down)


def finish_kernel(
    normed_ref, first_ref, others_ref, gate_up_ref, out_shard_ref, dq_ref, dk_ref, dv_ref, cos_ref,
    sin_ref, tokens_ref, gain_ref, grad_residual_ref, grad_router_ref, grad_gain2_ref,
    input_grad_ref, shared_ref, small_all_ref, out_all_ref, gate_up_all_ref,
    normed_held, first_held, others_held, linear_ref, came_ref, first_t, others_t, sum_ref, part_ref,
    small_ref, head_in, small_in, shard_ref, small_shard_ref,
    g_send, g_recv, h_send, h_recv, s_send, s_recv, e_send, e_recv, f_send, f_recv, m_send, m_recv,
    c_send, c_recv, local,
):
    place = Place()
    me, z, depth = place.me, place.z, place.depth
    met = greet(place.others() + place.layers())
    fetches = [
        pltpu.make_async_copy(normed_ref, normed_held, local.at[0]),
        pltpu.make_async_copy(first_ref, first_held, local.at[1]),
        pltpu.make_async_copy(others_ref, others_held, local.at[2]),
    ]
    for fetch in fetches:
        fetch.start()
    rows, width = tokens_ref.shape
    size = width // depth

    def spread_of(source, out, send, receive):
        return Spread(
            place, source, lambda owner: out.at[owner], halves(source.shape[0]), send, receive
        )

    expert_spread = spread_of(gate_up_ref, gate_up_all_ref, e_send, e_recv)
    head_spread = spread_of(shard_ref, shared_ref, f_send, f_recv)
    small_spread = spread_of(small_shard_ref, small_all_ref, m_send, m_recv)
    out_spread = spread_of(out_shard_ref, out_all_ref, c_send, c_recv)
    moves = [
        pltpu.make_async_copy(gate_up_ref, gate_up_all_ref.at[me], local.at[3]),
        pltpu.make_async_copy(out_shard_ref, out_all_ref.at[me], local.at[4]),
        pltpu.make_async_copy(shard_ref, shared_ref.at[me], local.at[5]),
        pltpu.make_async_copy(small_shard_ref, small_all_ref.at[me], local.at[6]),
    ]
    moves[0].start()
    moves[1].start()

    def copy(j):
        to = lax.rem(me + j, GROUP)
        return remote(
            linear_ref.at[to], came_ref.at[me], g_send.at[j], g_recv.at[j], place.ctx(to)
        )

    def down(source, target, send, receive, j):
        to = lax.rem(z + j, depth)
        return remote(source.at[to], target.at[z], send.at[j], receive.at[j], place.fsdp(to))

    def turn_back(j, _):
        to = lax.rem(me + j, GROUP)
        cosine, sine = cos_ref[:, block(to)], -sin_ref[:, block(to)]
        dq = turned(dq_ref[:, block(to)], cosine, sine) * HEAD_DIM ** (-0.5)
        dk = turned(dk_ref[:, block(to)], cosine, sine)
        linear_ref[to, :QW, :] = dq.astype(bf16)
        linear_ref[to, QW : QW + HEAD_DIM, :] = dk.astype(bf16)
        linear_ref[to, QW + HEAD_DIM :, :] = dv_ref[:, block(to)].astype(bf16)
        pl.when(j == 1)(met)

        @pl.when(j < GROUP)
        def _():
            copy(j).start()

        return 0

    lax.fori_loop(1, GROUP + 1, turn_back, 0)
    came_ref[me] = linear_ref[me]
    out_spread.start()
    fetches[0].wait()

    def own_weights(j, _):
        to = lax.rem(z + j, depth)
        columns = block(to, size)
        total = None
        for b in range(GROUP):
            term = dot(linear_ref[b], normed_held[b, :, columns])
            total = term if total is None else total + term
        part_ref[to] = total.astype(bf16)

        @pl.when(j < depth)
        def _():
            down(part_ref, head_in, h_send, h_recv, j).start()

        return 0

    lax.fori_loop(1, depth + 1, own_weights, 0)
    for j in range(1, GROUP):
        copy(j).wait_send()
    expert_spread.start()
    fetches[1].wait()
    fetches[2].wait()
    for j in range(1, GROUP):
        copy(j).wait_recv()

    def turn(j, _):
        first_t[j] = came_ref[j, :FIRST, :].T
        others_t[j] = came_ref[j, FIRST:, :].T
        return 0

    lax.fori_loop(0, GROUP, turn, 0)

    def add_heads(s, _):
        total = None
        for j in range(GROUP):
            term = dot(first_t[j], first_held[j, s]) + dot(others_t[j], others_held[j, s])
            total = term if total is None else total + term
        sum_ref[:, block(s, size)] = total
        return 0

    lax.fori_loop(0, depth, add_heads, 0)
    out_spread.step1()
    x = tokens_ref[...].astype(f32)
    grad_normed = sum_ref[...]
    scale = lax.rsqrt(jnp.mean(x * x, axis=-1, keepdims=True) + epsilon)
    scaled = grad_normed * gain_ref[...]
    inner = jnp.mean(scaled * x, axis=-1, keepdims=True)
    grad = scale * scaled - x * (scale * scale * scale * inner)
    input_grad_ref[...] = grad_residual_ref[...] + grad
    gain1 = jnp.sum(grad_normed * x * scale, axis=0, keepdims=True)
    row = lax.broadcasted_iota(jnp.int32, (ROUTER, width), 0)
    small = jnp.where(row == ROUTER - 2, gain1, grad_router_ref[...])
    small = jnp.where(row == ROUTER - 1, grad_gain2_ref[...], small).astype(bf16)
    for s in range(depth):
        small_ref[s] = small[:, s * size : (s + 1) * size]
    smalls = [down(small_ref, small_in, s_send, s_recv, j) for j in range(1, depth)]
    heads = [down(part_ref, head_in, h_send, h_recv, j) for j in range(1, depth)]
    for one in smalls:
        one.start()
    expert_spread.step1()
    head_in[z] = part_ref[z]
    small_in[z] = small_ref[z]

    def total(ref):
        value = ref[0].astype(f32)
        for s in range(1, depth):
            value = value + ref[s].astype(f32)
        return value.astype(bf16)

    for one in heads:
        one.wait_recv()
    shard_ref[...] = total(head_in)
    head_spread.start()
    out_spread.step2()
    expert_spread.step2()
    for one in smalls:
        one.wait_recv()
    small_shard_ref[...] = total(small_in)
    small_spread.start()
    moves[2].start()
    moves[3].start()
    out_spread.step3()
    expert_spread.step3()
    spreads = (head_spread, small_spread)
    for spread in spreads:
        spread.step1()
    for spread in spreads:
        spread.step2()
    for spread in spreads:
        spread.step3()
    for spread in (out_spread, expert_spread, head_spread, small_spread):
        spread.last()
        spread.sent()
    for one in heads + smalls:
        one.wait_send()
    for move in moves:
        move.wait()


def finish_call(
    normed, first, others, gate_up, out_shard, dq, dk, dv, cosine, sine, tokens, gain, grad_residual,
    grad_router, grad_gain2, depth,
):
    rows, width = tokens.shape
    size = width // depth
    return pl.pallas_call(
        finish_kernel,
        out_shape=(
            shape((rows, width), f32),
            shape((GROUP, HW, size), bf16),
            shape((GROUP, ROUTER, size), bf16),
            shape((GROUP,) + out_shard.shape, bf16),
            shape((GROUP,) + gate_up.shape, bf16),
        ),
        in_specs=[IN_ANY] * 3 + [IN_VMEM] * 12,
        out_specs=(IN_VMEM,) + (IN_ANY,) * 4,
        scratch_shapes=[
            VMEM(normed.shape, bf16),
            VMEM(first.shape, bf16),
            VMEM(others.shape, bf16),
            VMEM((GROUP, HW, rows), bf16),
            VMEM((GROUP, HW, rows), bf16),
            VMEM((GROUP, rows, FIRST), bf16),
            VMEM((GROUP, rows, HW - FIRST), bf16),
            VMEM((rows, width), f32),
            VMEM((depth, HW, size), bf16),
            VMEM((depth, ROUTER, size), bf16),
            VMEM((depth, HW, size), bf16),
            VMEM((depth, ROUTER, size), bf16),
            VMEM((HW, size), bf16),
            VMEM((ROUTER, size), bf16),
        ]
        + [DMA((GROUP,))] * 2
        + [DMA((depth,))] * 4
        + [DMA((Spread.SEMS,))] * 8
        + [DMA((7,))],
        compiler_params=params(6),
        name="finish",
    )(
        normed, first, others, gate_up, out_shard, dq, dk, dv, cosine, sine, tokens, gain,
        grad_residual, grad_router, grad_gain2,
    )


def output_kernel(
    shared_ref, small_ref, out_ref, gate_up_ref, output_ref, input_grad_ref,
    q_ref, k_ref, v_ref, w_out_ref, router_ref, gain1_ref, gain2_ref, gate_ref, up_ref, final_ref,
    final_grad_ref, sum_ref,
):
    pair, i = shared_ref.shape[0], pl.program_id(0)
    hidden = gate_ref.shape[2]

    def rows(first, last):
        both = [shared_ref[p, first:last, :].astype(f32) for p in range(pair)]
        return jnp.concatenate(both, axis=0).T

    q_ref[...] = rows(0, QW)
    k_ref[...] = rows(QW, QW + HEAD_DIM)
    v_ref[...] = rows(QW + HEAD_DIM, HW)
    w_out_ref[...] = out_ref[...].astype(f32)
    final_ref[...] = output_ref[...]
    final_grad_ref[...] = input_grad_ref[...]
    gate_ref[...] = gate_up_ref[:, :, :hidden].astype(f32)
    up_ref[...] = gate_up_ref[:, :, hidden:].astype(f32)

    @pl.when(i == 0)
    def _():
        sum_ref[...] = jnp.zeros_like(sum_ref)

    for p in range(pair):
        sum_ref[...] += small_ref[p].astype(f32)

    @pl.when(i == pl.num_programs(0) - 1)
    def _():
        router_ref[...] = sum_ref[: router_ref.shape[0], :]
        gain1_ref[...] = sum_ref[ROUTER - 2, :]
        gain2_ref[...] = sum_ref[ROUTER - 1, :]


def output_call(shared, small, out, gate_up, output, input_grad, experts):
    count, _, size = shared.shape
    _, strip, width = out.shape
    hidden = gate_up.shape[2] // 2
    pair = 2
    rows = output.shape[0] // (count // pair)
    token = pl.BlockSpec((rows, width), lambda i: (i, 0))

    def first(*dims):
        return pl.BlockSpec((pair,) + dims, lambda i: (i,) + (0,) * len(dims))

    def columns(columns):
        return pl.BlockSpec((size, columns), lambda i: (0, i))

    def whole(*dims):
        return pl.BlockSpec(dims, lambda i: (0,) * len(dims))

    return pl.pallas_call(
        output_kernel,
        grid=(count // pair,),
        out_shape=(
            shape((size, count * QW), f32),
            shape((size, count * HEAD_DIM), f32),
            shape((size, count * HEAD_DIM), f32),
            shape(out.shape, f32),
            shape((experts, size), f32),
            shape((size,), f32),
            shape((size,), f32),
            shape((count, size, hidden), f32),
            shape((count, size, hidden), f32),
            shape(output.shape, bf16),
            shape(input_grad.shape, f32),
        ),
        in_specs=[
            first(*shared.shape[1:]), first(*small.shape[1:]), first(strip, width),
            first(*gate_up.shape[1:]), token, token,
        ],
        out_specs=(
            columns(pair * QW),
            columns(pair * HEAD_DIM),
            columns(pair * HEAD_DIM),
            first(strip, width),
            whole(experts, size),
            whole(size),
            whole(size),
            first(size, hidden),
            first(size, hidden),
            token,
            token,
        ),
        scratch_shapes=[VMEM((ROUTER, size), f32)],
        compiler_params=params(),
        name="output",
    )(shared, small, out, gate_up, output, input_grad)


def rotary_tables(length):
    frequencies = 10000.0 ** (-(np.arange(HEAD_DIM // 2) * 2.0) / HEAD_DIM)
    angles = frequencies[:, None] * np.arange(length)[None, :]
    return np.cos(angles).astype(np.float32), np.sin(angles).astype(np.float32)


def shards(
    tables,
    tokens,
    doc_ids,
    routes,
    slot_order,
    norm1_gain,
    norm2_gain,
    w_query,
    key_matrix,
    value_matrix,
    w_out,
    w_router,
    w_gate,
    w_up,
    w_down,
    cotangent,
):
    rows, width = tokens.shape[1:]
    ctx, depth = lax.axis_size("ctx"), lax.axis_size("fsdp")
    place = lax.axis_index("ctx")
    parts = ctx // GROUP
    head, part = place % GROUP, place // GROUP
    far = [[p * GROUP + i for p in range(parts)] for i in range(GROUP)]
    span = GROUP * rows
    experts = w_router.shape[1]
    hidden = w_gate.shape[2]

    def gather_z(value):
        return lax.all_gather(value, "fsdp", axis=0, tiled=True)

    def reduce_z(value):
        value = lax.psum_scatter(value.astype(bf16), "fsdp", scatter_dimension=0, tiled=True)
        if parts > 1:
            value = lax.psum(value, "ctx", axis_index_groups=far)
        return value

    cosine, sine = tables
    if parts > 1:
        cosine = lax.dynamic_slice_in_dim(cosine, part * span, span, 1)
        sine = lax.dynamic_slice_in_dim(sine, part * span, span, 1)
    own_tokens, own_cotangent = tokens[0], cotangent[0]
    gain1, gain2 = norm1_gain[None, :], norm2_gain[None, :]

    route_rows, order_rows = routes[0].T, slot_order[0].T
    (
        w_all, queries, keys_t, values_t, keys, values, docs, placed, placed_t, normed1, strips,
        first_all,
    ) = project_call(
        own_tokens, gain1, jnp.pad(w_router.T, ((0, ROUTER - experts), (0, 0))), cosine, sine, doc_ids,
        route_rows, order_rows, w_out, w_query, key_matrix, value_matrix, depth,
    )
    w_gate, w_up, w_down, docs = lax.optimization_barrier((w_gate, w_up, w_down, docs))
    gate_up = gather_z(
        jnp.concatenate(
            [
                lax.dynamic_index_in_dim(w_gate, head, 0, False),
                lax.dynamic_index_in_dim(w_up, head, 0, False),
            ],
            axis=1,
        )
    )
    down = gather_z(lax.dynamic_index_in_dim(w_down, head, 0, False))
    if parts > 1:

        def gather_far(value, axis):
            return lax.all_gather(value, "ctx", axis=axis, axis_index_groups=far, tiled=True)

        keys, values, docs = gather_far(keys, 0), gather_far(values, 0), gather_far(docs, 0)
        keys_t, values_t = gather_far(keys_t, 1), gather_far(values_t, 1)
    attended_f32, log_total, attended, out_weight, others_all = attend_call(
        queries, keys, values_t, docs, strips, w_all
    )
    out_weight = out_weight.reshape(width, width)
    (
        residual, normed2, gates, slot_gates, sent_rows, sent_grads, gate, up, active, grad_w_down,
        columns,
    ) = dispatch_call(
        attended, out_weight, gate_up, own_tokens, gain2, w_all, route_rows, placed, own_cotangent
    )
    grad_w_down = reduce_z(grad_w_down)
    expert_out, grad_buffer, grad_w_gate_up = expert_call(
        active, down, sent_grads.reshape(GROUP * CAP, width), sent_rows.reshape(GROUP * CAP, width),
        gate, up, gate_up,
    )
    grad_w_gate_up = reduce_z(grad_w_gate_up)
    output, grad_residual, heads, attn, grad_router, grad_gain2 = combine_call(
        expert_out, grad_buffer.reshape(sent_rows.shape), out_weight,
        residual, normed2, gates, placed, placed_t, slot_gates, own_cotangent, gain2, w_all,
    )
    dq, dk, dv, out_shard, down_w = backward_call(
        queries, keys, keys_t, values, heads, attended_f32, log_total, docs, attn, columns,
        grad_w_down,
    )
    if parts > 1:
        dk = lax.psum_scatter(dk, "ctx", scatter_dimension=1, axis_index_groups=far, tiled=True)
        dv = lax.psum_scatter(dv, "ctx", scatter_dimension=1, axis_index_groups=far, tiled=True)
    if parts > 1:
        out_shard = lax.psum(out_shard, "ctx", axis_index_groups=far)
    input_grad, shared, small, out_w, gate_up_w = finish_call(
        normed1, first_all, others_all, grad_w_gate_up, out_shard, dq, dk, dv, cosine, sine,
        own_tokens, gain1, grad_residual, grad_router, grad_gain2, depth,
    )
    if parts > 1:
        shared, small = lax.psum((shared, small), "ctx", axis_index_groups=far)

    q_w, k_w, v_w, out_w, router_w, gain1_w, gain2_w, gate_w, up_w, output, input_grad = output_call(
        shared, small, out_w, gate_up_w, output, input_grad, experts
    )
    return (
        output[None],
        input_grad[None],
        gain1_w,
        gain2_w,
        q_w,
        k_w,
        v_w,
        out_w.reshape(-1, width),
        router_w.T,
        gate_w,
        up_w,
        down_w.astype(f32),
    )


def solution(mesh):
    token_spec = P("fsdp", "ctx", None)
    row_spec, expert_spec = P("fsdp", None), P(None, "fsdp", None)
    tables = rotary_tables(mesh.shape["ctx"] * TOK_DEV)

    def program(*arguments):
        return jax.shard_map(
            functools.partial(shards, tuple(jnp.asarray(t) for t in tables)),
            mesh=mesh,
            in_specs=(
                token_spec,
                P("fsdp", "ctx"),
                token_spec,
                token_spec,
                P(),
                P(),
                row_spec,
                row_spec,
                row_spec,
                row_spec,
                row_spec,
                expert_spec,
                expert_spec,
                expert_spec,
                token_spec,
            ),
            out_specs=(
                token_spec,
                token_spec,
                P("fsdp"),
                P("fsdp"),
                row_spec,
                row_spec,
                row_spec,
                row_spec,
                row_spec,
                expert_spec,
                expert_spec,
                expert_spec,
            ),
            check_vma=False,
        )(*arguments)

    return program
```

```python
import functools

import jax
import jax.numpy as jnp
import numpy as np
from jax import lax
from jax.experimental import pallas as pl
from jax.experimental.pallas import tpu as pltpu
from jax.sharding import PartitionSpec as P

QUERY_HEADS = 24
KEY_VALUE_HEADS = 8
HEAD_DIM = 64
TOPK = 8
EXP_WIN = 8
TOK_DEV = 256
CAP = 64
GROUP = 8
HEADS = QUERY_HEADS // KEY_VALUE_HEADS
QW = HEADS * HEAD_DIM
HW = QW + 2 * HEAD_DIM
ROUTER = 48
ALL = HW + ROUTER
FIRST = 96

epsilon = 1e-06
score_masked = -1e30
bf16 = jnp.bfloat16
f32 = jnp.float32
VMEM = pltpu.VMEM
MESH = pl.DeviceIdType.MESH
DMA = pltpu.SemaphoreType.DMA
IN_VMEM = pl.BlockSpec(memory_space=VMEM)
IN_ANY = pl.BlockSpec(memory_space=pl.ANY)


def dot(left, right, dims=((1,), (0,))):
    return lax.dot_general(left, right, (dims, ((), ())), preferred_element_type=f32)


def block(index, size=TOK_DEV):
    return pl.ds(pl.multiple_of(index * size, size), size)


def shape(dims, dtype):
    return jax.ShapeDtypeStruct(dims, dtype)


def params(collective_id=None, limit=56):
    return pltpu.CompilerParams(
        collective_id=collective_id,
        has_side_effects=collective_id is not None,
        vmem_limit_bytes=limit << 20,
    )


class Staged:
    def __init__(self, fetches, puts):
        self.fetches, self.puts, self.out = fetches, puts, []

    def need(self, *refs):
        for ref in refs:
            self.fetches.pop(id(ref)).wait()

    def put(self, *refs):
        for ref in refs:
            copy = self.puts.pop(id(ref))
            copy.start()
            self.out.append(copy)

    def finish(self):
        for copy in self.fetches.values():
            copy.wait()
        for copy in self.puts.values():
            copy.start()
        for copy in self.out + list(self.puts.values()):
            copy.wait()


def staged_call(body, name, collective_id, ins, outs, scratch):
    held_in = [i for i, (how, _) in enumerate(ins) if how == "h"]
    held_out = [i for i, (how, _) in enumerate(outs) if how == "h"]

    def kernel(*refs):
        refs = list(refs)
        given, refs = refs[: len(ins)], refs[len(ins) :]
        results, refs = refs[: len(outs)], refs[len(outs) :]
        own, refs = refs[: len(scratch)], refs[len(scratch) :]
        in_held, refs = refs[: len(held_in)], refs[len(held_in) :]
        out_held, (in_sems, out_sems) = refs[: len(held_out)], refs[len(held_out) :]
        fetches, puts = {}, {}
        for n, i in enumerate(held_in):
            copy = pltpu.make_async_copy(given[i], in_held[n], in_sems.at[n])
            copy.start()
            given[i] = in_held[n]
            fetches[id(given[i])] = copy
        for n, i in enumerate(held_out):
            puts[id(out_held[n])] = pltpu.make_async_copy(out_held[n], results[i], out_sems.at[n])
            results[i] = out_held[n]
        stage = Staged(fetches, puts)
        body(stage, *given, *results, *own)
        stage.finish()

    return pl.pallas_call(
        kernel,
        out_shape=tuple(one for _, one in outs),
        in_specs=[IN_VMEM if how == "v" else IN_ANY for how, _ in ins],
        out_specs=tuple(IN_VMEM if how == "v" else IN_ANY for how, _ in outs),
        scratch_shapes=list(scratch)
        + [VMEM(ins[i][1].shape, ins[i][1].dtype) for i in held_in]
        + [VMEM(outs[i][1].shape, outs[i][1].dtype) for i in held_out]
        + [DMA((max(len(held_in), 1),)), DMA((max(len(held_out), 1),))],
        compiler_params=params(collective_id),
        name=name,
    )(*(array for _, array in ins))


def flip(index, bit):
    return index + (1 - 2 * ((index // bit) % 2)) * bit


class Place:
    def __init__(self):
        ctx = lax.axis_index("ctx")
        self.base = (ctx // GROUP) * GROUP
        self.me = ctx - self.base
        self.z = lax.axis_index("fsdp")
        self.depth = lax.axis_size("fsdp")
        self.near = [flip(self.me, bit) for bit in (1, 2, 4)]

    def ctx(self, index):
        return {"ctx": self.base + index}

    def fsdp(self, index):
        return {"fsdp": index}

    def others(self):
        return [self.ctx(lax.rem(self.me + j, GROUP)) for j in range(1, GROUP)]

    def layers(self):
        return [self.fsdp(lax.rem(self.z + j, self.depth)) for j in range(1, self.depth)]


def greet(devices):
    ready = pltpu.get_barrier_semaphore()
    for device in devices:
        pl.semaphore_signal(ready, inc=1, device_id=device, device_id_type=MESH)
    return lambda: pl.semaphore_wait(ready, len(devices))


def remote(source, target, send, receive, device):
    return pltpu.make_async_remote_copy(
        src_ref=source,
        dst_ref=target,
        send_sem=send,
        recv_sem=receive,
        device_id=device,
        device_id_type=MESH,
    )


def halves(count):
    cut = -(-count // 32) * 16

    def part(ref, half):
        return ref.at[pl.ds(0, cut)] if half == 0 else ref.at[pl.ds(cut, count - cut)]

    return part


class Spread:
    SEMS = 14

    def __init__(self, place, source, land, part, send, receive):
        me = place.me
        core, side, row = place.near
        across = flip(side, 4)

        def plan(slot, owner, half, device):
            target = part(land(owner), half)
            first = part(source, half) if slot < 6 else target
            return remote(first, target, send.at[slot], receive.at[slot], place.ctx(device))

        self.copies = [
            plan(0, me, 0, side), plan(1, me, 1, side), plan(2, me, 0, row), plan(3, me, 1, row),
            plan(4, me, 0, core), plan(5, me, 1, core), plan(6, side, 0, core),
            plan(7, side, 1, core), plan(8, row, 0, core), plan(9, row, 1, core),
            plan(10, side, 1, row), plan(11, row, 0, side), plan(12, across, 0, core),
            plan(13, across, 1, core),
        ]

    def go(self, *slots):
        for slot in slots:
            self.copies[slot].start()

    def wait(self, *slots):
        for slot in slots:
            self.copies[slot].wait_recv()

    def start(self):
        self.go(1, 2, 0, 3, 4, 5)

    def step1(self):
        self.wait(1)
        self.go(10, 7)
        self.wait(2)
        self.go(11, 8)

    def step2(self):
        self.wait(0)
        self.go(6)
        self.wait(3)
        self.go(9)

    def step3(self):
        self.wait(10)
        self.go(13)
        self.wait(11)
        self.go(12)

    def sent(self):
        for copy in self.copies:
            copy.wait_send()

    def last(self):
        self.wait(4, 5, 6, 7, 8, 9, 12, 13)


NEVER = 4096.0


def turned(values, cosine, sine):
    half = HEAD_DIM // 2
    out = []
    for at in range(0, values.shape[0], HEAD_DIM):
        low, high = values[at : at + half], values[at + half : at + HEAD_DIM]
        out += [low * cosine - high * sine, high * cosine + low * sine]
    return jnp.concatenate(out, axis=0)


def place_slots(routes_ref, order_ref, placed_ref):
    rows = routes_ref.shape[1]
    expert = lax.broadcasted_iota(jnp.int32, (EXP_WIN, rows), 0)
    priority = jnp.full((EXP_WIN, rows), NEVER, f32)
    for k in range(TOPK):
        pick = expert == routes_ref[k : k + 1, :]
        priority = jnp.where(pick, order_ref[k : k + 1, :].astype(f32), priority)
    priority_turned = priority.T
    slot = lax.broadcasted_iota(jnp.int32, (CAP, rows), 0).astype(f32)
    for e in range(EXP_WIN):
        mine = priority[e : e + 1, :]
        before = jnp.where(priority_turned[:, e : e + 1] < mine, 1.0, 0.0)
        before = jnp.sum(before, axis=0, keepdims=True)
        placed = (slot == before) & (mine < NEVER)
        placed_ref[e] = jnp.where(placed, 1.0, 0.0).astype(bf16)


def project_kernel(
    stage, tokens_ref, gain_ref, router_ref, cos_ref, sin_ref, docs_ref, routes_ref, order_ref, w_out_ref,
    w_query_ref, key_matrix_ref, value_matrix_ref,
    w_all_ref, qt_ref, kt_ref, vt_ref, k_ref, v_ref, docs_all_ref, placed_ref, turned_ref, normed_ref,
    strips_ref, weights_ref,
    held_ref, own_out, query_held, key_held, value_held,
    w_send, w_recv, o_send, o_recv, d_send, d_recv, c_send, c_recv, q_send, q_recv, local,
):
    place = Place()
    me, z = place.me, place.z
    met = greet(place.others() + place.layers())
    strip = strips_ref.shape[1]
    odd = lax.rem(me, 2)

    def window(first, size):
        return pl.ds(pl.multiple_of(first * 128, 128), size)

    pair = lax.div(me, 2)
    fetches = [
        pltpu.make_async_copy(
            w_query_ref.at[:, window(pair * 3 + odd, 2 * 128)], query_held, local.at[GROUP]
        ),
        pltpu.make_async_copy(
            key_matrix_ref.at[:, window(pair, 128)], key_held, local.at[GROUP + 1]
        ),
        pltpu.make_async_copy(
            value_matrix_ref.at[:, window(pair, 128)], value_held, local.at[GROUP + 2]
        ),
        pltpu.make_async_copy(
            w_out_ref.at[pl.ds(pl.multiple_of(me * strip, strip), strip), :], own_out,
            local.at[GROUP + 3],
        ),
    ]
    for fetch in fetches:
        fetch.start()
    stage.need(tokens_ref)
    x = tokens_ref[...].astype(f32)
    scale = lax.rsqrt(jnp.mean(x * x, axis=-1, keepdims=True) + epsilon)
    held_ref[me] = (x * scale * gain_ref[...].reshape(1, -1)).astype(bf16)
    for fetch in fetches:
        fetch.wait()

    def half(held, columns):
        turned_rows = held[...].T
        return jnp.where(odd == 1, turned_rows[HEAD_DIM:], turned_rows[:columns])

    own = w_all_ref.at[z]
    own[:QW, :] = half(query_held, QW)
    own[QW : QW + HEAD_DIM, :] = half(key_held, HEAD_DIM)
    own[QW + HEAD_DIM : HW, :] = half(value_held, HEAD_DIM)
    router = router_ref[...].astype(f32)
    empty = jnp.zeros((ROUTER - router.shape[0], router.shape[1]), f32)
    own[HW:, :] = jnp.concatenate([router, empty], axis=0).astype(bf16)
    met()
    spread = Spread(
        place, held_ref.at[me], lambda owner: held_ref.at[owner],
        halves(TOK_DEV), c_send, c_recv,
    )
    sent = []
    for j, device in enumerate(place.layers()):
        sent.append(remote(own, own, w_send.at[j], w_recv.at[j], device))
        sent[-1].start()
    spread.start()
    docs_all_ref[me] = docs_ref[...]
    others = []
    for j, device in enumerate(place.others()):
        others.append(remote(docs_ref, docs_all_ref.at[me], d_send.at[j], d_recv.at[j], device))
        others[-1].start()
    place_slots(routes_ref, order_ref, placed_ref)
    turned_ref[...] = placed_ref[...].reshape(EXP_WIN * CAP, -1).T
    stage.put(placed_ref, turned_ref)
    spread.step1()
    spread.step2()
    spread.step3()
    for copy in sent:
        copy.wait_recv()
    for j, device in enumerate(place.layers()):
        others.append(remote(own_out, strips_ref.at[z], o_send.at[j], o_recv.at[j], device))
        others[-1].start()
    stage.put(w_all_ref)
    stage.need(cos_ref, sin_ref)
    depth = w_all_ref.shape[0]
    weights = Spread(
        place, w_all_ref.at[:, :FIRST], lambda owner: weights_ref.at[owner],
        lambda ref, h: ref.at[pl.ds(h * (depth // 2), depth // 2)], q_send, q_recv,
    )
    weights.start()
    own_moves = [
        pltpu.make_async_copy(own_out, strips_ref.at[z], local.at[GROUP]),
        pltpu.make_async_copy(w_all_ref.at[:, :FIRST], weights_ref.at[me], local.at[GROUP + 1]),
    ]
    for move in own_moves:
        move.start()
    core, side, row = place.near
    across = flip(side, 4)
    order = [me, side, row, across, core, flip(side, 1), flip(row, 1), flip(across, 1)]

    def to_normed(owner):
        return pltpu.make_async_copy(held_ref.at[owner], normed_ref.at[owner], local.at[owner])

    def project(i, _):
        for at, slots in ((4, (4, 5)), (5, (6, 7)), (6, (8, 9)), (7, (12, 13))):

            @pl.when(i == at)
            def _(slots=slots):
                spread.wait(*slots)

        pl.when(i == 5)(weights.step1)
        pl.when(i == 7)(weights.step2)
        owner = order[-1]
        for at in range(GROUP - 1):
            owner = jnp.where(i == at, order[at], owner)
        to_normed(owner).start()
        linear = None
        for s in range(w_all_ref.shape[0]):
            size = w_all_ref.shape[2]
            term = dot(
                w_all_ref[s, :HW, :], held_ref[owner, :, s * size : (s + 1) * size], ((1,), (1,))
            )
            linear = term if linear is None else linear + term
        tokens = block(owner)
        cosine, sine = cos_ref[:, tokens], sin_ref[:, tokens]
        queries = turned(linear[:QW], cosine, sine) * HEAD_DIM ** (-0.5)
        qt_ref[:, tokens] = queries.astype(bf16)
        keys = turned(linear[QW : QW + HEAD_DIM], cosine, sine)
        kt_ref[:, tokens] = keys.astype(bf16)
        k_ref[tokens, :] = keys.T.astype(bf16)
        values = linear[QW + HEAD_DIM :]
        vt_ref[:, tokens] = values.astype(bf16)
        v_ref[tokens, :] = values.T.astype(bf16)
        return 0

    lax.fori_loop(0, GROUP, project, 0)
    stage.put(qt_ref, kt_ref, vt_ref, k_ref, v_ref)
    weights.step3()
    for copy in sent:
        copy.wait_send()
    for copy in others:
        copy.wait()
    for move in own_moves:
        move.wait()
    for owner in range(GROUP):
        to_normed(owner).wait()
    spread.sent()
    weights.last()
    weights.sent()


def project_call(
    tokens, gain, router, cosine, sine, docs, routes, order, w_out, w_query, key_matrix,
    value_matrix, depth,
):
    rows, width = tokens.shape
    span = GROUP * rows
    strip = w_out.shape[0] // GROUP
    size = w_out.shape[0]
    return staged_call(
        project_kernel,
        "project",
        1,
        [
            ("h", tokens),
            ("v", gain),
            ("v", router),
            ("h", cosine),
            ("h", sine),
            ("v", docs),
            ("v", routes),
            ("v", order),
            ("a", w_out),
            ("a", w_query),
            ("a", key_matrix),
            ("a", value_matrix),
        ],
        [
            ("h", shape((depth, ALL, size), bf16)),
            ("h", shape((QW, span), bf16)),
            ("h", shape((HEAD_DIM, span), bf16)),
            ("h", shape((HEAD_DIM, span), bf16)),
            ("h", shape((span, HEAD_DIM), bf16)),
            ("h", shape((span, HEAD_DIM), bf16)),
            ("v", shape((GROUP,) + docs.shape, jnp.int32)),
            ("h", shape((EXP_WIN, CAP, rows), bf16)),
            ("h", shape((rows, EXP_WIN * CAP), bf16)),
            ("a", shape((GROUP, rows, width), bf16)),
            ("a", shape((depth, strip, w_out.shape[1]), bf16)),
            ("a", shape((GROUP, depth, FIRST, size), bf16)),
        ],
        [
            VMEM((GROUP, rows, width), bf16),
            VMEM((strip, width), bf16),
            VMEM((size, 2 * 128), bf16),
            VMEM((size, 128), bf16),
            VMEM((size, 128), bf16),
        ]
        + [DMA((depth - 1,))] * 4
        + [DMA((GROUP - 1,))] * 2
        + [DMA((Spread.SEMS,))] * 4
        + [DMA((GROUP + 4,))],
    )


def docs_column(row):
    return jnp.broadcast_to(row.astype(f32), (8, row.shape[1])).T[:, :1]


def attend_kernel(
    n_blocks, stage, qt_ref, k_ref, vt_ref, docs_ref, strips_ref, w_all_ref,
    o_ref, lse_ref, attended_ref, out_weight_ref, weights_ref,
    staged_ref, docs_col_ref, top_ref, sum_ref, acc_ref,
    a_send, a_recv, s_send, s_recv, w_send, w_recv, local,
):
    T = TOK_DEV
    place = Place()
    me = place.me
    first = place.base
    met = greet(place.others())
    depth = strips_ref.shape[0]
    moves = [
        pltpu.make_async_copy(strips_ref, out_weight_ref.at[:, me], local.at[0]),
        pltpu.make_async_copy(w_all_ref.at[:, FIRST:HW], weights_ref.at[me], local.at[1]),
    ]

    def layers(ref, h):
        return ref.at[pl.ds(h * (depth // 2), depth // 2)]

    spreads = [
        Spread(place, strips_ref, lambda owner: out_weight_ref.at[:, owner], layers, s_send, s_recv),
        Spread(
            place, w_all_ref.at[:, FIRST:HW], lambda owner: weights_ref.at[owner], layers, w_send, w_recv
        ),
    ]

    def turn(i, _):
        docs_col_ref[i] = docs_column(docs_ref[i])
        return 0

    lax.fori_loop(0, n_blocks, turn, 0)
    stage.need(strips_ref, w_all_ref)
    met()
    spreads[0].start()
    for move in moves:
        move.start()
    stage.need(qt_ref, k_ref, vt_ref)

    def tile(kb, qb, mask):
        kt = k_ref[block(kb), :]
        vt = vt_ref[:, block(kb)]
        heads = range(HEADS)
        parts = [slice(h * HEAD_DIM, (h + 1) * HEAD_DIM) for h in heads]
        s = [dot(kt, qt_ref[parts[h], block(qb)]) for h in heads]
        if mask is not None:
            s = [jnp.where(mask, x, score_masked) for x in s]
        old = [top_ref[h : h + 1, :] for h in heads]
        new = [jnp.maximum(old[h], jnp.max(s[h], axis=0, keepdims=True)) for h in heads]
        p = [jnp.exp(s[h] - new[h]) for h in heads]
        factor = [jnp.exp(old[h] - new[h]) for h in heads]
        total = [
            sum_ref[h : h + 1, :] * factor[h] + jnp.sum(p[h], axis=0, keepdims=True) for h in heads
        ]
        mixed = [acc_ref[parts[h], :] * factor[h] + dot(vt, p[h].astype(bf16)) for h in heads]
        for h in heads:
            top_ref[h : h + 1, :] = new[h]
            sum_ref[h : h + 1, :] = total[h]
            acc_ref[parts[h], :] = mixed[h]

    def same(kb, gq):
        return docs_col_ref[kb] == docs_ref[gq].astype(f32)

    def attended_copy(to, slot):
        return remote(
            staged_ref.at[to], attended_ref.at[slot], a_send.at[to], a_recv.at[slot], place.ctx(to)
        )

    def q_block(j, _):
        for at, act in (
            (2, spreads[0].step1), (4, spreads[0].step2), (4, spreads[1].start),
            (6, spreads[0].step3),
        ):
            pl.when(j == at)(act)
        qb = GROUP - 1 - j
        gq = first + qb
        top_ref[...] = jnp.full_like(top_ref, score_masked)
        sum_ref[...] = jnp.ones_like(sum_ref)
        acc_ref[...] = jnp.zeros_like(acc_ref)
        last = gq == n_blocks - 1

        def k_block(kb, _):
            edge = jnp.logical_or(kb == 0, last)

            @pl.when(edge)
            def _():
                tile(kb, qb, same(kb, gq))

            @pl.when(jnp.logical_not(edge))
            def _():
                tile(kb, qb, None)

            return 0

        lax.fori_loop(0, gq, k_block, 0)
        keys = lax.broadcasted_iota(jnp.int32, (T, T), 0)
        queries = lax.broadcasted_iota(jnp.int32, (T, T), 1)
        tile(gq, qb, same(gq, gq) & (keys <= queries))
        lse_ref[qb] = top_ref[...] + jnp.log(sum_ref[...])
        for h in range(HEADS):
            part = slice(h * HEAD_DIM, (h + 1) * HEAD_DIM)
            mixed = acc_ref[part, :] / sum_ref[h : h + 1, :]
            o_ref[part, block(qb)] = mixed
            staged_ref[qb, part, :] = mixed.astype(bf16)

        @pl.when(qb != me)
        def _():
            attended_copy(qb, me).start()

        return 0

    lax.fori_loop(0, GROUP, q_block, 0)
    stage.put(o_ref, lse_ref)
    own = pltpu.make_async_copy(staged_ref.at[me], attended_ref.at[me], local.at[2])
    own.start()
    spreads[1].step1()
    spreads[1].step2()
    spreads[1].step3()
    for j in range(1, GROUP):
        other = lax.rem(me + j, GROUP)
        attended_copy(other, other).wait()
    for spread in spreads:
        spread.last()
        spread.sent()
    for move in moves:
        move.wait()
    own.wait()


def attend_call(qt, k, vt, docs, strips, w_all):
    n = k.shape[0] // TOK_DEV
    span = qt.shape[1]
    depth, _, size = w_all.shape
    return staged_call(
        functools.partial(attend_kernel, n),
        "attend",
        2,
        [
            ("h", qt),
            ("h", k),
            ("h", vt),
            ("v", docs),
            ("h", strips),
            ("h", w_all),
        ],
        [
            ("h", shape((QW, span), f32)),
            ("h", shape((GROUP, 8, TOK_DEV), f32)),
            ("a", shape((GROUP, QW, TOK_DEV), bf16)),
            ("a", shape((depth, GROUP) + strips.shape[1:], bf16)),
            ("a", shape((GROUP, depth, HW - FIRST, size), bf16)),
        ],
        [
            VMEM((GROUP, QW, TOK_DEV), bf16),
            VMEM((n, TOK_DEV, 1), f32),
            VMEM((8, TOK_DEV), f32),
            VMEM((8, TOK_DEV), f32),
            VMEM((QW, TOK_DEV), f32),
            DMA((GROUP,)),
            DMA((GROUP,)),
        ]
        + [DMA((Spread.SEMS,))] * 4
        + [DMA((3,))],
    )


def router_of(w_all_ref):
    return [w_all_ref[s, HW:, :] for s in range(w_all_ref.shape[0])]


def dispatch_kernel(
    stage, attended_ref, weight_ref, gate_up_ref, tokens_ref, gain_ref, w_all_ref, routes_ref, placed_ref,
    cotangent_ref,
    residual_ref, normed_ref, gates_ref, slot_gates_ref, rows_ref, grads_ref, gate_ref, up_ref,
    active_ref, grad_down_ref, columns_ref,
    held_ref, weight_held, gate_up_held, mixed_ref, own_rows, own_grads,
    r_send, r_recv, g_send, g_recv, c_send, c_recv, local,
):
    place = Place()
    me = place.me
    fetches = [
        pltpu.make_async_copy(attended_ref, held_ref, local.at[0]),
        pltpu.make_async_copy(weight_ref, weight_held, local.at[1]),
        pltpu.make_async_copy(gate_up_ref, gate_up_held, local.at[3]),
    ]
    met = greet(place.others())
    for fetch in fetches:
        fetch.start()
    rows, width = tokens_ref.shape
    experts_wide = gates_ref.shape[0]

    def copy(source, target, send, receive, j):
        to = lax.rem(me + j, GROUP)
        return remote(source.at[to], target.at[me], send.at[j], receive.at[j], place.ctx(to))

    def strip_copy(j):
        to = lax.rem(me + j, GROUP)
        return remote(
            attended_ref.at[:, to], columns_ref.at[me], c_send.at[j], c_recv.at[j], place.ctx(to)
        )

    fetches[0].wait()
    met()
    for j in range(1, GROUP):
        strip_copy(j).start()
    own_strip = pltpu.make_async_copy(held_ref.at[:, me], columns_ref.at[me], local.at[2])
    own_strip.start()
    mixed_ref[...] = held_ref[...].reshape(width, rows).T
    fetches[1].wait()
    stage.need(tokens_ref)

    def out_columns(i, _):
        columns = block(i)
        residual_ref[:, columns] = tokens_ref[:, columns].astype(f32) + dot(
            mixed_ref[...], weight_held[:, columns]
        )
        return 0

    lax.fori_loop(0, width // TOK_DEV, out_columns, 0)
    residual = residual_ref[...]
    scale = lax.rsqrt(jnp.mean(residual * residual, axis=-1, keepdims=True) + epsilon)
    normed_ref[...] = (residual * scale * gain_ref[...].reshape(1, -1)).astype(bf16)
    stage.put(residual_ref, normed_ref)
    stage.need(w_all_ref)
    logits = None
    for s, router in enumerate(router_of(w_all_ref)):
        size = router.shape[1]
        term = dot(router, normed_ref[:, s * size : (s + 1) * size], ((1,), (1,)))
        logits = term if logits is None else logits + term
    expert = lax.broadcasted_iota(jnp.int32, (experts_wide, rows), 0)
    chosen = expert < 0
    for k in range(TOPK):
        chosen = chosen | (expert == routes_ref[k : k + 1, :])
    logits = jnp.where(chosen, logits, score_masked)
    top = jnp.max(logits, axis=0, keepdims=True)
    gates = jnp.where(chosen, jnp.exp(logits - top), 0.0)
    gates = gates / jnp.sum(gates, axis=0, keepdims=True)
    gates_ref[...] = gates
    stage.need(placed_ref, cotangent_ref)
    for e in range(EXP_WIN):
        slot_gates_ref[e] = jnp.sum(
            placed_ref[e].astype(f32) * gates[e : e + 1, :], axis=1, keepdims=True
        )

    def send_rows(j, _):
        to = lax.rem(me + j, GROUP)
        own_rows[to] = dot(placed_ref[to], normed_ref[...]).astype(bf16)

        @pl.when(j < GROUP)
        def _():
            copy(own_rows, rows_ref, r_send, r_recv, j).start()

        return 0

    def send_grads(j, _):
        to = lax.rem(me + j, GROUP)
        routed = dot(placed_ref[to], cotangent_ref[...])
        own_grads[to] = (routed * slot_gates_ref[to]).astype(bf16)

        @pl.when(j < GROUP)
        def _():
            copy(own_grads, grads_ref, g_send, g_recv, j).start()

        return 0

    lax.fori_loop(1, GROUP + 1, send_rows, 0)
    lax.fori_loop(1, GROUP + 1, send_grads, 0)
    stage.put(gates_ref, slot_gates_ref)
    rows_ref[me] = own_rows[me]
    grads_ref[me] = own_grads[me]
    fetches[2].wait()
    for j in range(1, GROUP):
        copy(own_rows, rows_ref, r_send, r_recv, j).wait_recv()
    stage.put(rows_ref)
    slots = GROUP * CAP
    hidden = gate_ref.shape[1]
    tiles = hidden // TOK_DEV

    def expert_up(i, _):
        came = rows_ref[...].reshape(slots, width)
        gate = dot(came, gate_up_held[:, block(i)])
        up = dot(came, gate_up_held[:, block(tiles + i)])
        gate_ref[:, block(i)] = gate
        up_ref[:, block(i)] = up
        active_ref[:, block(i)] = (gate * jax.nn.sigmoid(gate) * up).astype(bf16)
        return 0

    lax.fori_loop(0, tiles, expert_up, 0)
    stage.put(gate_ref, up_ref, active_ref)
    for j in range(1, GROUP):
        copy(own_grads, grads_ref, g_send, g_recv, j).wait_recv()
    stage.put(grads_ref)

    def expert_over(i, _):
        grad_down_ref[:, block(i)] = dot(
            active_ref[...], grads_ref[:, :, block(i)].reshape(slots, TOK_DEV), ((0,), (0,))
        ).astype(bf16)
        return 0

    lax.fori_loop(0, width // TOK_DEV, expert_over, 0)
    stage.put(grad_down_ref)
    for j in range(1, GROUP):
        strip_copy(j).wait()
        copy(own_rows, rows_ref, r_send, r_recv, j).wait_send()
        copy(own_grads, grads_ref, g_send, g_recv, j).wait_send()
    own_strip.wait()


def dispatch_call(attended, weight, gate_up, tokens, gain, w_all, routes, placed, cotangent):
    rows, width = tokens.shape
    hidden = gate_up.shape[1] // 2
    count = GROUP * CAP
    slots = (GROUP, CAP, width)
    depth = w_all.shape[0]
    attended = attended.reshape(depth, GROUP, -1, rows)
    return staged_call(
        dispatch_kernel,
        "dispatch",
        3,
        [
            ("a", attended),
            ("a", weight),
            ("a", gate_up),
            ("h", tokens),
            ("v", gain),
            ("h", w_all),
            ("v", routes),
            ("h", placed),
            ("h", cotangent),
        ],
        [
            ("h", shape((rows, width), f32)),
            ("h", shape((rows, width), bf16)),
            ("h", shape((ROUTER, rows), f32)),
            ("h", shape((EXP_WIN, CAP, 1), f32)),
            ("h", shape(slots, bf16)),
            ("h", shape(slots, bf16)),
            ("h", shape((count, hidden), f32)),
            ("h", shape((count, hidden), f32)),
            ("h", shape((count, hidden), bf16)),
            ("h", shape((hidden, width), bf16)),
            ("a", shape((GROUP, depth) + attended.shape[2:], bf16)),
        ],
        [
            VMEM(attended.shape, bf16),
            VMEM(weight.shape, bf16),
            VMEM(gate_up.shape, bf16),
            VMEM((rows, width), bf16),
            VMEM(slots, bf16),
            VMEM(slots, bf16),
        ]
        + [DMA((GROUP,))] * 6
        + [DMA((4,))],
    )


def expert_kernel(
    stage, active_ref, down_ref, grads_ref, rows_ref, gate_ref, up_ref, gate_up_ref,
    out_ref, back_ref, grad_gate_up_ref,
    grads_held, rows_held, gate_up_held, own_ref, grad_ref, send, receive, local,
):
    place = Place()
    me = place.me
    met = greet(place.others())
    fetches = [
        pltpu.make_async_copy(grads_ref, grads_held, local.at[0]),
        pltpu.make_async_copy(rows_ref, rows_held, local.at[1]),
        pltpu.make_async_copy(gate_up_ref, gate_up_held, local.at[2]),
    ]
    for fetch in fetches:
        fetch.start()
    count, hidden = active_ref.shape
    width = down_ref.shape[1]
    T = TOK_DEV
    tiles = hidden // T

    def copy(j):
        to = lax.rem(me + j, GROUP)
        return remote(own_ref.at[to], out_ref.at[me], send.at[j], receive.at[j], place.ctx(to))

    stage.need(active_ref, down_ref)

    def out(i, _):
        value = dot(active_ref[...], down_ref[:, block(i)]).astype(bf16)
        own_ref[:, :, block(i)] = value.reshape(GROUP, CAP, T)
        return 0

    lax.fori_loop(0, width // T, out, 0)
    met()
    for j in range(1, GROUP):
        copy(j).start()
    move = pltpu.make_async_copy(own_ref.at[me], out_ref.at[me], local.at[3])
    move.start()
    fetches[0].wait()
    stage.need(gate_ref, up_ref)

    def back(i, _):
        grad = dot(grads_held[...], down_ref[block(i), :], ((1,), (1,)))
        gate, up = gate_ref[:, block(i)], up_ref[:, block(i)]
        sigmoid = jax.nn.sigmoid(gate)
        grad_gate = grad * up * sigmoid * (1.0 + gate * (1.0 - sigmoid))
        grad_ref[:, block(i)] = grad_gate.astype(bf16)
        grad_ref[:, block(tiles + i)] = (grad * gate * sigmoid).astype(bf16)
        return 0

    lax.fori_loop(0, tiles, back, 0)
    fetches[1].wait()
    fetches[2].wait()

    def over(i, _):
        grad_gate_up_ref[block(i), :] = dot(
            rows_held[:, block(i)], grad_ref[...], ((0,), (0,))
        ).astype(bf16)
        back_ref[:, block(i)] = dot(
            grad_ref[...], gate_up_held[block(i), :], ((1,), (1,))
        ).astype(bf16)
        return 0

    lax.fori_loop(0, width // T, over, 0)
    stage.put(back_ref, grad_gate_up_ref)
    for j in range(1, GROUP):
        copy(j).wait()
    move.wait()


def expert_call(active, down, grads, rows, gate, up, gate_up):
    count, width = rows.shape
    hidden = down.shape[0]
    slots = (GROUP, CAP, width)
    return staged_call(
        expert_kernel,
        "expert",
        7,
        [
            ("h", active),
            ("h", down),
            ("a", grads),
            ("a", rows),
            ("h", gate),
            ("h", up),
            ("a", gate_up),
        ],
        [
            ("a", shape(slots, bf16)),
            ("h", shape((count, width), bf16)),
            ("h", shape((width, 2 * hidden), bf16)),
        ],
        [
            VMEM(grads.shape, bf16),
            VMEM(rows.shape, bf16),
            VMEM(gate_up.shape, bf16),
            VMEM(slots, bf16),
            VMEM((count, 2 * hidden), bf16),
            DMA((GROUP,)),
            DMA((GROUP,)),
            DMA((4,)),
        ],
    )


def combine_kernel(
    stage, out_ref, sent_grad_ref, weight_ref, residual_ref, normed_ref, gates_ref, placed_ref,
    placed_t_ref, slot_gates_ref, cotangent_ref, gain_ref, w_all_ref,
    output_ref, grad_residual_ref, heads_ref, attn_ref, grad_router_ref, grad_gain_ref,
    back_ref, weight_held, sum_ref, turned_ref, staged_ref, scaled_ref,
    b_send, b_recv, h_send, h_recv, local,
):
    place = Place()
    me = place.me
    met = greet(place.others())
    fetch = pltpu.make_async_copy(weight_ref, weight_held, local.at[0])
    fetch.start()
    rows, width = residual_ref.shape

    def copy(source, target, send, receive, j):
        to = lax.rem(me + j, GROUP)
        return remote(source.at[to], target.at[me], send.at[j], receive.at[j], place.ctx(to))

    backs = [copy(sent_grad_ref, back_ref, b_send, b_recv, j) for j in range(1, GROUP)]
    met()
    for one in backs:
        one.start()
    move = pltpu.make_async_copy(sent_grad_ref.at[me], back_ref.at[me], local.at[1])
    move.start()
    turned_ref[...] = jnp.zeros_like(turned_ref)
    stage.need(out_ref, placed_ref, slot_gates_ref, cotangent_ref)

    def add_expert(e, _):
        came = out_ref[e].astype(f32)
        scaled_ref[e] = (came * slot_gates_ref[e]).astype(bf16)
        routed = dot(placed_ref[e], cotangent_ref[...])
        slot_grad = jnp.sum(routed * came, axis=1, keepdims=True)
        turned_ref[pl.ds(e, 1), :] = jnp.sum(
            placed_ref[e].astype(f32) * slot_grad, axis=0, keepdims=True
        )
        return 0

    lax.fori_loop(0, EXP_WIN, add_expert, 0)
    stage.need(placed_t_ref, residual_ref, gates_ref, w_all_ref, normed_ref)
    slots = EXP_WIN * CAP

    def mix(i, _):
        columns = block(i)
        mixed = dot(placed_t_ref[...], scaled_ref[:, :, columns].reshape(slots, TOK_DEV))
        output_ref[:, columns] = (residual_ref[:, columns] + mixed).astype(bf16)
        return 0

    lax.fori_loop(0, width // TOK_DEV, mix, 0)
    stage.put(output_ref)
    gates = gates_ref[...]
    grad_gates = turned_ref[...]
    weighted = jnp.sum(gates * grad_gates, axis=0, keepdims=True)
    grad_logits = (gates * (grad_gates - weighted)).astype(bf16)
    for s, router in enumerate(router_of(w_all_ref)):
        size = router.shape[1]
        sum_ref[:, s * size : (s + 1) * size] = dot(grad_logits, router, ((0,), (0,)))
    grad_router_ref[...] = dot(grad_logits, normed_ref[...])
    fetch.wait()
    move.wait()
    for one in backs:
        one.wait_recv()

    def add_back(i, _):
        columns = block(i)
        sum_ref[:, columns] += dot(
            placed_t_ref[...], back_ref[:, :, columns].reshape(slots, TOK_DEV)
        )
        return 0

    lax.fori_loop(0, width // TOK_DEV, add_back, 0)
    residual = residual_ref[...]
    grad_normed = sum_ref[...]
    scale = lax.rsqrt(jnp.mean(residual * residual, axis=-1, keepdims=True) + epsilon)
    scaled = grad_normed * gain_ref[...].reshape(1, -1)
    inner = jnp.mean(scaled * residual, axis=-1, keepdims=True)
    grad = scale * scaled - residual * (scale * scale * scale * inner)
    grad_gain_ref[...] = jnp.sum(grad_normed * residual * scale, axis=0, keepdims=True)
    grad_residual = cotangent_ref[...].astype(f32) + grad
    grad_residual_ref[...] = grad_residual
    attn_ref[...] = grad_residual.astype(bf16)
    stage.put(grad_residual_ref, attn_ref, grad_router_ref, grad_gain_ref)

    def head_rows(j, _):
        to = lax.rem(me + j, GROUP)
        staged_ref[to] = dot(weight_held[block(to, QW), :], attn_ref[...], ((1,), (1,))).astype(bf16)

        @pl.when(j < GROUP)
        def _():
            copy(staged_ref, heads_ref, h_send, h_recv, j).start()

        return 0

    lax.fori_loop(1, GROUP + 1, head_rows, 0)
    move = pltpu.make_async_copy(staged_ref.at[me], heads_ref.at[me], local.at[2])
    move.start()
    for one in backs:
        one.wait_send()
    for j in range(1, GROUP):
        copy(staged_ref, heads_ref, h_send, h_recv, j).wait()
    move.wait()


def combine_call(
    out, sent_grad, weight, residual, normed, gates, placed, placed_t, slot_gates, cotangent,
    gain, w_all,
):
    rows, width = residual.shape
    slots = (GROUP, CAP, width)
    return staged_call(
        combine_kernel,
        "combine",
        4,
        [
            ("h", out),
            ("a", sent_grad),
            ("a", weight),
            ("h", residual),
            ("h", normed),
            ("h", gates),
            ("h", placed),
            ("h", placed_t),
            ("h", slot_gates),
            ("h", cotangent),
            ("v", gain),
            ("h", w_all),
        ],
        [
            ("h", shape((rows, width), bf16)),
            ("h", shape((rows, width), f32)),
            ("a", shape((GROUP, QW, rows), bf16)),
            ("h", shape((rows, width), bf16)),
            ("h", shape((ROUTER, width), f32)),
            ("h", shape((1, width), f32)),
        ],
        [
            VMEM(slots, bf16),
            VMEM(weight.shape, bf16),
            VMEM((rows, width), f32),
            VMEM((ROUTER, rows), f32),
            VMEM((GROUP, QW, rows), bf16),
            VMEM(slots, bf16),
        ]
        + [DMA((GROUP,))] * 4
        + [DMA((3,))],
    )


def backward_kernel(
    n_blocks, stage, qt_ref, k_ref, kt_ref, v_ref, heads_ref, o_ref, lse_ref, docs_ref, attn_ref,
    columns_ref, down_ref,
    dq_ref, dk_ref, dv_ref, grad_out_ref, down_all_ref,
    attn_all_ref, docs_col_ref, delta_ref, dk_acc, dv_acc, a_send, a_recv, e_send, e_recv, local,
):
    T = TOK_DEV
    place = Place()
    me = place.me
    first = place.base
    met = greet([place.ctx(i) for i in place.near])
    stage.need(attn_ref)
    move = pltpu.make_async_copy(attn_ref, attn_all_ref.at[me], local.at[0])
    move.start()
    spread = Spread(
        place, attn_ref, lambda owner: attn_all_ref.at[owner],
        halves(T), a_send, a_recv,
    )
    met()
    spread.start()
    down_move = pltpu.make_async_copy(down_ref, down_all_ref.at[me], local.at[1])
    stage.need(down_ref)
    down_move.start()
    down_spread = Spread(
        place, down_ref, lambda owner: down_all_ref.at[owner],
        halves(down_ref.shape[0]), e_send, e_recv,
    )

    def turn(i, _):
        docs_col_ref[i] = docs_column(docs_ref[i])
        return 0

    lax.fori_loop(0, n_blocks, turn, 0)
    heads = range(HEADS)
    parts = [slice(h * HEAD_DIM, (h + 1) * HEAD_DIM) for h in heads]

    stage.need(heads_ref, o_ref, lse_ref, qt_ref, k_ref, kt_ref, v_ref, columns_ref)

    def prepare(i, _):
        for h in heads:
            product = o_ref[parts[h], block(i)] * heads_ref[i, parts[h], :].astype(f32)
            delta_ref[i, h : h + 1, :] = jnp.sum(product, axis=0, keepdims=True)
        return 0

    lax.fori_loop(0, GROUP, prepare, 0)
    dq_ref[...] = jnp.zeros_like(dq_ref)

    def tile(kb, qb, mask):
        k = k_ref[block(kb), :]
        v = v_ref[block(kb), :]
        kt = kt_ref[:, block(kb)]
        q = [qt_ref[part, block(qb)] for part in parts]
        do = [heads_ref[qb, part, :] for part in parts]
        s = [dot(k, x) for x in q]
        dp = [dot(v, x) for x in do]
        p = [jnp.exp(s[h] - lse_ref[qb, h : h + 1, :]) for h in heads]
        if mask is not None:
            p = [jnp.where(mask, x, 0.0) for x in p]
        ds = [(p[h] * (dp[h] - delta_ref[qb, h : h + 1, :])).astype(bf16) for h in heads]
        pb = [x.astype(bf16) for x in p]
        turn = ((1,), (1,))
        dv_acc[...] += dot(pb[0], do[0], turn) + dot(pb[1], do[1], turn) + dot(pb[2], do[2], turn)
        dk_acc[...] += dot(ds[0], q[0], turn) + dot(ds[1], q[1], turn) + dot(ds[2], q[2], turn)
        for h in heads:
            dq_ref[parts[h], block(qb)] += dot(kt, ds[h])

    def same(kb, gq):
        return docs_col_ref[kb] == docs_ref[gq].astype(f32)

    depth, strip, width = grad_out_ref.shape

    def out_weights():
        move.wait()
        spread.last()

        def columns(i, _):
            total = None
            for b in range(GROUP):
                term = dot(columns_ref[b].reshape(depth * strip, T), attn_all_ref[b, :, block(i)])
                total = term if total is None else total + term
            grad_out_ref[:, :, block(i)] = total.astype(bf16).reshape(depth, strip, T)
            return 0

        lax.fori_loop(0, width // T, columns, 0)

    def k_block(kb, _):
        for at, act in (
            (2, spread.step1), (3, spread.step2), (3, down_spread.start), (5, spread.step3),
            (6, down_spread.step1), (7, out_weights),
        ):
            pl.when(kb == first + at)(act)
        dk_acc[...] = jnp.zeros_like(dk_acc)
        dv_acc[...] = jnp.zeros_like(dv_acc)

        @pl.when(kb >= first)
        def _():
            keys = lax.broadcasted_iota(jnp.int32, (T, T), 0)
            queries = lax.broadcasted_iota(jnp.int32, (T, T), 1)
            tile(kb, kb - first, same(kb, kb) & (keys <= queries))

        def q_block(qb, _):
            gq = first + qb
            edge = jnp.logical_or(kb == 0, gq == n_blocks - 1)

            @pl.when(edge)
            def _():
                tile(kb, qb, same(kb, gq))

            @pl.when(jnp.logical_not(edge))
            def _():
                tile(kb, qb, None)

            return 0

        lax.fori_loop(jnp.maximum(kb - first + 1, 0), GROUP, q_block, 0)
        dk_ref[:, block(kb)] = dk_acc[...].T
        dv_ref[:, block(kb)] = dv_acc[...].T
        return 0

    lax.fori_loop(0, first + GROUP, k_block, 0)

    def clear(kb, _):
        dk_ref[:, block(kb)] = jnp.zeros((HEAD_DIM, T), f32)
        dv_ref[:, block(kb)] = jnp.zeros((HEAD_DIM, T), f32)
        return 0

    lax.fori_loop(first + GROUP, n_blocks, clear, 0)
    stage.put(dq_ref, dk_ref, dv_ref, grad_out_ref)
    down_spread.step2()
    down_spread.step3()
    down_spread.last()
    down_spread.sent()
    down_move.wait()
    spread.sent()


def backward_call(qt, k, kt, v, heads, o, lse, docs, attn, columns, down):
    n = k.shape[0] // TOK_DEV
    span = qt.shape[1]
    rows, width = attn.shape
    _, depth, strip, _ = columns.shape
    return staged_call(
        functools.partial(backward_kernel, n),
        "backward",
        5,
        [
            ("h", qt),
            ("h", k),
            ("h", kt),
            ("h", v),
            ("h", heads),
            ("h", o),
            ("h", lse),
            ("v", docs),
            ("h", attn),
            ("h", columns),
            ("h", down),
        ],
        [
            ("h", shape((QW, span), f32)),
            ("h", shape(kt.shape, f32)),
            ("h", shape(kt.shape, f32)),
            ("h", shape((depth, strip, width), bf16)),
            ("a", shape((GROUP,) + down.shape, bf16)),
        ],
        [
            VMEM((GROUP, rows, width), bf16),
            VMEM((n, TOK_DEV, 1), f32),
            VMEM((GROUP, 8, TOK_DEV), f32),
            VMEM((TOK_DEV, HEAD_DIM), f32),
            VMEM((TOK_DEV, HEAD_DIM), f32),
        ]
        + [DMA((Spread.SEMS,))] * 4
        + [DMA((2,))],
    )


def finish_kernel(
    stage, normed_ref, first_ref, others_ref, gate_up_ref, grad_out_ref, dq_ref, dk_ref, dv_ref, cos_ref,
    sin_ref, tokens_ref, gain_ref, grad_residual_ref, grad_router_ref, grad_gain2_ref,
    input_grad_ref, shared_ref, small_all_ref, out_all_ref, gate_up_all_ref,
    normed_held, first_held, others_held, linear_ref, came_ref, first_t, others_t, sum_ref, part_ref,
    small_ref, head_in, small_in, out_in, shard_ref, small_shard_ref, out_shard_ref,
    g_send, g_recv, h_send, h_recv, s_send, s_recv, o_send, o_recv, e_send, e_recv, f_send, f_recv,
    m_send, m_recv, c_send, c_recv, local,
):
    place = Place()
    me, z, depth = place.me, place.z, place.depth
    met = greet(place.others() + place.layers())
    fetches = [
        pltpu.make_async_copy(normed_ref, normed_held, local.at[0]),
        pltpu.make_async_copy(first_ref, first_held, local.at[1]),
        pltpu.make_async_copy(others_ref, others_held, local.at[2]),
    ]
    for fetch in fetches:
        fetch.start()
    rows, width = tokens_ref.shape
    size = width // depth

    def spread_of(source, out, send, receive):
        return Spread(
            place, source, lambda owner: out.at[owner], halves(source.shape[0]), send, receive
        )

    expert_spread = spread_of(gate_up_ref, gate_up_all_ref, e_send, e_recv)
    head_spread = spread_of(shard_ref, shared_ref, f_send, f_recv)
    small_spread = spread_of(small_shard_ref, small_all_ref, m_send, m_recv)
    out_spread = spread_of(out_shard_ref, out_all_ref, c_send, c_recv)
    moves = [
        pltpu.make_async_copy(gate_up_ref, gate_up_all_ref.at[me], local.at[3]),
        pltpu.make_async_copy(out_shard_ref, out_all_ref.at[me], local.at[4]),
        pltpu.make_async_copy(shard_ref, shared_ref.at[me], local.at[5]),
        pltpu.make_async_copy(small_shard_ref, small_all_ref.at[me], local.at[6]),
    ]
    stage.need(gate_up_ref)
    moves[0].start()

    def copy(j):
        to = lax.rem(me + j, GROUP)
        return remote(
            linear_ref.at[to], came_ref.at[me], g_send.at[j], g_recv.at[j], place.ctx(to)
        )

    def down(source, target, send, receive, j):
        to = lax.rem(z + j, depth)
        return remote(source.at[to], target.at[z], send.at[j], receive.at[j], place.fsdp(to))

    stage.need(dq_ref, dk_ref, dv_ref, cos_ref, sin_ref)

    def turn_back(j, _):
        to = lax.rem(me + j, GROUP)
        cosine, sine = cos_ref[:, block(to)], -sin_ref[:, block(to)]
        dq = turned(dq_ref[:, block(to)], cosine, sine) * HEAD_DIM ** (-0.5)
        dk = turned(dk_ref[:, block(to)], cosine, sine)
        linear_ref[to, :QW, :] = dq.astype(bf16)
        linear_ref[to, QW : QW + HEAD_DIM, :] = dk.astype(bf16)
        linear_ref[to, QW + HEAD_DIM :, :] = dv_ref[:, block(to)].astype(bf16)
        pl.when(j == 1)(met)

        @pl.when(j < GROUP)
        def _():
            copy(j).start()

        return 0

    lax.fori_loop(1, GROUP + 1, turn_back, 0)
    stage.need(grad_out_ref)
    outs = [down(grad_out_ref, out_in, o_send, o_recv, j) for j in range(1, depth)]
    for one in outs:
        one.start()
    out_in[z] = grad_out_ref[z]
    came_ref[me] = linear_ref[me]
    fetches[0].wait()

    def own_weights(j, _):
        to = lax.rem(z + j, depth)
        columns = block(to, size)
        total = None
        for b in range(GROUP):
            term = dot(linear_ref[b], normed_held[b, :, columns])
            total = term if total is None else total + term
        part_ref[to] = total.astype(bf16)

        @pl.when(j < depth)
        def _():
            down(part_ref, head_in, h_send, h_recv, j).start()

        return 0

    lax.fori_loop(1, depth + 1, own_weights, 0)

    def total(ref):
        value = ref[0].astype(f32)
        for s in range(1, depth):
            value = value + ref[s].astype(f32)
        return value.astype(bf16)

    for j in range(1, GROUP):
        copy(j).wait_send()
    expert_spread.start()
    for one in outs:
        one.wait_recv()
    out_shard_ref[...] = total(out_in)
    out_spread.start()
    moves[1].start()
    fetches[1].wait()
    fetches[2].wait()
    for j in range(1, GROUP):
        copy(j).wait_recv()

    def turn(j, _):
        first_t[j] = came_ref[j, :FIRST, :].T
        others_t[j] = came_ref[j, FIRST:, :].T
        return 0

    lax.fori_loop(0, GROUP, turn, 0)

    def add_heads(s, _):
        total = None
        for j in range(GROUP):
            term = dot(first_t[j], first_held[j, s]) + dot(others_t[j], others_held[j, s])
            total = term if total is None else total + term
        sum_ref[:, block(s, size)] = total
        return 0

    lax.fori_loop(0, depth, add_heads, 0)
    out_spread.step1()
    stage.need(tokens_ref, grad_residual_ref, grad_router_ref, grad_gain2_ref)
    x = tokens_ref[...].astype(f32)
    grad_normed = sum_ref[...]
    scale = lax.rsqrt(jnp.mean(x * x, axis=-1, keepdims=True) + epsilon)
    scaled = grad_normed * gain_ref[...].reshape(1, -1)
    inner = jnp.mean(scaled * x, axis=-1, keepdims=True)
    grad = scale * scaled - x * (scale * scale * scale * inner)
    input_grad_ref[...] = grad_residual_ref[...] + grad
    stage.put(input_grad_ref)
    gain1 = jnp.sum(grad_normed * x * scale, axis=0, keepdims=True)
    row = lax.broadcasted_iota(jnp.int32, (ROUTER, width), 0)
    small = jnp.where(row == ROUTER - 2, gain1, grad_router_ref[...])
    small = jnp.where(row == ROUTER - 1, grad_gain2_ref[...], small).astype(bf16)
    for s in range(depth):
        small_ref[s] = small[:, s * size : (s + 1) * size]
    smalls = [down(small_ref, small_in, s_send, s_recv, j) for j in range(1, depth)]
    heads = [down(part_ref, head_in, h_send, h_recv, j) for j in range(1, depth)]
    for one in smalls:
        one.start()
    expert_spread.step1()
    head_in[z] = part_ref[z]
    small_in[z] = small_ref[z]

    for one in heads:
        one.wait_recv()
    shard_ref[...] = total(head_in)
    head_spread.start()
    out_spread.step2()
    expert_spread.step2()
    for one in smalls:
        one.wait_recv()
    small_shard_ref[...] = total(small_in)
    small_spread.start()
    moves[2].start()
    moves[3].start()
    out_spread.step3()
    expert_spread.step3()
    spreads = (head_spread, small_spread)
    for spread in spreads:
        spread.step1()
    for spread in spreads:
        spread.step2()
    for spread in spreads:
        spread.step3()
    for spread in (out_spread, expert_spread, head_spread, small_spread):
        spread.last()
        spread.sent()
    for one in heads + smalls + outs:
        one.wait_send()
    for move in moves:
        move.wait()


def finish_call(
    normed, first, others, gate_up, grad_out, dq, dk, dv, cosine, sine, tokens, gain, grad_residual,
    grad_router, grad_gain2,
):
    rows, width = tokens.shape
    depth, strip, _ = grad_out.shape
    size = width // depth
    return staged_call(
        finish_kernel,
        "finish",
        6,
        [
            ("a", normed),
            ("a", first),
            ("a", others),
            ("h", gate_up),
            ("h", grad_out),
            ("h", dq),
            ("h", dk),
            ("h", dv),
            ("h", cosine),
            ("h", sine),
            ("h", tokens),
            ("v", gain),
            ("h", grad_residual),
            ("h", grad_router),
            ("h", grad_gain2),
        ],
        [
            ("h", shape((rows, width), f32)),
            ("a", shape((GROUP, HW, size), bf16)),
            ("a", shape((GROUP, ROUTER, size), bf16)),
            ("a", shape((GROUP, strip, width), bf16)),
            ("a", shape((GROUP,) + gate_up.shape, bf16)),
        ],
        [
            VMEM(normed.shape, bf16),
            VMEM(first.shape, bf16),
            VMEM(others.shape, bf16),
            VMEM((GROUP, HW, rows), bf16),
            VMEM((GROUP, HW, rows), bf16),
            VMEM((GROUP, rows, FIRST), bf16),
            VMEM((GROUP, rows, HW - FIRST), bf16),
            VMEM((rows, width), f32),
            VMEM((depth, HW, size), bf16),
            VMEM((depth, ROUTER, size), bf16),
            VMEM((depth, HW, size), bf16),
            VMEM((depth, ROUTER, size), bf16),
            VMEM((depth, strip, width), bf16),
            VMEM((HW, size), bf16),
            VMEM((ROUTER, size), bf16),
            VMEM((strip, width), bf16),
        ]
        + [DMA((GROUP,))] * 2
        + [DMA((depth,))] * 6
        + [DMA((Spread.SEMS,))] * 8
        + [DMA((7,))],
    )


def output_kernel(
    shared_ref, small_ref, out_ref, gate_up_ref, down_ref, output_ref, input_grad_ref,
    q_ref, k_ref, v_ref, w_out_ref, router_ref, gain1_ref, gain2_ref, gate_ref, up_ref, w_down_ref,
    final_ref, final_grad_ref,
):
    pair, i = shared_ref.shape[0], pl.program_id(0)
    hidden = gate_ref.shape[2]

    def rows(first, last):
        both = [shared_ref[p, first:last, :].astype(f32) for p in range(pair)]
        return jnp.concatenate(both, axis=0).T

    @pl.when(lax.rem(i, pair) == 0)
    def _():
        q_ref[...] = rows(0, QW)
        k_ref[...] = rows(QW, QW + HEAD_DIM)
        v_ref[...] = rows(QW + HEAD_DIM, HW)

    w_out_ref[...] = out_ref[...].astype(f32)
    gate_ref[...] = gate_up_ref[:, :, :hidden].astype(f32)
    up_ref[...] = gate_up_ref[:, :, hidden:].astype(f32)
    w_down_ref[...] = down_ref[...].astype(f32)
    final_ref[...] = output_ref[...]
    final_grad_ref[...] = input_grad_ref[...]

    @pl.when(i == 0)
    def _():
        total = jnp.sum(small_ref[...].astype(f32), axis=0)
        router_ref[...] = total[: router_ref.shape[0], :]
        gain1_ref[...] = total[ROUTER - 2, :]
        gain2_ref[...] = total[ROUTER - 1, :]


def output_call(shared, small, out, gate_up, down, output, input_grad, experts):
    count, _, size = shared.shape
    _, strip, width = out.shape
    hidden = gate_up.shape[2] // 2
    pair = 2
    rows = output.shape[0] // count
    token = pl.BlockSpec((rows, width), lambda i: (i, 0))

    def first(*dims):
        return pl.BlockSpec((1,) + dims, lambda i: (i,) + (0,) * len(dims))

    def columns(columns):
        return pl.BlockSpec((size, columns), lambda i: (0, i // pair))

    def whole(*dims):
        return pl.BlockSpec(dims, lambda i: (0,) * len(dims))

    return pl.pallas_call(
        output_kernel,
        grid=(count,),
        out_shape=(
            shape((size, count * QW), f32),
            shape((size, count * HEAD_DIM), f32),
            shape((size, count * HEAD_DIM), f32),
            shape(out.shape, f32),
            shape((experts, size), f32),
            shape((size,), f32),
            shape((size,), f32),
            shape((count, size, hidden), f32),
            shape((count, size, hidden), f32),
            shape(down.shape, f32),
            shape(output.shape, bf16),
            shape(input_grad.shape, f32),
        ),
        in_specs=[
            pl.BlockSpec((pair,) + shared.shape[1:], lambda i: (i // pair, 0, 0)),
            whole(*small.shape), first(strip, width), first(*gate_up.shape[1:]),
            first(*down.shape[1:]), token, token,
        ],
        out_specs=(
            columns(pair * QW),
            columns(pair * HEAD_DIM),
            columns(pair * HEAD_DIM),
            first(strip, width),
            whole(experts, size),
            whole(size),
            whole(size),
            first(size, hidden),
            first(size, hidden),
            first(*down.shape[1:]),
            token,
            token,
        ),
        compiler_params=params(),
        name="output",
    )(shared, small, out, gate_up, down, output, input_grad)


def rotary_tables(length):
    frequencies = 10000.0 ** (-(np.arange(HEAD_DIM // 2) * 2.0) / HEAD_DIM)
    angles = frequencies[:, None] * np.arange(length)[None, :]
    return np.cos(angles).astype(np.float32), np.sin(angles).astype(np.float32)


def shards(
    tables,
    tokens,
    doc_ids,
    routes,
    slot_order,
    norm1_gain,
    norm2_gain,
    w_query,
    key_matrix,
    value_matrix,
    w_out,
    w_router,
    w_gate,
    w_up,
    w_down,
    cotangent,
):
    rows, width = tokens.shape[1:]
    ctx, depth = lax.axis_size("ctx"), lax.axis_size("fsdp")
    place = lax.axis_index("ctx")
    parts = ctx // GROUP
    head, part = place % GROUP, place // GROUP
    far = [[p * GROUP + i for p in range(parts)] for i in range(GROUP)]
    span = GROUP * rows
    experts = w_router.shape[1]
    hidden = w_gate.shape[2]

    def gather_z(value):
        return lax.all_gather(value, "fsdp", axis=0, tiled=True)

    def reduce_z(value):
        value = lax.psum_scatter(value.astype(bf16), "fsdp", scatter_dimension=0, tiled=True)
        if parts > 1:
            value = lax.psum(value, "ctx", axis_index_groups=far)
        return value

    cosine, sine = tables
    if parts > 1:
        cosine = lax.dynamic_slice_in_dim(cosine, part * span, span, 1)
        sine = lax.dynamic_slice_in_dim(sine, part * span, span, 1)
    own_tokens, own_cotangent = tokens[0], cotangent[0]

    route_rows, order_rows = routes[0].T, slot_order[0].T
    (
        w_all, queries, keys_t, values_t, keys, values, docs, placed, placed_t, normed1, strips,
        first_all,
    ) = project_call(
        own_tokens, norm1_gain, w_router.T, cosine, sine, doc_ids,
        route_rows, order_rows, w_out, w_query, key_matrix, value_matrix, depth,
    )
    w_gate, w_up, w_down, docs = lax.optimization_barrier((w_gate, w_up, w_down, docs))
    gate_up = gather_z(
        jnp.concatenate(
            [
                lax.dynamic_index_in_dim(w_gate, head, 0, False),
                lax.dynamic_index_in_dim(w_up, head, 0, False),
            ],
            axis=1,
        )
    )
    down = gather_z(lax.dynamic_index_in_dim(w_down, head, 0, False))
    if parts > 1:

        def gather_far(value, axis):
            return lax.all_gather(value, "ctx", axis=axis, axis_index_groups=far, tiled=True)

        keys, values, docs = gather_far(keys, 0), gather_far(values, 0), gather_far(docs, 0)
        keys_t, values_t = gather_far(keys_t, 1), gather_far(values_t, 1)
    attended_f32, log_total, attended, out_weight, others_all = attend_call(
        queries, keys, values_t, docs, strips, w_all
    )
    out_weight = out_weight.reshape(width, width)
    (
        residual, normed2, gates, slot_gates, sent_rows, sent_grads, gate, up, active, grad_w_down,
        columns,
    ) = dispatch_call(
        attended, out_weight, gate_up, own_tokens, norm2_gain, w_all, route_rows, placed, own_cotangent
    )
    grad_w_down = reduce_z(grad_w_down)
    expert_out, grad_buffer, grad_w_gate_up = expert_call(
        active, down, sent_grads.reshape(GROUP * CAP, width), sent_rows.reshape(GROUP * CAP, width),
        gate, up, gate_up,
    )
    grad_w_gate_up = reduce_z(grad_w_gate_up)
    output, grad_residual, heads, attn, grad_router, grad_gain2 = combine_call(
        expert_out, grad_buffer.reshape(sent_rows.shape), out_weight,
        residual, normed2, gates, placed, placed_t, slot_gates, own_cotangent, norm2_gain, w_all,
    )
    dq, dk, dv, grad_out, down_w = backward_call(
        queries, keys, keys_t, values, heads, attended_f32, log_total, docs, attn, columns,
        grad_w_down,
    )
    if parts > 1:
        dk = lax.psum_scatter(dk, "ctx", scatter_dimension=1, axis_index_groups=far, tiled=True)
        dv = lax.psum_scatter(dv, "ctx", scatter_dimension=1, axis_index_groups=far, tiled=True)
    input_grad, shared, small, out_w, gate_up_w = finish_call(
        normed1, first_all, others_all, grad_w_gate_up, grad_out, dq, dk, dv, cosine, sine,
        own_tokens, norm1_gain, grad_residual, grad_router, grad_gain2,
    )
    if parts > 1:
        shared, small, out_w = lax.psum((shared, small, out_w), "ctx", axis_index_groups=far)

    (
        q_w, k_w, v_w, out_w, router_w, gain1_w, gain2_w, gate_w, up_w, down_w, output, input_grad
    ) = output_call(shared, small, out_w, gate_up_w, down_w, output, input_grad, experts)
    return (
        output[None],
        input_grad[None],
        gain1_w,
        gain2_w,
        q_w,
        k_w,
        v_w,
        out_w.reshape(-1, width),
        router_w.T,
        gate_w,
        up_w,
        down_w,
    )


def solution(mesh):
    token_spec = P("fsdp", "ctx", None)
    row_spec, expert_spec = P("fsdp", None), P(None, "fsdp", None)
    tables = rotary_tables(mesh.shape["ctx"] * TOK_DEV)

    def program(*arguments):
        return jax.shard_map(
            functools.partial(shards, tuple(jnp.asarray(t) for t in tables)),
            mesh=mesh,
            in_specs=(
                token_spec,
                P("fsdp", "ctx"),
                token_spec,
                token_spec,
                P(),
                P(),
                row_spec,
                row_spec,
                row_spec,
                row_spec,
                row_spec,
                expert_spec,
                expert_spec,
                expert_spec,
                token_spec,
            ),
            out_specs=(
                token_spec,
                token_spec,
                P("fsdp"),
                P("fsdp"),
                row_spec,
                row_spec,
                row_spec,
                row_spec,
                row_spec,
                expert_spec,
                expert_spec,
                expert_spec,
            ),
            check_vma=False,
        )(*arguments)

    return program
```

```python
import functools

import jax
import jax.numpy as jnp
import numpy as np
from jax import lax
from jax.experimental import pallas as pl
from jax.experimental.pallas import tpu as pltpu
from jax.sharding import PartitionSpec as P

QUERY_HEADS = 24
KEY_VALUE_HEADS = 8
HEAD_DIM = 64
TOPK = 8
EXP_WIN = 8
TOK_DEV = 256
CAP = 64
GROUP = 8
HEADS = QUERY_HEADS // KEY_VALUE_HEADS
QW = HEADS * HEAD_DIM
HW = QW + 2 * HEAD_DIM
ROUTER = 48
ALL = HW + ROUTER

NEVER = 4096.0
epsilon = 1e-06
score_masked = -1e30
bf16 = jnp.bfloat16
f32 = jnp.float32
VMEM = pltpu.VMEM
MESH = pl.DeviceIdType.MESH
DMA = pltpu.SemaphoreType.DMA
IN_VMEM = pl.BlockSpec(memory_space=VMEM)
IN_ANY = pl.BlockSpec(memory_space=pl.ANY)


def dot(left, right, dims=((1,), (0,))):
    return lax.dot_general(left, right, (dims, ((), ())), preferred_element_type=f32)


def block(index, size=TOK_DEV):
    return pl.ds(pl.multiple_of(index * size, size), size)


def shape(dims, dtype):
    return jax.ShapeDtypeStruct(dims, dtype)


def params(collective_id=None, limit=56):
    return pltpu.CompilerParams(
        collective_id=collective_id,
        has_side_effects=collective_id is not None,
        vmem_limit_bytes=limit << 20,
    )


class Staged:
    def __init__(self, fetches, puts):
        self.fetches, self.puts, self.out = fetches, puts, []

    def need(self, *refs):
        for ref in refs:
            self.fetches.pop(id(ref)).wait()

    def put(self, *refs):
        for ref in refs:
            copy = self.puts.pop(id(ref))
            copy.start()
            self.out.append(copy)

    def finish(self):
        for copy in self.fetches.values():
            copy.wait()
        for copy in self.puts.values():
            copy.start()
        for copy in self.out + list(self.puts.values()):
            copy.wait()


def staged_call(body, name, collective_id, ins, outs, scratch):
    held_in = [i for i, (how, _) in enumerate(ins) if how == "h"]
    held_out = [i for i, (how, _) in enumerate(outs) if how == "h"]

    def kernel(*refs):
        refs = list(refs)
        given, refs = refs[: len(ins)], refs[len(ins) :]
        results, refs = refs[: len(outs)], refs[len(outs) :]
        own, refs = refs[: len(scratch)], refs[len(scratch) :]
        in_held, refs = refs[: len(held_in)], refs[len(held_in) :]
        out_held, (in_sems, out_sems) = refs[: len(held_out)], refs[len(held_out) :]
        fetches, puts = {}, {}
        for n, i in enumerate(held_in):
            copy = pltpu.make_async_copy(given[i], in_held[n], in_sems.at[n])
            copy.start()
            given[i] = in_held[n]
            fetches[id(given[i])] = copy
        for n, i in enumerate(held_out):
            puts[id(out_held[n])] = pltpu.make_async_copy(out_held[n], results[i], out_sems.at[n])
            results[i] = out_held[n]
        stage = Staged(fetches, puts)
        body(stage, *given, *results, *own)
        stage.finish()

    return pl.pallas_call(
        kernel,
        out_shape=tuple(one for _, one in outs),
        in_specs=[IN_VMEM if how == "v" else IN_ANY for how, _ in ins],
        out_specs=tuple(IN_VMEM if how == "v" else IN_ANY for how, _ in outs),
        scratch_shapes=list(scratch)
        + [VMEM(ins[i][1].shape, ins[i][1].dtype) for i in held_in]
        + [VMEM(outs[i][1].shape, outs[i][1].dtype) for i in held_out]
        + [DMA((max(len(held_in), 1),)), DMA((max(len(held_out), 1),))],
        compiler_params=params(collective_id),
        name=name,
    )(*(array for _, array in ins))


def flip(index, bit):
    return index + (1 - 2 * ((index // bit) % 2)) * bit


class Place:
    def __init__(self):
        ctx = lax.axis_index("ctx")
        self.base = (ctx // GROUP) * GROUP
        self.me = ctx - self.base
        self.z = lax.axis_index("fsdp")
        self.depth = lax.axis_size("fsdp")
        self.near = [flip(self.me, bit) for bit in (1, 2, 4)]

    def ctx(self, index):
        return {"ctx": self.base + index}

    def fsdp(self, index):
        return {"fsdp": index}

    def others(self):
        return [self.ctx(lax.rem(self.me + j, GROUP)) for j in range(1, GROUP)]

    def layers(self):
        return [self.fsdp(lax.rem(self.z + j, self.depth)) for j in range(1, self.depth)]


def greet(devices):
    ready = pltpu.get_barrier_semaphore()
    for device in devices:
        pl.semaphore_signal(ready, inc=1, device_id=device, device_id_type=MESH)
    return lambda: pl.semaphore_wait(ready, len(devices))


def remote(source, target, send, receive, device):
    return pltpu.make_async_remote_copy(
        src_ref=source,
        dst_ref=target,
        send_sem=send,
        recv_sem=receive,
        device_id=device,
        device_id_type=MESH,
    )


def halves(count):
    cut = -(-count // 32) * 16

    def part(ref, half):
        return ref.at[pl.ds(0, cut)] if half == 0 else ref.at[pl.ds(cut, count - cut)]

    return part


class Spread:
    SEMS = 14

    def __init__(self, place, source, land, part, send, receive):
        me = place.me
        core, side, row = place.near
        across = flip(side, 4)

        def plan(slot, owner, half, device):
            target = part(land(owner), half)
            first = part(source, half) if slot < 6 else target
            return remote(first, target, send.at[slot], receive.at[slot], place.ctx(device))

        self.copies = [
            plan(0, me, 0, side), plan(1, me, 1, side), plan(2, me, 0, row), plan(3, me, 1, row),
            plan(4, me, 0, core), plan(5, me, 1, core), plan(6, side, 0, core),
            plan(7, side, 1, core), plan(8, row, 0, core), plan(9, row, 1, core),
            plan(10, side, 1, row), plan(11, row, 0, side), plan(12, across, 0, core),
            plan(13, across, 1, core),
        ]

    def go(self, *slots):
        for slot in slots:
            self.copies[slot].start()

    def wait(self, *slots):
        for slot in slots:
            self.copies[slot].wait_recv()

    def start(self):
        self.go(1, 2, 0, 3, 4, 5)

    def step1(self):
        self.wait(1)
        self.go(10, 7)
        self.wait(2)
        self.go(11, 8)

    def step2(self):
        self.wait(0)
        self.go(6)
        self.wait(3)
        self.go(9)

    def step3(self):
        self.wait(10)
        self.go(13)
        self.wait(11)
        self.go(12)

    def sent(self):
        for copy in self.copies:
            copy.wait_send()

    def last(self):
        self.wait(4, 5, 6, 7, 8, 9, 12, 13)


class Line:
    def __init__(self, place, land, send, receive):
        self.z, self.depth = place.z, place.depth
        z, most = self.z, place.depth - 1
        ways = ((jnp.minimum(z + 1, most), -1), (jnp.maximum(z - 1, 0), 1))
        self.copies = []
        for way, (device, sign) in enumerate(ways):
            self.copies.append([])
            for step in range(most):
                held = land(jnp.clip(z + sign * step, 0, most))
                self.copies[way].append(
                    remote(
                        held, held, send.at[way, step], receive.at[way, step], place.fsdp(device)
                    )
                )

    def each(self, step):
        z, most = self.z, self.depth - 1
        up, down = self.copies
        at = min(step, most - 1)
        return ((z + 1 <= most, z - step >= 0, up[at]), (z - 1 >= 0, z + step <= most, down[at]))

    def start(self):
        for open_way, _, copy in self.each(0):
            pl.when(open_way)(copy.start)

    def step(self, step):
        before = self.each(step - 1)
        for (open_way, here, copy), (_, _, came) in zip(self.each(step), before):
            pl.when(here)(came.wait_recv)
            if step < self.depth - 1:
                pl.when(jnp.logical_and(open_way, here))(copy.start)

    def last(self):
        self.step(self.depth - 1)

    def sent(self):
        for step in range(self.depth - 1):
            for open_way, here, copy in self.each(step):
                pl.when(jnp.logical_and(open_way, here))(copy.wait_send)


def place_slots(routes_ref, order_ref, placed_ref):
    rows = routes_ref.shape[1]
    expert = lax.broadcasted_iota(jnp.int32, (EXP_WIN, rows), 0)
    priority = jnp.full((EXP_WIN, rows), NEVER, f32)
    for k in range(TOPK):
        pick = expert == routes_ref[k : k + 1, :]
        priority = jnp.where(pick, order_ref[k : k + 1, :].astype(f32), priority)
    priority_turned = priority.T
    slot = lax.broadcasted_iota(jnp.int32, (CAP, rows), 0).astype(f32)
    for e in range(EXP_WIN):
        mine = priority[e : e + 1, :]
        before = jnp.where(priority_turned[:, e : e + 1] < mine, 1.0, 0.0)
        before = jnp.sum(before, axis=0, keepdims=True)
        placed = (slot == before) & (mine < NEVER)
        placed_ref[e] = jnp.where(placed, 1.0, 0.0).astype(bf16)


def gather_kernel(
    stage, tokens_ref, gain_ref, router_ref, docs_ref, routes_ref, order_ref, w_query_ref,
    key_matrix_ref, value_matrix_ref, w_out_ref,
    docs_all_ref, placed_ref, turned_ref, normed_ref, w_all_ref, strips_ref,
    held_ref, query_held, key_held, value_held,
    w_send, w_recv, o_send, o_recv, d_send, d_recv, c_send, c_recv, local,
):
    place = Place()
    me, z = place.me, place.z
    met = greet(place.others() + place.layers())
    odd = lax.rem(me, 2)
    pair = lax.div(me, 2)
    depth, strip, _ = strips_ref.shape

    def window(first, size):
        return pl.ds(pl.multiple_of(first * 128, 128), size)

    fetches = [
        pltpu.make_async_copy(
            w_query_ref.at[:, window(pair * 3 + odd, 2 * 128)], query_held, local.at[0]
        ),
        pltpu.make_async_copy(key_matrix_ref.at[:, window(pair, 128)], key_held, local.at[1]),
        pltpu.make_async_copy(value_matrix_ref.at[:, window(pair, 128)], value_held, local.at[2]),
        pltpu.make_async_copy(
            w_out_ref.at[pl.ds(pl.multiple_of(me * strip, strip), strip), :], strips_ref.at[z],
            local.at[3],
        ),
    ]
    for fetch in fetches:
        fetch.start()
    stage.need(tokens_ref)
    x = tokens_ref[...].astype(f32)
    scale = lax.rsqrt(jnp.mean(x * x, axis=-1, keepdims=True) + epsilon)
    held_ref[...] = (x * scale * gain_ref[...].reshape(1, -1)).astype(bf16)
    met()
    spread = Spread(
        place, held_ref, lambda owner: normed_ref.at[owner], halves(TOK_DEV), c_send, c_recv
    )
    spread.start()
    for fetch in fetches:
        fetch.wait()

    def half(held, columns):
        turned_rows = held[...].T
        return jnp.where(odd == 1, turned_rows[HEAD_DIM:], turned_rows[:columns])

    own = w_all_ref.at[z]
    own[:QW, :] = half(query_held, QW)
    own[QW : QW + HEAD_DIM, :] = half(key_held, HEAD_DIM)
    own[QW + HEAD_DIM : HW, :] = half(value_held, HEAD_DIM)
    router = router_ref[...].astype(f32)
    empty = jnp.zeros((ROUTER - router.shape[0], router.shape[1]), f32)
    own[HW:, :] = jnp.concatenate([router, empty], axis=0).astype(bf16)
    lines = [
        Line(place, lambda layer: w_all_ref.at[layer], w_send, w_recv),
        Line(place, lambda layer: strips_ref.at[layer], o_send, o_recv),
    ]
    for line in lines:
        line.start()
    docs_all_ref[me] = docs_ref[...]
    sent = []
    for j, device in enumerate(place.others()):
        sent.append(remote(docs_ref, docs_all_ref.at[me], d_send.at[j], d_recv.at[j], device))
    for copy in sent:
        copy.start()
    move = pltpu.make_async_copy(held_ref, normed_ref.at[me], local.at[4])
    move.start()
    place_slots(routes_ref, order_ref, placed_ref)
    turned_ref[...] = placed_ref[...].reshape(EXP_WIN * CAP, -1).T
    stage.put(placed_ref, turned_ref)
    steps = (spread.step1, spread.step2)
    for step in range(1, depth - 1):
        for act in steps[step - 1 : step]:
            act()
        for line in lines:
            line.step(step)
    for act in steps[depth - 2 :]:
        act()
    spread.step3()
    for line in lines:
        line.last()
    stage.put(w_all_ref, strips_ref)
    spread.last()
    for copy in sent:
        copy.wait()
    move.wait()
    for line in lines:
        line.sent()
    spread.sent()


def gather_call(
    tokens, gain, router, docs, routes, order, w_query, key_matrix, value_matrix, w_out, depth
):
    rows, width = tokens.shape
    strip = w_out.shape[0] // GROUP
    size = w_query.shape[0]
    return staged_call(
        gather_kernel,
        "gather",
        1,
        [
            ("h", tokens),
            ("v", gain),
            ("v", router),
            ("v", docs),
            ("v", routes),
            ("v", order),
            ("a", w_query),
            ("a", key_matrix),
            ("a", value_matrix),
            ("a", w_out),
        ],
        [
            ("v", shape((GROUP,) + docs.shape, jnp.int32)),
            ("h", shape((EXP_WIN, CAP, rows), bf16)),
            ("h", shape((rows, EXP_WIN * CAP), bf16)),
            ("a", shape((GROUP, rows, width), bf16)),
            ("h", shape((depth, ALL, size), bf16)),
            ("h", shape((depth, strip, width), bf16)),
        ],
        [
            VMEM((rows, width), bf16),
            VMEM((size, 2 * 128), bf16),
            VMEM((size, 128), bf16),
            VMEM((size, 128), bf16),
        ]
        + [DMA((2, depth - 1))] * 4
        + [DMA((GROUP - 1,))] * 2
        + [DMA((Spread.SEMS,))] * 2
        + [DMA((5,))],
    )


def turned(values, cosine, sine):
    half = HEAD_DIM // 2
    out = []
    for at in range(0, values.shape[0], HEAD_DIM):
        low, high = values[at : at + half], values[at + half : at + HEAD_DIM]
        out += [low * cosine - high * sine, high * cosine + low * sine]
    return jnp.concatenate(out, axis=0)


def project_block(
    owner, normed_ref, w_all_ref, cos_ref, sin_ref, qt_ref, kt_ref, vt_ref, k_ref, v_ref
):
    linear = None
    for s in range(w_all_ref.shape[0]):
        size = w_all_ref.shape[2]
        term = dot(
            w_all_ref[s, :HW, :], normed_ref[owner, :, s * size : (s + 1) * size], ((1,), (1,))
        )
        linear = term if linear is None else linear + term
    tokens = block(owner)
    cosine, sine = cos_ref[:, tokens], sin_ref[:, tokens]
    queries = turned(linear[:QW], cosine, sine) * HEAD_DIM ** (-0.5)
    qt_ref[:, tokens] = queries.astype(bf16)
    keys = turned(linear[QW : QW + HEAD_DIM], cosine, sine)
    kt_ref[:, tokens] = keys.astype(bf16)
    k_ref[tokens, :] = keys.T.astype(bf16)
    values = linear[QW + HEAD_DIM :]
    vt_ref[:, tokens] = values.astype(bf16)
    v_ref[tokens, :] = values.T.astype(bf16)


def projected(span):
    return [
        ("h", shape((QW, span), bf16)),
        ("h", shape((HEAD_DIM, span), bf16)),
        ("h", shape((HEAD_DIM, span), bf16)),
        ("h", shape((span, HEAD_DIM), bf16)),
        ("h", shape((span, HEAD_DIM), bf16)),
    ]


def project_kernel(stage, normed_ref, w_all_ref, cos_ref, sin_ref, *outs):
    stage.need(normed_ref, w_all_ref, cos_ref, sin_ref)

    def project(i, _):
        project_block(i, normed_ref, w_all_ref, cos_ref, sin_ref, *outs)
        return 0

    lax.fori_loop(0, GROUP, project, 0)


def project_call(normed, w_all, cosine, sine):
    return staged_call(
        project_kernel,
        "project",
        None,
        [("h", normed), ("h", w_all), ("h", cosine), ("h", sine)],
        projected(normed.shape[0] * normed.shape[1]),
        [],
    )


def docs_column(row):
    return jnp.broadcast_to(row.astype(f32), (8, row.shape[1])).T[:, :1]


def attend_after_project(
    n_blocks, stage, w_all_ref, normed_ref, cos_ref, sin_ref, *rest,
):
    given, (qt_ref, kt_ref, vt_ref, k_ref, v_ref), rest = rest[:6], rest[6:11], rest[11:]

    def project_all():
        stage.need(normed_ref, cos_ref, sin_ref)

        def project(i, _):
            project_block(
                i, normed_ref, w_all_ref, cos_ref, sin_ref, qt_ref, kt_ref, vt_ref, k_ref, v_ref
            )
            return 0

        lax.fori_loop(0, GROUP, project, 0)
        stage.put(qt_ref, kt_ref, vt_ref, k_ref, v_ref)

    attend_body(n_blocks, stage, project_all, w_all_ref, qt_ref, k_ref, vt_ref, *given, *rest)


def attend_kernel(n_blocks, stage, w_all_ref, qt_ref, k_ref, vt_ref, *rest):
    def fetch_all():
        stage.need(qt_ref, k_ref, vt_ref)

    attend_body(n_blocks, stage, fetch_all, w_all_ref, qt_ref, k_ref, vt_ref, *rest)


def router_of(w_all_ref):
    return [w_all_ref[s, HW:, :] for s in range(w_all_ref.shape[0])]


def attend_body(
    n_blocks, stage, prepare, w_all_ref, qt_ref, k_ref, vt_ref,
    docs_ref, strips_ref, tokens_ref, gain_ref, routes_ref, placed_ref,
    o_ref, lse_ref, attended_ref, out_weight_ref, weights_ref, residual_ref, normed2_ref, gates_ref,
    slot_gates_ref, rows_ref,
    staged_ref, docs_col_ref, top_ref, sum_ref, acc_ref, mixed_ref,
    a_send, a_recv, s_send, s_recv, w_send, w_recv, local,
):
    T = TOK_DEV
    place = Place()
    me, z = place.me, place.z
    first = place.base
    met = greet(place.others())
    depth, strip, _ = strips_ref.shape
    move = pltpu.make_async_copy(w_all_ref.at[:, :HW], weights_ref.at[me], local.at[1])

    def layers(ref, h):
        return ref.at[pl.ds(h * (depth // 2), depth // 2)]

    weights = Spread(
        place, w_all_ref.at[:, :HW], lambda owner: weights_ref.at[owner], layers, w_send, w_recv
    )
    strips = Spread(
        place, strips_ref, lambda owner: out_weight_ref.at[:, owner], layers, s_send, s_recv
    )
    def turn(i, _):
        docs_col_ref[i] = docs_column(docs_ref[i])
        return 0

    lax.fori_loop(0, n_blocks, turn, 0)
    stage.need(strips_ref)
    met()
    strips.start()
    out_weight_ref[:, me] = strips_ref[...]
    stage.need(w_all_ref)
    move.start()
    prepare()
    weights.start()

    def tile(kb, qb, mask):
        kt = k_ref[block(kb), :]
        vt = vt_ref[:, block(kb)]
        heads = range(HEADS)
        parts = [slice(h * HEAD_DIM, (h + 1) * HEAD_DIM) for h in heads]
        s = [dot(kt, qt_ref[parts[h], block(qb)]) for h in heads]
        if mask is not None:
            s = [jnp.where(mask, x, score_masked) for x in s]
        old = [top_ref[h : h + 1, :] for h in heads]
        new = [jnp.maximum(old[h], jnp.max(s[h], axis=0, keepdims=True)) for h in heads]
        p = [jnp.exp(s[h] - new[h]) for h in heads]
        factor = [jnp.exp(old[h] - new[h]) for h in heads]
        total = [
            sum_ref[h : h + 1, :] * factor[h] + jnp.sum(p[h], axis=0, keepdims=True) for h in heads
        ]
        mixed = [acc_ref[parts[h], :] * factor[h] + dot(vt, p[h].astype(bf16)) for h in heads]
        for h in heads:
            top_ref[h : h + 1, :] = new[h]
            sum_ref[h : h + 1, :] = total[h]
            acc_ref[parts[h], :] = mixed[h]

    def same(kb, gq):
        return docs_col_ref[kb] == docs_ref[gq].astype(f32)

    def head_rows(head):
        per = GROUP * depth // GROUP
        return attended_ref.at[lax.div(head * depth, GROUP), pl.ds(lax.rem(head * depth, GROUP), per)]

    def attended_copy(to, slot):
        return remote(
            staged_ref.at[to], head_rows(slot), a_send.at[to], a_recv.at[slot], place.ctx(to)
        )

    def q_block(j, _):
        for at, act in ((1, strips.step1), (2, strips.step2), (5, strips.step3)):
            pl.when(j == at)(act)
        qb = GROUP - 1 - j
        gq = first + qb
        top_ref[...] = jnp.full_like(top_ref, score_masked)
        sum_ref[...] = jnp.ones_like(sum_ref)
        acc_ref[...] = jnp.zeros_like(acc_ref)
        last = gq == n_blocks - 1

        def k_block(kb, _):
            edge = jnp.logical_or(kb == 0, last)

            @pl.when(edge)
            def _():
                tile(kb, qb, same(kb, gq))

            @pl.when(jnp.logical_not(edge))
            def _():
                tile(kb, qb, None)

            return 0

        lax.fori_loop(0, gq, k_block, 0)
        keys = lax.broadcasted_iota(jnp.int32, (T, T), 0)
        queries = lax.broadcasted_iota(jnp.int32, (T, T), 1)
        tile(gq, qb, same(gq, gq) & (keys <= queries))
        lse_ref[qb] = top_ref[...] + jnp.log(sum_ref[...])
        for h in range(HEADS):
            part = slice(h * HEAD_DIM, (h + 1) * HEAD_DIM)
            acc_ref[part, :] = acc_ref[part, :] / sum_ref[h : h + 1, :]
        o_ref[:, block(qb)] = acc_ref[...]
        staged_ref[qb] = acc_ref[...].astype(bf16).reshape(depth, strip, T)

        @pl.when(qb != me)
        def _():
            attended_copy(qb, me).start()

        return 0

    lax.fori_loop(0, GROUP, q_block, 0)
    stage.put(o_ref, lse_ref)
    own = pltpu.make_async_copy(staged_ref.at[me], head_rows(me), local.at[2])
    own.start()
    own.wait()
    weights.step1()
    weights.step2()
    for j in range(1, GROUP):
        other = lax.rem(me + j, GROUP)
        attended_copy(other, other).wait()
    stage.put(attended_ref)
    strips.last()
    stage.put(out_weight_ref)

    rows, width = tokens_ref.shape
    stage.need(tokens_ref, placed_ref)
    mixed_ref[...] = attended_ref[...].reshape(width, rows).T

    def out_columns(i, _):
        columns = block(i)
        weight = out_weight_ref[:, :, :, columns].reshape(width, T)
        residual_ref[:, columns] = tokens_ref[:, columns].astype(f32) + dot(mixed_ref[...], weight)
        return 0

    lax.fori_loop(0, width // T, out_columns, 0)
    residual = residual_ref[...]
    scale = lax.rsqrt(jnp.mean(residual * residual, axis=-1, keepdims=True) + epsilon)
    normed2_ref[...] = (residual * scale * gain_ref[...].reshape(1, -1)).astype(bf16)
    stage.put(residual_ref, normed2_ref)
    logits = None
    for s, router in enumerate(router_of(w_all_ref)):
        size = router.shape[1]
        term = dot(router, normed2_ref[:, s * size : (s + 1) * size], ((1,), (1,)))
        logits = term if logits is None else logits + term
    expert = lax.broadcasted_iota(jnp.int32, gates_ref.shape, 0)
    chosen = expert < 0
    for k in range(TOPK):
        chosen = chosen | (expert == routes_ref[k : k + 1, :])
    logits = jnp.where(chosen, logits, score_masked)
    top = jnp.max(logits, axis=0, keepdims=True)
    gates = jnp.where(chosen, jnp.exp(logits - top), 0.0)
    gates = gates / jnp.sum(gates, axis=0, keepdims=True)
    gates_ref[...] = gates
    for e in range(EXP_WIN):
        slot_gates_ref[e] = jnp.sum(
            placed_ref[e].astype(f32) * gates[e : e + 1, :], axis=1, keepdims=True
        )

    def pick_rows(e, _):
        rows_ref[e] = dot(placed_ref[e], normed2_ref[...]).astype(bf16)
        return 0

    lax.fori_loop(0, EXP_WIN, pick_rows, 0)
    stage.put(gates_ref, slot_gates_ref, rows_ref)
    weights.step3()
    weights.last()
    weights.sent()
    strips.sent()
    move.wait()


def attend_call(
    kernel, ins, docs, strips, tokens, gain, routes, placed, w_all, span, projections
):
    n = docs.shape[0]
    rows, width = tokens.shape
    depth, _, size = w_all.shape
    strip = strips.shape[1]
    return staged_call(
        functools.partial(kernel, n),
        "attend",
        2,
        [("h", one) for one in ins]
        + [("v", docs), ("h", strips), ("h", tokens), ("v", gain), ("v", routes), ("h", placed)],
        projections
        + [
            ("h", shape((QW, span), f32)),
            ("h", shape((GROUP, 8, TOK_DEV), f32)),
            ("h", shape((depth, GROUP, strip, TOK_DEV), bf16)),
            ("h", shape((depth, GROUP) + strips.shape[1:], bf16)),
            ("a", shape((GROUP, depth, HW, size), bf16)),
            ("h", shape((rows, width), f32)),
            ("h", shape((rows, width), bf16)),
            ("h", shape((ROUTER, rows), f32)),
            ("h", shape((EXP_WIN, CAP, 1), f32)),
            ("h", shape((EXP_WIN, CAP, width), bf16)),
        ],
        [
            VMEM((GROUP, depth, strip, TOK_DEV), bf16),
            VMEM((n, TOK_DEV, 1), f32),
            VMEM((8, TOK_DEV), f32),
            VMEM((8, TOK_DEV), f32),
            VMEM((QW, TOK_DEV), f32),
            VMEM((rows, width), bf16),
        ]
        + [DMA((GROUP,))] * 2
        + [DMA((Spread.SEMS,))] * 4
        + [DMA((3,))],
    )


def dispatch_kernel(
    stage, sent_rows_ref, gate_up_ref, placed_ref, cotangent_ref, slot_gates_ref,
    rows_ref, grads_ref, gate_ref, up_ref, active_ref, grad_down_ref,
    gate_up_held, own_grads, r_send, r_recv, g_send, g_recv, local,
):
    place = Place()
    me = place.me
    met = greet(place.others())
    width = cotangent_ref.shape[1]

    def copy(source, target, send, receive, j):
        to = lax.rem(me + j, GROUP)
        return remote(source.at[to], target.at[me], send.at[j], receive.at[j], place.ctx(to))

    met()
    for j in range(1, GROUP):
        copy(sent_rows_ref, rows_ref, r_send, r_recv, j).start()
    own = pltpu.make_async_copy(sent_rows_ref.at[me], rows_ref.at[me], local.at[0])
    own.start()
    fetch = pltpu.make_async_copy(gate_up_ref, gate_up_held, local.at[1])
    fetch.start()
    stage.need(placed_ref, cotangent_ref, slot_gates_ref)

    def send_grads(j, _):
        to = lax.rem(me + j, GROUP)
        routed = dot(placed_ref[to], cotangent_ref[...])
        own_grads[to] = (routed * slot_gates_ref[to]).astype(bf16)

        @pl.when(j < GROUP)
        def _():
            copy(own_grads, grads_ref, g_send, g_recv, j).start()

        return 0

    lax.fori_loop(1, GROUP + 1, send_grads, 0)
    grads_ref[me] = own_grads[me]
    fetch.wait()
    own.wait()
    for j in range(1, GROUP):
        copy(sent_rows_ref, rows_ref, r_send, r_recv, j).wait_recv()
    stage.put(rows_ref)
    slots = GROUP * CAP
    hidden = gate_ref.shape[1]
    tiles = hidden // TOK_DEV

    def expert_up(i, _):
        came = rows_ref[...].reshape(slots, width)
        gate = dot(came, gate_up_held[:, block(i)])
        up = dot(came, gate_up_held[:, block(tiles + i)])
        gate_ref[:, block(i)] = gate
        up_ref[:, block(i)] = up
        active_ref[:, block(i)] = (gate * jax.nn.sigmoid(gate) * up).astype(bf16)
        return 0

    lax.fori_loop(0, tiles, expert_up, 0)
    stage.put(gate_ref, up_ref, active_ref)
    for j in range(1, GROUP):
        copy(own_grads, grads_ref, g_send, g_recv, j).wait_recv()
    stage.put(grads_ref)

    def expert_over(i, _):
        grad_down_ref[:, block(i)] = dot(
            active_ref[...], grads_ref[:, :, block(i)].reshape(slots, TOK_DEV), ((0,), (0,))
        ).astype(bf16)
        return 0

    lax.fori_loop(0, width // TOK_DEV, expert_over, 0)
    stage.put(grad_down_ref)
    for j in range(1, GROUP):
        copy(sent_rows_ref, rows_ref, r_send, r_recv, j).wait_send()
        copy(own_grads, grads_ref, g_send, g_recv, j).wait_send()


def dispatch_call(sent_rows, gate_up, placed, cotangent, slot_gates):
    slots = sent_rows.shape
    count, width = GROUP * CAP, slots[2]
    hidden = gate_up.shape[1] // 2
    return staged_call(
        dispatch_kernel,
        "dispatch",
        3,
        [
            ("a", sent_rows),
            ("a", gate_up),
            ("h", placed),
            ("h", cotangent),
            ("h", slot_gates),
        ],
        [
            ("h", shape(slots, bf16)),
            ("h", shape(slots, bf16)),
            ("h", shape((count, hidden), f32)),
            ("h", shape((count, hidden), f32)),
            ("h", shape((count, hidden), bf16)),
            ("h", shape((hidden, width), bf16)),
        ],
        [VMEM(gate_up.shape, bf16), VMEM(slots, bf16)] + [DMA((GROUP,))] * 4 + [DMA((2,))],
    )


def expert_kernel(
    stage, active_ref, down_ref, grads_ref, rows_ref, gate_ref, up_ref, gate_up_ref,
    out_ref, back_ref, grad_gate_up_ref,
    grads_held, rows_held, gate_up_held, own_ref, grad_ref, send, receive, local,
):
    place = Place()
    me = place.me
    met = greet(place.others())
    fetches = [
        pltpu.make_async_copy(grads_ref, grads_held, local.at[0]),
        pltpu.make_async_copy(rows_ref, rows_held, local.at[1]),
        pltpu.make_async_copy(gate_up_ref, gate_up_held, local.at[2]),
    ]
    for fetch in fetches:
        fetch.start()
    count, hidden = active_ref.shape
    width = down_ref.shape[1]
    T = TOK_DEV
    tiles = hidden // T

    def copy(j):
        to = lax.rem(me + j, GROUP)
        return remote(own_ref.at[to], out_ref.at[me], send.at[j], receive.at[j], place.ctx(to))

    stage.need(active_ref, down_ref)

    def out(i, _):
        value = dot(active_ref[...], down_ref[:, block(i)]).astype(bf16)
        own_ref[:, :, block(i)] = value.reshape(GROUP, CAP, T)
        return 0

    lax.fori_loop(0, width // T, out, 0)
    met()
    for j in range(1, GROUP):
        copy(j).start()
    move = pltpu.make_async_copy(own_ref.at[me], out_ref.at[me], local.at[3])
    move.start()
    fetches[0].wait()
    stage.need(gate_ref, up_ref)

    def back(i, _):
        grad = dot(grads_held[...], down_ref[block(i), :], ((1,), (1,)))
        gate, up = gate_ref[:, block(i)], up_ref[:, block(i)]
        sigmoid = jax.nn.sigmoid(gate)
        grad_gate = grad * up * sigmoid * (1.0 + gate * (1.0 - sigmoid))
        grad_ref[:, block(i)] = grad_gate.astype(bf16)
        grad_ref[:, block(tiles + i)] = (grad * gate * sigmoid).astype(bf16)
        return 0

    lax.fori_loop(0, tiles, back, 0)
    fetches[1].wait()
    fetches[2].wait()

    def over(i, _):
        grad_gate_up_ref[block(i), :] = dot(
            rows_held[:, block(i)], grad_ref[...], ((0,), (0,))
        ).astype(bf16)
        back_ref[:, block(i)] = dot(
            grad_ref[...], gate_up_held[block(i), :], ((1,), (1,))
        ).astype(bf16)
        return 0

    lax.fori_loop(0, width // T, over, 0)
    stage.put(back_ref, grad_gate_up_ref)
    for j in range(1, GROUP):
        copy(j).wait()
    move.wait()


def expert_call(active, down, grads, rows, gate, up, gate_up):
    count, width = rows.shape
    hidden = down.shape[0]
    slots = (GROUP, CAP, width)
    return staged_call(
        expert_kernel,
        "expert",
        7,
        [
            ("h", active),
            ("h", down),
            ("a", grads),
            ("a", rows),
            ("h", gate),
            ("h", up),
            ("a", gate_up),
        ],
        [
            ("a", shape(slots, bf16)),
            ("h", shape((count, width), bf16)),
            ("h", shape((width, 2 * hidden), bf16)),
        ],
        [
            VMEM(grads.shape, bf16),
            VMEM(rows.shape, bf16),
            VMEM(gate_up.shape, bf16),
            VMEM(slots, bf16),
            VMEM((count, 2 * hidden), bf16),
            DMA((GROUP,)),
            DMA((GROUP,)),
            DMA((4,)),
        ],
    )


def combine_kernel(
    stage, out_ref, sent_grad_ref, weight_ref, residual_ref, normed_ref, gates_ref, placed_ref,
    placed_t_ref, slot_gates_ref, cotangent_ref, gain_ref, w_all_ref,
    output_ref, grad_residual_ref, heads_ref, attn_ref, grad_router_ref, grad_gain_ref,
    back_ref, weight_held, sum_ref, turned_ref, staged_ref, scaled_ref,
    b_send, b_recv, h_send, h_recv, local,
):
    place = Place()
    me = place.me
    met = greet(place.others())
    fetch = pltpu.make_async_copy(weight_ref, weight_held, local.at[0])
    fetch.start()
    rows, width = residual_ref.shape

    def copy(source, target, send, receive, j):
        to = lax.rem(me + j, GROUP)
        return remote(source.at[to], target.at[me], send.at[j], receive.at[j], place.ctx(to))

    backs = [copy(sent_grad_ref, back_ref, b_send, b_recv, j) for j in range(1, GROUP)]
    met()
    for one in backs:
        one.start()
    move = pltpu.make_async_copy(sent_grad_ref.at[me], back_ref.at[me], local.at[1])
    move.start()
    turned_ref[...] = jnp.zeros_like(turned_ref)
    stage.need(out_ref, placed_ref, slot_gates_ref, cotangent_ref)

    def add_expert(e, _):
        came = out_ref[e].astype(f32)
        scaled_ref[e] = (came * slot_gates_ref[e]).astype(bf16)
        routed = dot(placed_ref[e], cotangent_ref[...])
        slot_grad = jnp.sum(routed * came, axis=1, keepdims=True)
        turned_ref[pl.ds(e, 1), :] = jnp.sum(
            placed_ref[e].astype(f32) * slot_grad, axis=0, keepdims=True
        )
        return 0

    lax.fori_loop(0, EXP_WIN, add_expert, 0)
    stage.need(placed_t_ref, residual_ref, gates_ref, w_all_ref, normed_ref)
    slots = EXP_WIN * CAP

    def mix(i, _):
        columns = block(i)
        mixed = dot(placed_t_ref[...], scaled_ref[:, :, columns].reshape(slots, TOK_DEV))
        output_ref[:, columns] = (residual_ref[:, columns] + mixed).astype(bf16)
        return 0

    lax.fori_loop(0, width // TOK_DEV, mix, 0)
    stage.put(output_ref)
    gates = gates_ref[...]
    grad_gates = turned_ref[...]
    weighted = jnp.sum(gates * grad_gates, axis=0, keepdims=True)
    grad_logits = (gates * (grad_gates - weighted)).astype(bf16)
    for s, router in enumerate(router_of(w_all_ref)):
        size = router.shape[1]
        sum_ref[:, s * size : (s + 1) * size] = dot(grad_logits, router, ((0,), (0,)))
    grad_router_ref[...] = dot(grad_logits, normed_ref[...])
    fetch.wait()
    move.wait()
    for one in backs:
        one.wait_recv()

    def add_back(i, _):
        columns = block(i)
        sum_ref[:, columns] += dot(
            placed_t_ref[...], back_ref[:, :, columns].reshape(slots, TOK_DEV)
        )
        return 0

    lax.fori_loop(0, width // TOK_DEV, add_back, 0)
    residual = residual_ref[...]
    grad_normed = sum_ref[...]
    scale = lax.rsqrt(jnp.mean(residual * residual, axis=-1, keepdims=True) + epsilon)
    scaled = grad_normed * gain_ref[...].reshape(1, -1)
    inner = jnp.mean(scaled * residual, axis=-1, keepdims=True)
    grad = scale * scaled - residual * (scale * scale * scale * inner)
    grad_gain_ref[...] = jnp.sum(grad_normed * residual * scale, axis=0, keepdims=True)
    grad_residual = cotangent_ref[...].astype(f32) + grad
    grad_residual_ref[...] = grad_residual
    attn_ref[...] = grad_residual.astype(bf16)
    stage.put(grad_residual_ref, attn_ref, grad_router_ref, grad_gain_ref)

    def head_rows(j, _):
        to = lax.rem(me + j, GROUP)
        staged_ref[to] = dot(weight_held[block(to, QW), :], attn_ref[...], ((1,), (1,))).astype(bf16)

        @pl.when(j < GROUP)
        def _():
            copy(staged_ref, heads_ref, h_send, h_recv, j).start()

        return 0

    lax.fori_loop(1, GROUP + 1, head_rows, 0)
    move = pltpu.make_async_copy(staged_ref.at[me], heads_ref.at[me], local.at[2])
    move.start()
    for one in backs:
        one.wait_send()
    for j in range(1, GROUP):
        copy(staged_ref, heads_ref, h_send, h_recv, j).wait()
    move.wait()


def combine_call(
    out, sent_grad, weight, residual, normed, gates, placed, placed_t, slot_gates, cotangent,
    gain, w_all,
):
    rows, width = residual.shape
    slots = (GROUP, CAP, width)
    return staged_call(
        combine_kernel,
        "combine",
        4,
        [
            ("h", out),
            ("a", sent_grad),
            ("a", weight),
            ("h", residual),
            ("h", normed),
            ("h", gates),
            ("h", placed),
            ("h", placed_t),
            ("h", slot_gates),
            ("h", cotangent),
            ("v", gain),
            ("h", w_all),
        ],
        [
            ("h", shape((rows, width), bf16)),
            ("h", shape((rows, width), f32)),
            ("a", shape((GROUP, QW, rows), bf16)),
            ("h", shape((rows, width), bf16)),
            ("h", shape((ROUTER, width), f32)),
            ("h", shape((1, width), f32)),
        ],
        [
            VMEM(slots, bf16),
            VMEM(weight.shape, bf16),
            VMEM((rows, width), f32),
            VMEM((ROUTER, rows), f32),
            VMEM((GROUP, QW, rows), bf16),
            VMEM(slots, bf16),
        ]
        + [DMA((GROUP,))] * 4
        + [DMA((3,))],
    )


def backward_kernel(
    n_blocks, stage, attn_ref, attended_ref, down_ref, heads_ref, o_ref, lse_ref, qt_ref, k_ref,
    kt_ref, v_ref, docs_ref,
    dq_ref, dk_ref, dv_ref, grad_out_ref, down_all_ref,
    part_ref, pair_ref, strip_ref, came_ref, docs_col_ref, delta_ref, dk_acc, dv_acc,
    p_send, p_recv, s_send, s_recv, e_send, e_recv, local,
):
    T = TOK_DEV
    place = Place()
    me = place.me
    first = place.base
    core, side, row = place.near
    across = flip(side, 4)
    met = greet([place.ctx(i) for i in (core, side, row, across)])
    half = GROUP // 2
    depth, strip, width = grad_out_ref.shape
    parity = lax.rem(me, 2)

    def strip_of(n, parity):
        return 2 * n + parity

    def part(n, parity):
        rows = attended_ref[:, strip_of(n, parity)].reshape(depth * strip, T)
        return dot(rows, attn_ref[...])

    def pair_copy(n):
        return remote(
            part_ref.at[n], pair_ref.at[n], p_send.at[n], p_recv.at[n], place.ctx(core)
        )

    def pair_part(n, _):
        part_ref[n] = part(n, 1 - parity).astype(bf16)
        pair_copy(n).start()
        return 0

    down_move = pltpu.make_async_copy(down_ref, down_all_ref.at[me], local.at[0])
    down_spread = Spread(
        place, down_ref, lambda owner: down_all_ref.at[owner], halves(down_ref.shape[0]), e_send, e_recv
    )
    stage.need(attn_ref, attended_ref)
    met()
    lax.fori_loop(0, half, pair_part, 0)
    stage.need(down_ref)
    down_spread.start()
    down_move.start()

    def own_part(n, _):
        strip_ref[n] = part(n, parity).astype(bf16)
        return 0

    lax.fori_loop(0, half, own_part, 0)
    for n in range(half):
        pair_copy(n).wait_recv()

    def add_pair(n, _):
        strip_ref[n] = (strip_ref[n].astype(f32) + pair_ref[n].astype(f32)).astype(bf16)
        return 0

    lax.fori_loop(0, half, add_pair, 0)
    strips = [
        remote(
            strip_ref.at[lax.div(device, 2)], came_ref.at[n], s_send.at[n], s_recv.at[n],
            place.ctx(device),
        )
        for n, device in enumerate((across, side, row))
    ]
    for copy in strips:
        copy.start()

    def turn(i, _):
        docs_col_ref[i] = docs_column(docs_ref[i])
        return 0

    lax.fori_loop(0, n_blocks, turn, 0)
    heads = range(HEADS)
    parts = [slice(h * HEAD_DIM, (h + 1) * HEAD_DIM) for h in heads]

    stage.need(heads_ref, o_ref, lse_ref, qt_ref, k_ref, kt_ref, v_ref)

    def prepare(i, _):
        for h in heads:
            product = o_ref[parts[h], block(i)] * heads_ref[i, parts[h], :].astype(f32)
            delta_ref[i, h : h + 1, :] = jnp.sum(product, axis=0, keepdims=True)
        return 0

    lax.fori_loop(0, GROUP, prepare, 0)
    dq_ref[...] = jnp.zeros_like(dq_ref)

    def tile(kb, qb, mask):
        k = k_ref[block(kb), :]
        v = v_ref[block(kb), :]
        kt = kt_ref[:, block(kb)]
        q = [qt_ref[part, block(qb)] for part in parts]
        do = [heads_ref[qb, part, :] for part in parts]
        s = [dot(k, x) for x in q]
        dp = [dot(v, x) for x in do]
        p = [jnp.exp(s[h] - lse_ref[qb, h : h + 1, :]) for h in heads]
        if mask is not None:
            p = [jnp.where(mask, x, 0.0) for x in p]
        ds = [(p[h] * (dp[h] - delta_ref[qb, h : h + 1, :])).astype(bf16) for h in heads]
        pb = [x.astype(bf16) for x in p]
        turn = ((1,), (1,))
        dv_acc[...] += dot(pb[0], do[0], turn) + dot(pb[1], do[1], turn) + dot(pb[2], do[2], turn)
        dk_acc[...] += dot(ds[0], q[0], turn) + dot(ds[1], q[1], turn) + dot(ds[2], q[2], turn)
        for h in heads:
            dq_ref[parts[h], block(qb)] += dot(kt, ds[h])

    def same(kb, gq):
        return docs_col_ref[kb] == docs_ref[gq].astype(f32)

    def k_block(kb, _):
        for at, act in (
            (2, down_spread.step1), (4, down_spread.step2), (7, down_spread.step3),
        ):
            pl.when(kb == first + at)(act)
        dk_acc[...] = jnp.zeros_like(dk_acc)
        dv_acc[...] = jnp.zeros_like(dv_acc)

        @pl.when(kb >= first)
        def _():
            keys = lax.broadcasted_iota(jnp.int32, (T, T), 0)
            queries = lax.broadcasted_iota(jnp.int32, (T, T), 1)
            tile(kb, kb - first, same(kb, kb) & (keys <= queries))

        def q_block(qb, _):
            gq = first + qb
            edge = jnp.logical_or(kb == 0, gq == n_blocks - 1)

            @pl.when(edge)
            def _():
                tile(kb, qb, same(kb, gq))

            @pl.when(jnp.logical_not(edge))
            def _():
                tile(kb, qb, None)

            return 0

        lax.fori_loop(jnp.maximum(kb - first + 1, 0), GROUP, q_block, 0)
        dk_ref[:, block(kb)] = dk_acc[...].T
        dv_ref[:, block(kb)] = dv_acc[...].T
        return 0

    lax.fori_loop(0, first + GROUP, k_block, 0)

    def clear(kb, _):
        dk_ref[:, block(kb)] = jnp.zeros((HEAD_DIM, T), f32)
        dv_ref[:, block(kb)] = jnp.zeros((HEAD_DIM, T), f32)
        return 0

    lax.fori_loop(first + GROUP, n_blocks, clear, 0)
    stage.put(dq_ref, dk_ref, dv_ref)
    for copy in strips:
        copy.wait_recv()
    total = strip_ref[lax.div(me, 2)].astype(f32)
    for n in range(len(strips)):
        total = total + came_ref[n].astype(f32)
    grad_out_ref[...] = total.astype(bf16).reshape(depth, strip, width)
    stage.put(grad_out_ref)
    down_spread.last()
    down_spread.sent()
    for n in range(half):
        pair_copy(n).wait_send()
    for copy in strips:
        copy.wait_send()
    down_move.wait()


def backward_call(attn, attended, down, heads, o, lse, qt, k, kt, v, docs):
    n = k.shape[0] // TOK_DEV
    span = qt.shape[1]
    rows, width = attn.shape
    depth, _, strip, _ = attended.shape
    block_rows = depth * strip
    half = GROUP // 2
    return staged_call(
        functools.partial(backward_kernel, n),
        "backward",
        5,
        [("h", one) for one in (attn, attended, down, heads, o, lse, qt, k, kt, v)] + [("v", docs)],
        [
            ("h", shape((QW, span), f32)),
            ("h", shape(kt.shape, f32)),
            ("h", shape(kt.shape, f32)),
            ("h", shape((depth, strip, width), bf16)),
            ("a", shape((GROUP,) + down.shape, bf16)),
        ],
        [
            VMEM((half, block_rows, width), bf16),
            VMEM((half, block_rows, width), bf16),
            VMEM((half, block_rows, width), bf16),
            VMEM((3, block_rows, width), bf16),
            VMEM((n, TOK_DEV, 1), f32),
            VMEM((GROUP, 8, TOK_DEV), f32),
            VMEM((TOK_DEV, HEAD_DIM), f32),
            VMEM((TOK_DEV, HEAD_DIM), f32),
        ]
        + [DMA((half,))] * 2
        + [DMA((3,))] * 2
        + [DMA((Spread.SEMS,))] * 2
        + [DMA((1,))],
    )


def finish_kernel(
    stage, normed_ref, weights_ref, gate_up_ref, grad_out_ref, dq_ref, dk_ref, dv_ref, cos_ref,
    sin_ref, tokens_ref, gain_ref, grad_residual_ref, grad_router_ref, grad_gain2_ref,
    input_grad_ref, shared_ref, small_all_ref, out_all_ref, gate_up_all_ref,
    normed_held, weights_held, linear_ref, came_ref, came_t, sum_ref, part_ref,
    small_ref, head_in, small_in, out_in, shard_ref, small_shard_ref, out_shard_ref,
    g_send, g_recv, h_send, h_recv, s_send, s_recv, o_send, o_recv, e_send, e_recv, f_send, f_recv,
    m_send, m_recv, c_send, c_recv, local,
):
    place = Place()
    me, z, depth = place.me, place.z, place.depth
    met = greet(place.others() + place.layers())
    fetches = [
        pltpu.make_async_copy(normed_ref, normed_held, local.at[0]),
        pltpu.make_async_copy(weights_ref, weights_held, local.at[1]),
    ]
    for fetch in fetches:
        fetch.start()
    rows, width = tokens_ref.shape
    size = width // depth

    def spread_of(source, out, send, receive):
        return Spread(
            place, source, lambda owner: out.at[owner], halves(source.shape[0]), send, receive
        )

    expert_spread = spread_of(gate_up_ref, gate_up_all_ref, e_send, e_recv)
    head_spread = spread_of(shard_ref, shared_ref, f_send, f_recv)
    small_spread = spread_of(small_shard_ref, small_all_ref, m_send, m_recv)
    out_spread = spread_of(out_shard_ref, out_all_ref, c_send, c_recv)
    moves = [
        pltpu.make_async_copy(gate_up_ref, gate_up_all_ref.at[me], local.at[3]),
        pltpu.make_async_copy(out_shard_ref, out_all_ref.at[me], local.at[4]),
        pltpu.make_async_copy(shard_ref, shared_ref.at[me], local.at[5]),
        pltpu.make_async_copy(small_shard_ref, small_all_ref.at[me], local.at[6]),
    ]
    stage.need(gate_up_ref)
    moves[0].start()

    def copy(j):
        to = lax.rem(me + j, GROUP)
        return remote(
            linear_ref.at[to], came_ref.at[me], g_send.at[j], g_recv.at[j], place.ctx(to)
        )

    def down(source, target, send, receive, j):
        to = lax.rem(z + j, depth)
        return remote(source.at[to], target.at[z], send.at[j], receive.at[j], place.fsdp(to))

    stage.need(dq_ref, dk_ref, dv_ref, cos_ref, sin_ref)

    def turn_back(j, _):
        to = lax.rem(me + j, GROUP)
        cosine, sine = cos_ref[:, block(to)], -sin_ref[:, block(to)]
        dq = turned(dq_ref[:, block(to)], cosine, sine) * HEAD_DIM ** (-0.5)
        dk = turned(dk_ref[:, block(to)], cosine, sine)
        linear_ref[to, :QW, :] = dq.astype(bf16)
        linear_ref[to, QW : QW + HEAD_DIM, :] = dk.astype(bf16)
        linear_ref[to, QW + HEAD_DIM :, :] = dv_ref[:, block(to)].astype(bf16)
        pl.when(j == 1)(met)

        @pl.when(j < GROUP)
        def _():
            copy(j).start()

        return 0

    lax.fori_loop(1, GROUP + 1, turn_back, 0)
    stage.need(grad_out_ref)
    outs = [down(grad_out_ref, out_in, o_send, o_recv, j) for j in range(1, depth)]
    for one in outs:
        one.start()
    out_in[z] = grad_out_ref[z]
    came_ref[me] = linear_ref[me]
    fetches[0].wait()

    def own_weights(j, _):
        to = lax.rem(z + j, depth)
        columns = block(to, size)
        total = None
        for b in range(GROUP):
            term = dot(linear_ref[b], normed_held[b, :, columns])
            total = term if total is None else total + term
        part_ref[to] = total.astype(bf16)

        @pl.when(j < depth)
        def _():
            down(part_ref, head_in, h_send, h_recv, j).start()

        return 0

    lax.fori_loop(1, depth + 1, own_weights, 0)

    def total(ref):
        value = ref[0].astype(f32)
        for s in range(1, depth):
            value = value + ref[s].astype(f32)
        return value.astype(bf16)

    for j in range(1, GROUP):
        copy(j).wait_send()
    expert_spread.start()
    for one in outs:
        one.wait_recv()
    out_shard_ref[...] = total(out_in)
    out_spread.start()
    moves[1].start()
    fetches[1].wait()
    for j in range(1, GROUP):
        copy(j).wait_recv()

    def turn(j, _):
        came_t[j] = came_ref[j].T
        return 0

    lax.fori_loop(0, GROUP, turn, 0)

    def add_heads(s, _):
        total = None
        for j in range(GROUP):
            term = dot(came_t[j], weights_held[j, s])
            total = term if total is None else total + term
        sum_ref[:, block(s, size)] = total
        return 0

    lax.fori_loop(0, depth, add_heads, 0)
    out_spread.step1()
    stage.need(tokens_ref, grad_residual_ref, grad_router_ref, grad_gain2_ref)
    x = tokens_ref[...].astype(f32)
    grad_normed = sum_ref[...]
    scale = lax.rsqrt(jnp.mean(x * x, axis=-1, keepdims=True) + epsilon)
    scaled = grad_normed * gain_ref[...].reshape(1, -1)
    inner = jnp.mean(scaled * x, axis=-1, keepdims=True)
    grad = scale * scaled - x * (scale * scale * scale * inner)
    input_grad_ref[...] = grad_residual_ref[...] + grad
    stage.put(input_grad_ref)
    gain1 = jnp.sum(grad_normed * x * scale, axis=0, keepdims=True)
    row = lax.broadcasted_iota(jnp.int32, (ROUTER, width), 0)
    small = jnp.where(row == ROUTER - 2, gain1, grad_router_ref[...])
    small = jnp.where(row == ROUTER - 1, grad_gain2_ref[...], small).astype(bf16)
    for s in range(depth):
        small_ref[s] = small[:, s * size : (s + 1) * size]
    smalls = [down(small_ref, small_in, s_send, s_recv, j) for j in range(1, depth)]
    heads = [down(part_ref, head_in, h_send, h_recv, j) for j in range(1, depth)]
    for one in smalls:
        one.start()
    expert_spread.step1()
    head_in[z] = part_ref[z]
    small_in[z] = small_ref[z]

    for one in heads:
        one.wait_recv()
    shard_ref[...] = total(head_in)
    head_spread.start()
    out_spread.step2()
    expert_spread.step2()
    for one in smalls:
        one.wait_recv()
    small_shard_ref[...] = total(small_in)
    small_spread.start()
    moves[2].start()
    moves[3].start()
    out_spread.step3()
    expert_spread.step3()
    spreads = (head_spread, small_spread)
    for spread in spreads:
        spread.step1()
    for spread in spreads:
        spread.step2()
    for spread in spreads:
        spread.step3()
    for spread in (out_spread, expert_spread, head_spread, small_spread):
        spread.last()
        spread.sent()
    for one in heads + smalls + outs:
        one.wait_send()
    for move in moves:
        move.wait()


def finish_call(
    normed, weights, gate_up, grad_out, dq, dk, dv, cosine, sine, tokens, gain, grad_residual,
    grad_router, grad_gain2,
):
    rows, width = tokens.shape
    depth, strip, _ = grad_out.shape
    size = width // depth
    return staged_call(
        finish_kernel,
        "finish",
        6,
        [
            ("a", normed),
            ("a", weights),
            ("h", gate_up),
            ("h", grad_out),
            ("h", dq),
            ("h", dk),
            ("h", dv),
            ("h", cosine),
            ("h", sine),
            ("h", tokens),
            ("v", gain),
            ("h", grad_residual),
            ("h", grad_router),
            ("h", grad_gain2),
        ],
        [
            ("h", shape((rows, width), f32)),
            ("a", shape((GROUP, HW, size), bf16)),
            ("a", shape((GROUP, ROUTER, size), bf16)),
            ("a", shape((GROUP, strip, width), bf16)),
            ("a", shape((GROUP,) + gate_up.shape, bf16)),
        ],
        [
            VMEM(normed.shape, bf16),
            VMEM(weights.shape, bf16),
            VMEM((GROUP, HW, rows), bf16),
            VMEM((GROUP, HW, rows), bf16),
            VMEM((GROUP, rows, HW), bf16),
            VMEM((rows, width), f32),
            VMEM((depth, HW, size), bf16),
            VMEM((depth, ROUTER, size), bf16),
            VMEM((depth, HW, size), bf16),
            VMEM((depth, ROUTER, size), bf16),
            VMEM((depth, strip, width), bf16),
            VMEM((HW, size), bf16),
            VMEM((ROUTER, size), bf16),
            VMEM((strip, width), bf16),
        ]
        + [DMA((GROUP,))] * 2
        + [DMA((depth,))] * 6
        + [DMA((Spread.SEMS,))] * 8
        + [DMA((7,))],
    )


def output_kernel(
    shared_ref, small_ref, out_ref, gate_up_ref, down_ref, output_ref, input_grad_ref,
    q_ref, k_ref, v_ref, w_out_ref, router_ref, gain1_ref, gain2_ref, gate_ref, up_ref, w_down_ref,
    final_ref, final_grad_ref,
):
    pair, i = shared_ref.shape[0], pl.program_id(0)
    hidden = gate_ref.shape[2]

    def rows(first, last):
        both = [shared_ref[p, first:last, :].astype(f32) for p in range(pair)]
        return jnp.concatenate(both, axis=0).T

    @pl.when(lax.rem(i, pair) == 0)
    def _():
        q_ref[...] = rows(0, QW)
        k_ref[...] = rows(QW, QW + HEAD_DIM)
        v_ref[...] = rows(QW + HEAD_DIM, HW)

    w_out_ref[...] = out_ref[...].astype(f32)
    gate_ref[...] = gate_up_ref[:, :, :hidden].astype(f32)
    up_ref[...] = gate_up_ref[:, :, hidden:].astype(f32)
    w_down_ref[...] = down_ref[...].astype(f32)
    final_ref[...] = output_ref[...]
    final_grad_ref[...] = input_grad_ref[...]

    @pl.when(i == 0)
    def _():
        total = jnp.sum(small_ref[...].astype(f32), axis=0)
        router_ref[...] = total[: router_ref.shape[0], :]
        gain1_ref[...] = total[ROUTER - 2, :]
        gain2_ref[...] = total[ROUTER - 1, :]


def output_call(shared, small, out, gate_up, down, output, input_grad, experts):
    count, _, size = shared.shape
    _, strip, width = out.shape
    hidden = gate_up.shape[2] // 2
    pair = 2
    rows = output.shape[0] // count
    token = pl.BlockSpec((rows, width), lambda i: (i, 0))

    def first(*dims):
        return pl.BlockSpec((1,) + dims, lambda i: (i,) + (0,) * len(dims))

    def columns(columns):
        return pl.BlockSpec((size, columns), lambda i: (0, i // pair))

    def whole(*dims):
        return pl.BlockSpec(dims, lambda i: (0,) * len(dims))

    return pl.pallas_call(
        output_kernel,
        grid=(count,),
        out_shape=(
            shape((size, count * QW), f32),
            shape((size, count * HEAD_DIM), f32),
            shape((size, count * HEAD_DIM), f32),
            shape(out.shape, f32),
            shape((experts, size), f32),
            shape((size,), f32),
            shape((size,), f32),
            shape((count, size, hidden), f32),
            shape((count, size, hidden), f32),
            shape(down.shape, f32),
            shape(output.shape, bf16),
            shape(input_grad.shape, f32),
        ),
        in_specs=[
            pl.BlockSpec((pair,) + shared.shape[1:], lambda i: (i // pair, 0, 0)),
            whole(*small.shape), first(strip, width), first(*gate_up.shape[1:]),
            first(*down.shape[1:]), token, token,
        ],
        out_specs=(
            columns(pair * QW),
            columns(pair * HEAD_DIM),
            columns(pair * HEAD_DIM),
            first(strip, width),
            whole(experts, size),
            whole(size),
            whole(size),
            first(size, hidden),
            first(size, hidden),
            first(*down.shape[1:]),
            token,
            token,
        ),
        compiler_params=params(),
        name="output",
    )(shared, small, out, gate_up, down, output, input_grad)


def rotary_tables(length):
    frequencies = 10000.0 ** (-(np.arange(HEAD_DIM // 2) * 2.0) / HEAD_DIM)
    angles = frequencies[:, None] * np.arange(length)[None, :]
    return np.cos(angles).astype(np.float32), np.sin(angles).astype(np.float32)


def shards(
    tables,
    tokens,
    doc_ids,
    routes,
    slot_order,
    norm1_gain,
    norm2_gain,
    w_query,
    key_matrix,
    value_matrix,
    w_out,
    w_router,
    w_gate,
    w_up,
    w_down,
    cotangent,
):
    rows, width = tokens.shape[1:]
    ctx, depth = lax.axis_size("ctx"), lax.axis_size("fsdp")
    place = lax.axis_index("ctx")
    parts = ctx // GROUP
    head, part = place % GROUP, place // GROUP
    far = [[p * GROUP + i for p in range(parts)] for i in range(GROUP)]
    span = GROUP * rows
    experts = w_router.shape[1]
    hidden = w_gate.shape[2]

    def gather_z(value):
        return lax.all_gather(value, "fsdp", axis=0, tiled=True)

    def reduce_z(value):
        value = lax.psum_scatter(value.astype(bf16), "fsdp", scatter_dimension=0, tiled=True)
        if parts > 1:
            value = lax.psum(value, "ctx", axis_index_groups=far)
        return value

    cosine, sine = tables
    if parts > 1:
        cosine = lax.dynamic_slice_in_dim(cosine, part * span, span, 1)
        sine = lax.dynamic_slice_in_dim(sine, part * span, span, 1)
    own_tokens, own_cotangent = tokens[0], cotangent[0]

    route_rows, order_rows = routes[0].T, slot_order[0].T
    docs, placed, placed_t, normed1, w_all, strips = gather_call(
        own_tokens, norm1_gain, w_router.T, doc_ids, route_rows, order_rows, w_query, key_matrix,
        value_matrix, w_out, depth,
    )
    w_gate, w_up, w_down, docs = lax.optimization_barrier((w_gate, w_up, w_down, docs))
    gate_up = gather_z(
        jnp.concatenate(
            [
                lax.dynamic_index_in_dim(w_gate, head, 0, False),
                lax.dynamic_index_in_dim(w_up, head, 0, False),
            ],
            axis=1,
        )
    )
    down = gather_z(lax.dynamic_index_in_dim(w_down, head, 0, False))
    if parts > 1:

        def gather_far(value, axis):
            return lax.all_gather(value, "ctx", axis=axis, axis_index_groups=far, tiled=True)

        queries, keys_t, values_t, keys, values = project_call(normed1, w_all, cosine, sine)
        keys, values, docs = gather_far(keys, 0), gather_far(values, 0), gather_far(docs, 0)
        keys_t, values_t = gather_far(keys_t, 1), gather_far(values_t, 1)
        after = attend_call(
            attend_kernel, [w_all, queries, keys, values_t], docs, strips, own_tokens, norm2_gain,
            route_rows, placed, w_all, span, [],
        )
    else:
        queries, keys_t, values_t, keys, values, *after = attend_call(
            attend_after_project, [w_all, normed1, cosine, sine], docs, strips, own_tokens, norm2_gain,
            route_rows, placed, w_all, span, projected(span),
        )
    (
        attended_f32, log_total, attended, out_weight, weights_all, residual, normed2, gates,
        slot_gates, rows_out,
    ) = after
    out_weight = out_weight.reshape(width, width)
    sent_rows, sent_grads, gate, up, active, grad_w_down = dispatch_call(
        rows_out, gate_up, placed, own_cotangent, slot_gates
    )
    grad_w_down = reduce_z(grad_w_down)
    expert_out, grad_buffer, grad_w_gate_up = expert_call(
        active, down, sent_grads.reshape(GROUP * CAP, width), sent_rows.reshape(GROUP * CAP, width),
        gate, up, gate_up,
    )
    grad_w_gate_up = reduce_z(grad_w_gate_up)
    output, grad_residual, heads, attn, grad_router, grad_gain2 = combine_call(
        expert_out, grad_buffer.reshape(sent_rows.shape), out_weight,
        residual, normed2, gates, placed, placed_t, slot_gates, own_cotangent, norm2_gain, w_all,
    )
    dq, dk, dv, grad_out, down_w = backward_call(
        attn, attended, grad_w_down, heads, attended_f32, log_total, queries, keys, keys_t, values,
        docs,
    )
    if parts > 1:
        dk = lax.psum_scatter(dk, "ctx", scatter_dimension=1, axis_index_groups=far, tiled=True)
        dv = lax.psum_scatter(dv, "ctx", scatter_dimension=1, axis_index_groups=far, tiled=True)
    input_grad, shared, small, out_w, gate_up_w = finish_call(
        normed1, weights_all, grad_w_gate_up, grad_out, dq, dk, dv, cosine, sine,
        own_tokens, norm1_gain, grad_residual, grad_router, grad_gain2,
    )
    if parts > 1:
        shared, small, out_w = lax.psum((shared, small, out_w), "ctx", axis_index_groups=far)

    (
        q_w, k_w, v_w, out_w, router_w, gain1_w, gain2_w, gate_w, up_w, down_w, output, input_grad
    ) = output_call(shared, small, out_w, gate_up_w, down_w, output, input_grad, experts)
    return (
        output[None],
        input_grad[None],
        gain1_w,
        gain2_w,
        q_w,
        k_w,
        v_w,
        out_w.reshape(-1, width),
        router_w.T,
        gate_w,
        up_w,
        down_w,
    )


def solution(mesh):
    token_spec = P("fsdp", "ctx", None)
    row_spec, expert_spec = P("fsdp", None), P(None, "fsdp", None)
    tables = rotary_tables(mesh.shape["ctx"] * TOK_DEV)

    def program(*arguments):
        return jax.shard_map(
            functools.partial(shards, tuple(jnp.asarray(t) for t in tables)),
            mesh=mesh,
            in_specs=(
                token_spec,
                P("fsdp", "ctx"),
                token_spec,
                token_spec,
                P(),
                P(),
                row_spec,
                row_spec,
                row_spec,
                row_spec,
                row_spec,
                expert_spec,
                expert_spec,
                expert_spec,
                token_spec,
            ),
            out_specs=(
                token_spec,
                token_spec,
                P("fsdp"),
                P("fsdp"),
                row_spec,
                row_spec,
                row_spec,
                row_spec,
                row_spec,
                expert_spec,
                expert_spec,
                expert_spec,
            ),
            check_vma=False,
        )(*arguments)

    return program
```

```python
import functools

import jax
import jax.numpy as jnp
import numpy as np
from jax import lax
from jax.experimental import pallas as pl
from jax.experimental.pallas import tpu as pltpu
from jax.sharding import PartitionSpec as P

QUERY_HEADS = 24
KEY_VALUE_HEADS = 8
HEAD_DIM = 64
TOPK = 8
EXP_WIN = 8
TOK_DEV = 256
CAP = 64
GROUP = 8
HEADS = QUERY_HEADS // KEY_VALUE_HEADS
QW = HEADS * HEAD_DIM
HW = QW + 2 * HEAD_DIM
ROUTER = 48
ALL = HW + ROUTER

NEVER = 4096.0
epsilon = 1e-06
score_masked = -1e30
bf16 = jnp.bfloat16
f32 = jnp.float32
VMEM = pltpu.VMEM
MESH = pl.DeviceIdType.MESH
DMA = pltpu.SemaphoreType.DMA
IN_VMEM = pl.BlockSpec(memory_space=VMEM)
IN_ANY = pl.BlockSpec(memory_space=pl.ANY)


def dot(left, right, dims=((1,), (0,))):
    return lax.dot_general(left, right, (dims, ((), ())), preferred_element_type=f32)


def block(index, size=TOK_DEV):
    return pl.ds(pl.multiple_of(index * size, size), size)


def shape(dims, dtype):
    return jax.ShapeDtypeStruct(dims, dtype)


def params(collective_id=None, limit=56):
    return pltpu.CompilerParams(
        collective_id=collective_id,
        has_side_effects=collective_id is not None,
        vmem_limit_bytes=limit << 20,
    )


class Staged:
    def __init__(self, fetches, later, puts):
        self.fetches, self.later, self.puts, self.out = fetches, later, puts, []

    def begin(self):
        for copy in self.later:
            copy.start()
        self.later = []

    def need(self, *refs):
        for ref in refs:
            self.fetches.pop(id(ref)).wait()

    def put(self, *refs):
        for ref in refs:
            copy = self.puts.pop(id(ref))
            copy.start()
            self.out.append(copy)

    def finish(self):
        self.begin()
        for copy in self.fetches.values():
            copy.wait()
        for copy in self.puts.values():
            copy.start()
        for copy in self.out + list(self.puts.values()):
            copy.wait()


def staged_call(body, name, collective_id, ins, outs, scratch):
    held_in = [i for i, (how, _) in enumerate(ins) if how in "hl"]
    held_out = [i for i, (how, _) in enumerate(outs) if how == "h"]

    def kernel(*refs):
        refs = list(refs)
        given, refs = refs[: len(ins)], refs[len(ins) :]
        results, refs = refs[: len(outs)], refs[len(outs) :]
        own, refs = refs[: len(scratch)], refs[len(scratch) :]
        in_held, refs = refs[: len(held_in)], refs[len(held_in) :]
        out_held, (in_sems, out_sems) = refs[: len(held_out)], refs[len(held_out) :]
        fetches, later, puts = {}, [], {}
        for n, i in enumerate(held_in):
            copy = pltpu.make_async_copy(given[i], in_held[n], in_sems.at[n])
            if ins[i][0] == "l":
                later.append(copy)
            else:
                copy.start()
            given[i] = in_held[n]
            fetches[id(given[i])] = copy
        for n, i in enumerate(held_out):
            puts[id(out_held[n])] = pltpu.make_async_copy(out_held[n], results[i], out_sems.at[n])
            results[i] = out_held[n]
        stage = Staged(fetches, later, puts)
        body(stage, *given, *results, *own)
        stage.finish()

    return pl.pallas_call(
        kernel,
        out_shape=tuple(one for _, one in outs),
        in_specs=[IN_VMEM if how == "v" else IN_ANY for how, _ in ins],
        out_specs=tuple(IN_VMEM if how == "v" else IN_ANY for how, _ in outs),
        scratch_shapes=list(scratch)
        + [VMEM(ins[i][1].shape, ins[i][1].dtype) for i in held_in]
        + [VMEM(outs[i][1].shape, outs[i][1].dtype) for i in held_out]
        + [DMA((max(len(held_in), 1),)), DMA((max(len(held_out), 1),))],
        compiler_params=params(collective_id),
        name=name,
    )(*(array for _, array in ins))


def flip(index, bit):
    return index + (1 - 2 * ((index // bit) % 2)) * bit


class Place:
    def __init__(self):
        ctx = lax.axis_index("ctx")
        self.base = (ctx // GROUP) * GROUP
        self.me = ctx - self.base
        self.z = lax.axis_index("fsdp")
        self.depth = lax.axis_size("fsdp")
        self.near = [flip(self.me, bit) for bit in (1, 2, 4)]

    def ctx(self, index):
        return {"ctx": self.base + index}

    def fsdp(self, index):
        return {"fsdp": index}

    def others(self):
        return [self.ctx(lax.rem(self.me + j, GROUP)) for j in range(1, GROUP)]

    def layers(self):
        return [self.fsdp(lax.rem(self.z + j, self.depth)) for j in range(1, self.depth)]


def greet(devices):
    ready = pltpu.get_barrier_semaphore()
    for device in devices:
        pl.semaphore_signal(ready, inc=1, device_id=device, device_id_type=MESH)
    return lambda: pl.semaphore_wait(ready, len(devices))


def remote(source, target, send, receive, device):
    return pltpu.make_async_remote_copy(
        src_ref=source,
        dst_ref=target,
        send_sem=send,
        recv_sem=receive,
        device_id=device,
        device_id_type=MESH,
    )


def halves(count):
    cut = -(-count // 32) * 16

    def part(ref, half):
        return ref.at[pl.ds(0, cut)] if half == 0 else ref.at[pl.ds(cut, count - cut)]

    return part


class Spread:
    SEMS = 14

    def __init__(self, place, source, land, part, send, receive):
        me = place.me
        core, side, row = place.near
        across = flip(side, 4)

        def plan(slot, owner, half, device):
            target = part(land(owner), half)
            first = part(source, half) if slot < 6 else target
            return remote(first, target, send.at[slot], receive.at[slot], place.ctx(device))

        self.copies = [
            plan(0, me, 0, side), plan(1, me, 1, side), plan(2, me, 0, row), plan(3, me, 1, row),
            plan(4, me, 0, core), plan(5, me, 1, core), plan(6, side, 0, core),
            plan(7, side, 1, core), plan(8, row, 0, core), plan(9, row, 1, core),
            plan(10, side, 1, row), plan(11, row, 0, side), plan(12, across, 0, core),
            plan(13, across, 1, core),
        ]

    def go(self, *slots):
        for slot in slots:
            self.copies[slot].start()

    def wait(self, *slots):
        for slot in slots:
            self.copies[slot].wait_recv()

    def start(self):
        self.go(1, 2, 0, 3, 4, 5)

    def step1(self):
        self.wait(1)
        self.go(10, 7)
        self.wait(2)
        self.go(11, 8)

    def step2(self):
        self.wait(0)
        self.go(6)
        self.wait(3)
        self.go(9)

    def step3(self):
        self.wait(10)
        self.go(13)
        self.wait(11)
        self.go(12)

    def sent(self):
        for copy in self.copies:
            copy.wait_send()

    def last(self):
        self.wait(4, 5, 6, 7, 8, 9, 12, 13)


class Line:
    def __init__(self, place, land, send, receive):
        self.z, self.depth = place.z, place.depth
        z, most = self.z, place.depth - 1
        ways = ((jnp.minimum(z + 1, most), -1), (jnp.maximum(z - 1, 0), 1))
        self.copies = []
        for way, (device, sign) in enumerate(ways):
            self.copies.append([])
            for step in range(most):
                held = land(jnp.clip(z + sign * step, 0, most))
                self.copies[way].append(
                    remote(
                        held, held, send.at[way, step], receive.at[way, step], place.fsdp(device)
                    )
                )

    def each(self, step):
        z, most = self.z, self.depth - 1
        up, down = self.copies
        at = min(step, most - 1)
        return ((z + 1 <= most, z - step >= 0, up[at]), (z - 1 >= 0, z + step <= most, down[at]))

    def start(self):
        for open_way, _, copy in self.each(0):
            pl.when(open_way)(copy.start)

    def step(self, step):
        before = self.each(step - 1)
        for (open_way, here, copy), (_, _, came) in zip(self.each(step), before):
            pl.when(here)(came.wait_recv)
            if step < self.depth - 1:
                pl.when(jnp.logical_and(open_way, here))(copy.start)

    def last(self):
        self.step(self.depth - 1)

    def sent(self):
        for step in range(self.depth - 1):
            for open_way, here, copy in self.each(step):
                pl.when(jnp.logical_and(open_way, here))(copy.wait_send)


def place_slots(routes_ref, order_ref, placed_ref):
    rows = routes_ref.shape[1]
    expert = lax.broadcasted_iota(jnp.int32, (EXP_WIN, rows), 0)
    priority = jnp.full((EXP_WIN, rows), NEVER, f32)
    for k in range(TOPK):
        pick = expert == routes_ref[k : k + 1, :]
        priority = jnp.where(pick, order_ref[k : k + 1, :].astype(f32), priority)
    priority_turned = priority.T
    slot = lax.broadcasted_iota(jnp.int32, (CAP, rows), 0).astype(f32)
    for e in range(EXP_WIN):
        mine = priority[e : e + 1, :]
        before = jnp.where(priority_turned[:, e : e + 1] < mine, 1.0, 0.0)
        before = jnp.sum(before, axis=0, keepdims=True)
        placed = (slot == before) & (mine < NEVER)
        placed_ref[e] = jnp.where(placed, 1.0, 0.0).astype(bf16)


def gather_kernel(
    stage, tokens_ref, router_ref, docs_ref, routes_ref, order_ref, w_query_ref,
    key_matrix_ref, value_matrix_ref, w_out_ref, w_gate_ref, w_up_ref, w_down_ref,
    docs_all_ref, placed_ref, turned_ref, tokens_all_ref, w_all_ref, strips_ref, gate_up_ref, down_ref,
    held_ref, query_held, key_held, value_held,
    w_send, w_recv, o_send, o_recv, d_send, d_recv, c_send, c_recv, local,
):
    place = Place()
    me, z = place.me, place.z
    met = greet(place.others() + place.layers())
    odd = lax.rem(me, 2)
    pair = lax.div(me, 2)
    depth, strip, _ = strips_ref.shape

    def window(first, size):
        return pl.ds(pl.multiple_of(first * 128, 128), size)

    fetches = [
        pltpu.make_async_copy(
            w_query_ref.at[:, window(pair * 3 + odd, 2 * 128)], query_held, local.at[0]
        ),
        pltpu.make_async_copy(key_matrix_ref.at[:, window(pair, 128)], key_held, local.at[1]),
        pltpu.make_async_copy(value_matrix_ref.at[:, window(pair, 128)], value_held, local.at[2]),
        pltpu.make_async_copy(
            w_out_ref.at[pl.ds(pl.multiple_of(me * strip, strip), strip), :], strips_ref.at[z],
            local.at[3],
        ),
        pltpu.make_async_copy(tokens_ref, held_ref, local.at[4]),
    ]
    hidden = w_gate_ref.shape[2]
    shards = [
        pltpu.make_async_copy(w_gate_ref.at[me], gate_up_ref.at[:, pl.ds(0, hidden)], local.at[5]),
        pltpu.make_async_copy(w_up_ref.at[me], gate_up_ref.at[:, pl.ds(hidden, hidden)], local.at[6]),
        pltpu.make_async_copy(w_down_ref.at[me], down_ref, local.at[7]),
    ]
    for fetch in fetches:
        fetch.start()
    met()
    spread = Spread(
        place, tokens_ref, lambda owner: tokens_all_ref.at[owner], halves(TOK_DEV), c_send, c_recv
    )
    spread.start()
    lines = [
        Line(place, lambda layer: strips_ref.at[layer], o_send, o_recv),
        Line(place, lambda layer: w_all_ref.at[layer], w_send, w_recv),
    ]
    fetches[3].wait()
    lines[0].start()
    for fetch in fetches[:3] + fetches[4:]:
        fetch.wait()

    def half(held, columns):
        turned_rows = held[...].T
        return jnp.where(odd == 1, turned_rows[HEAD_DIM:], turned_rows[:columns])

    own = w_all_ref.at[z]
    own[:QW, :] = half(query_held, QW)
    own[QW : QW + HEAD_DIM, :] = half(key_held, HEAD_DIM)
    own[QW + HEAD_DIM : HW, :] = half(value_held, HEAD_DIM)
    router = router_ref[...].astype(f32)
    empty = jnp.zeros((ROUTER - router.shape[0], router.shape[1]), f32)
    own[HW:, :] = jnp.concatenate([router, empty], axis=0).astype(bf16)
    lines[1].start()
    for shard in shards:
        shard.start()
    docs_all_ref[me] = docs_ref[...]
    sent = []
    for j, device in enumerate(place.others()):
        sent.append(remote(docs_ref, docs_all_ref.at[me], d_send.at[j], d_recv.at[j], device))
    for copy in sent:
        copy.start()
    move = pltpu.make_async_copy(held_ref, tokens_all_ref.at[me], local.at[8])
    move.start()
    place_slots(routes_ref, order_ref, placed_ref)
    turned_ref[...] = placed_ref[...].reshape(EXP_WIN * CAP, -1).T
    stage.put(placed_ref, turned_ref)
    for shard in shards:
        shard.wait()
    stage.put(gate_up_ref, down_ref)
    steps = (spread.step1, spread.step2)
    for step in range(1, depth - 1):
        for act in steps[step - 1 : step]:
            act()
        for line in lines:
            line.step(step)
    for act in steps[depth - 2 :]:
        act()
    spread.step3()
    for line in lines:
        line.last()
    stage.put(w_all_ref, strips_ref)
    spread.last()
    for copy in sent:
        copy.wait()
    move.wait()
    for line in lines:
        line.sent()
    spread.sent()


def gather_call(
    tokens, router, docs, routes, order, w_query, key_matrix, value_matrix, w_out, w_gate, w_up, w_down,
    depth,
):
    rows, width = tokens.shape
    strip = w_out.shape[0] // GROUP
    size = w_query.shape[0]
    return staged_call(
        gather_kernel,
        "gather",
        1,
        [
            ("a", tokens),
            ("v", router),
            ("v", docs),
            ("v", routes),
            ("v", order),
            ("a", w_query),
            ("a", key_matrix),
            ("a", value_matrix),
            ("a", w_out),
            ("a", w_gate),
            ("a", w_up),
            ("a", w_down),
        ],
        [
            ("v", shape((GROUP,) + docs.shape, jnp.int32)),
            ("h", shape((EXP_WIN, CAP, rows), bf16)),
            ("h", shape((rows, EXP_WIN * CAP), bf16)),
            ("a", shape((GROUP, rows, width), bf16)),
            ("h", shape((depth, ALL, size), bf16)),
            ("h", shape((depth, strip, width), bf16)),
            ("h", shape((w_gate.shape[1], 2 * w_gate.shape[2]), bf16)),
            ("h", shape(w_down.shape[1:], bf16)),
        ],
        [
            VMEM((rows, width), bf16),
            VMEM((size, 2 * 128), bf16),
            VMEM((size, 128), bf16),
            VMEM((size, 128), bf16),
        ]
        + [DMA((2, depth - 1))] * 4
        + [DMA((GROUP - 1,))] * 2
        + [DMA((Spread.SEMS,))] * 2
        + [DMA((9,))],
    )


def turned(values, cosine, sine):
    half = HEAD_DIM // 2
    out = []
    for at in range(0, values.shape[0], HEAD_DIM):
        low, high = values[at : at + half], values[at + half : at + HEAD_DIM]
        out += [low * cosine - high * sine, high * cosine + low * sine]
    return jnp.concatenate(out, axis=0)


def project_block(
    owner, tokens_ref, gain_ref, w_all_ref, cos_ref, sin_ref,
    normed_ref, qt_ref, kt_ref, vt_ref, k_ref, v_ref,
):
    x = tokens_ref[owner].astype(f32)
    scale = lax.rsqrt(jnp.mean(x * x, axis=-1, keepdims=True) + epsilon)
    normed_ref[owner] = (x * scale * gain_ref[...].reshape(1, -1)).astype(bf16)
    linear = None
    for s in range(w_all_ref.shape[0]):
        size = w_all_ref.shape[2]
        term = dot(
            w_all_ref[s, :HW, :], normed_ref[owner, :, s * size : (s + 1) * size], ((1,), (1,))
        )
        linear = term if linear is None else linear + term
    tokens = block(owner)
    cosine, sine = cos_ref[:, tokens], sin_ref[:, tokens]
    queries = turned(linear[:QW], cosine, sine) * HEAD_DIM ** (-0.5)
    qt_ref[:, tokens] = queries.astype(bf16)
    keys = turned(linear[QW : QW + HEAD_DIM], cosine, sine)
    kt_ref[:, tokens] = keys.astype(bf16)
    k_ref[tokens, :] = keys.T.astype(bf16)
    values = linear[QW + HEAD_DIM :]
    vt_ref[:, tokens] = values.astype(bf16)
    v_ref[tokens, :] = values.T.astype(bf16)


def projected(tokens):
    span = tokens.shape[0] * tokens.shape[1]
    return [
        ("h", shape(tokens.shape, bf16)),
        ("h", shape((QW, span), bf16)),
        ("h", shape((HEAD_DIM, span), bf16)),
        ("h", shape((HEAD_DIM, span), bf16)),
        ("h", shape((span, HEAD_DIM), bf16)),
        ("h", shape((span, HEAD_DIM), bf16)),
    ]


def project_kernel(stage, tokens_ref, gain_ref, w_all_ref, cos_ref, sin_ref, *outs):
    stage.need(tokens_ref, w_all_ref, cos_ref, sin_ref)

    def project(i, _):
        project_block(i, tokens_ref, gain_ref, w_all_ref, cos_ref, sin_ref, *outs)
        return 0

    lax.fori_loop(0, GROUP, project, 0)


def project_call(tokens, gain, w_all, cosine, sine):
    return staged_call(
        project_kernel,
        "project",
        None,
        [("h", tokens), ("v", gain), ("h", w_all), ("h", cosine), ("h", sine)],
        projected(tokens),
        [],
    )


def docs_column(row):
    return jnp.broadcast_to(row.astype(f32), (8, row.shape[1])).T[:, :1]


def attend_after_project(
    n_blocks, stage, w_all_ref, tokens_ref, cos_ref, sin_ref, gain_ref, *rest,
):
    given, outs, rest = rest[:6], rest[6:12], rest[12:]
    _, qt_ref, _, vt_ref, k_ref, _ = outs

    def project_all():
        stage.need(tokens_ref, cos_ref, sin_ref)

        def project(i, _):
            project_block(i, tokens_ref, gain_ref, w_all_ref, cos_ref, sin_ref, *outs)
            return 0

        lax.fori_loop(0, GROUP, project, 0)
        stage.put(*outs)

    attend_body(n_blocks, stage, project_all, w_all_ref, qt_ref, k_ref, vt_ref, *given, *rest)


def attend_kernel(n_blocks, stage, w_all_ref, qt_ref, k_ref, vt_ref, *rest):
    def fetch_all():
        stage.need(qt_ref, k_ref, vt_ref)

    attend_body(n_blocks, stage, fetch_all, w_all_ref, qt_ref, k_ref, vt_ref, *rest)


def router_of(w_all_ref):
    return [w_all_ref[s, HW:, :] for s in range(w_all_ref.shape[0])]


def attend_body(
    n_blocks, stage, prepare, w_all_ref, qt_ref, k_ref, vt_ref,
    docs_ref, strips_ref, tokens_ref, gain_ref, routes_ref, placed_ref,
    o_ref, lse_ref, attended_ref, out_weight_ref, weights_ref, residual_ref, normed2_ref, gates_ref,
    slot_gates_ref, rows_ref,
    staged_ref, docs_col_ref, top_ref, sum_ref, acc_ref, mixed_ref,
    a_send, a_recv, s_send, s_recv, w_send, w_recv, local,
):
    T = TOK_DEV
    place = Place()
    me, z = place.me, place.z
    first = place.base
    met = greet(place.others())
    depth, strip, _ = strips_ref.shape
    move = pltpu.make_async_copy(w_all_ref.at[:, :HW], weights_ref.at[me], local.at[1])

    def layers(ref, h):
        return ref.at[pl.ds(h * (depth // 2), depth // 2)]

    weights = Spread(
        place, w_all_ref.at[:, :HW], lambda owner: weights_ref.at[owner], layers, w_send, w_recv
    )
    strips = Spread(
        place, strips_ref, lambda owner: out_weight_ref.at[:, owner], layers, s_send, s_recv
    )
    def turn(i, _):
        docs_col_ref[i] = docs_column(docs_ref[i])
        return 0

    lax.fori_loop(0, n_blocks, turn, 0)
    stage.need(strips_ref)
    stage.begin()
    met()
    strips.start()
    out_weight_ref[:, me] = strips_ref[...]
    stage.need(w_all_ref)
    move.start()
    prepare()
    weights.start()

    def tile(kb, qb, mask):
        kt = k_ref[block(kb), :]
        vt = vt_ref[:, block(kb)]
        heads = range(HEADS)
        parts = [slice(h * HEAD_DIM, (h + 1) * HEAD_DIM) for h in heads]
        s = [dot(kt, qt_ref[parts[h], block(qb)]) for h in heads]
        if mask is not None:
            s = [jnp.where(mask, x, score_masked) for x in s]
        old = [top_ref[h : h + 1, :] for h in heads]
        new = [jnp.maximum(old[h], jnp.max(s[h], axis=0, keepdims=True)) for h in heads]
        p = [jnp.exp(s[h] - new[h]) for h in heads]
        factor = [jnp.exp(old[h] - new[h]) for h in heads]
        total = [
            sum_ref[h : h + 1, :] * factor[h] + jnp.sum(p[h], axis=0, keepdims=True) for h in heads
        ]
        mixed = [acc_ref[parts[h], :] * factor[h] + dot(vt, p[h].astype(bf16)) for h in heads]
        for h in heads:
            top_ref[h : h + 1, :] = new[h]
            sum_ref[h : h + 1, :] = total[h]
            acc_ref[parts[h], :] = mixed[h]

    def same(kb, gq):
        return docs_col_ref[kb] == docs_ref[gq].astype(f32)

    def head_rows(head):
        per = GROUP * depth // GROUP
        return attended_ref.at[lax.div(head * depth, GROUP), pl.ds(lax.rem(head * depth, GROUP), per)]

    def attended_copy(to, slot):
        return remote(
            staged_ref.at[to], head_rows(slot), a_send.at[to], a_recv.at[slot], place.ctx(to)
        )

    def q_block(j, _):
        for at, act in ((1, strips.step1), (2, strips.step2), (5, strips.step3)):
            pl.when(j == at)(act)
        qb = GROUP - 1 - j
        gq = first + qb
        top_ref[...] = jnp.full_like(top_ref, score_masked)
        sum_ref[...] = jnp.ones_like(sum_ref)
        acc_ref[...] = jnp.zeros_like(acc_ref)
        last = gq == n_blocks - 1

        def k_block(kb, _):
            edge = jnp.logical_or(kb == 0, last)

            @pl.when(edge)
            def _():
                tile(kb, qb, same(kb, gq))

            @pl.when(jnp.logical_not(edge))
            def _():
                tile(kb, qb, None)

            return 0

        lax.fori_loop(0, gq, k_block, 0)
        keys = lax.broadcasted_iota(jnp.int32, (T, T), 0)
        queries = lax.broadcasted_iota(jnp.int32, (T, T), 1)
        tile(gq, qb, same(gq, gq) & (keys <= queries))
        lse_ref[qb] = top_ref[...] + jnp.log(sum_ref[...])
        for h in range(HEADS):
            part = slice(h * HEAD_DIM, (h + 1) * HEAD_DIM)
            acc_ref[part, :] = acc_ref[part, :] / sum_ref[h : h + 1, :]
        o_ref[:, block(qb)] = acc_ref[...]
        staged_ref[qb] = acc_ref[...].astype(bf16).reshape(depth, strip, T)

        @pl.when(qb != me)
        def _():
            attended_copy(qb, me).start()

        return 0

    lax.fori_loop(0, GROUP, q_block, 0)
    stage.put(o_ref, lse_ref)
    own = pltpu.make_async_copy(staged_ref.at[me], head_rows(me), local.at[2])
    own.start()
    own.wait()
    weights.step1()
    weights.step2()
    for j in range(1, GROUP):
        other = lax.rem(me + j, GROUP)
        attended_copy(other, other).wait()
    stage.put(attended_ref)
    strips.last()
    stage.put(out_weight_ref)

    rows, width = tokens_ref.shape
    stage.need(tokens_ref, placed_ref)
    mixed_ref[...] = attended_ref[...].reshape(width, rows).T

    def out_columns(i, _):
        columns = block(i)
        weight = out_weight_ref[:, :, :, columns].reshape(width, T)
        residual_ref[:, columns] = tokens_ref[:, columns].astype(f32) + dot(mixed_ref[...], weight)
        return 0

    lax.fori_loop(0, width // T, out_columns, 0)
    residual = residual_ref[...]
    scale = lax.rsqrt(jnp.mean(residual * residual, axis=-1, keepdims=True) + epsilon)
    normed2_ref[...] = (residual * scale * gain_ref[...].reshape(1, -1)).astype(bf16)
    stage.put(residual_ref, normed2_ref)
    logits = None
    for s, router in enumerate(router_of(w_all_ref)):
        size = router.shape[1]
        term = dot(router, normed2_ref[:, s * size : (s + 1) * size], ((1,), (1,)))
        logits = term if logits is None else logits + term
    expert = lax.broadcasted_iota(jnp.int32, gates_ref.shape, 0)
    chosen = expert < 0
    for k in range(TOPK):
        chosen = chosen | (expert == routes_ref[k : k + 1, :])
    logits = jnp.where(chosen, logits, score_masked)
    top = jnp.max(logits, axis=0, keepdims=True)
    gates = jnp.where(chosen, jnp.exp(logits - top), 0.0)
    gates = gates / jnp.sum(gates, axis=0, keepdims=True)
    gates_ref[...] = gates
    for e in range(EXP_WIN):
        slot_gates_ref[e] = jnp.sum(
            placed_ref[e].astype(f32) * gates[e : e + 1, :], axis=1, keepdims=True
        )

    def pick_rows(e, _):
        rows_ref[e] = dot(placed_ref[e], normed2_ref[...]).astype(bf16)
        return 0

    lax.fori_loop(0, EXP_WIN, pick_rows, 0)
    stage.put(gates_ref, slot_gates_ref, rows_ref)
    weights.step3()
    weights.last()
    weights.sent()
    strips.sent()
    move.wait()


def attend_call(
    kernel, ins, gains, docs, strips, tokens, gain, routes, placed, w_all, span, projections
):
    n = docs.shape[0]
    rows, width = tokens.shape
    depth, _, size = w_all.shape
    strip = strips.shape[1]
    return staged_call(
        functools.partial(kernel, n),
        "attend",
        2,
        [("l", one) for one in ins]
        + [("v", one) for one in gains]
        + [("v", docs), ("h", strips), ("l", tokens), ("v", gain), ("v", routes), ("l", placed)],
        projections
        + [
            ("h", shape((QW, span), f32)),
            ("h", shape((GROUP, 8, TOK_DEV), f32)),
            ("h", shape((depth, GROUP, strip, TOK_DEV), bf16)),
            ("h", shape((depth, GROUP) + strips.shape[1:], bf16)),
            ("a", shape((GROUP, depth, HW, size), bf16)),
            ("h", shape((rows, width), f32)),
            ("h", shape((rows, width), bf16)),
            ("h", shape((ROUTER, rows), f32)),
            ("h", shape((EXP_WIN, CAP, 1), f32)),
            ("h", shape((EXP_WIN, CAP, width), bf16)),
        ],
        [
            VMEM((GROUP, depth, strip, TOK_DEV), bf16),
            VMEM((n, TOK_DEV, 1), f32),
            VMEM((8, TOK_DEV), f32),
            VMEM((8, TOK_DEV), f32),
            VMEM((QW, TOK_DEV), f32),
            VMEM((rows, width), bf16),
        ]
        + [DMA((GROUP,))] * 2
        + [DMA((Spread.SEMS,))] * 4
        + [DMA((3,))],
    )


def dispatch_kernel(
    stage, sent_rows_ref, gate_up_ref, placed_ref, cotangent_ref, slot_gates_ref,
    rows_ref, grads_ref, gate_ref, up_ref, active_ref, grad_down_ref,
    gate_up_held, own_grads, r_send, r_recv, g_send, g_recv, local,
):
    place = Place()
    me = place.me
    met = greet(place.others())
    width = cotangent_ref.shape[1]

    def copy(source, target, send, receive, j):
        to = lax.rem(me + j, GROUP)
        return remote(source.at[to], target.at[me], send.at[j], receive.at[j], place.ctx(to))

    met()
    for j in range(1, GROUP):
        copy(sent_rows_ref, rows_ref, r_send, r_recv, j).start()
    own = pltpu.make_async_copy(sent_rows_ref.at[me], rows_ref.at[me], local.at[0])
    own.start()
    fetch = pltpu.make_async_copy(gate_up_ref, gate_up_held, local.at[1])
    fetch.start()
    stage.need(placed_ref, cotangent_ref, slot_gates_ref)

    def send_grads(n, _):
        j = GROUP - n
        to = lax.rem(me + j, GROUP)
        routed = dot(placed_ref[to], cotangent_ref[...])
        own_grads[to] = (routed * slot_gates_ref[to]).astype(bf16)

        @pl.when(j > 0)
        def _():
            copy(own_grads, grads_ref, g_send, g_recv, j).start()

        return 0

    lax.fori_loop(1, GROUP + 1, send_grads, 0)
    grads_ref[me] = own_grads[me]
    fetch.wait()
    own.wait()
    for j in range(1, GROUP):
        copy(sent_rows_ref, rows_ref, r_send, r_recv, j).wait_recv()
    stage.put(rows_ref)
    slots = GROUP * CAP
    hidden = gate_ref.shape[1]
    tiles = hidden // TOK_DEV

    def expert_up(i, _):
        came = rows_ref[...].reshape(slots, width)
        gate = dot(came, gate_up_held[:, block(i)])
        up = dot(came, gate_up_held[:, block(tiles + i)])
        gate_ref[:, block(i)] = gate
        up_ref[:, block(i)] = up
        active_ref[:, block(i)] = (gate * jax.nn.sigmoid(gate) * up).astype(bf16)
        return 0

    lax.fori_loop(0, tiles, expert_up, 0)
    stage.put(gate_ref, up_ref, active_ref)
    for j in range(1, GROUP):
        copy(own_grads, grads_ref, g_send, g_recv, j).wait_recv()
    stage.put(grads_ref)

    def expert_over(i, _):
        grad_down_ref[:, block(i)] = dot(
            active_ref[...], grads_ref[:, :, block(i)].reshape(slots, TOK_DEV), ((0,), (0,))
        ).astype(bf16)
        return 0

    lax.fori_loop(0, width // TOK_DEV, expert_over, 0)
    stage.put(grad_down_ref)
    for j in range(1, GROUP):
        copy(sent_rows_ref, rows_ref, r_send, r_recv, j).wait_send()
        copy(own_grads, grads_ref, g_send, g_recv, j).wait_send()


def dispatch_call(sent_rows, gate_up, placed, cotangent, slot_gates):
    slots = sent_rows.shape
    count, width = GROUP * CAP, slots[2]
    hidden = gate_up.shape[1] // 2
    return staged_call(
        dispatch_kernel,
        "dispatch",
        3,
        [
            ("a", sent_rows),
            ("a", gate_up),
            ("h", placed),
            ("h", cotangent),
            ("h", slot_gates),
        ],
        [
            ("h", shape(slots, bf16)),
            ("h", shape(slots, bf16)),
            ("h", shape((count, hidden), f32)),
            ("h", shape((count, hidden), f32)),
            ("h", shape((count, hidden), bf16)),
            ("h", shape((hidden, width), bf16)),
        ],
        [VMEM(gate_up.shape, bf16), VMEM(slots, bf16)] + [DMA((GROUP,))] * 4 + [DMA((2,))],
    )


def expert_kernel(
    stage, active_ref, down_ref, grads_ref, rows_ref, gate_ref, up_ref, gate_up_ref,
    out_ref, back_ref, grad_gate_up_ref,
    grads_held, rows_held, gate_up_held, own_ref, grad_ref, send, receive, local,
):
    place = Place()
    me = place.me
    met = greet(place.others())
    fetches = [
        pltpu.make_async_copy(grads_ref, grads_held, local.at[0]),
        pltpu.make_async_copy(rows_ref, rows_held, local.at[1]),
        pltpu.make_async_copy(gate_up_ref, gate_up_held, local.at[2]),
    ]
    count, hidden = active_ref.shape
    width = down_ref.shape[1]
    T = TOK_DEV
    tiles = hidden // T

    def copy(j, half):
        to = lax.rem(me + j, GROUP)
        columns = pl.ds(half * (width // 2), width // 2)
        return remote(
            own_ref.at[to, :, columns], out_ref.at[me, :, columns], send.at[half, j],
            receive.at[half, j], place.ctx(to),
        )

    stage.need(active_ref, down_ref)
    for fetch in fetches:
        fetch.start()
    stage.begin()

    def out(i, _):
        value = dot(active_ref[...], down_ref[:, block(i)]).astype(bf16)
        own_ref[:, :, block(i)] = value.reshape(GROUP, CAP, T)
        return 0

    for half in range(2):
        tiles_half = width // T // 2
        lax.fori_loop(half * tiles_half, (half + 1) * tiles_half, out, 0)
        if half == 0:
            met()
        for j in range(1, GROUP):
            copy(j, half).start()
    move = pltpu.make_async_copy(own_ref.at[me], out_ref.at[me], local.at[3])
    move.start()
    fetches[0].wait()
    stage.need(gate_ref, up_ref)

    def back(i, _):
        grad = dot(grads_held[...], down_ref[block(i), :], ((1,), (1,)))
        gate, up = gate_ref[:, block(i)], up_ref[:, block(i)]
        sigmoid = jax.nn.sigmoid(gate)
        grad_gate = grad * up * sigmoid * (1.0 + gate * (1.0 - sigmoid))
        grad_ref[:, block(i)] = grad_gate.astype(bf16)
        grad_ref[:, block(tiles + i)] = (grad * gate * sigmoid).astype(bf16)
        return 0

    lax.fori_loop(0, tiles, back, 0)
    fetches[1].wait()
    fetches[2].wait()

    def over(i, _):
        grad_gate_up_ref[block(i), :] = dot(
            rows_held[:, block(i)], grad_ref[...], ((0,), (0,))
        ).astype(bf16)
        back_ref[:, block(i)] = dot(
            grad_ref[...], gate_up_held[block(i), :], ((1,), (1,))
        ).astype(bf16)
        return 0

    lax.fori_loop(0, width // T, over, 0)
    stage.put(back_ref, grad_gate_up_ref)
    for half in range(2):
        for j in range(1, GROUP):
            copy(j, half).wait()
    move.wait()


def expert_call(active, down, grads, rows, gate, up, gate_up):
    count, width = rows.shape
    hidden = down.shape[0]
    slots = (GROUP, CAP, width)
    return staged_call(
        expert_kernel,
        "expert",
        7,
        [
            ("h", active),
            ("h", down),
            ("a", grads),
            ("a", rows),
            ("l", gate),
            ("l", up),
            ("a", gate_up),
        ],
        [
            ("a", shape(slots, bf16)),
            ("h", shape((count, width), bf16)),
            ("h", shape((width, 2 * hidden), bf16)),
        ],
        [
            VMEM(grads.shape, bf16),
            VMEM(rows.shape, bf16),
            VMEM(gate_up.shape, bf16),
            VMEM(slots, bf16),
            VMEM((count, 2 * hidden), bf16),
            DMA((2, GROUP)),
            DMA((2, GROUP)),
            DMA((4,)),
        ],
    )


def combine_kernel(
    stage, out_ref, sent_grad_ref, weight_ref, residual_ref, normed_ref, gates_ref, placed_ref,
    placed_t_ref, slot_gates_ref, cotangent_ref, gain_ref, w_all_ref,
    output_ref, grad_residual_ref, heads_ref, attn_ref, grad_router_ref, grad_gain_ref,
    back_ref, weight_held, sum_ref, turned_ref, staged_ref, scaled_ref,
    b_send, b_recv, h_send, h_recv, local,
):
    place = Place()
    me = place.me
    met = greet(place.others())
    fetch = pltpu.make_async_copy(weight_ref, weight_held, local.at[0])
    rows, width = residual_ref.shape

    def copy(source, target, send, receive, j):
        to = lax.rem(me + j, GROUP)
        return remote(source.at[to], target.at[me], send.at[j], receive.at[j], place.ctx(to))

    backs = [copy(sent_grad_ref, back_ref, b_send, b_recv, j) for j in range(1, GROUP)]
    met()
    for one in backs:
        one.start()
    move = pltpu.make_async_copy(sent_grad_ref.at[me], back_ref.at[me], local.at[1])
    move.start()
    turned_ref[...] = jnp.zeros_like(turned_ref)
    stage.need(out_ref, placed_ref, slot_gates_ref, cotangent_ref)
    stage.begin()
    fetch.start()

    def add_expert(e, _):
        came = out_ref[e].astype(f32)
        scaled_ref[e] = (came * slot_gates_ref[e]).astype(bf16)
        routed = dot(placed_ref[e], cotangent_ref[...])
        slot_grad = jnp.sum(routed * came, axis=1, keepdims=True)
        turned_ref[pl.ds(e, 1), :] = jnp.sum(
            placed_ref[e].astype(f32) * slot_grad, axis=0, keepdims=True
        )
        return 0

    lax.fori_loop(0, EXP_WIN, add_expert, 0)
    stage.need(placed_t_ref, residual_ref, gates_ref, w_all_ref, normed_ref)
    slots = EXP_WIN * CAP

    def mix(i, _):
        columns = block(i)
        mixed = dot(placed_t_ref[...], scaled_ref[:, :, columns].reshape(slots, TOK_DEV))
        output_ref[:, columns] = (residual_ref[:, columns] + mixed).astype(bf16)
        return 0

    lax.fori_loop(0, width // TOK_DEV, mix, 0)
    stage.put(output_ref)
    gates = gates_ref[...]
    grad_gates = turned_ref[...]
    weighted = jnp.sum(gates * grad_gates, axis=0, keepdims=True)
    grad_logits = (gates * (grad_gates - weighted)).astype(bf16)
    for s, router in enumerate(router_of(w_all_ref)):
        size = router.shape[1]
        sum_ref[:, s * size : (s + 1) * size] = dot(grad_logits, router, ((0,), (0,)))
    grad_router_ref[...] = dot(grad_logits, normed_ref[...])
    fetch.wait()
    move.wait()
    for one in backs:
        one.wait_recv()

    def add_back(i, _):
        columns = block(i)
        sum_ref[:, columns] += dot(
            placed_t_ref[...], back_ref[:, :, columns].reshape(slots, TOK_DEV)
        )
        return 0

    lax.fori_loop(0, width // TOK_DEV, add_back, 0)
    residual = residual_ref[...]
    grad_normed = sum_ref[...]
    scale = lax.rsqrt(jnp.mean(residual * residual, axis=-1, keepdims=True) + epsilon)
    scaled = grad_normed * gain_ref[...].reshape(1, -1)
    inner = jnp.mean(scaled * residual, axis=-1, keepdims=True)
    grad = scale * scaled - residual * (scale * scale * scale * inner)
    grad_gain_ref[...] = jnp.sum(grad_normed * residual * scale, axis=0, keepdims=True)
    grad_residual = cotangent_ref[...].astype(f32) + grad
    grad_residual_ref[...] = grad_residual
    attn_ref[...] = grad_residual.astype(bf16)
    stage.put(grad_residual_ref, attn_ref, grad_router_ref, grad_gain_ref)

    def head_rows(j, _):
        to = lax.rem(me + j, GROUP)
        staged_ref[to] = dot(weight_held[block(to, QW), :], attn_ref[...], ((1,), (1,))).astype(bf16)

        @pl.when(j < GROUP)
        def _():
            copy(staged_ref, heads_ref, h_send, h_recv, j).start()

        return 0

    lax.fori_loop(1, GROUP + 1, head_rows, 0)
    move = pltpu.make_async_copy(staged_ref.at[me], heads_ref.at[me], local.at[2])
    move.start()
    for one in backs:
        one.wait_send()
    for j in range(1, GROUP):
        copy(staged_ref, heads_ref, h_send, h_recv, j).wait()
    move.wait()


def combine_call(
    out, sent_grad, weight, residual, normed, gates, placed, placed_t, slot_gates, cotangent,
    gain, w_all,
):
    rows, width = residual.shape
    slots = (GROUP, CAP, width)
    return staged_call(
        combine_kernel,
        "combine",
        4,
        [
            ("h", out),
            ("a", sent_grad),
            ("a", weight),
            ("l", residual),
            ("l", normed),
            ("l", gates),
            ("h", placed),
            ("l", placed_t),
            ("h", slot_gates),
            ("h", cotangent),
            ("v", gain),
            ("l", w_all),
        ],
        [
            ("h", shape((rows, width), bf16)),
            ("h", shape((rows, width), f32)),
            ("a", shape((GROUP, QW, rows), bf16)),
            ("h", shape((rows, width), bf16)),
            ("h", shape((ROUTER, width), f32)),
            ("h", shape((1, width), f32)),
        ],
        [
            VMEM(slots, bf16),
            VMEM(weight.shape, bf16),
            VMEM((rows, width), f32),
            VMEM((ROUTER, rows), f32),
            VMEM((GROUP, QW, rows), bf16),
            VMEM(slots, bf16),
        ]
        + [DMA((GROUP,))] * 4
        + [DMA((3,))],
    )


def backward_kernel(
    n_blocks, stage, attn_ref, attended_ref, down_ref, heads_ref, o_ref, lse_ref, qt_ref, k_ref,
    kt_ref, v_ref, docs_ref,
    dq_ref, dk_ref, dv_ref, grad_out_ref, down_all_ref,
    part_ref, pair_ref, strip_ref, came_ref, docs_col_ref, delta_ref, dk_acc, dv_acc,
    p_send, p_recv, s_send, s_recv, e_send, e_recv, local,
):
    T = TOK_DEV
    place = Place()
    me = place.me
    first = place.base
    core, side, row = place.near
    across = flip(side, 4)
    met = greet([place.ctx(i) for i in (core, side, row, across)])
    half = GROUP // 2
    depth, strip, width = grad_out_ref.shape
    parity = lax.rem(me, 2)

    def strip_of(n, parity):
        return 2 * n + parity

    def part(n, parity):
        rows = attended_ref[:, strip_of(n, parity)].reshape(depth * strip, T)
        return dot(rows, attn_ref[...])

    def pair_copy(n):
        return remote(
            part_ref.at[n], pair_ref.at[n], p_send.at[n], p_recv.at[n], place.ctx(core)
        )

    def pair_part(n, _):
        part_ref[n] = part(n, 1 - parity).astype(bf16)
        pair_copy(n).start()
        return 0

    down_move = pltpu.make_async_copy(down_ref, down_all_ref.at[me], local.at[0])
    down_spread = Spread(
        place, down_ref, lambda owner: down_all_ref.at[owner], halves(down_ref.shape[0]), e_send, e_recv
    )
    stage.need(attn_ref, attended_ref)
    stage.begin()
    met()
    lax.fori_loop(0, half, pair_part, 0)
    stage.need(down_ref)
    down_spread.start()
    down_move.start()

    heads = range(HEADS)
    parts = [slice(h * HEAD_DIM, (h + 1) * HEAD_DIM) for h in heads]
    stage.need(heads_ref, o_ref)

    def prepare(i, _):
        for h in heads:
            product = o_ref[parts[h], block(i)] * heads_ref[i, parts[h], :].astype(f32)
            delta_ref[i, h : h + 1, :] = jnp.sum(product, axis=0, keepdims=True)
        return 0

    lax.fori_loop(0, GROUP, prepare, 0)
    for n in range(half):
        pair_copy(n).wait_recv()

    def add_pair(n, _):
        strip_ref[n] = (part(n, parity) + pair_ref[n].astype(f32)).astype(bf16)
        return 0

    lax.fori_loop(0, half, add_pair, 0)
    strips = [
        remote(
            strip_ref.at[lax.div(device, 2)], came_ref.at[n], s_send.at[n], s_recv.at[n],
            place.ctx(device),
        )
        for n, device in enumerate((across, side, row))
    ]
    for copy in strips:
        copy.start()

    def turn(i, _):
        docs_col_ref[i] = docs_column(docs_ref[i])
        return 0

    lax.fori_loop(0, n_blocks, turn, 0)
    stage.need(lse_ref, qt_ref, k_ref, kt_ref, v_ref)
    dq_ref[...] = jnp.zeros_like(dq_ref)

    def tile(kb, qb, mask):
        k = k_ref[block(kb), :]
        v = v_ref[block(kb), :]
        kt = kt_ref[:, block(kb)]
        q = [qt_ref[part, block(qb)] for part in parts]
        do = [heads_ref[qb, part, :] for part in parts]
        s = [dot(k, x) for x in q]
        dp = [dot(v, x) for x in do]
        p = [jnp.exp(s[h] - lse_ref[qb, h : h + 1, :]) for h in heads]
        if mask is not None:
            p = [jnp.where(mask, x, 0.0) for x in p]
        ds = [(p[h] * (dp[h] - delta_ref[qb, h : h + 1, :])).astype(bf16) for h in heads]
        pb = [x.astype(bf16) for x in p]
        turn = ((1,), (1,))
        dv_acc[...] += dot(pb[0], do[0], turn) + dot(pb[1], do[1], turn) + dot(pb[2], do[2], turn)
        dk_acc[...] += dot(ds[0], q[0], turn) + dot(ds[1], q[1], turn) + dot(ds[2], q[2], turn)
        for h in heads:
            dq_ref[parts[h], block(qb)] += dot(kt, ds[h])

    def same(kb, gq):
        return docs_col_ref[kb] == docs_ref[gq].astype(f32)

    def k_block(kb, _):
        for at, act in (
            (2, down_spread.step1), (4, down_spread.step2), (7, down_spread.step3),
        ):
            pl.when(kb == first + at)(act)
        dk_acc[...] = jnp.zeros_like(dk_acc)
        dv_acc[...] = jnp.zeros_like(dv_acc)

        @pl.when(kb >= first)
        def _():
            keys = lax.broadcasted_iota(jnp.int32, (T, T), 0)
            queries = lax.broadcasted_iota(jnp.int32, (T, T), 1)
            tile(kb, kb - first, same(kb, kb) & (keys <= queries))

        def q_block(qb, _):
            gq = first + qb
            edge = jnp.logical_or(kb == 0, gq == n_blocks - 1)

            @pl.when(edge)
            def _():
                tile(kb, qb, same(kb, gq))

            @pl.when(jnp.logical_not(edge))
            def _():
                tile(kb, qb, None)

            return 0

        lax.fori_loop(jnp.maximum(kb - first + 1, 0), GROUP, q_block, 0)
        dk_ref[:, block(kb)] = dk_acc[...].T
        dv_ref[:, block(kb)] = dv_acc[...].T
        return 0

    lax.fori_loop(0, first + GROUP, k_block, 0)

    def clear(kb, _):
        dk_ref[:, block(kb)] = jnp.zeros((HEAD_DIM, T), f32)
        dv_ref[:, block(kb)] = jnp.zeros((HEAD_DIM, T), f32)
        return 0

    lax.fori_loop(first + GROUP, n_blocks, clear, 0)
    stage.put(dq_ref, dk_ref, dv_ref)
    for copy in strips:
        copy.wait_recv()
    total = strip_ref[lax.div(me, 2)].astype(f32)
    for n in range(len(strips)):
        total = total + came_ref[n].astype(f32)
    grad_out_ref[...] = total.astype(bf16).reshape(depth, strip, width)
    stage.put(grad_out_ref)
    down_spread.last()
    down_spread.sent()
    for n in range(half):
        pair_copy(n).wait_send()
    for copy in strips:
        copy.wait_send()
    down_move.wait()


def backward_call(attn, attended, down, heads, o, lse, qt, k, kt, v, docs):
    n = k.shape[0] // TOK_DEV
    span = qt.shape[1]
    rows, width = attn.shape
    depth, _, strip, _ = attended.shape
    block_rows = depth * strip
    half = GROUP // 2
    return staged_call(
        functools.partial(backward_kernel, n),
        "backward",
        5,
        [("h", attn), ("h", attended)]
        + [("l", one) for one in (down, heads, o, lse, qt, k, kt, v)]
        + [("v", docs)],
        [
            ("h", shape((QW, span), f32)),
            ("h", shape(kt.shape, f32)),
            ("h", shape(kt.shape, f32)),
            ("h", shape((depth, strip, width), bf16)),
            ("a", shape((GROUP,) + down.shape, bf16)),
        ],
        [
            VMEM((half, block_rows, width), bf16),
            VMEM((half, block_rows, width), bf16),
            VMEM((half, block_rows, width), bf16),
            VMEM((3, block_rows, width), bf16),
            VMEM((n, TOK_DEV, 1), f32),
            VMEM((GROUP, 8, TOK_DEV), f32),
            VMEM((TOK_DEV, HEAD_DIM), f32),
            VMEM((TOK_DEV, HEAD_DIM), f32),
        ]
        + [DMA((half,))] * 2
        + [DMA((3,))] * 2
        + [DMA((Spread.SEMS,))] * 2
        + [DMA((1,))],
    )


def finish_kernel(
    stage, normed_ref, weights_ref, gate_up_ref, grad_out_ref, dq_ref, dk_ref, dv_ref, cos_ref,
    sin_ref, tokens_ref, gain_ref, grad_residual_ref, grad_router_ref, grad_gain2_ref,
    input_grad_ref, shared_ref, small_all_ref, out_all_ref, gate_up_all_ref,
    normed_held, weights_held, linear_ref, came_ref, came_t, sum_ref, part_ref,
    small_ref, head_in, small_in, out_in, shard_ref, small_shard_ref, out_shard_ref,
    g_send, g_recv, h_send, h_recv, s_send, s_recv, o_send, o_recv, e_send, e_recv, f_send, f_recv,
    m_send, m_recv, c_send, c_recv, local,
):
    place = Place()
    me, z, depth = place.me, place.z, place.depth
    met = greet(place.others() + place.layers())
    fetches = [
        pltpu.make_async_copy(normed_ref, normed_held, local.at[0]),
        pltpu.make_async_copy(weights_ref, weights_held, local.at[1]),
    ]
    rows, width = tokens_ref.shape
    size = width // depth

    def spread_of(source, out, send, receive):
        return Spread(
            place, source, lambda owner: out.at[owner], halves(source.shape[0]), send, receive
        )

    expert_spread = spread_of(gate_up_ref, gate_up_all_ref, e_send, e_recv)
    head_spread = spread_of(shard_ref, shared_ref, f_send, f_recv)
    small_spread = spread_of(small_shard_ref, small_all_ref, m_send, m_recv)
    out_spread = spread_of(out_shard_ref, out_all_ref, c_send, c_recv)
    moves = [
        pltpu.make_async_copy(gate_up_ref, gate_up_all_ref.at[me], local.at[3]),
        pltpu.make_async_copy(out_shard_ref, out_all_ref.at[me], local.at[4]),
        pltpu.make_async_copy(shard_ref, shared_ref.at[me], local.at[5]),
        pltpu.make_async_copy(small_shard_ref, small_all_ref.at[me], local.at[6]),
    ]

    def copy(j):
        to = lax.rem(me + j, GROUP)
        return remote(
            linear_ref.at[to], came_ref.at[me], g_send.at[j], g_recv.at[j], place.ctx(to)
        )

    def down(source, target, send, receive, j):
        to = lax.rem(z + j, depth)
        return remote(source.at[to], target.at[z], send.at[j], receive.at[j], place.fsdp(to))

    stage.need(dq_ref, dk_ref, dv_ref, cos_ref, sin_ref)
    stage.begin()
    for fetch in fetches:
        fetch.start()

    def turn_back(j, _):
        to = lax.rem(me + j, GROUP)
        cosine, sine = cos_ref[:, block(to)], -sin_ref[:, block(to)]
        dq = turned(dq_ref[:, block(to)], cosine, sine) * HEAD_DIM ** (-0.5)
        dk = turned(dk_ref[:, block(to)], cosine, sine)
        linear_ref[to, :QW, :] = dq.astype(bf16)
        linear_ref[to, QW : QW + HEAD_DIM, :] = dk.astype(bf16)
        linear_ref[to, QW + HEAD_DIM :, :] = dv_ref[:, block(to)].astype(bf16)
        pl.when(j == 1)(met)

        @pl.when(j < GROUP)
        def _():
            copy(j).start()

        return 0

    lax.fori_loop(1, GROUP + 1, turn_back, 0)
    stage.need(gate_up_ref, grad_out_ref)
    moves[0].start()
    outs = [down(grad_out_ref, out_in, o_send, o_recv, j) for j in range(1, depth)]
    for one in outs:
        one.start()
    out_in[z] = grad_out_ref[z]
    came_ref[me] = linear_ref[me]
    fetches[0].wait()

    def own_weights(j, _):
        to = lax.rem(z + j, depth)
        columns = block(to, size)
        total = None
        for b in range(GROUP):
            term = dot(linear_ref[b], normed_held[b, :, columns])
            total = term if total is None else total + term
        part_ref[to] = total.astype(bf16)

        @pl.when(j < depth)
        def _():
            down(part_ref, head_in, h_send, h_recv, j).start()

        return 0

    lax.fori_loop(1, depth + 1, own_weights, 0)

    def total(ref):
        value = ref[0].astype(f32)
        for s in range(1, depth):
            value = value + ref[s].astype(f32)
        return value.astype(bf16)

    for j in range(1, GROUP):
        copy(j).wait_send()
    expert_spread.start()
    for one in outs:
        one.wait_recv()
    out_shard_ref[...] = total(out_in)
    out_spread.start()
    moves[1].start()
    fetches[1].wait()
    for j in range(1, GROUP):
        copy(j).wait_recv()

    def turn(j, _):
        came_t[j] = came_ref[j].T
        return 0

    lax.fori_loop(0, GROUP, turn, 0)

    def add_heads(s, _):
        total = None
        for j in range(GROUP):
            term = dot(came_t[j], weights_held[j, s])
            total = term if total is None else total + term
        sum_ref[:, block(s, size)] = total
        return 0

    lax.fori_loop(0, depth, add_heads, 0)
    out_spread.step1()
    stage.need(tokens_ref, grad_residual_ref, grad_router_ref, grad_gain2_ref)
    x = tokens_ref[...].astype(f32)
    grad_normed = sum_ref[...]
    scale = lax.rsqrt(jnp.mean(x * x, axis=-1, keepdims=True) + epsilon)
    scaled = grad_normed * gain_ref[...].reshape(1, -1)
    inner = jnp.mean(scaled * x, axis=-1, keepdims=True)
    grad = scale * scaled - x * (scale * scale * scale * inner)
    input_grad_ref[...] = grad_residual_ref[...] + grad
    stage.put(input_grad_ref)
    gain1 = jnp.sum(grad_normed * x * scale, axis=0, keepdims=True)
    row = lax.broadcasted_iota(jnp.int32, (ROUTER, width), 0)
    small = jnp.where(row == ROUTER - 2, gain1, grad_router_ref[...])
    small = jnp.where(row == ROUTER - 1, grad_gain2_ref[...], small).astype(bf16)
    for s in range(depth):
        small_ref[s] = small[:, s * size : (s + 1) * size]
    smalls = [down(small_ref, small_in, s_send, s_recv, j) for j in range(1, depth)]
    heads = [down(part_ref, head_in, h_send, h_recv, j) for j in range(1, depth)]
    for one in smalls:
        one.start()
    expert_spread.step1()
    head_in[z] = part_ref[z]
    small_in[z] = small_ref[z]

    for one in heads:
        one.wait_recv()
    shard_ref[...] = total(head_in)
    head_spread.start()
    out_spread.step2()
    expert_spread.step2()
    for one in smalls:
        one.wait_recv()
    small_shard_ref[...] = total(small_in)
    small_spread.start()
    moves[2].start()
    moves[3].start()
    out_spread.step3()
    expert_spread.step3()
    spreads = (head_spread, small_spread)
    for spread in spreads:
        spread.step1()
    for spread in spreads:
        spread.step2()
    for spread in spreads:
        spread.step3()
    for spread in (out_spread, expert_spread, head_spread, small_spread):
        spread.last()
        spread.sent()
    for one in heads + smalls + outs:
        one.wait_send()
    for move in moves:
        move.wait()


def finish_call(
    normed, weights, gate_up, grad_out, dq, dk, dv, cosine, sine, tokens, gain, grad_residual,
    grad_router, grad_gain2,
):
    rows, width = tokens.shape
    depth, strip, _ = grad_out.shape
    size = width // depth
    return staged_call(
        finish_kernel,
        "finish",
        6,
        [
            ("a", normed),
            ("a", weights),
            ("l", gate_up),
            ("l", grad_out),
            ("h", dq),
            ("h", dk),
            ("h", dv),
            ("h", cosine),
            ("h", sine),
            ("l", tokens),
            ("v", gain),
            ("l", grad_residual),
            ("l", grad_router),
            ("l", grad_gain2),
        ],
        [
            ("h", shape((rows, width), f32)),
            ("a", shape((GROUP, HW, size), bf16)),
            ("a", shape((GROUP, ROUTER, size), bf16)),
            ("a", shape((GROUP, strip, width), bf16)),
            ("a", shape((GROUP,) + gate_up.shape, bf16)),
        ],
        [
            VMEM(normed.shape, bf16),
            VMEM(weights.shape, bf16),
            VMEM((GROUP, HW, rows), bf16),
            VMEM((GROUP, HW, rows), bf16),
            VMEM((GROUP, rows, HW), bf16),
            VMEM((rows, width), f32),
            VMEM((depth, HW, size), bf16),
            VMEM((depth, ROUTER, size), bf16),
            VMEM((depth, HW, size), bf16),
            VMEM((depth, ROUTER, size), bf16),
            VMEM((depth, strip, width), bf16),
            VMEM((HW, size), bf16),
            VMEM((ROUTER, size), bf16),
            VMEM((strip, width), bf16),
        ]
        + [DMA((GROUP,))] * 2
        + [DMA((depth,))] * 6
        + [DMA((Spread.SEMS,))] * 8
        + [DMA((7,))],
    )


def output_kernel(
    shared_ref, small_ref, out_ref, gate_up_ref, down_ref, output_ref, input_grad_ref,
    q_ref, k_ref, v_ref, w_out_ref, router_ref, gain1_ref, gain2_ref, gate_ref, up_ref, w_down_ref,
    final_ref, final_grad_ref,
):
    pair, i = shared_ref.shape[0], pl.program_id(0)
    hidden = gate_ref.shape[2]

    def rows(first, last):
        both = [shared_ref[p, first:last, :].astype(f32) for p in range(pair)]
        return jnp.concatenate(both, axis=0).T

    @pl.when(lax.rem(i, pair) == 0)
    def _():
        q_ref[...] = rows(0, QW)
        k_ref[...] = rows(QW, QW + HEAD_DIM)
        v_ref[...] = rows(QW + HEAD_DIM, HW)

    w_out_ref[...] = out_ref[...].astype(f32)
    gate_ref[...] = gate_up_ref[:, :, :hidden].astype(f32)
    up_ref[...] = gate_up_ref[:, :, hidden:].astype(f32)
    w_down_ref[...] = down_ref[...].astype(f32)
    final_ref[...] = output_ref[...]
    final_grad_ref[...] = input_grad_ref[...]

    @pl.when(i == 0)
    def _():
        total = jnp.sum(small_ref[...].astype(f32), axis=0)
        router_ref[...] = total[: router_ref.shape[0], :]
        gain1_ref[...] = total[ROUTER - 2, :]
        gain2_ref[...] = total[ROUTER - 1, :]


def output_call(shared, small, out, gate_up, down, output, input_grad, experts):
    count, _, size = shared.shape
    _, strip, width = out.shape
    hidden = gate_up.shape[2] // 2
    pair = 2
    rows = output.shape[0] // count
    token = pl.BlockSpec((rows, width), lambda i: (i, 0))

    def first(*dims):
        return pl.BlockSpec((1,) + dims, lambda i: (i,) + (0,) * len(dims))

    def columns(columns):
        return pl.BlockSpec((size, columns), lambda i: (0, i // pair))

    def whole(*dims):
        return pl.BlockSpec(dims, lambda i: (0,) * len(dims))

    return pl.pallas_call(
        output_kernel,
        grid=(count,),
        out_shape=(
            shape((size, count * QW), f32),
            shape((size, count * HEAD_DIM), f32),
            shape((size, count * HEAD_DIM), f32),
            shape(out.shape, f32),
            shape((experts, size), f32),
            shape((size,), f32),
            shape((size,), f32),
            shape((count, size, hidden), f32),
            shape((count, size, hidden), f32),
            shape(down.shape, f32),
            shape(output.shape, bf16),
            shape(input_grad.shape, f32),
        ),
        in_specs=[
            pl.BlockSpec((pair,) + shared.shape[1:], lambda i: (i // pair, 0, 0)),
            whole(*small.shape), first(strip, width), first(*gate_up.shape[1:]),
            first(*down.shape[1:]), token, token,
        ],
        out_specs=(
            columns(pair * QW),
            columns(pair * HEAD_DIM),
            columns(pair * HEAD_DIM),
            first(strip, width),
            whole(experts, size),
            whole(size),
            whole(size),
            first(size, hidden),
            first(size, hidden),
            first(*down.shape[1:]),
            token,
            token,
        ),
        compiler_params=params(),
        name="output",
    )(shared, small, out, gate_up, down, output, input_grad)


def rotary_tables(length):
    frequencies = 10000.0 ** (-(np.arange(HEAD_DIM // 2) * 2.0) / HEAD_DIM)
    angles = frequencies[:, None] * np.arange(length)[None, :]
    return np.cos(angles).astype(np.float32), np.sin(angles).astype(np.float32)


def shards(
    tables,
    tokens,
    doc_ids,
    routes,
    slot_order,
    norm1_gain,
    norm2_gain,
    w_query,
    key_matrix,
    value_matrix,
    w_out,
    w_router,
    w_gate,
    w_up,
    w_down,
    cotangent,
):
    rows, width = tokens.shape[1:]
    ctx, depth = lax.axis_size("ctx"), lax.axis_size("fsdp")
    place = lax.axis_index("ctx")
    parts = ctx // GROUP
    head, part = place % GROUP, place // GROUP
    far = [[p * GROUP + i for p in range(parts)] for i in range(GROUP)]
    span = GROUP * rows
    experts = w_router.shape[1]
    hidden = w_gate.shape[2]

    def gather_z(value):
        return lax.all_gather(value, "fsdp", axis=0, tiled=True)

    def reduce_z(value):
        value = lax.psum_scatter(value.astype(bf16), "fsdp", scatter_dimension=0, tiled=True)
        if parts > 1:
            value = lax.psum(value, "ctx", axis_index_groups=far)
        return value

    cosine, sine = tables
    if parts > 1:
        cosine = lax.dynamic_slice_in_dim(cosine, part * span, span, 1)
        sine = lax.dynamic_slice_in_dim(sine, part * span, span, 1)
    own_tokens, own_cotangent = tokens[0], cotangent[0]

    route_rows, order_rows = routes[0].T, slot_order[0].T
    docs, placed, placed_t, tokens_all, w_all, strips, gate_up, down = gather_call(
        own_tokens, w_router.T, doc_ids, route_rows, order_rows, w_query, key_matrix, value_matrix,
        w_out, w_gate, w_up, w_down, depth,
    )
    gate_up, down = gather_z(gate_up), gather_z(down)
    if parts > 1:

        def gather_far(value, axis):
            return lax.all_gather(value, "ctx", axis=axis, axis_index_groups=far, tiled=True)

        normed1, queries, keys_t, values_t, keys, values = project_call(
            tokens_all, norm1_gain, w_all, cosine, sine
        )
        keys, values, docs = gather_far(keys, 0), gather_far(values, 0), gather_far(docs, 0)
        keys_t, values_t = gather_far(keys_t, 1), gather_far(values_t, 1)
        after = attend_call(
            attend_kernel, [w_all, queries, keys, values_t], [], docs, strips, own_tokens, norm2_gain,
            route_rows, placed, w_all, span, [],
        )
    else:
        normed1, queries, keys_t, values_t, keys, values, *after = attend_call(
            attend_after_project, [w_all, tokens_all, cosine, sine], [norm1_gain], docs, strips,
            own_tokens, norm2_gain, route_rows, placed, w_all, span, projected(tokens_all),
        )
    (
        attended_f32, log_total, attended, out_weight, weights_all, residual, normed2, gates,
        slot_gates, rows_out,
    ) = after
    out_weight = out_weight.reshape(width, width)
    sent_rows, sent_grads, gate, up, active, grad_w_down = dispatch_call(
        rows_out, gate_up, placed, own_cotangent, slot_gates
    )
    grad_w_down = reduce_z(grad_w_down)
    expert_out, grad_buffer, grad_w_gate_up = expert_call(
        active, down, sent_grads.reshape(GROUP * CAP, width), sent_rows.reshape(GROUP * CAP, width),
        gate, up, gate_up,
    )
    grad_w_gate_up = reduce_z(grad_w_gate_up)
    output, grad_residual, heads, attn, grad_router, grad_gain2 = combine_call(
        expert_out, grad_buffer.reshape(sent_rows.shape), out_weight,
        residual, normed2, gates, placed, placed_t, slot_gates, own_cotangent, norm2_gain, w_all,
    )
    dq, dk, dv, grad_out, down_w = backward_call(
        attn, attended, grad_w_down, heads, attended_f32, log_total, queries, keys, keys_t, values,
        docs,
    )
    if parts > 1:
        dk = lax.psum_scatter(dk, "ctx", scatter_dimension=1, axis_index_groups=far, tiled=True)
        dv = lax.psum_scatter(dv, "ctx", scatter_dimension=1, axis_index_groups=far, tiled=True)
    input_grad, shared, small, out_w, gate_up_w = finish_call(
        normed1, weights_all, grad_w_gate_up, grad_out, dq, dk, dv, cosine, sine,
        own_tokens, norm1_gain, grad_residual, grad_router, grad_gain2,
    )
    if parts > 1:
        shared, small, out_w = lax.psum((shared, small, out_w), "ctx", axis_index_groups=far)

    (
        q_w, k_w, v_w, out_w, router_w, gain1_w, gain2_w, gate_w, up_w, down_w, output, input_grad
    ) = output_call(shared, small, out_w, gate_up_w, down_w, output, input_grad, experts)
    return (
        output[None],
        input_grad[None],
        gain1_w,
        gain2_w,
        q_w,
        k_w,
        v_w,
        out_w.reshape(-1, width),
        router_w.T,
        gate_w,
        up_w,
        down_w,
    )


def solution(mesh):
    token_spec = P("fsdp", "ctx", None)
    row_spec, expert_spec = P("fsdp", None), P(None, "fsdp", None)
    tables = rotary_tables(mesh.shape["ctx"] * TOK_DEV)

    def program(*arguments):
        return jax.shard_map(
            functools.partial(shards, tuple(jnp.asarray(t) for t in tables)),
            mesh=mesh,
            in_specs=(
                token_spec,
                P("fsdp", "ctx"),
                token_spec,
                token_spec,
                P(),
                P(),
                row_spec,
                row_spec,
                row_spec,
                row_spec,
                row_spec,
                expert_spec,
                expert_spec,
                expert_spec,
                token_spec,
            ),
            out_specs=(
                token_spec,
                token_spec,
                P("fsdp"),
                P("fsdp"),
                row_spec,
                row_spec,
                row_spec,
                row_spec,
                row_spec,
                expert_spec,
                expert_spec,
                expert_spec,
            ),
            check_vma=False,
        )(*arguments)

    return program
```

```python
import functools

import jax
import jax.numpy as jnp
import numpy as np
from jax import lax
from jax.experimental import pallas as pl
from jax.experimental.pallas import tpu as pltpu
from jax.sharding import PartitionSpec as P

QUERY_HEADS = 24
KEY_VALUE_HEADS = 8
HEAD_DIM = 64
TOPK = 8
EXP_WIN = 8
TOK_DEV = 256
CAP = 64
GROUP = 8
HEADS = QUERY_HEADS // KEY_VALUE_HEADS
QW = HEADS * HEAD_DIM
HW = QW + 2 * HEAD_DIM
ROUTER = 48
ALL = HW + ROUTER

NEVER = 4096.0
epsilon = 1e-06
score_masked = -1e30
bf16 = jnp.bfloat16
f32 = jnp.float32
VMEM = pltpu.VMEM
MESH = pl.DeviceIdType.MESH
DMA = pltpu.SemaphoreType.DMA
IN_VMEM = pl.BlockSpec(memory_space=VMEM)
IN_ANY = pl.BlockSpec(memory_space=pl.ANY)


def dot(left, right, dims=((1,), (0,))):
    return lax.dot_general(left, right, (dims, ((), ())), preferred_element_type=f32)


def block(index, size=TOK_DEV):
    return pl.ds(pl.multiple_of(index * size, size), size)


def shape(dims, dtype):
    return jax.ShapeDtypeStruct(dims, dtype)


def params(collective_id=None, limit=56):
    return pltpu.CompilerParams(
        collective_id=collective_id,
        has_side_effects=collective_id is not None,
        vmem_limit_bytes=limit << 20,
    )


class Staged:
    def __init__(self, fetches, later, puts):
        self.fetches, self.later, self.puts, self.out = fetches, later, puts, []

    def begin(self):
        for copy in self.later:
            copy.start()
        self.later = []

    def need(self, *refs):
        for ref in refs:
            self.fetches.pop(id(ref)).wait()

    def put(self, *refs):
        for ref in refs:
            copy = self.puts.pop(id(ref))
            copy.start()
            self.out.append(copy)

    def finish(self):
        self.begin()
        for copy in self.fetches.values():
            copy.wait()
        for copy in self.puts.values():
            copy.start()
        for copy in self.out + list(self.puts.values()):
            copy.wait()


def staged_call(body, name, collective_id, ins, outs, scratch):
    held_in = [i for i, (how, _) in enumerate(ins) if how in "hl"]
    held_out = [i for i, (how, _) in enumerate(outs) if how == "h"]

    def kernel(*refs):
        refs = list(refs)
        given, refs = refs[: len(ins)], refs[len(ins) :]
        results, refs = refs[: len(outs)], refs[len(outs) :]
        own, refs = refs[: len(scratch)], refs[len(scratch) :]
        in_held, refs = refs[: len(held_in)], refs[len(held_in) :]
        out_held, (in_sems, out_sems) = refs[: len(held_out)], refs[len(held_out) :]
        fetches, later, puts = {}, [], {}
        for n, i in enumerate(held_in):
            copy = pltpu.make_async_copy(given[i], in_held[n], in_sems.at[n])
            if ins[i][0] == "l":
                later.append(copy)
            else:
                copy.start()
            given[i] = in_held[n]
            fetches[id(given[i])] = copy
        for n, i in enumerate(held_out):
            puts[id(out_held[n])] = pltpu.make_async_copy(out_held[n], results[i], out_sems.at[n])
            results[i] = out_held[n]
        stage = Staged(fetches, later, puts)
        body(stage, *given, *results, *own)
        stage.finish()

    return pl.pallas_call(
        kernel,
        out_shape=tuple(one for _, one in outs),
        in_specs=[IN_VMEM if how == "v" else IN_ANY for how, _ in ins],
        out_specs=tuple(IN_VMEM if how == "v" else IN_ANY for how, _ in outs),
        scratch_shapes=list(scratch)
        + [VMEM(ins[i][1].shape, ins[i][1].dtype) for i in held_in]
        + [VMEM(outs[i][1].shape, outs[i][1].dtype) for i in held_out]
        + [DMA((max(len(held_in), 1),)), DMA((max(len(held_out), 1),))],
        compiler_params=params(collective_id),
        name=name,
    )(*(array for _, array in ins))


def flip(index, bit):
    return index + (1 - 2 * ((index // bit) % 2)) * bit


class Place:
    def __init__(self):
        ctx = lax.axis_index("ctx")
        self.base = (ctx // GROUP) * GROUP
        self.me = ctx - self.base
        self.z = lax.axis_index("fsdp")
        self.depth = lax.axis_size("fsdp")
        self.near = [flip(self.me, bit) for bit in (1, 2, 4)]

    def ctx(self, index):
        return {"ctx": self.base + index}

    def fsdp(self, index):
        return {"fsdp": index}

    def others(self):
        return [self.ctx(lax.rem(self.me + j, GROUP)) for j in range(1, GROUP)]

    def layers(self):
        return [self.fsdp(lax.rem(self.z + j, self.depth)) for j in range(1, self.depth)]


def greet(devices):
    ready = pltpu.get_barrier_semaphore()
    for device in devices:
        pl.semaphore_signal(ready, inc=1, device_id=device, device_id_type=MESH)
    return lambda: pl.semaphore_wait(ready, len(devices))


def remote(source, target, send, receive, device):
    return pltpu.make_async_remote_copy(
        src_ref=source,
        dst_ref=target,
        send_sem=send,
        recv_sem=receive,
        device_id=device,
        device_id_type=MESH,
    )


def halves(count):
    cut = -(-count // 32) * 16

    def part(ref, half):
        return ref.at[pl.ds(0, cut)] if half == 0 else ref.at[pl.ds(cut, count - cut)]

    return part


class Spread:
    SEMS = 14

    def __init__(self, place, source, land, part, send, receive):
        me = place.me
        core, side, row = place.near
        across = flip(side, 4)

        def plan(slot, owner, half, device):
            target = part(land(owner), half)
            first = part(source, half) if slot < 6 else target
            return remote(first, target, send.at[slot], receive.at[slot], place.ctx(device))

        self.copies = [
            plan(0, me, 0, side), plan(1, me, 1, side), plan(2, me, 0, row), plan(3, me, 1, row),
            plan(4, me, 0, core), plan(5, me, 1, core), plan(6, side, 0, core),
            plan(7, side, 1, core), plan(8, row, 0, core), plan(9, row, 1, core),
            plan(10, side, 1, row), plan(11, row, 0, side), plan(12, across, 0, core),
            plan(13, across, 1, core),
        ]

    def go(self, *slots):
        for slot in slots:
            self.copies[slot].start()

    def wait(self, *slots):
        for slot in slots:
            self.copies[slot].wait_recv()

    def start(self):
        self.go(1, 2, 0, 3, 4, 5)

    def step1(self):
        self.wait(1)
        self.go(10, 7)
        self.wait(2)
        self.go(11, 8)

    def step2(self):
        self.wait(0)
        self.go(6)
        self.wait(3)
        self.go(9)

    def step3(self):
        self.wait(10)
        self.go(13)
        self.wait(11)
        self.go(12)

    def sent(self):
        for copy in self.copies:
            copy.wait_send()

    def last(self):
        self.wait(4, 5, 6, 7, 8, 9, 12, 13)


class Line:
    def __init__(self, place, land, send, receive):
        self.z, self.depth = place.z, place.depth
        z, most = self.z, place.depth - 1
        ways = ((jnp.minimum(z + 1, most), -1), (jnp.maximum(z - 1, 0), 1))
        self.copies = []
        for way, (device, sign) in enumerate(ways):
            self.copies.append([])
            for step in range(most):
                held = land(jnp.clip(z + sign * step, 0, most))
                self.copies[way].append(
                    remote(
                        held, held, send.at[way, step], receive.at[way, step], place.fsdp(device)
                    )
                )

    def each(self, step):
        z, most = self.z, self.depth - 1
        up, down = self.copies
        at = min(step, most - 1)
        return ((z + 1 <= most, z - step >= 0, up[at]), (z - 1 >= 0, z + step <= most, down[at]))

    def start(self):
        for open_way, _, copy in self.each(0):
            pl.when(open_way)(copy.start)

    def step(self, step):
        before = self.each(step - 1)
        for (open_way, here, copy), (_, _, came) in zip(self.each(step), before):
            pl.when(here)(came.wait_recv)
            if step < self.depth - 1:
                pl.when(jnp.logical_and(open_way, here))(copy.start)

    def last(self):
        self.step(self.depth - 1)

    def sent(self):
        for step in range(self.depth - 1):
            for open_way, here, copy in self.each(step):
                pl.when(jnp.logical_and(open_way, here))(copy.wait_send)


def place_slots(routes_ref, order_ref, placed_ref):
    rows = routes_ref.shape[1]
    expert = lax.broadcasted_iota(jnp.int32, (EXP_WIN, rows), 0)
    priority = jnp.full((EXP_WIN, rows), NEVER, f32)
    for k in range(TOPK):
        pick = expert == routes_ref[k : k + 1, :]
        priority = jnp.where(pick, order_ref[k : k + 1, :].astype(f32), priority)
    priority_turned = priority.T
    slot = lax.broadcasted_iota(jnp.int32, (CAP, rows), 0).astype(f32)
    for e in range(EXP_WIN):
        mine = priority[e : e + 1, :]
        before = jnp.where(priority_turned[:, e : e + 1] < mine, 1.0, 0.0)
        before = jnp.sum(before, axis=0, keepdims=True)
        placed = (slot == before) & (mine < NEVER)
        placed_ref[e] = jnp.where(placed, 1.0, 0.0).astype(bf16)


def gather_kernel(
    stage, tokens_ref, router_ref, docs_ref, routes_ref, order_ref, w_query_ref,
    key_matrix_ref, value_matrix_ref, w_out_ref, w_gate_ref, w_up_ref, w_down_ref,
    docs_all_ref, placed_ref, turned_ref, tokens_all_ref, w_all_ref, strips_ref, gate_up_ref, down_ref,
    held_ref, query_held, key_held, value_held,
    w_send, w_recv, o_send, o_recv, d_send, d_recv, c_send, c_recv, local,
):
    place = Place()
    me, z = place.me, place.z
    met = greet(place.others() + place.layers())
    odd = lax.rem(me, 2)
    pair = lax.div(me, 2)
    depth, strip, _ = strips_ref.shape

    def window(first, size):
        return pl.ds(pl.multiple_of(first * 128, 128), size)

    fetches = [
        pltpu.make_async_copy(
            w_query_ref.at[:, window(pair * 3 + odd, 2 * 128)], query_held, local.at[0]
        ),
        pltpu.make_async_copy(key_matrix_ref.at[:, window(pair, 128)], key_held, local.at[1]),
        pltpu.make_async_copy(value_matrix_ref.at[:, window(pair, 128)], value_held, local.at[2]),
        pltpu.make_async_copy(
            w_out_ref.at[pl.ds(pl.multiple_of(me * strip, strip), strip), :], strips_ref.at[z],
            local.at[3],
        ),
        pltpu.make_async_copy(tokens_ref, held_ref, local.at[4]),
    ]
    hidden = w_gate_ref.shape[2]
    shards = [
        pltpu.make_async_copy(w_gate_ref.at[me], gate_up_ref.at[:, pl.ds(0, hidden)], local.at[5]),
        pltpu.make_async_copy(w_up_ref.at[me], gate_up_ref.at[:, pl.ds(hidden, hidden)], local.at[6]),
        pltpu.make_async_copy(w_down_ref.at[me], down_ref, local.at[7]),
    ]
    for fetch in fetches:
        fetch.start()
    met()
    spread = Spread(
        place, tokens_ref, lambda owner: tokens_all_ref.at[owner], halves(TOK_DEV), c_send, c_recv
    )
    spread.start()
    lines = [
        Line(place, lambda layer: strips_ref.at[layer], o_send, o_recv),
        Line(place, lambda layer: w_all_ref.at[layer], w_send, w_recv),
    ]
    fetches[3].wait()
    lines[0].start()
    for fetch in fetches[:3] + fetches[4:]:
        fetch.wait()

    def half(held, columns):
        turned_rows = held[...].T
        return jnp.where(odd == 1, turned_rows[HEAD_DIM:], turned_rows[:columns])

    own = w_all_ref.at[z]
    own[:QW, :] = half(query_held, QW)
    own[QW : QW + HEAD_DIM, :] = half(key_held, HEAD_DIM)
    own[QW + HEAD_DIM : HW, :] = half(value_held, HEAD_DIM)
    router = router_ref[...].astype(f32)
    empty = jnp.zeros((ROUTER - router.shape[0], router.shape[1]), f32)
    own[HW:, :] = jnp.concatenate([router, empty], axis=0).astype(bf16)
    lines[1].start()
    for shard in shards:
        shard.start()
    docs_all_ref[me] = docs_ref[...]
    sent = []
    for j, device in enumerate(place.others()):
        sent.append(remote(docs_ref, docs_all_ref.at[me], d_send.at[j], d_recv.at[j], device))
    for copy in sent:
        copy.start()
    move = pltpu.make_async_copy(held_ref, tokens_all_ref.at[me], local.at[8])
    move.start()
    place_slots(routes_ref, order_ref, placed_ref)
    turned_ref[...] = placed_ref[...].reshape(EXP_WIN * CAP, -1).T
    stage.put(placed_ref, turned_ref)
    for shard in shards:
        shard.wait()
    stage.put(gate_up_ref, down_ref)
    steps = (spread.step1, spread.step2)
    for step in range(1, depth - 1):
        for act in steps[step - 1 : step]:
            act()
        for line in lines:
            line.step(step)
    for act in steps[depth - 2 :]:
        act()
    spread.step3()
    for line in lines:
        line.last()
    stage.put(w_all_ref, strips_ref)
    spread.last()
    for copy in sent:
        copy.wait()
    move.wait()
    for line in lines:
        line.sent()
    spread.sent()


def gather_call(
    tokens, router, docs, routes, order, w_query, key_matrix, value_matrix, w_out, w_gate, w_up, w_down,
    depth,
):
    rows, width = tokens.shape
    strip = w_out.shape[0] // GROUP
    size = w_query.shape[0]
    return staged_call(
        gather_kernel,
        "gather",
        1,
        [
            ("a", tokens),
            ("v", router),
            ("v", docs),
            ("v", routes),
            ("v", order),
            ("a", w_query),
            ("a", key_matrix),
            ("a", value_matrix),
            ("a", w_out),
            ("a", w_gate),
            ("a", w_up),
            ("a", w_down),
        ],
        [
            ("v", shape((GROUP,) + docs.shape, jnp.int32)),
            ("h", shape((EXP_WIN, CAP, rows), bf16)),
            ("h", shape((rows, EXP_WIN * CAP), bf16)),
            ("a", shape((GROUP, rows, width), bf16)),
            ("h", shape((depth, ALL, size), bf16)),
            ("h", shape((depth, strip, width), bf16)),
            ("h", shape((w_gate.shape[1], 2 * w_gate.shape[2]), bf16)),
            ("h", shape(w_down.shape[1:], bf16)),
        ],
        [
            VMEM((rows, width), bf16),
            VMEM((size, 2 * 128), bf16),
            VMEM((size, 128), bf16),
            VMEM((size, 128), bf16),
        ]
        + [DMA((2, depth - 1))] * 4
        + [DMA((GROUP - 1,))] * 2
        + [DMA((Spread.SEMS,))] * 2
        + [DMA((9,))],
    )


def turned(values, cosine, sine):
    half = HEAD_DIM // 2
    out = []
    for at in range(0, values.shape[0], HEAD_DIM):
        low, high = values[at : at + half], values[at + half : at + HEAD_DIM]
        out += [low * cosine - high * sine, high * cosine + low * sine]
    return jnp.concatenate(out, axis=0)


def project_block(
    owner, tokens_ref, gain_ref, w_all_ref, cos_ref, sin_ref,
    normed_ref, qt_ref, kt_ref, vt_ref, k_ref, v_ref,
):
    x = tokens_ref[owner].astype(f32)
    scale = lax.rsqrt(jnp.mean(x * x, axis=-1, keepdims=True) + epsilon)
    normed_ref[owner] = (x * scale * gain_ref[...].reshape(1, -1)).astype(bf16)
    linear = None
    for s in range(w_all_ref.shape[0]):
        size = w_all_ref.shape[2]
        term = dot(
            w_all_ref[s, :HW, :], normed_ref[owner, :, s * size : (s + 1) * size], ((1,), (1,))
        )
        linear = term if linear is None else linear + term
    tokens = block(owner)
    cosine, sine = cos_ref[:, tokens], sin_ref[:, tokens]
    queries = turned(linear[:QW], cosine, sine) * HEAD_DIM ** (-0.5)
    qt_ref[:, tokens] = queries.astype(bf16)
    keys = turned(linear[QW : QW + HEAD_DIM], cosine, sine)
    kt_ref[:, tokens] = keys.astype(bf16)
    k_ref[tokens, :] = keys.T.astype(bf16)
    values = linear[QW + HEAD_DIM :]
    vt_ref[:, tokens] = values.astype(bf16)
    v_ref[tokens, :] = values.T.astype(bf16)


def projected(tokens):
    span = tokens.shape[0] * tokens.shape[1]
    return [
        ("h", shape(tokens.shape, bf16)),
        ("h", shape((QW, span), bf16)),
        ("h", shape((HEAD_DIM, span), bf16)),
        ("h", shape((HEAD_DIM, span), bf16)),
        ("h", shape((span, HEAD_DIM), bf16)),
        ("h", shape((span, HEAD_DIM), bf16)),
    ]


def project_kernel(stage, tokens_ref, gain_ref, w_all_ref, cos_ref, sin_ref, *outs):
    stage.need(tokens_ref, w_all_ref, cos_ref, sin_ref)

    def project(i, _):
        project_block(i, tokens_ref, gain_ref, w_all_ref, cos_ref, sin_ref, *outs)
        return 0

    lax.fori_loop(0, GROUP, project, 0)


def project_call(tokens, gain, w_all, cosine, sine):
    return staged_call(
        project_kernel,
        "project",
        None,
        [("h", tokens), ("v", gain), ("h", w_all), ("h", cosine), ("h", sine)],
        projected(tokens),
        [],
    )


def docs_column(row):
    return jnp.broadcast_to(row.astype(f32), (8, row.shape[1])).T[:, :1]


def attend_after_project(
    n_blocks, stage, w_all_ref, tokens_ref, cos_ref, sin_ref, gain_ref, *rest,
):
    given, outs, rest = rest[:6], rest[6:12], rest[12:]
    _, qt_ref, _, vt_ref, k_ref, _ = outs

    def project_all():
        stage.need(tokens_ref, cos_ref, sin_ref)

        def project(i, _):
            project_block(i, tokens_ref, gain_ref, w_all_ref, cos_ref, sin_ref, *outs)
            return 0

        lax.fori_loop(0, GROUP, project, 0)
        stage.put(*outs)

    attend_body(n_blocks, stage, project_all, w_all_ref, qt_ref, k_ref, vt_ref, *given, *rest)


def attend_kernel(n_blocks, stage, w_all_ref, qt_ref, k_ref, vt_ref, *rest):
    def fetch_all():
        stage.need(qt_ref, k_ref, vt_ref)

    attend_body(n_blocks, stage, fetch_all, w_all_ref, qt_ref, k_ref, vt_ref, *rest)


def router_of(w_all_ref):
    return [w_all_ref[s, HW:, :] for s in range(w_all_ref.shape[0])]


def attend_body(
    n_blocks, stage, prepare, w_all_ref, qt_ref, k_ref, vt_ref,
    docs_ref, strips_ref, tokens_ref, gain_ref, routes_ref, placed_ref,
    o_ref, lse_ref, attended_ref, out_weight_ref, weights_ref, residual_ref, normed2_ref, gates_ref,
    slot_gates_ref, rows_ref,
    staged_ref, docs_col_ref, top_ref, sum_ref, acc_ref, mixed_ref,
    a_send, a_recv, s_send, s_recv, w_send, w_recv, local,
):
    T = TOK_DEV
    place = Place()
    me, z = place.me, place.z
    first = place.base
    met = greet(place.others())
    depth, strip, _ = strips_ref.shape
    move = pltpu.make_async_copy(w_all_ref.at[:, :HW], weights_ref.at[me], local.at[1])

    def layers(ref, h):
        return ref.at[pl.ds(h * (depth // 2), depth // 2)]

    weights = Spread(
        place, w_all_ref.at[:, :HW], lambda owner: weights_ref.at[owner], layers, w_send, w_recv
    )
    strips = Spread(
        place, strips_ref, lambda owner: out_weight_ref.at[:, owner], layers, s_send, s_recv
    )
    def turn(i, _):
        docs_col_ref[i] = docs_column(docs_ref[i])
        return 0

    lax.fori_loop(0, n_blocks, turn, 0)
    stage.need(strips_ref)
    stage.begin()
    met()
    strips.start()
    out_weight_ref[:, me] = strips_ref[...]
    stage.need(w_all_ref)
    move.start()
    weights.start()
    prepare()

    def tile(kb, qb, mask):
        kt = k_ref[block(kb), :]
        vt = vt_ref[:, block(kb)]
        heads = range(HEADS)
        parts = [slice(h * HEAD_DIM, (h + 1) * HEAD_DIM) for h in heads]
        s = [dot(kt, qt_ref[parts[h], block(qb)]) for h in heads]
        if mask is not None:
            s = [jnp.where(mask, x, score_masked) for x in s]
        old = [top_ref[h : h + 1, :] for h in heads]
        new = [jnp.maximum(old[h], jnp.max(s[h], axis=0, keepdims=True)) for h in heads]
        p = [jnp.exp(s[h] - new[h]) for h in heads]
        factor = [jnp.exp(old[h] - new[h]) for h in heads]
        total = [
            sum_ref[h : h + 1, :] * factor[h] + jnp.sum(p[h], axis=0, keepdims=True) for h in heads
        ]
        mixed = [acc_ref[parts[h], :] * factor[h] + dot(vt, p[h].astype(bf16)) for h in heads]
        for h in heads:
            top_ref[h : h + 1, :] = new[h]
            sum_ref[h : h + 1, :] = total[h]
            acc_ref[parts[h], :] = mixed[h]

    def same(kb, gq):
        return docs_col_ref[kb] == docs_ref[gq].astype(f32)

    def head_rows(head):
        per = GROUP * depth // GROUP
        return attended_ref.at[lax.div(head * depth, GROUP), pl.ds(lax.rem(head * depth, GROUP), per)]

    def attended_copy(to, slot):
        return remote(
            staged_ref.at[to], head_rows(slot), a_send.at[to], a_recv.at[slot], place.ctx(to)
        )

    def q_block(j, _):
        for at, act in ((1, strips.step1), (2, strips.step2), (5, strips.step3)):
            pl.when(j == at)(act)
        qb = jnp.where(j < GROUP // 2, GROUP - 1 - 2 * j, 2 * GROUP - 2 - 2 * j)
        gq = first + qb
        top_ref[...] = jnp.full_like(top_ref, score_masked)
        sum_ref[...] = jnp.ones_like(sum_ref)
        acc_ref[...] = jnp.zeros_like(acc_ref)
        last = gq == n_blocks - 1

        def k_block(kb, _):
            edge = jnp.logical_or(kb == 0, last)

            @pl.when(edge)
            def _():
                tile(kb, qb, same(kb, gq))

            @pl.when(jnp.logical_not(edge))
            def _():
                tile(kb, qb, None)

            return 0

        lax.fori_loop(0, gq, k_block, 0)
        keys = lax.broadcasted_iota(jnp.int32, (T, T), 0)
        queries = lax.broadcasted_iota(jnp.int32, (T, T), 1)
        tile(gq, qb, same(gq, gq) & (keys <= queries))
        lse_ref[qb] = top_ref[...] + jnp.log(sum_ref[...])
        for h in range(HEADS):
            part = slice(h * HEAD_DIM, (h + 1) * HEAD_DIM)
            acc_ref[part, :] = acc_ref[part, :] / sum_ref[h : h + 1, :]
        o_ref[:, block(qb)] = acc_ref[...]
        staged_ref[qb] = acc_ref[...].astype(bf16).reshape(depth, strip, T)

        @pl.when(qb != me)
        def _():
            attended_copy(qb, me).start()

        return 0

    lax.fori_loop(0, GROUP, q_block, 0)
    stage.put(o_ref, lse_ref)
    own = pltpu.make_async_copy(staged_ref.at[me], head_rows(me), local.at[2])
    own.start()
    own.wait()
    weights.step1()
    weights.step2()
    for j in range(1, GROUP):
        other = lax.rem(me + j, GROUP)
        attended_copy(other, other).wait()
    stage.put(attended_ref)
    strips.last()
    stage.put(out_weight_ref)

    rows, width = tokens_ref.shape
    stage.need(tokens_ref, placed_ref)
    mixed_ref[...] = attended_ref[...].reshape(width, rows).T

    def out_columns(i, _):
        columns = block(i)
        weight = out_weight_ref[:, :, :, columns].reshape(width, T)
        residual_ref[:, columns] = tokens_ref[:, columns].astype(f32) + dot(mixed_ref[...], weight)
        return 0

    lax.fori_loop(0, width // T, out_columns, 0)
    residual = residual_ref[...]
    scale = lax.rsqrt(jnp.mean(residual * residual, axis=-1, keepdims=True) + epsilon)
    normed2_ref[...] = (residual * scale * gain_ref[...].reshape(1, -1)).astype(bf16)
    stage.put(residual_ref, normed2_ref)
    logits = None
    for s, router in enumerate(router_of(w_all_ref)):
        size = router.shape[1]
        term = dot(router, normed2_ref[:, s * size : (s + 1) * size], ((1,), (1,)))
        logits = term if logits is None else logits + term
    expert = lax.broadcasted_iota(jnp.int32, gates_ref.shape, 0)
    chosen = expert < 0
    for k in range(TOPK):
        chosen = chosen | (expert == routes_ref[k : k + 1, :])
    logits = jnp.where(chosen, logits, score_masked)
    top = jnp.max(logits, axis=0, keepdims=True)
    gates = jnp.where(chosen, jnp.exp(logits - top), 0.0)
    gates = gates / jnp.sum(gates, axis=0, keepdims=True)
    gates_ref[...] = gates
    for e in range(EXP_WIN):
        slot_gates_ref[e] = jnp.sum(
            placed_ref[e].astype(f32) * gates[e : e + 1, :], axis=1, keepdims=True
        )

    def pick_rows(e, _):
        rows_ref[e] = dot(placed_ref[e], normed2_ref[...]).astype(bf16)
        return 0

    lax.fori_loop(0, EXP_WIN, pick_rows, 0)
    stage.put(gates_ref, slot_gates_ref, rows_ref)
    weights.step3()
    weights.last()
    weights.sent()
    strips.sent()
    move.wait()


def attend_call(
    kernel, ins, gains, docs, strips, tokens, gain, routes, placed, w_all, span, projections
):
    n = docs.shape[0]
    rows, width = tokens.shape
    depth, _, size = w_all.shape
    strip = strips.shape[1]
    return staged_call(
        functools.partial(kernel, n),
        "attend",
        2,
        [("l", one) for one in ins]
        + [("v", one) for one in gains]
        + [("v", docs), ("h", strips), ("l", tokens), ("v", gain), ("v", routes), ("l", placed)],
        projections
        + [
            ("h", shape((QW, span), f32)),
            ("h", shape((GROUP, 8, TOK_DEV), f32)),
            ("h", shape((depth, GROUP, strip, TOK_DEV), bf16)),
            ("h", shape((depth, GROUP) + strips.shape[1:], bf16)),
            ("a", shape((GROUP, depth, HW, size), bf16)),
            ("h", shape((rows, width), f32)),
            ("h", shape((rows, width), bf16)),
            ("h", shape((ROUTER, rows), f32)),
            ("h", shape((EXP_WIN, CAP, 1), f32)),
            ("h", shape((EXP_WIN, CAP, width), bf16)),
        ],
        [
            VMEM((GROUP, depth, strip, TOK_DEV), bf16),
            VMEM((n, TOK_DEV, 1), f32),
            VMEM((8, TOK_DEV), f32),
            VMEM((8, TOK_DEV), f32),
            VMEM((QW, TOK_DEV), f32),
            VMEM((rows, width), bf16),
        ]
        + [DMA((GROUP,))] * 2
        + [DMA((Spread.SEMS,))] * 4
        + [DMA((3,))],
    )


def dispatch_kernel(
    stage, sent_rows_ref, gate_up_ref, placed_ref, cotangent_ref, slot_gates_ref,
    rows_ref, grads_ref, gate_ref, up_ref, active_ref, grad_down_ref,
    gate_up_held, own_grads, r_send, r_recv, g_send, g_recv, local,
):
    place = Place()
    me = place.me
    met = greet(place.others())
    width = cotangent_ref.shape[1]

    def copy(source, target, send, receive, j):
        to = lax.rem(me + j, GROUP)
        return remote(source.at[to], target.at[me], send.at[j], receive.at[j], place.ctx(to))

    met()
    for j in range(1, GROUP):
        copy(sent_rows_ref, rows_ref, r_send, r_recv, j).start()
    own = pltpu.make_async_copy(sent_rows_ref.at[me], rows_ref.at[me], local.at[0])
    own.start()
    fetch = pltpu.make_async_copy(gate_up_ref, gate_up_held, local.at[1])
    fetch.start()
    stage.need(placed_ref, cotangent_ref, slot_gates_ref)

    def send_grads(n, _):
        j = GROUP - n
        to = lax.rem(me + j, GROUP)
        routed = dot(placed_ref[to], cotangent_ref[...])
        own_grads[to] = (routed * slot_gates_ref[to]).astype(bf16)

        @pl.when(j > 0)
        def _():
            copy(own_grads, grads_ref, g_send, g_recv, j).start()

        return 0

    lax.fori_loop(1, GROUP + 1, send_grads, 0)
    grads_ref[me] = own_grads[me]
    fetch.wait()
    own.wait()
    for j in range(1, GROUP):
        copy(sent_rows_ref, rows_ref, r_send, r_recv, j).wait_recv()
    stage.put(rows_ref)
    slots = GROUP * CAP
    hidden = gate_ref.shape[1]
    tiles = hidden // TOK_DEV

    def expert_up(i, _):
        came = rows_ref[...].reshape(slots, width)
        gate = dot(came, gate_up_held[:, block(i)])
        up = dot(came, gate_up_held[:, block(tiles + i)])
        gate_ref[:, block(i)] = gate
        up_ref[:, block(i)] = up
        active_ref[:, block(i)] = (gate * jax.nn.sigmoid(gate) * up).astype(bf16)
        return 0

    lax.fori_loop(0, tiles, expert_up, 0)
    stage.put(gate_ref, up_ref, active_ref)
    for j in range(1, GROUP):
        copy(own_grads, grads_ref, g_send, g_recv, j).wait_recv()
    stage.put(grads_ref)

    def expert_over(i, _):
        grad_down_ref[:, block(i)] = dot(
            active_ref[...], grads_ref[:, :, block(i)].reshape(slots, TOK_DEV), ((0,), (0,))
        ).astype(bf16)
        return 0

    lax.fori_loop(0, width // TOK_DEV, expert_over, 0)
    stage.put(grad_down_ref)
    for j in range(1, GROUP):
        copy(sent_rows_ref, rows_ref, r_send, r_recv, j).wait_send()
        copy(own_grads, grads_ref, g_send, g_recv, j).wait_send()


def dispatch_call(sent_rows, gate_up, placed, cotangent, slot_gates):
    slots = sent_rows.shape
    count, width = GROUP * CAP, slots[2]
    hidden = gate_up.shape[1] // 2
    return staged_call(
        dispatch_kernel,
        "dispatch",
        3,
        [
            ("a", sent_rows),
            ("a", gate_up),
            ("h", placed),
            ("h", cotangent),
            ("h", slot_gates),
        ],
        [
            ("h", shape(slots, bf16)),
            ("h", shape(slots, bf16)),
            ("h", shape((count, hidden), f32)),
            ("h", shape((count, hidden), f32)),
            ("h", shape((count, hidden), bf16)),
            ("h", shape((hidden, width), bf16)),
        ],
        [VMEM(gate_up.shape, bf16), VMEM(slots, bf16)] + [DMA((GROUP,))] * 4 + [DMA((2,))],
    )


def expert_kernel(
    stage, active_ref, down_ref, grads_ref, rows_ref, gate_ref, up_ref, gate_up_ref,
    out_ref, back_ref, grad_gate_up_ref,
    grads_held, rows_held, gate_up_held, own_ref, grad_ref, send, receive, local,
):
    place = Place()
    me = place.me
    met = greet(place.others())
    fetches = [
        pltpu.make_async_copy(grads_ref, grads_held, local.at[0]),
        pltpu.make_async_copy(rows_ref, rows_held, local.at[1]),
        pltpu.make_async_copy(gate_up_ref, gate_up_held, local.at[2]),
    ]
    count, hidden = active_ref.shape
    width = down_ref.shape[1]
    T = TOK_DEV
    tiles = hidden // T

    def copy(j, half):
        to = lax.rem(me + j, GROUP)
        columns = pl.ds(half * (width // 2), width // 2)
        return remote(
            own_ref.at[to, :, columns], out_ref.at[me, :, columns], send.at[half, j],
            receive.at[half, j], place.ctx(to),
        )

    stage.need(active_ref, down_ref)
    for fetch in fetches:
        fetch.start()
    stage.begin()

    def out(i, _):
        value = dot(active_ref[...], down_ref[:, block(i)]).astype(bf16)
        own_ref[:, :, block(i)] = value.reshape(GROUP, CAP, T)
        return 0

    for half in range(2):
        tiles_half = width // T // 2
        lax.fori_loop(half * tiles_half, (half + 1) * tiles_half, out, 0)
        if half == 0:
            met()
        for j in range(1, GROUP):
            copy(j, half).start()
    move = pltpu.make_async_copy(own_ref.at[me], out_ref.at[me], local.at[3])
    move.start()
    fetches[0].wait()
    stage.need(gate_ref, up_ref)

    def back(i, _):
        grad = dot(grads_held[...], down_ref[block(i), :], ((1,), (1,)))
        gate, up = gate_ref[:, block(i)], up_ref[:, block(i)]
        sigmoid = jax.nn.sigmoid(gate)
        grad_gate = grad * up * sigmoid * (1.0 + gate * (1.0 - sigmoid))
        grad_ref[:, block(i)] = grad_gate.astype(bf16)
        grad_ref[:, block(tiles + i)] = (grad * gate * sigmoid).astype(bf16)
        return 0

    lax.fori_loop(0, tiles, back, 0)
    fetches[1].wait()
    fetches[2].wait()

    def over(i, _):
        grad_gate_up_ref[block(i), :] = dot(
            rows_held[:, block(i)], grad_ref[...], ((0,), (0,))
        ).astype(bf16)
        back_ref[:, block(i)] = dot(
            grad_ref[...], gate_up_held[block(i), :], ((1,), (1,))
        ).astype(bf16)
        return 0

    lax.fori_loop(0, width // T, over, 0)
    stage.put(back_ref, grad_gate_up_ref)
    for half in range(2):
        for j in range(1, GROUP):
            copy(j, half).wait()
    move.wait()


def expert_call(active, down, grads, rows, gate, up, gate_up):
    count, width = rows.shape
    hidden = down.shape[0]
    slots = (GROUP, CAP, width)
    return staged_call(
        expert_kernel,
        "expert",
        7,
        [
            ("h", active),
            ("h", down),
            ("a", grads),
            ("a", rows),
            ("l", gate),
            ("l", up),
            ("a", gate_up),
        ],
        [
            ("a", shape(slots, bf16)),
            ("h", shape((count, width), bf16)),
            ("h", shape((width, 2 * hidden), bf16)),
        ],
        [
            VMEM(grads.shape, bf16),
            VMEM(rows.shape, bf16),
            VMEM(gate_up.shape, bf16),
            VMEM(slots, bf16),
            VMEM((count, 2 * hidden), bf16),
            DMA((2, GROUP)),
            DMA((2, GROUP)),
            DMA((4,)),
        ],
    )


def combine_kernel(
    stage, out_ref, sent_grad_ref, weight_ref, residual_ref, normed_ref, gates_ref, placed_ref,
    placed_t_ref, slot_gates_ref, cotangent_ref, gain_ref, w_all_ref,
    output_ref, grad_residual_ref, heads_ref, attn_ref, grad_router_ref, grad_gain_ref,
    back_ref, weight_held, sum_ref, turned_ref, staged_ref, scaled_ref,
    b_send, b_recv, h_send, h_recv, local,
):
    place = Place()
    me = place.me
    met = greet(place.others())
    fetch = pltpu.make_async_copy(weight_ref, weight_held, local.at[0])
    rows, width = residual_ref.shape

    def copy(source, target, send, receive, j):
        to = lax.rem(me + j, GROUP)
        return remote(source.at[to], target.at[me], send.at[j], receive.at[j], place.ctx(to))

    backs = [copy(sent_grad_ref, back_ref, b_send, b_recv, j) for j in range(1, GROUP)]
    met()
    for one in backs:
        one.start()
    move = pltpu.make_async_copy(sent_grad_ref.at[me], back_ref.at[me], local.at[1])
    move.start()
    turned_ref[...] = jnp.zeros_like(turned_ref)
    stage.need(out_ref, placed_ref, slot_gates_ref, cotangent_ref)
    stage.begin()
    fetch.start()

    def add_expert(e, _):
        came = out_ref[e].astype(f32)
        scaled_ref[e] = (came * slot_gates_ref[e]).astype(bf16)
        routed = dot(placed_ref[e], cotangent_ref[...])
        slot_grad = jnp.sum(routed * came, axis=1, keepdims=True)
        turned_ref[pl.ds(e, 1), :] = jnp.sum(
            placed_ref[e].astype(f32) * slot_grad, axis=0, keepdims=True
        )
        return 0

    lax.fori_loop(0, EXP_WIN, add_expert, 0)
    stage.need(placed_t_ref, residual_ref, gates_ref, w_all_ref, normed_ref)
    slots = EXP_WIN * CAP

    def mix(i, _):
        columns = block(i)
        mixed = dot(placed_t_ref[...], scaled_ref[:, :, columns].reshape(slots, TOK_DEV))
        output_ref[:, columns] = (residual_ref[:, columns] + mixed).astype(bf16)
        return 0

    lax.fori_loop(0, width // TOK_DEV, mix, 0)
    stage.put(output_ref)
    gates = gates_ref[...]
    grad_gates = turned_ref[...]
    weighted = jnp.sum(gates * grad_gates, axis=0, keepdims=True)
    grad_logits = (gates * (grad_gates - weighted)).astype(bf16)
    for s, router in enumerate(router_of(w_all_ref)):
        size = router.shape[1]
        sum_ref[:, s * size : (s + 1) * size] = dot(grad_logits, router, ((0,), (0,)))
    grad_router_ref[...] = dot(grad_logits, normed_ref[...])
    fetch.wait()
    move.wait()
    for one in backs:
        one.wait_recv()

    def add_back(i, _):
        columns = block(i)
        sum_ref[:, columns] += dot(
            placed_t_ref[...], back_ref[:, :, columns].reshape(slots, TOK_DEV)
        )
        return 0

    lax.fori_loop(0, width // TOK_DEV, add_back, 0)
    residual = residual_ref[...]
    grad_normed = sum_ref[...]
    scale = lax.rsqrt(jnp.mean(residual * residual, axis=-1, keepdims=True) + epsilon)
    scaled = grad_normed * gain_ref[...].reshape(1, -1)
    inner = jnp.mean(scaled * residual, axis=-1, keepdims=True)
    grad = scale * scaled - residual * (scale * scale * scale * inner)
    grad_gain_ref[...] = jnp.sum(grad_normed * residual * scale, axis=0, keepdims=True)
    grad_residual = cotangent_ref[...].astype(f32) + grad
    grad_residual_ref[...] = grad_residual
    attn_ref[...] = grad_residual.astype(bf16)
    stage.put(grad_residual_ref, attn_ref, grad_router_ref, grad_gain_ref)

    def head_rows(j, _):
        to = lax.rem(me + j, GROUP)
        staged_ref[to] = dot(weight_held[block(to, QW), :], attn_ref[...], ((1,), (1,))).astype(bf16)

        @pl.when(j < GROUP)
        def _():
            copy(staged_ref, heads_ref, h_send, h_recv, j).start()

        return 0

    lax.fori_loop(1, GROUP + 1, head_rows, 0)
    move = pltpu.make_async_copy(staged_ref.at[me], heads_ref.at[me], local.at[2])
    move.start()
    for one in backs:
        one.wait_send()
    for j in range(1, GROUP):
        copy(staged_ref, heads_ref, h_send, h_recv, j).wait()
    move.wait()


def combine_call(
    out, sent_grad, weight, residual, normed, gates, placed, placed_t, slot_gates, cotangent,
    gain, w_all,
):
    rows, width = residual.shape
    slots = (GROUP, CAP, width)
    return staged_call(
        combine_kernel,
        "combine",
        4,
        [
            ("h", out),
            ("a", sent_grad),
            ("a", weight),
            ("l", residual),
            ("l", normed),
            ("l", gates),
            ("h", placed),
            ("l", placed_t),
            ("h", slot_gates),
            ("h", cotangent),
            ("v", gain),
            ("l", w_all),
        ],
        [
            ("h", shape((rows, width), bf16)),
            ("h", shape((rows, width), f32)),
            ("a", shape((GROUP, QW, rows), bf16)),
            ("h", shape((rows, width), bf16)),
            ("h", shape((ROUTER, width), f32)),
            ("h", shape((1, width), f32)),
        ],
        [
            VMEM(slots, bf16),
            VMEM(weight.shape, bf16),
            VMEM((rows, width), f32),
            VMEM((ROUTER, rows), f32),
            VMEM((GROUP, QW, rows), bf16),
            VMEM(slots, bf16),
        ]
        + [DMA((GROUP,))] * 4
        + [DMA((3,))],
    )


def backward_kernel(
    n_blocks, stage, attn_ref, attended_ref, down_ref, heads_ref, o_ref, lse_ref, qt_ref, k_ref,
    kt_ref, v_ref, docs_ref,
    dq_ref, dk_ref, dv_ref, grad_out_ref, down_all_ref,
    part_ref, pair_ref, strip_ref, came_ref, docs_col_ref, delta_ref, dk_acc, dv_acc,
    p_send, p_recv, s_send, s_recv, e_send, e_recv, local,
):
    T = TOK_DEV
    place = Place()
    me = place.me
    first = place.base
    core, side, row = place.near
    across = flip(side, 4)
    met = greet([place.ctx(i) for i in (core, side, row, across)])
    half = GROUP // 2
    depth, strip, width = grad_out_ref.shape
    parity = lax.rem(me, 2)

    def strip_of(n, parity):
        return 2 * n + parity

    def part(n, parity):
        rows = attended_ref[:, strip_of(n, parity)].reshape(depth * strip, T)
        return dot(rows, attn_ref[...])

    def pair_copy(n):
        return remote(
            part_ref.at[n], pair_ref.at[n], p_send.at[n], p_recv.at[n], place.ctx(core)
        )

    def pair_part(n, _):
        part_ref[n] = part(n, 1 - parity).astype(bf16)
        pair_copy(n).start()
        return 0

    down_move = pltpu.make_async_copy(down_ref, down_all_ref.at[me], local.at[0])
    down_spread = Spread(
        place, down_ref, lambda owner: down_all_ref.at[owner], halves(down_ref.shape[0]), e_send, e_recv
    )
    stage.need(attn_ref, attended_ref)
    stage.begin()
    met()
    lax.fori_loop(0, half, pair_part, 0)
    stage.need(down_ref)
    down_spread.start()
    down_move.start()

    heads = range(HEADS)
    parts = [slice(h * HEAD_DIM, (h + 1) * HEAD_DIM) for h in heads]
    stage.need(heads_ref, o_ref)

    def prepare(i, _):
        for h in heads:
            product = o_ref[parts[h], block(i)] * heads_ref[i, parts[h], :].astype(f32)
            delta_ref[i, h : h + 1, :] = jnp.sum(product, axis=0, keepdims=True)
        return 0

    lax.fori_loop(0, GROUP, prepare, 0)
    for n in range(half):
        pair_copy(n).wait_recv()

    def add_pair(n, _):
        strip_ref[n] = (part(n, parity) + pair_ref[n].astype(f32)).astype(bf16)
        return 0

    lax.fori_loop(0, half, add_pair, 0)
    strips = [
        remote(
            strip_ref.at[lax.div(device, 2)], came_ref.at[n], s_send.at[n], s_recv.at[n],
            place.ctx(device),
        )
        for n, device in enumerate((across, side, row))
    ]
    for copy in strips:
        copy.start()

    def turn(i, _):
        docs_col_ref[i] = docs_column(docs_ref[i])
        return 0

    lax.fori_loop(0, n_blocks, turn, 0)
    stage.need(lse_ref, qt_ref, k_ref, kt_ref, v_ref)
    dq_ref[...] = jnp.zeros_like(dq_ref)

    def tile(kb, qb, mask):
        k = k_ref[block(kb), :]
        v = v_ref[block(kb), :]
        kt = kt_ref[:, block(kb)]
        q = [qt_ref[part, block(qb)] for part in parts]
        do = [heads_ref[qb, part, :] for part in parts]
        s = [dot(k, x) for x in q]
        dp = [dot(v, x) for x in do]
        p = [jnp.exp(s[h] - lse_ref[qb, h : h + 1, :]) for h in heads]
        if mask is not None:
            p = [jnp.where(mask, x, 0.0) for x in p]
        ds = [(p[h] * (dp[h] - delta_ref[qb, h : h + 1, :])).astype(bf16) for h in heads]
        pb = [x.astype(bf16) for x in p]
        turn = ((1,), (1,))
        dv_acc[...] += dot(pb[0], do[0], turn) + dot(pb[1], do[1], turn) + dot(pb[2], do[2], turn)
        dk_acc[...] += dot(ds[0], q[0], turn) + dot(ds[1], q[1], turn) + dot(ds[2], q[2], turn)
        for h in heads:
            dq_ref[parts[h], block(qb)] += dot(kt, ds[h])

    def same(kb, gq):
        return docs_col_ref[kb] == docs_ref[gq].astype(f32)

    def k_block(kb, _):
        for at, act in (
            (2, down_spread.step1), (4, down_spread.step2), (7, down_spread.step3),
        ):
            pl.when(kb == first + at)(act)
        dk_acc[...] = jnp.zeros_like(dk_acc)
        dv_acc[...] = jnp.zeros_like(dv_acc)

        @pl.when(kb >= first)
        def _():
            keys = lax.broadcasted_iota(jnp.int32, (T, T), 0)
            queries = lax.broadcasted_iota(jnp.int32, (T, T), 1)
            tile(kb, kb - first, same(kb, kb) & (keys <= queries))

        def q_block(qb, _):
            gq = first + qb
            edge = jnp.logical_or(kb == 0, gq == n_blocks - 1)

            @pl.when(edge)
            def _():
                tile(kb, qb, same(kb, gq))

            @pl.when(jnp.logical_not(edge))
            def _():
                tile(kb, qb, None)

            return 0

        lax.fori_loop(jnp.maximum(kb - first + 1, 0), GROUP, q_block, 0)
        dk_ref[:, block(kb)] = dk_acc[...].T
        dv_ref[:, block(kb)] = dv_acc[...].T
        return 0

    lax.fori_loop(0, first + GROUP, k_block, 0)

    def clear(kb, _):
        dk_ref[:, block(kb)] = jnp.zeros((HEAD_DIM, T), f32)
        dv_ref[:, block(kb)] = jnp.zeros((HEAD_DIM, T), f32)
        return 0

    lax.fori_loop(first + GROUP, n_blocks, clear, 0)
    stage.put(dq_ref, dk_ref, dv_ref)
    for copy in strips:
        copy.wait_recv()
    total = strip_ref[lax.div(me, 2)].astype(f32)
    for n in range(len(strips)):
        total = total + came_ref[n].astype(f32)
    grad_out_ref[...] = total.astype(bf16).reshape(depth, strip, width)
    stage.put(grad_out_ref)
    down_spread.last()
    down_spread.sent()
    for n in range(half):
        pair_copy(n).wait_send()
    for copy in strips:
        copy.wait_send()
    down_move.wait()


def backward_call(attn, attended, down, heads, o, lse, qt, k, kt, v, docs):
    n = k.shape[0] // TOK_DEV
    span = qt.shape[1]
    rows, width = attn.shape
    depth, _, strip, _ = attended.shape
    block_rows = depth * strip
    half = GROUP // 2
    return staged_call(
        functools.partial(backward_kernel, n),
        "backward",
        5,
        [("h", attn), ("h", attended)]
        + [("l", one) for one in (down, heads, o, lse, qt, k, kt, v)]
        + [("v", docs)],
        [
            ("h", shape((QW, span), f32)),
            ("h", shape(kt.shape, f32)),
            ("h", shape(kt.shape, f32)),
            ("h", shape((depth, strip, width), bf16)),
            ("a", shape((GROUP,) + down.shape, bf16)),
        ],
        [
            VMEM((half, block_rows, width), bf16),
            VMEM((half, block_rows, width), bf16),
            VMEM((half, block_rows, width), bf16),
            VMEM((3, block_rows, width), bf16),
            VMEM((n, TOK_DEV, 1), f32),
            VMEM((GROUP, 8, TOK_DEV), f32),
            VMEM((TOK_DEV, HEAD_DIM), f32),
            VMEM((TOK_DEV, HEAD_DIM), f32),
        ]
        + [DMA((half,))] * 2
        + [DMA((3,))] * 2
        + [DMA((Spread.SEMS,))] * 2
        + [DMA((1,))],
    )


def finish_kernel(
    stage, normed_ref, weights_ref, gate_up_ref, grad_out_ref, dq_ref, dk_ref, dv_ref, cos_ref,
    sin_ref, tokens_ref, gain_ref, grad_residual_ref, grad_router_ref, grad_gain2_ref,
    input_grad_ref, shared_ref, small_all_ref, out_all_ref, gate_up_all_ref,
    normed_held, weights_held, linear_ref, came_ref, came_t, sum_ref, part_ref,
    small_ref, head_in, small_in, out_in, shard_ref, small_shard_ref, out_shard_ref,
    g_send, g_recv, h_send, h_recv, s_send, s_recv, o_send, o_recv, e_send, e_recv, f_send, f_recv,
    m_send, m_recv, c_send, c_recv, local,
):
    place = Place()
    me, z, depth = place.me, place.z, place.depth
    met = greet(place.others() + place.layers())
    fetches = [
        pltpu.make_async_copy(normed_ref, normed_held, local.at[0]),
        pltpu.make_async_copy(weights_ref, weights_held, local.at[1]),
    ]
    rows, width = tokens_ref.shape
    size = width // depth

    def spread_of(source, out, send, receive):
        return Spread(
            place, source, lambda owner: out.at[owner], halves(source.shape[0]), send, receive
        )

    expert_spread = spread_of(gate_up_ref, gate_up_all_ref, e_send, e_recv)
    head_spread = spread_of(shard_ref, shared_ref, f_send, f_recv)
    small_spread = spread_of(small_shard_ref, small_all_ref, m_send, m_recv)
    out_spread = spread_of(out_shard_ref, out_all_ref, c_send, c_recv)
    moves = [
        pltpu.make_async_copy(gate_up_ref, gate_up_all_ref.at[me], local.at[3]),
        pltpu.make_async_copy(out_shard_ref, out_all_ref.at[me], local.at[4]),
        pltpu.make_async_copy(shard_ref, shared_ref.at[me], local.at[5]),
        pltpu.make_async_copy(small_shard_ref, small_all_ref.at[me], local.at[6]),
    ]

    def copy(j):
        to = lax.rem(me + j, GROUP)
        return remote(
            linear_ref.at[to], came_ref.at[me], g_send.at[j], g_recv.at[j], place.ctx(to)
        )

    def down(source, target, send, receive, j):
        to = lax.rem(z + j, depth)
        return remote(source.at[to], target.at[z], send.at[j], receive.at[j], place.fsdp(to))

    stage.need(dq_ref, dk_ref, dv_ref, cos_ref, sin_ref)
    stage.begin()
    for fetch in fetches:
        fetch.start()

    def turn_back(j, _):
        to = lax.rem(me + j, GROUP)
        cosine, sine = cos_ref[:, block(to)], -sin_ref[:, block(to)]
        dq = turned(dq_ref[:, block(to)], cosine, sine) * HEAD_DIM ** (-0.5)
        dk = turned(dk_ref[:, block(to)], cosine, sine)
        linear_ref[to, :QW, :] = dq.astype(bf16)
        linear_ref[to, QW : QW + HEAD_DIM, :] = dk.astype(bf16)
        linear_ref[to, QW + HEAD_DIM :, :] = dv_ref[:, block(to)].astype(bf16)
        pl.when(j == 1)(met)

        @pl.when(j < GROUP)
        def _():
            copy(j).start()

        return 0

    lax.fori_loop(1, GROUP + 1, turn_back, 0)
    stage.need(gate_up_ref, grad_out_ref)
    moves[0].start()
    outs = [down(grad_out_ref, out_in, o_send, o_recv, j) for j in range(1, depth)]
    out_in[z] = grad_out_ref[z]
    came_ref[me] = linear_ref[me]
    fetches[0].wait()

    def own_weights(j, _):
        to = lax.rem(z + j, depth)
        columns = block(to, size)
        total = None
        for b in range(GROUP):
            term = dot(linear_ref[b], normed_held[b, :, columns])
            total = term if total is None else total + term
        part_ref[to] = total.astype(bf16)

        @pl.when(j < depth)
        def _():
            down(part_ref, head_in, h_send, h_recv, j).start()

        return 0

    lax.fori_loop(1, depth + 1, own_weights, 0)
    for one in outs:
        one.start()

    def total(ref):
        value = ref[0].astype(f32)
        for s in range(1, depth):
            value = value + ref[s].astype(f32)
        return value.astype(bf16)

    expert_spread.start()
    for j in range(1, GROUP):
        copy(j).wait_send()
    fetches[1].wait()
    for j in range(1, GROUP):
        copy(j).wait_recv()

    def turn(j, _):
        came_t[j] = came_ref[j].T
        return 0

    lax.fori_loop(0, GROUP, turn, 0)

    def add_heads(s, _):
        total = None
        for j in range(GROUP):
            term = dot(came_t[j], weights_held[j, s])
            total = term if total is None else total + term
        sum_ref[:, block(s, size)] = total
        return 0

    lax.fori_loop(0, depth, add_heads, 0)
    stage.need(tokens_ref, grad_residual_ref, grad_router_ref, grad_gain2_ref)
    x = tokens_ref[...].astype(f32)
    grad_normed = sum_ref[...]
    scale = lax.rsqrt(jnp.mean(x * x, axis=-1, keepdims=True) + epsilon)
    scaled = grad_normed * gain_ref[...].reshape(1, -1)
    inner = jnp.mean(scaled * x, axis=-1, keepdims=True)
    grad = scale * scaled - x * (scale * scale * scale * inner)
    input_grad_ref[...] = grad_residual_ref[...] + grad
    stage.put(input_grad_ref)
    gain1 = jnp.sum(grad_normed * x * scale, axis=0, keepdims=True)
    row = lax.broadcasted_iota(jnp.int32, (ROUTER, width), 0)
    small = jnp.where(row == ROUTER - 2, gain1, grad_router_ref[...])
    small = jnp.where(row == ROUTER - 1, grad_gain2_ref[...], small).astype(bf16)
    for s in range(depth):
        small_ref[s] = small[:, s * size : (s + 1) * size]
    smalls = [down(small_ref, small_in, s_send, s_recv, j) for j in range(1, depth)]
    heads = [down(part_ref, head_in, h_send, h_recv, j) for j in range(1, depth)]
    for one in smalls:
        one.start()
    expert_spread.step1()
    head_in[z] = part_ref[z]
    small_in[z] = small_ref[z]

    for one in heads:
        one.wait_recv()
    shard_ref[...] = total(head_in)
    head_spread.start()
    for one in outs:
        one.wait_recv()
    out_shard_ref[...] = total(out_in)
    out_spread.start()
    moves[1].start()
    expert_spread.step2()
    for one in smalls:
        one.wait_recv()
    small_shard_ref[...] = total(small_in)
    small_spread.start()
    moves[2].start()
    moves[3].start()
    expert_spread.step3()
    spreads = (head_spread, out_spread, small_spread)
    for spread in spreads:
        spread.step1()
    for spread in spreads:
        spread.step2()
    for spread in spreads:
        spread.step3()
    for spread in (out_spread, expert_spread, head_spread, small_spread):
        spread.last()
        spread.sent()
    for one in heads + smalls + outs:
        one.wait_send()
    for move in moves:
        move.wait()


def finish_call(
    normed, weights, gate_up, grad_out, dq, dk, dv, cosine, sine, tokens, gain, grad_residual,
    grad_router, grad_gain2,
):
    rows, width = tokens.shape
    depth, strip, _ = grad_out.shape
    size = width // depth
    return staged_call(
        finish_kernel,
        "finish",
        6,
        [
            ("a", normed),
            ("a", weights),
            ("l", gate_up),
            ("l", grad_out),
            ("h", dq),
            ("h", dk),
            ("h", dv),
            ("h", cosine),
            ("h", sine),
            ("l", tokens),
            ("v", gain),
            ("l", grad_residual),
            ("l", grad_router),
            ("l", grad_gain2),
        ],
        [
            ("h", shape((rows, width), f32)),
            ("a", shape((GROUP, HW, size), bf16)),
            ("a", shape((GROUP, ROUTER, size), bf16)),
            ("a", shape((GROUP, strip, width), bf16)),
            ("a", shape((GROUP,) + gate_up.shape, bf16)),
        ],
        [
            VMEM(normed.shape, bf16),
            VMEM(weights.shape, bf16),
            VMEM((GROUP, HW, rows), bf16),
            VMEM((GROUP, HW, rows), bf16),
            VMEM((GROUP, rows, HW), bf16),
            VMEM((rows, width), f32),
            VMEM((depth, HW, size), bf16),
            VMEM((depth, ROUTER, size), bf16),
            VMEM((depth, HW, size), bf16),
            VMEM((depth, ROUTER, size), bf16),
            VMEM((depth, strip, width), bf16),
            VMEM((HW, size), bf16),
            VMEM((ROUTER, size), bf16),
            VMEM((strip, width), bf16),
        ]
        + [DMA((GROUP,))] * 2
        + [DMA((depth,))] * 6
        + [DMA((Spread.SEMS,))] * 8
        + [DMA((7,))],
    )


def output_kernel(
    shared_ref, small_ref, out_ref, gate_up_ref, down_ref, output_ref, input_grad_ref,
    q_ref, k_ref, v_ref, w_out_ref, router_ref, gain1_ref, gain2_ref, gate_ref, up_ref, w_down_ref,
    final_ref, final_grad_ref,
):
    pair, i = shared_ref.shape[0], pl.program_id(0)
    hidden = gate_ref.shape[2]

    def rows(first, last):
        both = [shared_ref[p, first:last, :].astype(f32) for p in range(pair)]
        return jnp.concatenate(both, axis=0).T

    @pl.when(lax.rem(i, pair) == 0)
    def _():
        q_ref[...] = rows(0, QW)
        k_ref[...] = rows(QW, QW + HEAD_DIM)
        v_ref[...] = rows(QW + HEAD_DIM, HW)

    w_out_ref[...] = out_ref[...].astype(f32)
    gate_ref[...] = gate_up_ref[:, :, :hidden].astype(f32)
    up_ref[...] = gate_up_ref[:, :, hidden:].astype(f32)
    w_down_ref[...] = down_ref[...].astype(f32)
    final_ref[...] = output_ref[...]
    final_grad_ref[...] = input_grad_ref[...]

    @pl.when(i == 0)
    def _():
        total = jnp.sum(small_ref[...].astype(f32), axis=0)
        router_ref[...] = total[: router_ref.shape[0], :]
        gain1_ref[...] = total[ROUTER - 2, :]
        gain2_ref[...] = total[ROUTER - 1, :]


def output_call(shared, small, out, gate_up, down, output, input_grad, experts):
    count, _, size = shared.shape
    _, strip, width = out.shape
    hidden = gate_up.shape[2] // 2
    pair = 2
    rows = output.shape[0] // count
    token = pl.BlockSpec((rows, width), lambda i: (i, 0))

    def first(*dims):
        return pl.BlockSpec((1,) + dims, lambda i: (i,) + (0,) * len(dims))

    def columns(columns):
        return pl.BlockSpec((size, columns), lambda i: (0, i // pair))

    def whole(*dims):
        return pl.BlockSpec(dims, lambda i: (0,) * len(dims))

    return pl.pallas_call(
        output_kernel,
        grid=(count,),
        out_shape=(
            shape((size, count * QW), f32),
            shape((size, count * HEAD_DIM), f32),
            shape((size, count * HEAD_DIM), f32),
            shape(out.shape, f32),
            shape((experts, size), f32),
            shape((size,), f32),
            shape((size,), f32),
            shape((count, size, hidden), f32),
            shape((count, size, hidden), f32),
            shape(down.shape, f32),
            shape(output.shape, bf16),
            shape(input_grad.shape, f32),
        ),
        in_specs=[
            pl.BlockSpec((pair,) + shared.shape[1:], lambda i: (i // pair, 0, 0)),
            whole(*small.shape), first(strip, width), first(*gate_up.shape[1:]),
            first(*down.shape[1:]), token, token,
        ],
        out_specs=(
            columns(pair * QW),
            columns(pair * HEAD_DIM),
            columns(pair * HEAD_DIM),
            first(strip, width),
            whole(experts, size),
            whole(size),
            whole(size),
            first(size, hidden),
            first(size, hidden),
            first(*down.shape[1:]),
            token,
            token,
        ),
        compiler_params=params(),
        name="output",
    )(shared, small, out, gate_up, down, output, input_grad)


def rotary_tables(length):
    frequencies = 10000.0 ** (-(np.arange(HEAD_DIM // 2) * 2.0) / HEAD_DIM)
    angles = frequencies[:, None] * np.arange(length)[None, :]
    return np.cos(angles).astype(np.float32), np.sin(angles).astype(np.float32)


def shards(
    tables,
    tokens,
    doc_ids,
    routes,
    slot_order,
    norm1_gain,
    norm2_gain,
    w_query,
    key_matrix,
    value_matrix,
    w_out,
    w_router,
    w_gate,
    w_up,
    w_down,
    cotangent,
):
    rows, width = tokens.shape[1:]
    ctx, depth = lax.axis_size("ctx"), lax.axis_size("fsdp")
    place = lax.axis_index("ctx")
    parts = ctx // GROUP
    head, part = place % GROUP, place // GROUP
    far = [[p * GROUP + i for p in range(parts)] for i in range(GROUP)]
    span = GROUP * rows
    experts = w_router.shape[1]
    hidden = w_gate.shape[2]

    def gather_z(value):
        return lax.all_gather(value, "fsdp", axis=0, tiled=True)

    def reduce_z(value):
        value = lax.psum_scatter(value.astype(bf16), "fsdp", scatter_dimension=0, tiled=True)
        if parts > 1:
            value = lax.psum(value, "ctx", axis_index_groups=far)
        return value

    cosine, sine = tables
    if parts > 1:
        cosine = lax.dynamic_slice_in_dim(cosine, part * span, span, 1)
        sine = lax.dynamic_slice_in_dim(sine, part * span, span, 1)
    own_tokens, own_cotangent = tokens[0], cotangent[0]

    route_rows, order_rows = routes[0].T, slot_order[0].T
    docs, placed, placed_t, tokens_all, w_all, strips, gate_up, down = gather_call(
        own_tokens, w_router.T, doc_ids, route_rows, order_rows, w_query, key_matrix, value_matrix,
        w_out, w_gate, w_up, w_down, depth,
    )
    gate_up, down = gather_z(gate_up), gather_z(down)
    if parts > 1:

        def gather_far(value, axis):
            return lax.all_gather(value, "ctx", axis=axis, axis_index_groups=far, tiled=True)

        normed1, queries, keys_t, values_t, keys, values = project_call(
            tokens_all, norm1_gain, w_all, cosine, sine
        )
        keys, values, docs = gather_far(keys, 0), gather_far(values, 0), gather_far(docs, 0)
        keys_t, values_t = gather_far(keys_t, 1), gather_far(values_t, 1)
        after = attend_call(
            attend_kernel, [w_all, queries, keys, values_t], [], docs, strips, own_tokens, norm2_gain,
            route_rows, placed, w_all, span, [],
        )
    else:
        normed1, queries, keys_t, values_t, keys, values, *after = attend_call(
            attend_after_project, [w_all, tokens_all, cosine, sine], [norm1_gain], docs, strips,
            own_tokens, norm2_gain, route_rows, placed, w_all, span, projected(tokens_all),
        )
    (
        attended_f32, log_total, attended, out_weight, weights_all, residual, normed2, gates,
        slot_gates, rows_out,
    ) = after
    out_weight = out_weight.reshape(width, width)
    sent_rows, sent_grads, gate, up, active, grad_w_down = dispatch_call(
        rows_out, gate_up, placed, own_cotangent, slot_gates
    )
    grad_w_down = reduce_z(grad_w_down)
    expert_out, grad_buffer, grad_w_gate_up = expert_call(
        active, down, sent_grads.reshape(GROUP * CAP, width), sent_rows.reshape(GROUP * CAP, width),
        gate, up, gate_up,
    )
    grad_w_gate_up = reduce_z(grad_w_gate_up)
    output, grad_residual, heads, attn, grad_router, grad_gain2 = combine_call(
        expert_out, grad_buffer.reshape(sent_rows.shape), out_weight,
        residual, normed2, gates, placed, placed_t, slot_gates, own_cotangent, norm2_gain, w_all,
    )
    dq, dk, dv, grad_out, down_w = backward_call(
        attn, attended, grad_w_down, heads, attended_f32, log_total, queries, keys, keys_t, values,
        docs,
    )
    if parts > 1:
        dk = lax.psum_scatter(dk, "ctx", scatter_dimension=1, axis_index_groups=far, tiled=True)
        dv = lax.psum_scatter(dv, "ctx", scatter_dimension=1, axis_index_groups=far, tiled=True)
    input_grad, shared, small, out_w, gate_up_w = finish_call(
        normed1, weights_all, grad_w_gate_up, grad_out, dq, dk, dv, cosine, sine,
        own_tokens, norm1_gain, grad_residual, grad_router, grad_gain2,
    )
    if parts > 1:
        shared, small, out_w = lax.psum((shared, small, out_w), "ctx", axis_index_groups=far)

    (
        q_w, k_w, v_w, out_w, router_w, gain1_w, gain2_w, gate_w, up_w, down_w, output, input_grad
    ) = output_call(shared, small, out_w, gate_up_w, down_w, output, input_grad, experts)
    return (
        output[None],
        input_grad[None],
        gain1_w,
        gain2_w,
        q_w,
        k_w,
        v_w,
        out_w.reshape(-1, width),
        router_w.T,
        gate_w,
        up_w,
        down_w,
    )


def solution(mesh):
    token_spec = P("fsdp", "ctx", None)
    row_spec, expert_spec = P("fsdp", None), P(None, "fsdp", None)
    tables = rotary_tables(mesh.shape["ctx"] * TOK_DEV)

    def program(*arguments):
        return jax.shard_map(
            functools.partial(shards, tuple(jnp.asarray(t) for t in tables)),
            mesh=mesh,
            in_specs=(
                token_spec,
                P("fsdp", "ctx"),
                token_spec,
                token_spec,
                P(),
                P(),
                row_spec,
                row_spec,
                row_spec,
                row_spec,
                row_spec,
                expert_spec,
                expert_spec,
                expert_spec,
                token_spec,
            ),
            out_specs=(
                token_spec,
                token_spec,
                P("fsdp"),
                P("fsdp"),
                row_spec,
                row_spec,
                row_spec,
                row_spec,
                row_spec,
                expert_spec,
                expert_spec,
                expert_spec,
            ),
            check_vma=False,
        )(*arguments)

    return program
```

```python
import functools

import jax
import jax.numpy as jnp
import numpy as np
from jax import lax
from jax.experimental import pallas as pl
from jax.experimental.pallas import tpu as pltpu
from jax.sharding import PartitionSpec as P

QUERY_HEADS = 24
KEY_VALUE_HEADS = 8
HEAD_DIM = 64
TOPK = 8
EXP_WIN = 8
TOK_DEV = 256
CAP = 64
GROUP = 8
HEADS = QUERY_HEADS // KEY_VALUE_HEADS
QW = HEADS * HEAD_DIM
HW = QW + 2 * HEAD_DIM
ROUTER = 48
ALL = HW + ROUTER

NEVER = 4096.0
epsilon = 1e-06
score_masked = -1e30
bf16 = jnp.bfloat16
f32 = jnp.float32
VMEM = pltpu.VMEM
MESH = pl.DeviceIdType.MESH
DMA = pltpu.SemaphoreType.DMA
IN_VMEM = pl.BlockSpec(memory_space=VMEM)
IN_ANY = pl.BlockSpec(memory_space=pl.ANY)


def dot(left, right, dims=((1,), (0,))):
    return lax.dot_general(left, right, (dims, ((), ())), preferred_element_type=f32)


def block(index, size=TOK_DEV):
    return pl.ds(pl.multiple_of(index * size, size), size)


def shape(dims, dtype):
    return jax.ShapeDtypeStruct(dims, dtype)


def params(collective_id=None, limit=56):
    return pltpu.CompilerParams(
        collective_id=collective_id,
        has_side_effects=collective_id is not None,
        vmem_limit_bytes=limit << 20,
    )


class Staged:
    def __init__(self, fetches, later, puts):
        self.fetches, self.later, self.puts, self.out = fetches, later, puts, []

    def begin(self):
        for copy in self.later:
            copy.start()
        self.later = []

    def need(self, *refs):
        for ref in refs:
            self.fetches.pop(id(ref)).wait()

    def put(self, *refs):
        for ref in refs:
            copy = self.puts.pop(id(ref))
            copy.start()
            self.out.append(copy)

    def finish(self):
        self.begin()
        for copy in self.fetches.values():
            copy.wait()
        for copy in self.puts.values():
            copy.start()
        for copy in self.out + list(self.puts.values()):
            copy.wait()


def staged_call(body, name, collective_id, ins, outs, scratch):
    held_in = [i for i, (how, _) in enumerate(ins) if how in "hl"]
    held_out = [i for i, (how, _) in enumerate(outs) if how == "h"]

    def kernel(*refs):
        refs = list(refs)
        given, refs = refs[: len(ins)], refs[len(ins) :]
        results, refs = refs[: len(outs)], refs[len(outs) :]
        own, refs = refs[: len(scratch)], refs[len(scratch) :]
        in_held, refs = refs[: len(held_in)], refs[len(held_in) :]
        out_held, (in_sems, out_sems) = refs[: len(held_out)], refs[len(held_out) :]
        fetches, later, puts = {}, [], {}
        for n, i in enumerate(held_in):
            copy = pltpu.make_async_copy(given[i], in_held[n], in_sems.at[n])
            if ins[i][0] == "l":
                later.append(copy)
            else:
                copy.start()
            given[i] = in_held[n]
            fetches[id(given[i])] = copy
        for n, i in enumerate(held_out):
            puts[id(out_held[n])] = pltpu.make_async_copy(out_held[n], results[i], out_sems.at[n])
            results[i] = out_held[n]
        stage = Staged(fetches, later, puts)
        body(stage, *given, *results, *own)
        stage.finish()

    return pl.pallas_call(
        kernel,
        out_shape=tuple(one for _, one in outs),
        in_specs=[IN_VMEM if how == "v" else IN_ANY for how, _ in ins],
        out_specs=tuple(IN_VMEM if how == "v" else IN_ANY for how, _ in outs),
        scratch_shapes=list(scratch)
        + [VMEM(ins[i][1].shape, ins[i][1].dtype) for i in held_in]
        + [VMEM(outs[i][1].shape, outs[i][1].dtype) for i in held_out]
        + [DMA((max(len(held_in), 1),)), DMA((max(len(held_out), 1),))],
        compiler_params=params(collective_id),
        name=name,
    )(*(array for _, array in ins))


def flip(index, bit):
    return index + (1 - 2 * ((index // bit) % 2)) * bit


class Place:
    def __init__(self):
        ctx = lax.axis_index("ctx")
        self.base = (ctx // GROUP) * GROUP
        self.me = ctx - self.base
        self.z = lax.axis_index("fsdp")
        self.depth = lax.axis_size("fsdp")
        self.near = [flip(self.me, bit) for bit in (1, 2, 4)]

    def ctx(self, index):
        return {"ctx": self.base + index}

    def fsdp(self, index):
        return {"fsdp": index}

    def others(self):
        return [self.ctx(lax.rem(self.me + j, GROUP)) for j in range(1, GROUP)]

    def layers(self):
        return [self.fsdp(lax.rem(self.z + j, self.depth)) for j in range(1, self.depth)]


def greet(devices):
    ready = pltpu.get_barrier_semaphore()
    for device in devices:
        pl.semaphore_signal(ready, inc=1, device_id=device, device_id_type=MESH)
    return lambda: pl.semaphore_wait(ready, len(devices))


def remote(source, target, send, receive, device):
    return pltpu.make_async_remote_copy(
        src_ref=source,
        dst_ref=target,
        send_sem=send,
        recv_sem=receive,
        device_id=device,
        device_id_type=MESH,
    )


def halves(count):
    cut = -(-count // 32) * 16

    def part(ref, half):
        return ref.at[pl.ds(0, cut)] if half == 0 else ref.at[pl.ds(cut, count - cut)]

    return part


class Spread:
    SEMS = 14

    def __init__(self, place, source, land, part, send, receive):
        me = place.me
        core, side, row = place.near
        across = flip(side, 4)

        def plan(slot, owner, half, device):
            target = part(land(owner), half)
            first = part(source, half) if slot < 6 else target
            return remote(first, target, send.at[slot], receive.at[slot], place.ctx(device))

        self.copies = [
            plan(0, me, 0, side), plan(1, me, 1, side), plan(2, me, 0, row), plan(3, me, 1, row),
            plan(4, me, 0, core), plan(5, me, 1, core), plan(6, side, 0, core),
            plan(7, side, 1, core), plan(8, row, 0, core), plan(9, row, 1, core),
            plan(10, side, 1, row), plan(11, row, 0, side), plan(12, across, 0, core),
            plan(13, across, 1, core),
        ]

    def go(self, *slots):
        for slot in slots:
            self.copies[slot].start()

    def wait(self, *slots):
        for slot in slots:
            self.copies[slot].wait_recv()

    def start(self):
        self.go(1, 2, 0, 3, 4, 5)

    def step1(self):
        self.wait(1)
        self.go(10, 7)
        self.wait(2)
        self.go(11, 8)

    def step2(self):
        self.wait(0)
        self.go(6)
        self.wait(3)
        self.go(9)

    def step3(self):
        self.wait(10)
        self.go(13)
        self.wait(11)
        self.go(12)

    def sent(self):
        for copy in self.copies:
            copy.wait_send()

    def last(self):
        self.wait(4, 5, 6, 7, 8, 9, 12, 13)


class Line:
    def __init__(self, place, land, send, receive):
        self.z, self.depth = place.z, place.depth
        z, most = self.z, place.depth - 1
        ways = ((jnp.minimum(z + 1, most), -1), (jnp.maximum(z - 1, 0), 1))
        self.copies = []
        for way, (device, sign) in enumerate(ways):
            self.copies.append([])
            for step in range(most):
                held = land(jnp.clip(z + sign * step, 0, most))
                self.copies[way].append(
                    remote(
                        held, held, send.at[way, step], receive.at[way, step], place.fsdp(device)
                    )
                )

    def each(self, step):
        z, most = self.z, self.depth - 1
        up, down = self.copies
        at = min(step, most - 1)
        return ((z + 1 <= most, z - step >= 0, up[at]), (z - 1 >= 0, z + step <= most, down[at]))

    def start(self):
        for open_way, _, copy in self.each(0):
            pl.when(open_way)(copy.start)

    def step(self, step):
        before = self.each(step - 1)
        for (open_way, here, copy), (_, _, came) in zip(self.each(step), before):
            pl.when(here)(came.wait_recv)
            if step < self.depth - 1:
                pl.when(jnp.logical_and(open_way, here))(copy.start)

    def last(self):
        self.step(self.depth - 1)

    def sent(self):
        for step in range(self.depth - 1):
            for open_way, here, copy in self.each(step):
                pl.when(jnp.logical_and(open_way, here))(copy.wait_send)


def place_slots(routes_ref, order_ref, placed_ref):
    rows = routes_ref.shape[1]
    expert = lax.broadcasted_iota(jnp.int32, (EXP_WIN, rows), 0)
    priority = jnp.full((EXP_WIN, rows), NEVER, f32)
    for k in range(TOPK):
        pick = expert == routes_ref[k : k + 1, :]
        priority = jnp.where(pick, order_ref[k : k + 1, :].astype(f32), priority)
    priority_turned = priority.T
    slot = lax.broadcasted_iota(jnp.int32, (CAP, rows), 0).astype(f32)
    for e in range(EXP_WIN):
        mine = priority[e : e + 1, :]
        before = jnp.where(priority_turned[:, e : e + 1] < mine, 1.0, 0.0)
        before = jnp.sum(before, axis=0, keepdims=True)
        placed = (slot == before) & (mine < NEVER)
        placed_ref[e] = jnp.where(placed, 1.0, 0.0).astype(bf16)


def gather_kernel(
    stage, tokens_ref, router_ref, docs_ref, routes_ref, order_ref, w_query_ref,
    key_matrix_ref, value_matrix_ref, w_out_ref, w_gate_ref, w_up_ref, w_down_ref,
    docs_all_ref, placed_ref, turned_ref, tokens_all_ref, w_all_ref, strips_ref, gate_up_ref, down_ref,
    held_ref, query_held, key_held, value_held,
    w_send, w_recv, o_send, o_recv, d_send, d_recv, c_send, c_recv, local,
):
    place = Place()
    me, z = place.me, place.z
    met = greet(place.others() + place.layers())
    odd = lax.rem(me, 2)
    pair = lax.div(me, 2)
    depth, strip, _ = strips_ref.shape

    def window(first, size):
        return pl.ds(pl.multiple_of(first * 128, 128), size)

    fetches = [
        pltpu.make_async_copy(
            w_query_ref.at[:, window(pair * 3 + odd, 2 * 128)], query_held, local.at[0]
        ),
        pltpu.make_async_copy(key_matrix_ref.at[:, window(pair, 128)], key_held, local.at[1]),
        pltpu.make_async_copy(value_matrix_ref.at[:, window(pair, 128)], value_held, local.at[2]),
        pltpu.make_async_copy(
            w_out_ref.at[pl.ds(pl.multiple_of(me * strip, strip), strip), :], strips_ref.at[z],
            local.at[3],
        ),
        pltpu.make_async_copy(tokens_ref, held_ref, local.at[4]),
    ]
    hidden = w_gate_ref.shape[2]
    shards = [
        pltpu.make_async_copy(w_gate_ref.at[me], gate_up_ref.at[:, pl.ds(0, hidden)], local.at[5]),
        pltpu.make_async_copy(w_up_ref.at[me], gate_up_ref.at[:, pl.ds(hidden, hidden)], local.at[6]),
        pltpu.make_async_copy(w_down_ref.at[me], down_ref, local.at[7]),
    ]
    for fetch in fetches:
        fetch.start()
    met()
    spread = Spread(
        place, tokens_ref, lambda owner: tokens_all_ref.at[owner], halves(TOK_DEV), c_send, c_recv
    )
    spread.start()
    lines = [
        Line(place, lambda layer: strips_ref.at[layer], o_send, o_recv),
        Line(place, lambda layer: w_all_ref.at[layer], w_send, w_recv),
    ]
    fetches[3].wait()
    lines[0].start()
    for fetch in fetches[:3] + fetches[4:]:
        fetch.wait()

    def half(held, columns):
        turned_rows = held[...].T
        return jnp.where(odd == 1, turned_rows[HEAD_DIM:], turned_rows[:columns])

    own = w_all_ref.at[z]
    own[:QW, :] = half(query_held, QW)
    own[QW : QW + HEAD_DIM, :] = half(key_held, HEAD_DIM)
    own[QW + HEAD_DIM : HW, :] = half(value_held, HEAD_DIM)
    router = router_ref[...].astype(f32)
    empty = jnp.zeros((ROUTER - router.shape[0], router.shape[1]), f32)
    own[HW:, :] = jnp.concatenate([router, empty], axis=0).astype(bf16)
    lines[1].start()
    for shard in shards:
        shard.start()
    docs_all_ref[me] = docs_ref[...]
    sent = []
    for j, device in enumerate(place.others()):
        sent.append(remote(docs_ref, docs_all_ref.at[me], d_send.at[j], d_recv.at[j], device))
    for copy in sent:
        copy.start()
    move = pltpu.make_async_copy(held_ref, tokens_all_ref.at[me], local.at[8])
    move.start()
    place_slots(routes_ref, order_ref, placed_ref)
    turned_ref[...] = placed_ref[...].reshape(EXP_WIN * CAP, -1).T
    stage.put(placed_ref, turned_ref)
    for shard in shards:
        shard.wait()
    stage.put(gate_up_ref, down_ref)
    steps = (spread.step1, spread.step2)
    for step in range(1, depth - 1):
        for act in steps[step - 1 : step]:
            act()
        for line in lines:
            line.step(step)
    for act in steps[depth - 2 :]:
        act()
    spread.step3()
    for line in lines:
        line.last()
    stage.put(w_all_ref, strips_ref)
    spread.last()
    for copy in sent:
        copy.wait()
    move.wait()
    for line in lines:
        line.sent()
    spread.sent()


def gather_call(
    tokens, router, docs, routes, order, w_query, key_matrix, value_matrix, w_out, w_gate, w_up, w_down,
    depth,
):
    rows, width = tokens.shape
    strip = w_out.shape[0] // GROUP
    size = w_query.shape[0]
    return staged_call(
        gather_kernel,
        "gather",
        1,
        [
            ("a", tokens),
            ("v", router),
            ("v", docs),
            ("v", routes),
            ("v", order),
            ("a", w_query),
            ("a", key_matrix),
            ("a", value_matrix),
            ("a", w_out),
            ("a", w_gate),
            ("a", w_up),
            ("a", w_down),
        ],
        [
            ("v", shape((GROUP,) + docs.shape, jnp.int32)),
            ("h", shape((EXP_WIN, CAP, rows), bf16)),
            ("h", shape((rows, EXP_WIN * CAP), bf16)),
            ("a", shape((GROUP, rows, width), bf16)),
            ("h", shape((depth, ALL, size), bf16)),
            ("h", shape((depth, strip, width), bf16)),
            ("h", shape((w_gate.shape[1], 2 * w_gate.shape[2]), bf16)),
            ("h", shape(w_down.shape[1:], bf16)),
        ],
        [
            VMEM((rows, width), bf16),
            VMEM((size, 2 * 128), bf16),
            VMEM((size, 128), bf16),
            VMEM((size, 128), bf16),
        ]
        + [DMA((2, depth - 1))] * 4
        + [DMA((GROUP - 1,))] * 2
        + [DMA((Spread.SEMS,))] * 2
        + [DMA((9,))],
    )


def turned(values, cosine, sine):
    half = HEAD_DIM // 2
    out = []
    for at in range(0, values.shape[0], HEAD_DIM):
        low, high = values[at : at + half], values[at + half : at + HEAD_DIM]
        out += [low * cosine - high * sine, high * cosine + low * sine]
    return jnp.concatenate(out, axis=0)


def project_block(
    owner, tokens_ref, gain_ref, w_all_ref, cos_ref, sin_ref,
    normed_ref, qt_ref, kt_ref, vt_ref, k_ref, v_ref,
):
    x = tokens_ref[owner].astype(f32)
    scale = lax.rsqrt(jnp.mean(x * x, axis=-1, keepdims=True) + epsilon)
    normed_ref[owner] = (x * scale * gain_ref[...].reshape(1, -1)).astype(bf16)
    linear = None
    for s in range(w_all_ref.shape[0]):
        size = w_all_ref.shape[2]
        term = dot(
            w_all_ref[s, :HW, :], normed_ref[owner, :, s * size : (s + 1) * size], ((1,), (1,))
        )
        linear = term if linear is None else linear + term
    tokens = block(owner)
    cosine, sine = cos_ref[:, tokens], sin_ref[:, tokens]
    queries = turned(linear[:QW], cosine, sine) * HEAD_DIM ** (-0.5)
    qt_ref[:, tokens] = queries.astype(bf16)
    keys = turned(linear[QW : QW + HEAD_DIM], cosine, sine)
    kt_ref[:, tokens] = keys.astype(bf16)
    k_ref[tokens, :] = keys.T.astype(bf16)
    values = linear[QW + HEAD_DIM :]
    vt_ref[:, tokens] = values.astype(bf16)
    v_ref[tokens, :] = values.T.astype(bf16)


def projected(tokens):
    span = tokens.shape[0] * tokens.shape[1]
    return [
        ("h", shape(tokens.shape, bf16)),
        ("h", shape((QW, span), bf16)),
        ("h", shape((HEAD_DIM, span), bf16)),
        ("h", shape((HEAD_DIM, span), bf16)),
        ("h", shape((span, HEAD_DIM), bf16)),
        ("h", shape((span, HEAD_DIM), bf16)),
    ]


def project_kernel(stage, tokens_ref, gain_ref, w_all_ref, cos_ref, sin_ref, *outs):
    stage.need(tokens_ref, w_all_ref, cos_ref, sin_ref)

    def project(i, _):
        project_block(i, tokens_ref, gain_ref, w_all_ref, cos_ref, sin_ref, *outs)
        return 0

    lax.fori_loop(0, GROUP, project, 0)


def project_call(tokens, gain, w_all, cosine, sine):
    return staged_call(
        project_kernel,
        "project",
        None,
        [("h", tokens), ("v", gain), ("h", w_all), ("h", cosine), ("h", sine)],
        projected(tokens),
        [],
    )


def docs_column(row):
    return jnp.broadcast_to(row.astype(f32), (8, row.shape[1])).T[:, :1]


def attend_after_project(
    n_blocks, stage, w_all_ref, tokens_ref, cos_ref, sin_ref, gain_ref, *rest,
):
    given, outs, rest = rest[:6], rest[6:12], rest[12:]
    _, qt_ref, _, vt_ref, k_ref, _ = outs

    def project_all():
        stage.need(tokens_ref, cos_ref, sin_ref)

        def project(i, _):
            project_block(i, tokens_ref, gain_ref, w_all_ref, cos_ref, sin_ref, *outs)
            return 0

        lax.fori_loop(0, GROUP, project, 0)
        stage.put(*outs)

    attend_body(n_blocks, stage, project_all, w_all_ref, qt_ref, k_ref, vt_ref, *given, *rest)


def attend_kernel(n_blocks, stage, w_all_ref, qt_ref, k_ref, vt_ref, *rest):
    def fetch_all():
        stage.need(qt_ref, k_ref, vt_ref)

    attend_body(n_blocks, stage, fetch_all, w_all_ref, qt_ref, k_ref, vt_ref, *rest)


def router_of(w_all_ref):
    return [w_all_ref[s, HW:, :] for s in range(w_all_ref.shape[0])]


def attend_body(
    n_blocks, stage, prepare, w_all_ref, qt_ref, k_ref, vt_ref,
    docs_ref, strips_ref, tokens_ref, gain_ref, routes_ref, placed_ref,
    o_ref, lse_ref, attended_ref, out_weight_ref, weights_ref, residual_ref, normed2_ref, gates_ref,
    slot_gates_ref, rows_ref,
    staged_ref, docs_col_ref, top_ref, sum_ref, acc_ref, mixed_ref,
    a_send, a_recv, s_send, s_recv, w_send, w_recv, local,
):
    T = TOK_DEV
    place = Place()
    me, z = place.me, place.z
    first = place.base
    met = greet(place.others())
    depth, strip, _ = strips_ref.shape
    move = pltpu.make_async_copy(w_all_ref.at[:, :HW], weights_ref.at[me], local.at[1])

    def layers(ref, h):
        return ref.at[pl.ds(h * (depth // 2), depth // 2)]

    weights = Spread(
        place, w_all_ref.at[:, :HW], lambda owner: weights_ref.at[owner], layers, w_send, w_recv
    )
    strips = Spread(
        place, strips_ref, lambda owner: out_weight_ref.at[:, owner], layers, s_send, s_recv
    )
    def turn(i, _):
        docs_col_ref[i] = docs_column(docs_ref[i])
        return 0

    lax.fori_loop(0, n_blocks, turn, 0)
    stage.need(strips_ref)
    stage.begin()
    met()
    strips.start()
    out_weight_ref[:, me] = strips_ref[...]
    stage.need(w_all_ref)
    move.start()
    weights.start()
    prepare()

    def tile(kb, qb, mask):
        kt = k_ref[block(kb), :]
        vt = vt_ref[:, block(kb)]
        heads = range(HEADS)
        parts = [slice(h * HEAD_DIM, (h + 1) * HEAD_DIM) for h in heads]
        s = [dot(kt, qt_ref[parts[h], block(qb)]) for h in heads]
        if mask is not None:
            s = [jnp.where(mask, x, score_masked) for x in s]
        old = [top_ref[h : h + 1, :] for h in heads]
        new = [jnp.maximum(old[h], jnp.max(s[h], axis=0, keepdims=True)) for h in heads]
        p = [jnp.exp(s[h] - new[h]) for h in heads]
        factor = [jnp.exp(old[h] - new[h]) for h in heads]
        total = [
            sum_ref[h : h + 1, :] * factor[h] + jnp.sum(p[h], axis=0, keepdims=True) for h in heads
        ]
        mixed = [acc_ref[parts[h], :] * factor[h] + dot(vt, p[h].astype(bf16)) for h in heads]
        for h in heads:
            top_ref[h : h + 1, :] = new[h]
            sum_ref[h : h + 1, :] = total[h]
            acc_ref[parts[h], :] = mixed[h]

    def same(kb, gq):
        return docs_col_ref[kb] == docs_ref[gq].astype(f32)

    def head_rows(head):
        per = GROUP * depth // GROUP
        return attended_ref.at[lax.div(head * depth, GROUP), pl.ds(lax.rem(head * depth, GROUP), per)]

    def attended_copy(to, slot):
        return remote(
            staged_ref.at[to], head_rows(slot), a_send.at[to], a_recv.at[slot], place.ctx(to)
        )

    def q_block(j, _):
        for at, act in ((1, strips.step1), (2, strips.step2), (5, strips.step3)):
            pl.when(j == at)(act)
        qb = jnp.where(j < GROUP // 2, GROUP - 1 - 2 * j, 2 * GROUP - 2 - 2 * j)
        gq = first + qb
        top_ref[...] = jnp.full_like(top_ref, score_masked)
        sum_ref[...] = jnp.ones_like(sum_ref)
        acc_ref[...] = jnp.zeros_like(acc_ref)
        last = gq == n_blocks - 1

        def k_block(kb, _):
            edge = jnp.logical_or(kb == 0, last)

            @pl.when(edge)
            def _():
                tile(kb, qb, same(kb, gq))

            @pl.when(jnp.logical_not(edge))
            def _():
                tile(kb, qb, None)

            return 0

        lax.fori_loop(0, gq, k_block, 0)
        keys = lax.broadcasted_iota(jnp.int32, (T, T), 0)
        queries = lax.broadcasted_iota(jnp.int32, (T, T), 1)
        tile(gq, qb, same(gq, gq) & (keys <= queries))
        lse_ref[qb] = top_ref[...] + jnp.log(sum_ref[...])
        for h in range(HEADS):
            part = slice(h * HEAD_DIM, (h + 1) * HEAD_DIM)
            acc_ref[part, :] = acc_ref[part, :] / sum_ref[h : h + 1, :]
        o_ref[:, block(qb)] = acc_ref[...]
        staged_ref[qb] = acc_ref[...].astype(bf16).reshape(depth, strip, T)

        @pl.when(qb != me)
        def _():
            attended_copy(qb, me).start()

        return 0

    lax.fori_loop(0, GROUP, q_block, 0)
    stage.put(o_ref, lse_ref)
    own = pltpu.make_async_copy(staged_ref.at[me], head_rows(me), local.at[2])
    own.start()
    own.wait()
    weights.step1()
    weights.step2()
    for j in range(1, GROUP):
        other = lax.rem(me + j, GROUP)
        attended_copy(other, other).wait()
    stage.put(attended_ref)
    strips.last()
    stage.put(out_weight_ref)

    rows, width = tokens_ref.shape
    stage.need(tokens_ref, placed_ref)
    mixed_ref[...] = attended_ref[...].reshape(width, rows).T

    def out_columns(i, _):
        columns = block(i)
        weight = out_weight_ref[:, :, :, columns].reshape(width, T)
        residual_ref[:, columns] = tokens_ref[:, columns].astype(f32) + dot(mixed_ref[...], weight)
        return 0

    lax.fori_loop(0, width // T, out_columns, 0)
    residual = residual_ref[...]
    scale = lax.rsqrt(jnp.mean(residual * residual, axis=-1, keepdims=True) + epsilon)
    normed2_ref[...] = (residual * scale * gain_ref[...].reshape(1, -1)).astype(bf16)
    stage.put(residual_ref, normed2_ref)
    logits = None
    for s, router in enumerate(router_of(w_all_ref)):
        size = router.shape[1]
        term = dot(router, normed2_ref[:, s * size : (s + 1) * size], ((1,), (1,)))
        logits = term if logits is None else logits + term
    expert = lax.broadcasted_iota(jnp.int32, gates_ref.shape, 0)
    chosen = expert < 0
    for k in range(TOPK):
        chosen = chosen | (expert == routes_ref[k : k + 1, :])
    logits = jnp.where(chosen, logits, score_masked)
    top = jnp.max(logits, axis=0, keepdims=True)
    gates = jnp.where(chosen, jnp.exp(logits - top), 0.0)
    gates = gates / jnp.sum(gates, axis=0, keepdims=True)
    gates_ref[...] = gates
    for e in range(EXP_WIN):
        slot_gates_ref[e] = jnp.sum(
            placed_ref[e].astype(f32) * gates[e : e + 1, :], axis=1, keepdims=True
        )

    def pick_rows(e, _):
        rows_ref[e] = dot(placed_ref[e], normed2_ref[...]).astype(bf16)
        return 0

    lax.fori_loop(0, EXP_WIN, pick_rows, 0)
    stage.put(gates_ref, slot_gates_ref, rows_ref)
    weights.step3()
    weights.last()
    weights.sent()
    strips.sent()
    move.wait()


def attend_call(
    kernel, ins, gains, docs, strips, tokens, gain, routes, placed, w_all, span, projections
):
    n = docs.shape[0]
    rows, width = tokens.shape
    depth, _, size = w_all.shape
    strip = strips.shape[1]
    return staged_call(
        functools.partial(kernel, n),
        "attend",
        2,
        [("l", one) for one in ins]
        + [("v", one) for one in gains]
        + [("v", docs), ("h", strips), ("l", tokens), ("v", gain), ("v", routes), ("l", placed)],
        projections
        + [
            ("h", shape((QW, span), f32)),
            ("h", shape((GROUP, 8, TOK_DEV), f32)),
            ("h", shape((depth, GROUP, strip, TOK_DEV), bf16)),
            ("h", shape((depth, GROUP) + strips.shape[1:], bf16)),
            ("a", shape((GROUP, depth, HW, size), bf16)),
            ("h", shape((rows, width), f32)),
            ("h", shape((rows, width), bf16)),
            ("h", shape((ROUTER, rows), f32)),
            ("h", shape((EXP_WIN, CAP, 1), f32)),
            ("h", shape((EXP_WIN, CAP, width), bf16)),
        ],
        [
            VMEM((GROUP, depth, strip, TOK_DEV), bf16),
            VMEM((n, TOK_DEV, 1), f32),
            VMEM((8, TOK_DEV), f32),
            VMEM((8, TOK_DEV), f32),
            VMEM((QW, TOK_DEV), f32),
            VMEM((rows, width), bf16),
        ]
        + [DMA((GROUP,))] * 2
        + [DMA((Spread.SEMS,))] * 4
        + [DMA((3,))],
    )


def dispatch_kernel(
    stage, sent_rows_ref, gate_up_ref, placed_ref, cotangent_ref, slot_gates_ref,
    rows_ref, grads_ref, gate_ref, up_ref, active_ref, grad_down_ref,
    gate_up_held, own_grads, r_send, r_recv, g_send, g_recv, local,
):
    place = Place()
    me = place.me
    met = greet(place.others())
    width = cotangent_ref.shape[1]

    def copy(source, target, send, receive, j):
        to = lax.rem(me + j, GROUP)
        return remote(source.at[to], target.at[me], send.at[j], receive.at[j], place.ctx(to))

    met()
    for j in range(1, GROUP):
        copy(sent_rows_ref, rows_ref, r_send, r_recv, j).start()
    own = pltpu.make_async_copy(sent_rows_ref.at[me], rows_ref.at[me], local.at[0])
    own.start()
    fetch = pltpu.make_async_copy(gate_up_ref, gate_up_held, local.at[1])
    fetch.start()
    stage.need(placed_ref, cotangent_ref, slot_gates_ref)

    def send_grads(n, _):
        j = GROUP - n
        to = lax.rem(me + j, GROUP)
        routed = dot(placed_ref[to], cotangent_ref[...])
        own_grads[to] = (routed * slot_gates_ref[to]).astype(bf16)

        @pl.when(j > 0)
        def _():
            copy(own_grads, grads_ref, g_send, g_recv, j).start()

        return 0

    lax.fori_loop(1, GROUP + 1, send_grads, 0)
    grads_ref[me] = own_grads[me]
    fetch.wait()
    own.wait()
    for j in range(1, GROUP):
        copy(sent_rows_ref, rows_ref, r_send, r_recv, j).wait_recv()
    stage.put(rows_ref)
    slots = GROUP * CAP
    hidden = gate_ref.shape[1]
    tiles = hidden // TOK_DEV

    def expert_up(i, _):
        came = rows_ref[...].reshape(slots, width)
        gate = dot(came, gate_up_held[:, block(i)])
        up = dot(came, gate_up_held[:, block(tiles + i)])
        gate_ref[:, block(i)] = gate
        up_ref[:, block(i)] = up
        active_ref[:, block(i)] = (gate * jax.nn.sigmoid(gate) * up).astype(bf16)
        return 0

    lax.fori_loop(0, tiles, expert_up, 0)
    stage.put(gate_ref, up_ref, active_ref)
    for j in range(1, GROUP):
        copy(own_grads, grads_ref, g_send, g_recv, j).wait_recv()
    stage.put(grads_ref)

    def expert_over(i, _):
        grad_down_ref[:, block(i)] = dot(
            active_ref[...], grads_ref[:, :, block(i)].reshape(slots, TOK_DEV), ((0,), (0,))
        ).astype(bf16)
        return 0

    lax.fori_loop(0, width // TOK_DEV, expert_over, 0)
    stage.put(grad_down_ref)
    for j in range(1, GROUP):
        copy(sent_rows_ref, rows_ref, r_send, r_recv, j).wait_send()
        copy(own_grads, grads_ref, g_send, g_recv, j).wait_send()


def dispatch_call(sent_rows, gate_up, placed, cotangent, slot_gates):
    slots = sent_rows.shape
    count, width = GROUP * CAP, slots[2]
    hidden = gate_up.shape[1] // 2
    return staged_call(
        dispatch_kernel,
        "dispatch",
        3,
        [
            ("a", sent_rows),
            ("a", gate_up),
            ("h", placed),
            ("h", cotangent),
            ("h", slot_gates),
        ],
        [
            ("h", shape(slots, bf16)),
            ("h", shape(slots, bf16)),
            ("h", shape((count, hidden), f32)),
            ("h", shape((count, hidden), f32)),
            ("h", shape((count, hidden), bf16)),
            ("h", shape((hidden, width), bf16)),
        ],
        [VMEM(gate_up.shape, bf16), VMEM(slots, bf16)] + [DMA((GROUP,))] * 4 + [DMA((2,))],
    )


def expert_kernel(
    stage, active_ref, down_ref, grads_ref, rows_ref, gate_ref, up_ref, gate_up_ref,
    out_ref, back_ref, grad_gate_up_ref,
    grads_held, rows_held, gate_up_held, own_ref, grad_ref, send, receive, local,
):
    place = Place()
    me = place.me
    met = greet(place.others())
    fetches = [
        pltpu.make_async_copy(grads_ref, grads_held, local.at[0]),
        pltpu.make_async_copy(rows_ref, rows_held, local.at[1]),
        pltpu.make_async_copy(gate_up_ref, gate_up_held, local.at[2]),
    ]
    count, hidden = active_ref.shape
    width = down_ref.shape[1]
    T = TOK_DEV
    tiles = hidden // T

    def copy(j, half):
        to = lax.rem(me + j, GROUP)
        columns = pl.ds(half * (width // 2), width // 2)
        return remote(
            own_ref.at[to, :, columns], out_ref.at[me, :, columns], send.at[half, j],
            receive.at[half, j], place.ctx(to),
        )

    stage.need(active_ref, down_ref)
    for fetch in fetches:
        fetch.start()
    stage.begin()

    def out(i, _):
        value = dot(active_ref[...], down_ref[:, block(i)]).astype(bf16)
        own_ref[:, :, block(i)] = value.reshape(GROUP, CAP, T)
        return 0

    for half in range(2):
        tiles_half = width // T // 2
        lax.fori_loop(half * tiles_half, (half + 1) * tiles_half, out, 0)
        if half == 0:
            met()
        for j in range(1, GROUP):
            copy(j, half).start()
    move = pltpu.make_async_copy(own_ref.at[me], out_ref.at[me], local.at[3])
    move.start()
    fetches[0].wait()
    stage.need(gate_ref, up_ref)

    def back(i, _):
        grad = dot(grads_held[...], down_ref[block(i), :], ((1,), (1,)))
        gate, up = gate_ref[:, block(i)], up_ref[:, block(i)]
        sigmoid = jax.nn.sigmoid(gate)
        grad_gate = grad * up * sigmoid * (1.0 + gate * (1.0 - sigmoid))
        grad_ref[:, block(i)] = grad_gate.astype(bf16)
        grad_ref[:, block(tiles + i)] = (grad * gate * sigmoid).astype(bf16)
        return 0

    lax.fori_loop(0, tiles, back, 0)
    fetches[1].wait()
    fetches[2].wait()

    def over(i, _):
        grad_gate_up_ref[block(i), :] = dot(
            rows_held[:, block(i)], grad_ref[...], ((0,), (0,))
        ).astype(bf16)
        back_ref[:, block(i)] = dot(
            grad_ref[...], gate_up_held[block(i), :], ((1,), (1,))
        ).astype(bf16)
        return 0

    lax.fori_loop(0, width // T, over, 0)
    stage.put(back_ref, grad_gate_up_ref)
    for half in range(2):
        for j in range(1, GROUP):
            copy(j, half).wait()
    move.wait()


def expert_call(active, down, grads, rows, gate, up, gate_up):
    count, width = rows.shape
    hidden = down.shape[0]
    slots = (GROUP, CAP, width)
    return staged_call(
        expert_kernel,
        "expert",
        7,
        [
            ("h", active),
            ("h", down),
            ("a", grads),
            ("a", rows),
            ("l", gate),
            ("l", up),
            ("a", gate_up),
        ],
        [
            ("a", shape(slots, bf16)),
            ("h", shape((count, width), bf16)),
            ("h", shape((width, 2 * hidden), bf16)),
        ],
        [
            VMEM(grads.shape, bf16),
            VMEM(rows.shape, bf16),
            VMEM(gate_up.shape, bf16),
            VMEM(slots, bf16),
            VMEM((count, 2 * hidden), bf16),
            DMA((2, GROUP)),
            DMA((2, GROUP)),
            DMA((4,)),
        ],
    )


def combine_kernel(
    stage, out_ref, sent_grad_ref, weight_ref, residual_ref, normed_ref, gates_ref, placed_ref,
    placed_t_ref, slot_gates_ref, cotangent_ref, gain_ref, w_all_ref,
    output_ref, grad_residual_ref, heads_ref, attn_ref, grad_router_ref, grad_gain_ref,
    back_ref, weight_held, sum_ref, turned_ref, staged_ref, scaled_ref,
    b_send, b_recv, h_send, h_recv, local,
):
    place = Place()
    me = place.me
    met = greet(place.others())
    fetch = pltpu.make_async_copy(weight_ref, weight_held, local.at[0])
    rows, width = residual_ref.shape

    def copy(source, target, send, receive, j):
        to = lax.rem(me + j, GROUP)
        return remote(source.at[to], target.at[me], send.at[j], receive.at[j], place.ctx(to))

    backs = [copy(sent_grad_ref, back_ref, b_send, b_recv, j) for j in range(1, GROUP)]
    met()
    for one in backs:
        one.start()
    move = pltpu.make_async_copy(sent_grad_ref.at[me], back_ref.at[me], local.at[1])
    move.start()
    turned_ref[...] = jnp.zeros_like(turned_ref)
    stage.need(out_ref, placed_ref, slot_gates_ref, cotangent_ref)
    stage.begin()
    fetch.start()

    def add_expert(e, _):
        came = out_ref[e].astype(f32)
        scaled_ref[e] = (came * slot_gates_ref[e]).astype(bf16)
        routed = dot(placed_ref[e], cotangent_ref[...])
        slot_grad = jnp.sum(routed * came, axis=1, keepdims=True)
        turned_ref[pl.ds(e, 1), :] = jnp.sum(
            placed_ref[e].astype(f32) * slot_grad, axis=0, keepdims=True
        )
        return 0

    lax.fori_loop(0, EXP_WIN, add_expert, 0)
    stage.need(placed_t_ref, residual_ref, gates_ref, w_all_ref, normed_ref)
    slots = EXP_WIN * CAP

    def mix(i, _):
        columns = block(i)
        mixed = dot(placed_t_ref[...], scaled_ref[:, :, columns].reshape(slots, TOK_DEV))
        output_ref[:, columns] = (residual_ref[:, columns] + mixed).astype(bf16)
        return 0

    lax.fori_loop(0, width // TOK_DEV, mix, 0)
    stage.put(output_ref)
    gates = gates_ref[...]
    grad_gates = turned_ref[...]
    weighted = jnp.sum(gates * grad_gates, axis=0, keepdims=True)
    grad_logits = (gates * (grad_gates - weighted)).astype(bf16)
    for s, router in enumerate(router_of(w_all_ref)):
        size = router.shape[1]
        sum_ref[:, s * size : (s + 1) * size] = dot(grad_logits, router, ((0,), (0,)))
    grad_router_ref[...] = dot(grad_logits, normed_ref[...])
    fetch.wait()
    move.wait()
    for one in backs:
        one.wait_recv()

    def add_back(i, _):
        columns = block(i)
        sum_ref[:, columns] += dot(
            placed_t_ref[...], back_ref[:, :, columns].reshape(slots, TOK_DEV)
        )
        return 0

    lax.fori_loop(0, width // TOK_DEV, add_back, 0)
    residual = residual_ref[...]
    grad_normed = sum_ref[...]
    scale = lax.rsqrt(jnp.mean(residual * residual, axis=-1, keepdims=True) + epsilon)
    scaled = grad_normed * gain_ref[...].reshape(1, -1)
    inner = jnp.mean(scaled * residual, axis=-1, keepdims=True)
    grad = scale * scaled - residual * (scale * scale * scale * inner)
    grad_gain_ref[...] = jnp.sum(grad_normed * residual * scale, axis=0, keepdims=True)
    grad_residual = cotangent_ref[...].astype(f32) + grad
    grad_residual_ref[...] = grad_residual
    attn_ref[...] = grad_residual.astype(bf16)
    stage.put(grad_residual_ref, attn_ref, grad_router_ref, grad_gain_ref)

    def head_rows(j, _):
        to = lax.rem(me + j, GROUP)
        staged_ref[to] = dot(weight_held[block(to, QW), :], attn_ref[...], ((1,), (1,))).astype(bf16)

        @pl.when(j < GROUP)
        def _():
            copy(staged_ref, heads_ref, h_send, h_recv, j).start()

        return 0

    lax.fori_loop(1, GROUP + 1, head_rows, 0)
    move = pltpu.make_async_copy(staged_ref.at[me], heads_ref.at[me], local.at[2])
    move.start()
    for one in backs:
        one.wait_send()
    for j in range(1, GROUP):
        copy(staged_ref, heads_ref, h_send, h_recv, j).wait()
    move.wait()


def combine_call(
    out, sent_grad, weight, residual, normed, gates, placed, placed_t, slot_gates, cotangent,
    gain, w_all,
):
    rows, width = residual.shape
    slots = (GROUP, CAP, width)
    return staged_call(
        combine_kernel,
        "combine",
        4,
        [
            ("h", out),
            ("a", sent_grad),
            ("a", weight),
            ("l", residual),
            ("l", normed),
            ("l", gates),
            ("h", placed),
            ("l", placed_t),
            ("h", slot_gates),
            ("h", cotangent),
            ("v", gain),
            ("l", w_all),
        ],
        [
            ("h", shape((rows, width), bf16)),
            ("h", shape((rows, width), f32)),
            ("a", shape((GROUP, QW, rows), bf16)),
            ("h", shape((rows, width), bf16)),
            ("h", shape((ROUTER, width), f32)),
            ("h", shape((1, width), f32)),
        ],
        [
            VMEM(slots, bf16),
            VMEM(weight.shape, bf16),
            VMEM((rows, width), f32),
            VMEM((ROUTER, rows), f32),
            VMEM((GROUP, QW, rows), bf16),
            VMEM(slots, bf16),
        ]
        + [DMA((GROUP,))] * 4
        + [DMA((3,))],
    )


def backward_kernel(
    n_blocks, stage, attn_ref, attended_ref, down_ref, heads_ref, o_ref, lse_ref, qt_ref, k_ref,
    kt_ref, v_ref, docs_ref,
    dq_ref, dk_ref, dv_ref, grad_out_ref, down_all_ref,
    part_ref, pair_ref, strip_ref, came_ref, docs_col_ref, delta_ref, dk_acc, dv_acc,
    p_send, p_recv, s_send, s_recv, e_send, e_recv, local,
):
    T = TOK_DEV
    place = Place()
    me = place.me
    first = place.base
    core, side, row = place.near
    across = flip(side, 4)
    met = greet([place.ctx(i) for i in (core, side, row, across)])
    half = GROUP // 2
    depth, strip, width = grad_out_ref.shape
    parity = lax.rem(me, 2)

    def strip_of(n, parity):
        return 2 * n + parity

    def part(n, parity):
        rows = attended_ref[:, strip_of(n, parity)].reshape(depth * strip, T)
        return dot(rows, attn_ref[...])

    def pair_copy(n):
        return remote(
            part_ref.at[n], pair_ref.at[n], p_send.at[n], p_recv.at[n], place.ctx(core)
        )

    def pair_part(n, _):
        part_ref[n] = part(n, 1 - parity).astype(bf16)
        pair_copy(n).start()
        return 0

    down_move = pltpu.make_async_copy(down_ref, down_all_ref.at[me], local.at[0])
    down_spread = Spread(
        place, down_ref, lambda owner: down_all_ref.at[owner], halves(down_ref.shape[0]), e_send, e_recv
    )
    stage.need(attn_ref, attended_ref)
    stage.begin()
    met()
    lax.fori_loop(0, half, pair_part, 0)
    stage.need(down_ref)
    down_spread.start()
    down_move.start()

    heads = range(HEADS)
    parts = [slice(h * HEAD_DIM, (h + 1) * HEAD_DIM) for h in heads]
    stage.need(heads_ref, o_ref)

    def prepare(i, _):
        for h in heads:
            product = o_ref[parts[h], block(i)] * heads_ref[i, parts[h], :].astype(f32)
            delta_ref[i, h : h + 1, :] = jnp.sum(product, axis=0, keepdims=True)
        return 0

    lax.fori_loop(0, GROUP, prepare, 0)
    for n in range(half):
        pair_copy(n).wait_recv()

    def add_pair(n, _):
        strip_ref[n] = (part(n, parity) + pair_ref[n].astype(f32)).astype(bf16)
        return 0

    lax.fori_loop(0, half, add_pair, 0)
    strips = [
        remote(
            strip_ref.at[lax.div(device, 2)], came_ref.at[n], s_send.at[n], s_recv.at[n],
            place.ctx(device),
        )
        for n, device in enumerate((across, side, row))
    ]
    for copy in strips:
        copy.start()

    def turn(i, _):
        docs_col_ref[i] = docs_column(docs_ref[i])
        return 0

    lax.fori_loop(0, n_blocks, turn, 0)
    stage.need(lse_ref, qt_ref, k_ref, kt_ref, v_ref)
    dq_ref[...] = jnp.zeros_like(dq_ref)

    def tile(kb, qb, mask):
        k = k_ref[block(kb), :]
        v = v_ref[block(kb), :]
        kt = kt_ref[:, block(kb)]
        q = [qt_ref[part, block(qb)] for part in parts]
        do = [heads_ref[qb, part, :] for part in parts]
        s = [dot(k, x) for x in q]
        dp = [dot(v, x) for x in do]
        p = [jnp.exp(s[h] - lse_ref[qb, h : h + 1, :]) for h in heads]
        if mask is not None:
            p = [jnp.where(mask, x, 0.0) for x in p]
        ds = [(p[h] * (dp[h] - delta_ref[qb, h : h + 1, :])).astype(bf16) for h in heads]
        pb = [x.astype(bf16) for x in p]
        turn = ((1,), (1,))
        dv_acc[...] += dot(pb[0], do[0], turn) + dot(pb[1], do[1], turn) + dot(pb[2], do[2], turn)
        dk_acc[...] += dot(ds[0], q[0], turn) + dot(ds[1], q[1], turn) + dot(ds[2], q[2], turn)
        for h in heads:
            dq_ref[parts[h], block(qb)] += dot(kt, ds[h])

    def same(kb, gq):
        return docs_col_ref[kb] == docs_ref[gq].astype(f32)

    def k_block(kb, _):
        for at, act in (
            (2, down_spread.step1), (4, down_spread.step2), (7, down_spread.step3),
        ):
            pl.when(kb == first + at)(act)
        dk_acc[...] = jnp.zeros_like(dk_acc)
        dv_acc[...] = jnp.zeros_like(dv_acc)

        @pl.when(kb >= first)
        def _():
            keys = lax.broadcasted_iota(jnp.int32, (T, T), 0)
            queries = lax.broadcasted_iota(jnp.int32, (T, T), 1)
            tile(kb, kb - first, same(kb, kb) & (keys <= queries))

        def q_block(qb, _):
            gq = first + qb
            edge = jnp.logical_or(kb == 0, gq == n_blocks - 1)

            @pl.when(edge)
            def _():
                tile(kb, qb, same(kb, gq))

            @pl.when(jnp.logical_not(edge))
            def _():
                tile(kb, qb, None)

            return 0

        lax.fori_loop(jnp.maximum(kb - first + 1, 0), GROUP, q_block, 0)
        dk_ref[:, block(kb)] = dk_acc[...].T
        dv_ref[:, block(kb)] = dv_acc[...].T
        return 0

    lax.fori_loop(0, first + GROUP, k_block, 0)

    def clear(kb, _):
        dk_ref[:, block(kb)] = jnp.zeros((HEAD_DIM, T), f32)
        dv_ref[:, block(kb)] = jnp.zeros((HEAD_DIM, T), f32)
        return 0

    lax.fori_loop(first + GROUP, n_blocks, clear, 0)
    stage.put(dq_ref, dk_ref, dv_ref)
    for copy in strips:
        copy.wait_recv()
    total = strip_ref[lax.div(me, 2)].astype(f32)
    for n in range(len(strips)):
        total = total + came_ref[n].astype(f32)
    grad_out_ref[...] = total.astype(bf16).reshape(depth, strip, width)
    stage.put(grad_out_ref)
    down_spread.last()
    down_spread.sent()
    for n in range(half):
        pair_copy(n).wait_send()
    for copy in strips:
        copy.wait_send()
    down_move.wait()


def backward_call(attn, attended, down, heads, o, lse, qt, k, kt, v, docs):
    n = k.shape[0] // TOK_DEV
    span = qt.shape[1]
    rows, width = attn.shape
    depth, _, strip, _ = attended.shape
    block_rows = depth * strip
    half = GROUP // 2
    return staged_call(
        functools.partial(backward_kernel, n),
        "backward",
        5,
        [("h", attn), ("h", attended)]
        + [("l", one) for one in (down, heads, o, lse, qt, k, kt, v)]
        + [("v", docs)],
        [
            ("h", shape((QW, span), f32)),
            ("h", shape(kt.shape, f32)),
            ("h", shape(kt.shape, f32)),
            ("h", shape((depth, strip, width), bf16)),
            ("a", shape((GROUP,) + down.shape, bf16)),
        ],
        [
            VMEM((half, block_rows, width), bf16),
            VMEM((half, block_rows, width), bf16),
            VMEM((half, block_rows, width), bf16),
            VMEM((3, block_rows, width), bf16),
            VMEM((n, TOK_DEV, 1), f32),
            VMEM((GROUP, 8, TOK_DEV), f32),
            VMEM((TOK_DEV, HEAD_DIM), f32),
            VMEM((TOK_DEV, HEAD_DIM), f32),
        ]
        + [DMA((half,))] * 2
        + [DMA((3,))] * 2
        + [DMA((Spread.SEMS,))] * 2
        + [DMA((1,))],
    )


def finish_kernel(
    stage, normed_ref, weights_ref, gate_up_ref, grad_out_ref, dq_ref, dk_ref, dv_ref, cos_ref,
    sin_ref, tokens_ref, gain_ref, grad_residual_ref, grad_router_ref, grad_gain2_ref,
    input_grad_ref, shared_ref, small_all_ref, out_all_ref, gate_up_all_ref,
    normed_held, weights_held, linear_ref, came_ref, came_t, sum_ref, part_ref,
    small_ref, head_in, small_in, out_in, shard_ref, small_shard_ref, out_shard_ref,
    g_send, g_recv, h_send, h_recv, s_send, s_recv, o_send, o_recv, e_send, e_recv, f_send, f_recv,
    m_send, m_recv, c_send, c_recv, local,
):
    place = Place()
    me, z, depth = place.me, place.z, place.depth
    met = greet(place.others() + place.layers())
    fetches = [
        pltpu.make_async_copy(normed_ref, normed_held, local.at[0]),
        pltpu.make_async_copy(weights_ref, weights_held, local.at[1]),
    ]
    rows, width = tokens_ref.shape
    size = width // depth

    def spread_of(source, out, send, receive):
        return Spread(
            place, source, lambda owner: out.at[owner], halves(source.shape[0]), send, receive
        )

    expert_spread = spread_of(gate_up_ref, gate_up_all_ref, e_send, e_recv)
    head_spread = spread_of(shard_ref, shared_ref, f_send, f_recv)
    small_spread = spread_of(small_shard_ref, small_all_ref, m_send, m_recv)
    out_spread = spread_of(out_shard_ref, out_all_ref, c_send, c_recv)
    moves = [
        pltpu.make_async_copy(gate_up_ref, gate_up_all_ref.at[me], local.at[3]),
        pltpu.make_async_copy(out_shard_ref, out_all_ref.at[me], local.at[4]),
        pltpu.make_async_copy(shard_ref, shared_ref.at[me], local.at[5]),
        pltpu.make_async_copy(small_shard_ref, small_all_ref.at[me], local.at[6]),
    ]

    def copy(j):
        to = lax.rem(me + j, GROUP)
        return remote(
            linear_ref.at[to], came_ref.at[me], g_send.at[j], g_recv.at[j], place.ctx(to)
        )

    def down(source, target, send, receive, j):
        to = lax.rem(z + j, depth)
        return remote(source.at[to], target.at[z], send.at[j], receive.at[j], place.fsdp(to))

    stage.need(dq_ref, dk_ref, dv_ref, cos_ref, sin_ref)
    stage.begin()
    for fetch in fetches:
        fetch.start()

    def turn_back(j, _):
        to = lax.rem(me + j, GROUP)
        cosine, sine = cos_ref[:, block(to)], -sin_ref[:, block(to)]
        dq = turned(dq_ref[:, block(to)], cosine, sine) * HEAD_DIM ** (-0.5)
        dk = turned(dk_ref[:, block(to)], cosine, sine)
        linear_ref[to, :QW, :] = dq.astype(bf16)
        linear_ref[to, QW : QW + HEAD_DIM, :] = dk.astype(bf16)
        linear_ref[to, QW + HEAD_DIM :, :] = dv_ref[:, block(to)].astype(bf16)
        pl.when(j == 1)(met)

        @pl.when(j < GROUP)
        def _():
            copy(j).start()

        return 0

    lax.fori_loop(1, GROUP + 1, turn_back, 0)
    stage.need(gate_up_ref, grad_out_ref)
    moves[0].start()
    outs = [down(grad_out_ref, out_in, o_send, o_recv, j) for j in range(1, depth)]
    out_in[z] = grad_out_ref[z]
    came_ref[me] = linear_ref[me]
    fetches[0].wait()

    def own_weights(j, _):
        to = lax.rem(z + j, depth)
        columns = block(to, size)
        total = None
        for b in range(GROUP):
            term = dot(linear_ref[b], normed_held[b, :, columns])
            total = term if total is None else total + term
        part_ref[to] = total.astype(bf16)

        @pl.when(j < depth)
        def _():
            down(part_ref, head_in, h_send, h_recv, j).start()

        return 0

    lax.fori_loop(1, depth + 1, own_weights, 0)
    for one in outs:
        one.start()

    def total(ref):
        value = ref[0].astype(f32)
        for s in range(1, depth):
            value = value + ref[s].astype(f32)
        return value.astype(bf16)

    expert_spread.start()
    for j in range(1, GROUP):
        copy(j).wait_send()
    fetches[1].wait()
    for j in range(1, GROUP):
        copy(j).wait_recv()

    def turn(j, _):
        came_t[j] = came_ref[j].T
        return 0

    lax.fori_loop(0, GROUP, turn, 0)

    def add_heads(s, _):
        total = None
        for j in range(GROUP):
            term = dot(came_t[j], weights_held[j, s])
            total = term if total is None else total + term
        sum_ref[:, block(s, size)] = total
        return 0

    lax.fori_loop(0, depth, add_heads, 0)
    stage.need(tokens_ref, grad_residual_ref, grad_router_ref, grad_gain2_ref)
    x = tokens_ref[...].astype(f32)
    grad_normed = sum_ref[...]
    scale = lax.rsqrt(jnp.mean(x * x, axis=-1, keepdims=True) + epsilon)
    scaled = grad_normed * gain_ref[...].reshape(1, -1)
    inner = jnp.mean(scaled * x, axis=-1, keepdims=True)
    grad = scale * scaled - x * (scale * scale * scale * inner)
    input_grad_ref[...] = grad_residual_ref[...] + grad
    stage.put(input_grad_ref)
    gain1 = jnp.sum(grad_normed * x * scale, axis=0, keepdims=True)
    row = lax.broadcasted_iota(jnp.int32, (ROUTER, width), 0)
    small = jnp.where(row == ROUTER - 2, gain1, grad_router_ref[...])
    small = jnp.where(row == ROUTER - 1, grad_gain2_ref[...], small).astype(bf16)
    for s in range(depth):
        small_ref[s] = small[:, s * size : (s + 1) * size]
    smalls = [down(small_ref, small_in, s_send, s_recv, j) for j in range(1, depth)]
    heads = [down(part_ref, head_in, h_send, h_recv, j) for j in range(1, depth)]
    for one in smalls:
        one.start()
    expert_spread.step1()
    head_in[z] = part_ref[z]
    small_in[z] = small_ref[z]

    for one in heads:
        one.wait_recv()
    shard_ref[...] = total(head_in)
    head_spread.start()
    expert_spread.step2()
    for one in outs:
        one.wait_recv()
    out_shard_ref[...] = total(out_in)
    out_spread.start()
    for one in smalls:
        one.wait_recv()
    small_shard_ref[...] = total(small_in)
    small_spread.start()
    head_spread.step1()
    for move in moves[1:]:
        move.start()
    expert_spread.step3()
    spreads = (head_spread, out_spread, small_spread)
    for spread in spreads[1:]:
        spread.step1()
    for spread in spreads:
        spread.step2()
    for spread in spreads:
        spread.step3()
    for spread in (out_spread, expert_spread, head_spread, small_spread):
        spread.last()
        spread.sent()
    for one in heads + smalls + outs:
        one.wait_send()
    for move in moves:
        move.wait()


def finish_call(
    normed, weights, gate_up, grad_out, dq, dk, dv, cosine, sine, tokens, gain, grad_residual,
    grad_router, grad_gain2,
):
    rows, width = tokens.shape
    depth, strip, _ = grad_out.shape
    size = width // depth
    return staged_call(
        finish_kernel,
        "finish",
        6,
        [
            ("a", normed),
            ("a", weights),
            ("l", gate_up),
            ("l", grad_out),
            ("h", dq),
            ("h", dk),
            ("h", dv),
            ("h", cosine),
            ("h", sine),
            ("l", tokens),
            ("v", gain),
            ("l", grad_residual),
            ("l", grad_router),
            ("l", grad_gain2),
        ],
        [
            ("h", shape((rows, width), f32)),
            ("a", shape((GROUP, HW, size), bf16)),
            ("a", shape((GROUP, ROUTER, size), bf16)),
            ("a", shape((GROUP, strip, width), bf16)),
            ("a", shape((GROUP,) + gate_up.shape, bf16)),
        ],
        [
            VMEM(normed.shape, bf16),
            VMEM(weights.shape, bf16),
            VMEM((GROUP, HW, rows), bf16),
            VMEM((GROUP, HW, rows), bf16),
            VMEM((GROUP, rows, HW), bf16),
            VMEM((rows, width), f32),
            VMEM((depth, HW, size), bf16),
            VMEM((depth, ROUTER, size), bf16),
            VMEM((depth, HW, size), bf16),
            VMEM((depth, ROUTER, size), bf16),
            VMEM((depth, strip, width), bf16),
            VMEM((HW, size), bf16),
            VMEM((ROUTER, size), bf16),
            VMEM((strip, width), bf16),
        ]
        + [DMA((GROUP,))] * 2
        + [DMA((depth,))] * 6
        + [DMA((Spread.SEMS,))] * 8
        + [DMA((7,))],
    )


def output_kernel(
    shared_ref, small_ref, out_ref, gate_up_ref, down_ref, output_ref, input_grad_ref,
    q_ref, k_ref, v_ref, w_out_ref, router_ref, gain1_ref, gain2_ref, gate_ref, up_ref, w_down_ref,
    final_ref, final_grad_ref,
):
    pair, i = shared_ref.shape[0], pl.program_id(0)
    hidden = gate_ref.shape[2]

    def rows(first, last):
        both = [shared_ref[p, first:last, :].astype(f32) for p in range(pair)]
        return jnp.concatenate(both, axis=0).T

    @pl.when(lax.rem(i, pair) == 0)
    def _():
        q_ref[...] = rows(0, QW)
        k_ref[...] = rows(QW, QW + HEAD_DIM)
        v_ref[...] = rows(QW + HEAD_DIM, HW)

    w_out_ref[...] = out_ref[...].astype(f32)
    gate_ref[...] = gate_up_ref[:, :, :hidden].astype(f32)
    up_ref[...] = gate_up_ref[:, :, hidden:].astype(f32)
    w_down_ref[...] = down_ref[...].astype(f32)
    final_ref[...] = output_ref[...]
    final_grad_ref[...] = input_grad_ref[...]

    @pl.when(i == 0)
    def _():
        total = jnp.sum(small_ref[...].astype(f32), axis=0)
        router_ref[...] = total[: router_ref.shape[0], :]
        gain1_ref[...] = total[ROUTER - 2, :]
        gain2_ref[...] = total[ROUTER - 1, :]


def output_call(shared, small, out, gate_up, down, output, input_grad, experts):
    count, _, size = shared.shape
    _, strip, width = out.shape
    hidden = gate_up.shape[2] // 2
    pair = 2
    rows = output.shape[0] // count
    token = pl.BlockSpec((rows, width), lambda i: (i, 0))

    def first(*dims):
        return pl.BlockSpec((1,) + dims, lambda i: (i,) + (0,) * len(dims))

    def columns(columns):
        return pl.BlockSpec((size, columns), lambda i: (0, i // pair))

    def whole(*dims):
        return pl.BlockSpec(dims, lambda i: (0,) * len(dims))

    return pl.pallas_call(
        output_kernel,
        grid=(count,),
        out_shape=(
            shape((size, count * QW), f32),
            shape((size, count * HEAD_DIM), f32),
            shape((size, count * HEAD_DIM), f32),
            shape(out.shape, f32),
            shape((experts, size), f32),
            shape((size,), f32),
            shape((size,), f32),
            shape((count, size, hidden), f32),
            shape((count, size, hidden), f32),
            shape(down.shape, f32),
            shape(output.shape, bf16),
            shape(input_grad.shape, f32),
        ),
        in_specs=[
            pl.BlockSpec((pair,) + shared.shape[1:], lambda i: (i // pair, 0, 0)),
            whole(*small.shape), first(strip, width), first(*gate_up.shape[1:]),
            first(*down.shape[1:]), token, token,
        ],
        out_specs=(
            columns(pair * QW),
            columns(pair * HEAD_DIM),
            columns(pair * HEAD_DIM),
            first(strip, width),
            whole(experts, size),
            whole(size),
            whole(size),
            first(size, hidden),
            first(size, hidden),
            first(*down.shape[1:]),
            token,
            token,
        ),
        compiler_params=params(),
        name="output",
    )(shared, small, out, gate_up, down, output, input_grad)


def rotary_tables(length):
    frequencies = 10000.0 ** (-(np.arange(HEAD_DIM // 2) * 2.0) / HEAD_DIM)
    angles = frequencies[:, None] * np.arange(length)[None, :]
    return np.cos(angles).astype(np.float32), np.sin(angles).astype(np.float32)


def shards(
    tables,
    tokens,
    doc_ids,
    routes,
    slot_order,
    norm1_gain,
    norm2_gain,
    w_query,
    key_matrix,
    value_matrix,
    w_out,
    w_router,
    w_gate,
    w_up,
    w_down,
    cotangent,
):
    rows, width = tokens.shape[1:]
    ctx, depth = lax.axis_size("ctx"), lax.axis_size("fsdp")
    place = lax.axis_index("ctx")
    parts = ctx // GROUP
    head, part = place % GROUP, place // GROUP
    far = [[p * GROUP + i for p in range(parts)] for i in range(GROUP)]
    span = GROUP * rows
    experts = w_router.shape[1]
    hidden = w_gate.shape[2]

    def gather_z(value):
        return lax.all_gather(value, "fsdp", axis=0, tiled=True)

    def reduce_z(value):
        value = lax.psum_scatter(value.astype(bf16), "fsdp", scatter_dimension=0, tiled=True)
        if parts > 1:
            value = lax.psum(value, "ctx", axis_index_groups=far)
        return value

    cosine, sine = tables
    if parts > 1:
        cosine = lax.dynamic_slice_in_dim(cosine, part * span, span, 1)
        sine = lax.dynamic_slice_in_dim(sine, part * span, span, 1)
    own_tokens, own_cotangent = tokens[0], cotangent[0]

    route_rows, order_rows = routes[0].T, slot_order[0].T
    docs, placed, placed_t, tokens_all, w_all, strips, gate_up, down = gather_call(
        own_tokens, w_router.T, doc_ids, route_rows, order_rows, w_query, key_matrix, value_matrix,
        w_out, w_gate, w_up, w_down, depth,
    )
    gate_up, down = gather_z(gate_up), gather_z(down)
    if parts > 1:

        def gather_far(value, axis):
            return lax.all_gather(value, "ctx", axis=axis, axis_index_groups=far, tiled=True)

        normed1, queries, keys_t, values_t, keys, values = project_call(
            tokens_all, norm1_gain, w_all, cosine, sine
        )
        keys, values, docs = gather_far(keys, 0), gather_far(values, 0), gather_far(docs, 0)
        keys_t, values_t = gather_far(keys_t, 1), gather_far(values_t, 1)
        after = attend_call(
            attend_kernel, [w_all, queries, keys, values_t], [], docs, strips, own_tokens, norm2_gain,
            route_rows, placed, w_all, span, [],
        )
    else:
        normed1, queries, keys_t, values_t, keys, values, *after = attend_call(
            attend_after_project, [w_all, tokens_all, cosine, sine], [norm1_gain], docs, strips,
            own_tokens, norm2_gain, route_rows, placed, w_all, span, projected(tokens_all),
        )
    (
        attended_f32, log_total, attended, out_weight, weights_all, residual, normed2, gates,
        slot_gates, rows_out,
    ) = after
    out_weight = out_weight.reshape(width, width)
    sent_rows, sent_grads, gate, up, active, grad_w_down = dispatch_call(
        rows_out, gate_up, placed, own_cotangent, slot_gates
    )
    grad_w_down = reduce_z(grad_w_down)
    expert_out, grad_buffer, grad_w_gate_up = expert_call(
        active, down, sent_grads.reshape(GROUP * CAP, width), sent_rows.reshape(GROUP * CAP, width),
        gate, up, gate_up,
    )
    grad_w_gate_up = reduce_z(grad_w_gate_up)
    output, grad_residual, heads, attn, grad_router, grad_gain2 = combine_call(
        expert_out, grad_buffer.reshape(sent_rows.shape), out_weight,
        residual, normed2, gates, placed, placed_t, slot_gates, own_cotangent, norm2_gain, w_all,
    )
    dq, dk, dv, grad_out, down_w = backward_call(
        attn, attended, grad_w_down, heads, attended_f32, log_total, queries, keys, keys_t, values,
        docs,
    )
    if parts > 1:
        dk = lax.psum_scatter(dk, "ctx", scatter_dimension=1, axis_index_groups=far, tiled=True)
        dv = lax.psum_scatter(dv, "ctx", scatter_dimension=1, axis_index_groups=far, tiled=True)
    input_grad, shared, small, out_w, gate_up_w = finish_call(
        normed1, weights_all, grad_w_gate_up, grad_out, dq, dk, dv, cosine, sine,
        own_tokens, norm1_gain, grad_residual, grad_router, grad_gain2,
    )
    if parts > 1:
        shared, small, out_w = lax.psum((shared, small, out_w), "ctx", axis_index_groups=far)

    (
        q_w, k_w, v_w, out_w, router_w, gain1_w, gain2_w, gate_w, up_w, down_w, output, input_grad
    ) = output_call(shared, small, out_w, gate_up_w, down_w, output, input_grad, experts)
    return (
        output[None],
        input_grad[None],
        gain1_w,
        gain2_w,
        q_w,
        k_w,
        v_w,
        out_w.reshape(-1, width),
        router_w.T,
        gate_w,
        up_w,
        down_w,
    )


def solution(mesh):
    token_spec = P("fsdp", "ctx", None)
    row_spec, expert_spec = P("fsdp", None), P(None, "fsdp", None)
    tables = rotary_tables(mesh.shape["ctx"] * TOK_DEV)

    def program(*arguments):
        return jax.shard_map(
            functools.partial(shards, tuple(jnp.asarray(t) for t in tables)),
            mesh=mesh,
            in_specs=(
                token_spec,
                P("fsdp", "ctx"),
                token_spec,
                token_spec,
                P(),
                P(),
                row_spec,
                row_spec,
                row_spec,
                row_spec,
                row_spec,
                expert_spec,
                expert_spec,
                expert_spec,
                token_spec,
            ),
            out_specs=(
                token_spec,
                token_spec,
                P("fsdp"),
                P("fsdp"),
                row_spec,
                row_spec,
                row_spec,
                row_spec,
                row_spec,
                expert_spec,
                expert_spec,
                expert_spec,
            ),
            check_vma=False,
        )(*arguments)

    return program
```
